32 devices in a mesh: dp: 4 (over z), seq: 8 (over y, x, core).
Axes of the slice: x: 2, y: 2, z: 4, core: 2. Of those that a mesh axis runs over, the one named last changes fastest.
Arguments:
- tokens: bfloat16 [8, 1024, 2048], P('dp', 'seq'), may hold values from -6 to 6
- doc_ids: int32 [8, 1024], P('dp'), may hold values from 0 to 4, as said below
- cotangent: bfloat16 [8, 1024, 2048], P('dp', 'seq'), may hold values from -6 to 6
- norm1_gain: bfloat16 [2048], P(('dp', 'seq')), may hold values from 0.099609375 to 1.8984375
- w_query: bfloat16 [2048, 2048], P(('dp', 'seq')), may hold values from -0.125 to 0.125
- w_key: bfloat16 [2048, 2048], P(('dp', 'seq')), may hold values from -0.125 to 0.125
- w_value: bfloat16 [2048, 2048], P(('dp', 'seq')), may hold values from -0.125 to 0.125
- w_out: bfloat16 [2048, 2048], P(('dp', 'seq')), may hold values from -1 to 1
- norm2_gain: bfloat16 [2048], P(('dp', 'seq')), may hold values from 0.099609375 to 1.8984375
- w_gate: bfloat16 [2048, 8192], P(('dp', 'seq')), may hold values from -0.125 to 0.125
- w_up: bfloat16 [2048, 8192], P(('dp', 'seq')), may hold values from -0.125 to 0.125
- w_down: bfloat16 [8192, 2048], P(('dp', 'seq')), may hold values from -0.0625 to 0.0625
Outputs:
- out_tokens: bfloat16 [8, 1024, 2048], P('dp', 'seq')
- grad_tokens: bfloat16 [8, 1024, 2048], P('dp', 'seq')
- grad_norm1: float32 [2048], P(('dp', 'seq'))
- grad_query: float32 [2048, 2048], P(('dp', 'seq'))
- grad_key: float32 [2048, 2048], P(('dp', 'seq'))
- grad_value: float32 [2048, 2048], P(('dp', 'seq'))
- grad_out: float32 [2048, 2048], P(('dp', 'seq'))
- grad_norm2: float32 [2048], P(('dp', 'seq'))
- grad_gate: float32 [2048, 8192], P(('dp', 'seq'))
- grad_up: float32 [2048, 8192], P(('dp', 'seq'))
- grad_down: float32 [8192, 2048], P(('dp', 'seq'))
The draws below stay inside these ranges and needn't reach their ends.
Inputs may be any that keep to these rules, and one draw needn't show every extreme that they name: `doc_ids`: each row holds exactly five documents numbered 0 to 4 in order, each of one token or more; document 2 begins within the first 128 tokens of its row and ends within the last 128.
All inputs are finite; a program needn't handle non-finite values.
Results may differ from the reference program's by a relative error of at most 0.017.
Values may be sent and summed in bfloat16 or wider, within the bound.
A program may use at most 640 MiB of HBM per device.

```python
from functools import partial
import jax
import jax.numpy as jnp
from jax import lax

D = 2048
H = 32
HD = 64
FF = 8192
LEN = 1024
SHARD_LEN = 128
ROWS = 8


def draw_doc_ids(key, part):
    key = jax.random.fold_in(key, 11)
    key_head, key_cut, key_tail, key_end = jax.random.split(key, 4)
    head_len = jax.random.randint(key_head, (ROWS,), 2, SHARD_LEN)
    first_cut = jax.random.randint(key_cut, (ROWS,), 1, head_len)
    tail_len = jax.random.randint(key_tail, (ROWS,), 2, SHARD_LEN)
    tail_cut = LEN - tail_len + jax.random.randint(key_end, (ROWS,), 1, tail_len)
    places = jnp.arange(LEN, dtype=jnp.int32)[None, :]
    doc_ids = (places >= first_cut[:, None]).astype(jnp.int32)
    doc_ids = doc_ids + (places >= head_len[:, None]).astype(jnp.int32)
    doc_ids = doc_ids + (places >= (LEN - tail_len)[:, None]).astype(jnp.int32)
    doc_ids = doc_ids + (places >= tail_cut[:, None]).astype(jnp.int32)
    return doc_ids.astype(jnp.int32)


def block_levels(key, extent, cuts, least, top_value):
    level, own = 1.0, jax.random.fold_in(key, 6)
    for dim, blocks in cuts:
        draws = jnp.exp(jax.random.uniform(jax.random.fold_in(own, dim), (blocks,), jnp.float32, least / len(cuts), top_value / len(cuts)))
        level = level * jnp.repeat(draws, extent[dim] // blocks).reshape([-1 if axis == dim else 1 for axis in range(len(extent))])
    return level


def normal_values(stream_key, shape, width, bound, pieces=(), held_as=jnp.bfloat16):
    values = width * jax.random.normal(stream_key, shape, jnp.float32)
    if pieces:
        values = values * block_levels(stream_key, shape, pieces, -0.22, 0.18)
    return jnp.clip(values, -bound, bound).astype(held_as)


def setup_inputs(seed: int = 0) -> dict:
    key_of = jax.random.split(jax.random.key(seed), 13)
    return {
        "tokens": normal_values(key_of[0], (ROWS, LEN, D), 1.0, 6.0, ((0, 4), (1, 8))),
        "doc_ids": draw_doc_ids(jax.random.fold_in(key_of[12], 71), 0),
        "cotangent": normal_values(key_of[2], (ROWS, LEN, D), 1.0, 6.0, ((0, 4), (1, 8))),
        "norm1_gain": jnp.clip(1.0 + 0.18 * jax.random.normal(key_of[3], (D,), jnp.float32), 0.099609375, 1.8984375).astype(jnp.bfloat16),
        "w_query": normal_values(key_of[4], (D, D), D ** -0.5, 0.125, ((0, 32),)),
        "w_key": normal_values(key_of[5], (D, D), D ** -0.5, 0.125, ((0, 32),)),
        "w_value": normal_values(key_of[6], (D, D), D ** -0.5, 0.125, ((0, 32),)),
        "w_out": normal_values(key_of[7], (D, D), (D // 64) ** -0.5, 1.0, ((0, 32),)),
        "norm2_gain": jnp.clip(1.0 + 0.18 * jax.random.normal(key_of[8], (D,), jnp.float32), 0.099609375, 1.8984375).astype(jnp.bfloat16),
        "w_gate": normal_values(key_of[9], (D, FF), D ** -0.5, 0.125, ((0, 32),)),
        "w_up": normal_values(key_of[10], (D, FF), D ** -0.5, 0.125, ((0, 32),)),
        "w_down": normal_values(key_of[11], (FF, D), FF ** -0.5, 0.0625, ((0, 32),)),
    }


rope_base = 130000.0
norm_eps = 1e-05
highest = lax.Precision.HIGHEST

@jax.custom_vjp
def low(v):
    return lax.optimization_barrier(v.astype(jnp.bfloat16)).astype(jnp.float32)

@jax.custom_vjp
def low_back(v):
    return v

def low_keep(v):
    return (low(v), None)

def low_pass(kept, grad):
    return (grad,)

def back_keep(v):
    return (v, None)

def back_low(kept, grad):
    return (low(grad),)
low.defvjp(low_keep, low_pass)
low_back.defvjp(back_keep, back_low)

def rope_angles(doc_ids, head_size):
    places = lax.broadcasted_iota(jnp.int32, doc_ids.shape, 1)
    earlier = jnp.concatenate([doc_ids[:, :1], doc_ids[:, :-1]], axis=1)
    starts = lax.cummax(jnp.where(doc_ids != earlier, places, 0), axis=1)
    positions = (places - starts).astype(jnp.float32)
    frequency = rope_base ** (-(jnp.arange(head_size // 2, dtype=jnp.float32) * 2.0 / head_size))
    angles = positions[..., None] * frequency
    return (jnp.cos(angles), jnp.sin(angles))

def rotate(v, cos_table, sin_table):
    half_size = v.shape[-1] // 2
    lower_half, upper_half = (v[..., :half_size], v[..., half_size:])
    cos_wide = cos_table[..., None, :]
    sin_wide = sin_table[..., None, :]
    return jnp.concatenate([lower_half * cos_wide - upper_half * sin_wide, upper_half * cos_wide + lower_half * sin_wide], axis=-1)

def matmul(left, right):
    return jnp.dot(left, right, precision=highest)

def rms_scale(values):
    return lax.rsqrt(lax.optimization_barrier(jnp.mean(values * values, axis=-1, keepdims=True)) + norm_eps)

def row_layer(weights, row_pair):
    tokens_row, ids_row = row_pair
    gain_one, query_weight, key_weight, value_weight, out_weight, gain_two, gate_weight, up_weight, down_weight = weights
    length = tokens_row.shape[0]
    normed_one = low(tokens_row * rms_scale(tokens_row) * gain_one)
    cos_table, sin_table = rope_angles(ids_row[None, :], HD)
    cos_table, sin_table = (cos_table[0], sin_table[0])
    query_pre = low_back(matmul(normed_one, query_weight)).reshape(length, H, HD)
    key_pre = low_back(matmul(normed_one, key_weight)).reshape(length, H, HD)
    value_low = low(low_back(matmul(normed_one, value_weight))).reshape(length, H, HD)
    query_rot = low(rotate(query_pre, cos_table, sin_table))
    key_rot = low(rotate(key_pre, cos_table, sin_table))
    places = jnp.arange(length, dtype=jnp.int32)
    block_size = min(512, length)

    def attend_block(block_inputs):
        query_block, block_ids, block_places = block_inputs
        raw_scores = low_back(jnp.einsum('qhd,khd->hqk', query_block, key_rot, precision=highest)) * 0.125
        allowed = (block_ids[:, None] == ids_row[None, :]) & (places[None, :] <= block_places[:, None])
        masked = jnp.where(allowed[None], raw_scores, -1e+30)
        row_peak = lax.optimization_barrier(jnp.max(masked, axis=-1, keepdims=True))
        exp_scores = jnp.exp(masked - row_peak)
        soft_probs = low(exp_scores / lax.optimization_barrier(jnp.sum(exp_scores, axis=-1, keepdims=True)))
        return jnp.einsum('hqk,khd->qhd', soft_probs, value_low, precision=highest)
    attended = lax.map(jax.checkpoint(attend_block), (query_rot.reshape(length // block_size, block_size, H, HD), ids_row.reshape(length // block_size, block_size), places.reshape(length // block_size, block_size)))
    attended = low(low_back(attended.reshape(length, H * HD)))
    hidden = tokens_row + low_back(matmul(attended, out_weight))
    normed_two = low(hidden * rms_scale(hidden) * gain_two)
    gate_pre = low_back(matmul(normed_two, gate_weight))
    up_pre = low_back(matmul(normed_two, up_weight))
    activated = low(jax.nn.silu(gate_pre) * up_pre)
    return hidden + low_back(matmul(activated, down_weight))

def reference(tokens, doc_ids, cotangent, norm1_gain, w_query, w_key, w_value, w_out, norm2_gain, w_gate, w_up, w_down):
    weights = tuple((weight_arg.astype(jnp.float32) for weight_arg in (norm1_gain, w_query, w_key, w_value, w_out, norm2_gain, w_gate, w_up, w_down)))
    inputs = tokens.astype(jnp.float32)

    def forward(inputs, weights):
        return lax.map(jax.checkpoint(partial(row_layer, weights)), (inputs, doc_ids))
    result, pullback = jax.vjp(forward, inputs, weights)
    grad_inputs, grad_weights = pullback(cotangent.astype(jnp.float32))
    return (result.astype(jnp.bfloat16), grad_inputs.astype(jnp.bfloat16), grad_weights[0], grad_weights[1], grad_weights[2], grad_weights[3], grad_weights[4], grad_weights[5], grad_weights[6], grad_weights[7], grad_weights[8])
```

```python
import functools

import jax
import jax.numpy as jnp
from jax import lax
from jax.experimental import pallas as pl
from jax.experimental.pallas import tpu as pltpu
from jax.sharding import PartitionSpec as P

H = 32
HD = 64
PAIR = 2 * HD

rope_base = 130000.0
norm_eps = 1e-05

bf16 = jnp.bfloat16
f32 = jnp.float32
MESH = pl.DeviceIdType.MESH
ANY = pl.BlockSpec(memory_space=pl.ANY)
VMEM = pl.BlockSpec(memory_space=pltpu.VMEM)
DMA = pltpu.SemaphoreType.DMA
MIB = 1 << 20


def plane():
    dp, s = lax.axis_index("dp"), lax.axis_index("seq")
    core, xb, yb = lax.rem(s, 2), lax.rem(lax.div(s, 2), 2), lax.div(s, 4)
    at = lambda y, x, c: y * 4 + x * 2 + c
    return dict(
        dp=dp,
        me=s,
        sib=at(yb, xb, 1 - core),
        xp=at(yb, 1 - xb, core),
        yp=at(1 - yb, xb, core),
        dg=at(1 - yb, 1 - xb, core),
        xs=at(yb, 1 - xb, 1 - core),
        ys=at(1 - yb, xb, 1 - core),
        ds=at(1 - yb, 1 - xb, 1 - core),
    )


def greet(p, names):
    barrier = pltpu.get_barrier_semaphore()
    for name in names:
        pl.semaphore_signal(barrier, inc=1, device_id=(p["dp"], p[name]), device_id_type=MESH)
    pl.semaphore_wait(barrier, len(names))


def remote(p, src, dst, send, recv, i, to):
    return pltpu.make_async_remote_copy(
        src_ref=src,
        dst_ref=dst,
        send_sem=send.at[i],
        recv_sem=recv.at[i],
        device_id=(p["dp"], p[to]),
        device_id_type=MESH,
    )


GATHER_SEMS = 25


def gather_start(p, src, out, send, recv, base):
    quarter = src.shape[0] // 4
    part = lambda ref, k: ref.at[pl.ds(k * quarter, quarter)]
    mine = out.at[p["me"]]
    sent = {}
    for j in range(4):
        kx, ky = j, (j + 2) % 4
        sent["x", kx] = remote(p, part(src, kx), part(mine, kx), send, recv, base + kx, "xp")
        sent["y", ky] = remote(p, part(src, ky), part(mine, ky), send, recv, base + 4 + ky, "yp")
        sent["x", kx].start()
        sent["y", ky].start()
    sent["s"] = remote(p, src, mine, send, recv, base + 8, "sib")
    sent["s"].start()
    return sent


def gather_finish(p, sent, src, out, send, recv, base):
    quarter = src.shape[0] // 4
    part = lambda ref, k: ref.at[pl.ds(k * quarter, quarter)]
    passed = []

    def forward(owner, k, i, to):
        ref = part(out.at[p[owner]], k)
        copy = remote(p, ref, ref, send, recv, base + i, to)
        copy.start()
        return copy

    for j in range(4):
        kx, ky = j, (j + 2) % 4
        sent["x", kx].wait_recv()
        if j < 2:
            sent["far", kx] = forward("xp", kx, 9 + kx, "yp")
        passed.append(forward("xp", kx, 13 + kx, "sib"))
        sent["y", ky].wait_recv()
        if j < 2:
            sent["far", ky] = forward("yp", ky, 9 + ky, "xp")
        passed.append(forward("yp", ky, 17 + ky, "sib"))
    for k in (0, 2, 1, 3):
        sent["far", k].wait_recv()
        passed.append(forward("dg", k, 21 + k, "sib"))
    sent["s"].wait_recv()
    for copy in passed:
        copy.wait_recv()
    for copy in list(sent.values()) + passed:
        copy.wait_send()


def gather_kernel(count, *refs):
    sources, outs = refs[:count], refs[count : 2 * count]
    send, recv, local = refs[2 * count :]
    p = plane()
    greet(p, ("sib", "xp", "yp"))
    sent, kept = [], []
    for i in range(count):
        sent.append(gather_start(p, sources[i], outs[i], send, recv, i * GATHER_SEMS))
        kept.append(pltpu.make_async_copy(sources[i], outs[i].at[p["me"]], local.at[i]))
        kept[i].start()
    for i in range(count):
        gather_finish(p, sent[i], sources[i], outs[i], send, recv, i * GATHER_SEMS)
    for copy in kept:
        copy.wait()


def gather_plane(arrays, shards, collective_id):
    if shards != 8:
        return [lax.all_gather(a, "seq") for a in arrays]
    count = len(arrays)
    return pl.pallas_call(
        functools.partial(gather_kernel, count),
        out_shape=[jax.ShapeDtypeStruct((8,) + a.shape, a.dtype) for a in arrays],
        in_specs=[ANY] * count,
        out_specs=[ANY] * count,
        scratch_shapes=[DMA((GATHER_SEMS * count,)), DMA((GATHER_SEMS * count,)), DMA((count,))],
        compiler_params=pltpu.CompilerParams(collective_id=collective_id, has_side_effects=True),
    )(*arrays)


def exchange_kernel(count, *refs):
    sources, outs = refs[:count], refs[count : 2 * count]
    send, recv, local = refs[2 * count :]
    p = plane()
    names = ("dg", "ds", "xp", "yp", "xs", "ys", "sib")
    greet(p, names)
    copies = []
    for i in range(count):
        for j, name in enumerate(names):
            copies.append(
                remote(
                    p, sources[i].at[p[name]], outs[i].at[p["me"]], send, recv, i * 7 + j, name
                )
            )
            copies[-1].start()
        copies.append(
            pltpu.make_async_copy(sources[i].at[p["me"]], outs[i].at[p["me"]], local.at[i])
        )
        copies[-1].start()
    for copy in copies:
        copy.wait()


def exchange_plane(arrays, shards, collective_id):
    if shards != 8:
        return [lax.all_to_all(a, "seq", split_axis=0, concat_axis=0) for a in arrays]
    count = len(arrays)
    return pl.pallas_call(
        functools.partial(exchange_kernel, count),
        out_shape=[jax.ShapeDtypeStruct(a.shape, a.dtype) for a in arrays],
        in_specs=[ANY] * count,
        out_specs=[ANY] * count,
        scratch_shapes=[DMA((7 * count,)), DMA((7 * count,)), DMA((count,))],
        compiler_params=pltpu.CompilerParams(collective_id=collective_id, has_side_effects=True),
    )(*arrays)


BLOCK = 16


def over_rows(rows, step):
    @pl.loop(0, rows // BLOCK)
    def _(i):
        step(pl.ds(pl.multiple_of(i * BLOCK, BLOCK), BLOCK))


def scatter_scratch(rows, width):
    return [
        pltpu.VMEM((4, rows, width), bf16),
        pltpu.VMEM((4, rows, width), bf16),
        pltpu.VMEM((2, rows // 2, width), bf16),
        pltpu.VMEM((2, rows, width), bf16),
        DMA((12,)),
        DMA((12,)),
        DMA((4,)),
    ]


def scatter_plane(p, terms, kept, paired, far, final, send, recv, local):
    rows = terms.shape[1]
    half = rows // 2
    low, high = pl.ds(0, half), pl.ds(half, half)
    order = ((3, "dg", "ds"), (1, "xp", "xs"), (2, "yp", "ys"), (0, "me", "sib"))
    loads, pairs, sends = {}, {}, []
    for i, own, other in order:
        loads[i] = pltpu.make_async_copy(terms.at[p[own]], kept.at[i], local.at[i])
        loads[i].start()
        pairs[i] = remote(p, terms.at[p[other]], paired.at[i], send, recv, i, "sib")
        pairs[i].start()

    def add_pair(i):
        loads[i].wait()
        pairs[i].wait_recv()

        def step(at):
            kept[i, at, :] = (kept[i, at, :].astype(f32) + paired[i, at, :].astype(f32)).astype(
                bf16
            )

        over_rows(rows, step)

    def put(src, dst, i, to):
        copy = remote(p, src, dst, send, recv, i, to)
        copy.start()
        sends.append(copy)
        return copy

    add_pair(3)
    far_x = put(kept.at[3, low], far.at[0], 4, "xp")
    far_y = put(kept.at[3, high], far.at[1], 5, "yp")
    add_pair(1)
    near = [put(kept.at[1, low], final.at[0, low], 6, "xp")]
    add_pair(2)
    near.append(put(kept.at[2, high], final.at[1, high], 7, "yp"))
    far_x.wait_recv()

    def step_x(at):
        kept[2, at, :] = (kept[2, at, :].astype(f32) + far[0, at, :].astype(f32)).astype(bf16)

    over_rows(half, step_x)
    near.append(put(kept.at[2, low], final.at[1, low], 8, "yp"))
    far_y.wait_recv()

    def step_y(at):
        up = pl.ds(pl.multiple_of(at.start + half, BLOCK), BLOCK)
        kept[1, up, :] = (kept[1, up, :].astype(f32) + far[1, at, :].astype(f32)).astype(bf16)

    over_rows(half, step_y)
    near.append(put(kept.at[1, high], final.at[0, high], 9, "xp"))
    loads[0].wait()
    pairs[0].wait_recv()
    for copy in near:
        copy.wait_recv()
    return sends + list(pairs.values())


def total(kept, paired, final, at):
    return (kept[0, at, :].astype(f32) + paired[0, at, :].astype(f32)) + (
        final[0, at, :].astype(f32) + final[1, at, :].astype(f32)
    )


def forward_kernel(
    terms, tokens, gain, hidden, normed, kept, paired, far, final, send, recv, local, mine, gsend, grecv
):
    p = plane()
    greet(p, ("sib", "xp", "yp"))
    sends = scatter_plane(p, terms, kept, paired, far, final, send, recv, local)

    def step(at):
        h = tokens[at, :].astype(f32) + total(kept, paired, final, at)
        hidden[at, :] = h
        scale = lax.rsqrt(jnp.mean(h * h, axis=-1, keepdims=True) + norm_eps)
        mine[at, :] = (h * scale * gain[...]).astype(bf16)

    over_rows(tokens.shape[0], step)
    sent = gather_start(p, mine, normed, gsend, grecv, 0)
    own = pltpu.make_async_copy(mine, normed.at[p["me"]], local.at[0])
    own.start()
    gather_finish(p, sent, mine, normed, gsend, grecv, 0)
    own.wait()
    for copy in sends:
        copy.wait_send()


def reduce_plane(terms):
    rows = terms.shape[1]
    return lax.psum_scatter(terms, "seq", scatter_dimension=0, tiled=False).astype(f32).reshape(
        rows, terms.shape[2]
    )


def rms_scale(values):
    return lax.rsqrt(jnp.mean(values * values, axis=-1, keepdims=True) + norm_eps)


def forward_plane(terms, tokens, gain, collective_id):
    shards, rows, width = terms.shape
    if shards != 8:
        hidden = tokens.astype(f32) + reduce_plane(terms)
        normed = (hidden * rms_scale(hidden) * gain).astype(bf16)
        return hidden, lax.all_gather(normed, "seq")
    return pl.pallas_call(
        forward_kernel,
        out_shape=[
            jax.ShapeDtypeStruct((rows, width), f32),
            jax.ShapeDtypeStruct((8, rows, width), bf16),
        ],
        in_specs=[ANY, VMEM, VMEM],
        out_specs=[VMEM, ANY],
        scratch_shapes=scatter_scratch(rows, width)
        + [pltpu.VMEM((rows, width), bf16), DMA((GATHER_SEMS,)), DMA((GATHER_SEMS,))],
        compiler_params=pltpu.CompilerParams(
            collective_id=collective_id, has_side_effects=True, vmem_limit_bytes=40 * MIB
        ),
    )(terms, tokens, gain)


def middle_kernel(
    terms,
    cotangent,
    hidden,
    gain,
    grad_hidden,
    gain_term,
    branch,
    kept,
    paired,
    far,
    final,
    send,
    recv,
    local,
    mine,
    gsend,
    grecv,
):
    p = plane()
    greet(p, ("sib", "xp", "yp"))
    sends = scatter_plane(p, terms, kept, paired, far, final, send, recv, local)
    gain_term[...] = jnp.zeros_like(gain_term)

    def step(at):
        g = total(kept, paired, final, at)
        h = hidden[at, :]
        scale = lax.rsqrt(jnp.mean(h * h, axis=-1, keepdims=True) + norm_eps)
        weighted = g * gain[...]
        inner = jnp.mean(weighted * h, axis=-1, keepdims=True)
        out = cotangent[at, :].astype(f32) + scale * weighted - h * (scale * scale * scale * inner)
        grad_hidden[at, :] = out
        mine[at, :] = out.astype(bf16)
        gain_term[...] += jnp.sum(g * h * scale, axis=0, keepdims=True)

    over_rows(hidden.shape[0], step)
    sent = gather_start(p, mine, branch, gsend, grecv, 0)
    own = pltpu.make_async_copy(mine, branch.at[p["me"]], local.at[0])
    own.start()
    gather_finish(p, sent, mine, branch, gsend, grecv, 0)
    own.wait()
    for copy in sends:
        copy.wait_send()


def norm_back(values, scale, gain, grad):
    weighted = grad * gain
    inner = jnp.mean(weighted * values, axis=-1, keepdims=True)
    return (
        scale * weighted - values * (scale * scale * scale) * inner,
        jnp.sum(grad * values * scale, axis=0, keepdims=True),
    )


def middle_plane(terms, cotangent, hidden, gain, collective_id):
    shards, rows, width = terms.shape
    if shards != 8:
        back, gain_term = norm_back(hidden, rms_scale(hidden), gain, reduce_plane(terms))
        grad_hidden = cotangent.astype(f32) + back
        return grad_hidden, gain_term, lax.all_gather(grad_hidden.astype(bf16), "seq")
    return pl.pallas_call(
        middle_kernel,
        out_shape=[
            jax.ShapeDtypeStruct((rows, width), f32),
            jax.ShapeDtypeStruct((1, width), f32),
            jax.ShapeDtypeStruct((8, rows, width), bf16),
        ],
        in_specs=[ANY, VMEM, VMEM, VMEM],
        out_specs=[VMEM, VMEM, ANY],
        scratch_shapes=scatter_scratch(rows, width)
        + [pltpu.VMEM((rows, width), bf16), DMA((GATHER_SEMS,)), DMA((GATHER_SEMS,))],
        compiler_params=pltpu.CompilerParams(
            collective_id=collective_id, has_side_effects=True, vmem_limit_bytes=44 * MIB
        ),
    )(terms, cotangent, hidden, gain)


def last_kernel(
    terms,
    out_terms,
    tokens,
    hidden,
    grad_hidden,
    gain,
    grad_tokens,
    gain_term,
    out_tokens,
    *scratch,
):
    p = plane()
    greet(p, ("sib", "xp", "yp"))
    kept, paired, far, final, send, recv, local = scratch[:7]
    sends = scatter_plane(p, terms, kept, paired, far, final, send, recv, local)
    gain_term[...] = jnp.zeros_like(gain_term)

    def step(at):
        g = total(kept, paired, final, at)
        t = tokens[at, :].astype(f32)
        scale = lax.rsqrt(jnp.mean(t * t, axis=-1, keepdims=True) + norm_eps)
        weighted = g * gain[...]
        inner = jnp.mean(weighted * t, axis=-1, keepdims=True)
        grad_tokens[at, :] = (
            grad_hidden[at, :] + scale * weighted - t * (scale * scale * scale * inner)
        ).astype(bf16)
        gain_term[...] += jnp.sum(g * t * scale, axis=0, keepdims=True)

    over_rows(tokens.shape[0], step)
    kept, paired, far, final, send, recv, local = scratch[7:]
    sends += scatter_plane(p, out_terms, kept, paired, far, final, send, recv, local)

    def step_out(at):
        out_tokens[at, :] = (hidden[at, :] + total(kept, paired, final, at)).astype(bf16)

    over_rows(tokens.shape[0], step_out)
    for copy in sends:
        copy.wait_send()


def last_plane(terms, out_terms, tokens, hidden, grad_hidden, gain, collective_id):
    shards, rows, width = terms.shape
    if shards != 8:
        values = tokens.astype(f32)
        back, gain_term = norm_back(values, rms_scale(values), gain, reduce_plane(terms))
        return (
            (grad_hidden + back).astype(bf16),
            gain_term,
            (hidden + reduce_plane(out_terms)).astype(bf16),
        )
    return pl.pallas_call(
        last_kernel,
        out_shape=[
            jax.ShapeDtypeStruct((rows, width), bf16),
            jax.ShapeDtypeStruct((1, width), f32),
            jax.ShapeDtypeStruct((rows, width), bf16),
        ],
        in_specs=[ANY, ANY, VMEM, VMEM, VMEM, VMEM],
        out_specs=[VMEM, VMEM, VMEM],
        scratch_shapes=scatter_scratch(rows, width) * 2,
        compiler_params=pltpu.CompilerParams(
            collective_id=collective_id, has_side_effects=True, vmem_limit_bytes=48 * MIB
        ),
    )(terms, out_terms, tokens, hidden, grad_hidden, gain)


def swap_halves(v, first):
    width = v.shape[-1]
    return jnp.where(first, pltpu.roll(v, width - HD // 2, 1), pltpu.roll(v, HD // 2, 1))


def dot_t(a, b):
    return lax.dot_general(a, b, (((1,), (1,)), ((), ())), preferred_element_type=f32)


def dot(a, b):
    return jnp.dot(a, b, preferred_element_type=f32)


def allowed_pairs(start, keys, queries, offset):
    key = lax.broadcasted_iota(jnp.int32, (keys, queries), 0)
    query = lax.broadcasted_iota(jnp.int32, (keys, queries), 1) + offset
    return (key >= start) & (key <= query)


def attend_kernel(pre, cos, sin, starts, rotated, attended, stats):
    shards, _, shard_len, _ = pre.shape
    length = shards * shard_len
    block = min(256, length)
    per = block // shard_len
    pre_all = pre[...].reshape(length, 3 * PAIR)
    lane = lax.broadcasted_iota(jnp.int32, (length, PAIR), 1)
    first = lax.rem(lane, HD) < HD // 2
    cos_all, sin_all = cos[...].reshape(length, PAIR), sin[...].reshape(length, PAIR)

    def rotate(v):
        return v * cos_all + swap_halves(v, first) * sin_all

    query = rotate(pre_all[:, :PAIR]).astype(bf16)
    key = rotate(pre_all[:, PAIR : 2 * PAIR]).astype(bf16)
    value = pre_all[:, 2 * PAIR :]
    value_t = value.T.astype(bf16)
    rotated[:, 0, :, :PAIR] = query.reshape(shards, shard_len, PAIR)
    rotated[:, 0, :, PAIR : 2 * PAIR] = key.reshape(shards, shard_len, PAIR)
    rotated[:, 0, :, 2 * PAIR :] = value.astype(bf16).reshape(shards, shard_len, PAIR)
    left = lax.broadcasted_iota(jnp.int32, (block, PAIR), 1) < HD
    top = lax.broadcasted_iota(jnp.int32, (PAIR, block), 0) < HD
    scaled = query * jnp.asarray(0.125, bf16)
    for i in range(length // block):
        keys = (i + 1) * block
        start = starts[0, :, i * block : (i + 1) * block]
        mask = allowed_pairs(start, keys, block, i * block)
        here = scaled[i * block : (i + 1) * block]
        results = []
        for h in range(2):
            own = jnp.where(left if h == 0 else ~left, here, jnp.zeros_like(here))
            scores = jnp.where(mask, dot_t(key[:keys], own), -1e30)
            peak = jnp.max(scores, axis=0, keepdims=True)
            shifted = jnp.exp(scores - peak)
            summed = jnp.sum(shifted, axis=0, keepdims=True)
            probs = (shifted * (1.0 / summed)).astype(bf16)
            results.append(dot(value_t[:, :keys], probs))
            stats[0, 0, h : h + 1, i * block : (i + 1) * block] = peak + jnp.log(summed)
        merged = jnp.where(top, results[0], results[1]).T.astype(bf16)
        attended[i * per : (i + 1) * per, 0, :, :] = merged.reshape(per, shard_len, PAIR)


def attend(pre, cos, sin, starts):
    shards, rows, shard_len, width = pre.shape
    pairs = width // (3 * PAIR)
    length = shards * shard_len
    wide = pl.BlockSpec((shards, 1, shard_len, 3 * PAIR), lambda r, p: (0, r, 0, p))
    narrow = pl.BlockSpec((shards, 1, shard_len, PAIR), lambda r, p: (0, r, 0, p))
    table = pl.BlockSpec((shards, 1, shard_len, PAIR), lambda r, p: (0, r, 0, 0))
    return pl.pallas_call(
        attend_kernel,
        grid=(rows, pairs),
        out_shape=[
            jax.ShapeDtypeStruct(pre.shape, bf16),
            jax.ShapeDtypeStruct((shards, rows, shard_len, pairs * PAIR), bf16),
            jax.ShapeDtypeStruct((rows, pairs, 2, length), f32),
        ],
        in_specs=[wide, table, table, pl.BlockSpec((1, 1, length), lambda r, p: (r, 0, 0))],
        out_specs=[wide, narrow, pl.BlockSpec((1, 1, 2, length), lambda r, p: (r, p, 0, 0))],
        compiler_params=pltpu.CompilerParams(vmem_limit_bytes=48 * MIB),
        cost_estimate=pl.CostEstimate(
            flops=rows * pairs * 2 * length * length * 256 * 2,
            bytes_accessed=pre.size * 8,
            transcendentals=rows * pairs * length * length,
        ),
    )(pre, cos, sin, starts)


def attend_back_kernel(rotated, grad, cos, sin, starts, stats, result, key_acc, value_acc):
    shards, _, shard_len, _ = rotated.shape
    length = shards * shard_len
    block = min(256, length)
    per = block // shard_len
    all_in = rotated[...].reshape(length, 3 * PAIR)
    query, key, value = all_in[:, :PAIR], all_in[:, PAIR : 2 * PAIR], all_in[:, 2 * PAIR :]
    grad_all = grad[...].reshape(length, PAIR)
    key_t = key.astype(f32).T.astype(bf16)
    left = lax.broadcasted_iota(jnp.int32, (block, PAIR), 1) < HD
    top = lax.broadcasted_iota(jnp.int32, (PAIR, block), 0) < HD
    first = lax.rem(lax.broadcasted_iota(jnp.int32, (length, PAIR), 1), HD) < HD // 2
    key_acc[...] = jnp.zeros_like(key_acc)
    value_acc[...] = jnp.zeros_like(value_acc)

    for i in range(length // block):
        keys = (i + 1) * block
        at = slice(i * block, (i + 1) * block)
        start = starts[0, :, at]
        mask = allowed_pairs(start, keys, block, i * block)
        results = []
        for h in range(2):
            side = left if h == 0 else ~left
            own = jnp.where(side, query[at], jnp.zeros_like(query[at]))
            own_grad = jnp.where(side, grad_all[at], jnp.zeros_like(grad_all[at]))
            scores = dot_t(key[:keys], own * jnp.asarray(0.125, bf16))
            probs = jnp.exp(jnp.where(mask, scores - stats[0, 0, h : h + 1, at], -1e30))
            grad_probs = dot_t(value[:keys], own_grad)
            inner = jnp.sum(probs * grad_probs, axis=0, keepdims=True)
            grad_scores = (probs * (grad_probs - inner) * 0.125).astype(bf16)
            key_acc[:keys, :] += dot(grad_scores, own)
            value_acc[:keys, :] += dot(probs.astype(bf16), own_grad)
            results.append(dot(key_t[:, :keys], grad_scores))
        merged = jnp.where(top, results[0], results[1]).T
        cos_here = cos[i * per : (i + 1) * per].reshape(block, PAIR)
        sin_here = sin[i * per : (i + 1) * per].reshape(block, PAIR)
        turned = merged * cos_here - swap_halves(merged, first[:block]) * sin_here
        result[i * per : (i + 1) * per, 0, :, :PAIR] = turned.astype(bf16).reshape(
            per, shard_len, PAIR
        )
    cos_all, sin_all = cos[...].reshape(length, PAIR), sin[...].reshape(length, PAIR)
    key_grad = key_acc[...]
    turned = key_grad * cos_all - swap_halves(key_grad, first) * sin_all
    result[:, 0, :, PAIR : 2 * PAIR] = turned.astype(bf16).reshape(shards, shard_len, PAIR)
    result[:, 0, :, 2 * PAIR :] = value_acc[...].astype(bf16).reshape(shards, shard_len, PAIR)


def attend_back(rotated, grad, cos, sin, starts, stats):
    shards, rows, shard_len, width = rotated.shape
    pairs = width // (3 * PAIR)
    length = shards * shard_len
    wide = pl.BlockSpec((shards, 1, shard_len, 3 * PAIR), lambda r, p: (0, r, 0, p))
    narrow = pl.BlockSpec((shards, 1, shard_len, PAIR), lambda r, p: (0, r, 0, p))
    table = pl.BlockSpec((shards, 1, shard_len, PAIR), lambda r, p: (0, r, 0, 0))
    return pl.pallas_call(
        attend_back_kernel,
        grid=(rows, pairs),
        out_shape=jax.ShapeDtypeStruct(rotated.shape, bf16),
        in_specs=[
            wide,
            narrow,
            table,
            table,
            pl.BlockSpec((1, 1, length), lambda r, p: (r, 0, 0)),
            pl.BlockSpec((1, 1, 2, length), lambda r, p: (r, p, 0, 0)),
        ],
        out_specs=wide,
        scratch_shapes=[pltpu.VMEM((length, PAIR), f32), pltpu.VMEM((length, PAIR), f32)],
        compiler_params=pltpu.CompilerParams(vmem_limit_bytes=48 * MIB),
        cost_estimate=pl.CostEstimate(
            flops=rows * pairs * 5 * length * length * 256 * 2,
            bytes_accessed=rotated.size * 6,
            transcendentals=rows * pairs * length * length,
        ),
    )(rotated, grad, cos, sin, starts, stats)


def rope_tables(doc_ids, shards):
    rows, length = doc_ids.shape
    places = lax.broadcasted_iota(jnp.int32, doc_ids.shape, 1)
    earlier = jnp.concatenate([doc_ids[:, :1], doc_ids[:, :-1]], axis=1)
    starts = lax.cummax(jnp.where(doc_ids != earlier, places, 0), axis=1)
    positions = (places - starts).astype(f32)
    frequency = rope_base ** (-(jnp.arange(HD // 2, dtype=f32) * 2.0 / HD))
    angles = positions[..., None] * frequency
    cos, sin = jnp.cos(angles), jnp.sin(angles)
    lay = lambda v: jnp.moveaxis(
        jnp.concatenate(v, axis=-1).reshape(rows, shards, length // shards, PAIR), 0, 1
    )
    return lay([cos] * 4), lay([-sin, sin, -sin, sin]), starts


def layer(
    groups,
    shards,
    tokens,
    doc_ids,
    cotangent,
    norm1_gain,
    w_query,
    w_key,
    w_value,
    w_out,
    norm2_gain,
    w_gate,
    w_up,
    w_down,
):
    rows, shard_len, width = tokens.shape
    count = rows * shard_len
    held = w_query.shape[0]
    hidden_held = w_down.shape[0]
    hidden_here = groups * hidden_held
    whole_heads = held % HD == 0
    outer, inner = (groups, held) if whole_heads else (1, width // shards)
    pairs = width // shards // PAIR
    flat = lambda v: v.reshape(shards * count, v.shape[-1])
    split = lambda v: v.reshape(shards, count, v.shape[-1])

    gains = lax.all_gather(
        jnp.stack([norm1_gain, norm2_gain]), ("dp", "seq"), axis=1, tiled=True
    ).astype(f32)
    gain_one, gain_two = gains[:1], gains[1:]

    def by_head(w):
        blocks = w.reshape(held, outer, shards, inner)
        return jnp.moveaxis(blocks, 2, 0).reshape(shards, held, pairs, PAIR)

    def by_unit(w):
        return jnp.moveaxis(w.reshape(held, groups, shards, hidden_held), 2, 0).reshape(
            shards, held, hidden_here
        )

    heads = jnp.stack([by_head(w) for w in (w_query, w_key, w_value)], axis=3)
    heads = heads.reshape(shards, held, 3 * pairs * PAIR)
    units = jnp.concatenate([by_unit(w_gate), by_unit(w_up)], axis=-1)
    heads, units = exchange_plane([heads, units], shards, 1)
    heads = heads.reshape(shards * held, heads.shape[-1])
    units = units.reshape(shards * held, units.shape[-1])
    qkv_weight = lax.all_gather(heads, "dp", axis=0, tiled=True)
    if whole_heads:
        out_weight = lax.all_gather(w_out, "dp", axis=0, tiled=True)
    else:
        whole = lax.all_gather(w_out, ("dp", "seq"), axis=0, tiled=True)
        out_weight = lax.dynamic_slice_in_dim(whole, lax.axis_index("seq") * inner, inner, 0)
    unit_weight = lax.all_gather(units, "dp", axis=0, tiled=True)
    down_weight = lax.all_gather(w_down, "dp", axis=0, tiled=True)

    own_tokens = tokens.reshape(count, width)
    own_cotangent = cotangent.reshape(count, width)
    inputs = own_tokens.astype(f32)
    own_normed = (inputs * rms_scale(inputs) * gain_one).astype(bf16)
    normed_one, cot = [flat(v) for v in gather_plane([own_normed, own_cotangent], shards, 2)]

    cos, sin, starts = rope_tables(doc_ids, shards)
    starts = starts[:, None, :]
    by_row = lambda v: v.reshape(shards, rows, shard_len, v.shape[-1])
    pre = by_row(dot(normed_one, qkv_weight))
    rotated, attended, stats = attend(pre, cos, sin, starts)
    attended = flat(attended)
    hidden, normed_two = forward_plane(
        split(dot(attended, out_weight).astype(bf16)), own_tokens, gain_two, 3
    )
    normed_two = flat(normed_two)

    gate_pre = dot(normed_two, unit_weight[:, :hidden_here])
    up_pre = dot(normed_two, unit_weight[:, hidden_here:])
    sigmoid = jax.nn.sigmoid(gate_pre)
    silu = gate_pre * sigmoid
    activated = (silu * up_pre).astype(bf16)
    out_terms = split(dot(activated, down_weight).astype(bf16))
    grad_act = dot_t(cot, down_weight)
    grad_gate_pre = (grad_act * up_pre * sigmoid * (1.0 + gate_pre * (1.0 - sigmoid))).astype(bf16)
    grad_up_pre = (grad_act * silu).astype(bf16)
    grad_units = jnp.concatenate([grad_gate_pre, grad_up_pre], axis=-1)
    middle_terms = split(dot_t(grad_units, unit_weight).astype(bf16))
    unit_terms = dot(normed_two.T, grad_units).astype(bf16)
    down_terms = dot(activated.T, cot).astype(bf16)
    unit_sums = lax.psum_scatter(unit_terms, "dp", scatter_dimension=0, tiled=True)
    down_sums = lax.psum_scatter(down_terms, "dp", scatter_dimension=0, tiled=True)

    grad_hidden, gain_two_term, branch = middle_plane(
        middle_terms, own_cotangent, hidden, gain_two, 4
    )
    branch = flat(branch)
    out_w_terms = dot(attended.T, branch).astype(bf16)
    if whole_heads:
        grad_out = lax.psum_scatter(out_w_terms, "dp", scatter_dimension=0, tiled=True)
    else:
        placed = lax.dynamic_update_slice_in_dim(
            jnp.zeros((width, width), bf16), out_w_terms, lax.axis_index("seq") * inner, 0
        )
        grad_out = lax.psum_scatter(placed, ("dp", "seq"), scatter_dimension=0, tiled=True)
    grad_attended = by_row(dot_t(branch, out_weight).astype(bf16))
    grad_pre = flat(attend_back(rotated, grad_attended, cos, sin, starts, stats))
    last_terms = split(dot_t(grad_pre, qkv_weight).astype(bf16))
    head_terms = dot(normed_one.T, grad_pre).astype(bf16)
    head_sums = lax.psum_scatter(head_terms, "dp", scatter_dimension=0, tiled=True)

    grad_tokens, gain_one_term, out_tokens = last_plane(
        last_terms, out_terms, own_tokens, hidden, grad_hidden, gain_one, 5
    )
    head_sums, unit_sums = exchange_plane(
        [head_sums.reshape(shards, held, -1), unit_sums.reshape(shards, held, -1)], shards, 6
    )

    head_sums = head_sums.reshape(shards, held, pairs, 3, PAIR)

    def heads_back(i):
        blocks = head_sums[:, :, :, i, :].reshape(shards, held, outer, inner)
        return jnp.moveaxis(blocks, 0, 2).reshape(held, width).astype(f32)

    def units_back(i):
        blocks = unit_sums[:, :, i * hidden_here : (i + 1) * hidden_here]
        blocks = blocks.reshape(shards, held, groups, hidden_held)
        return jnp.moveaxis(blocks, 0, 2).reshape(held, -1).astype(f32)

    gain_sums = lax.psum_scatter(
        jnp.concatenate([gain_one_term, gain_two_term]),
        ("dp", "seq"),
        scatter_dimension=1,
        tiled=True,
    )
    return (
        out_tokens.reshape(tokens.shape),
        grad_tokens.reshape(tokens.shape),
        gain_sums[0],
        heads_back(0),
        heads_back(1),
        heads_back(2),
        grad_out.astype(f32),
        gain_sums[1],
        units_back(0),
        units_back(1),
        down_sums.astype(f32),
    )


def solution(mesh):
    both = ("dp", "seq")
    return jax.shard_map(
        functools.partial(layer, mesh.shape["dp"], mesh.shape["seq"]),
        mesh=mesh,
        in_specs=(
            P("dp", "seq", None),
            P("dp", None),
            P("dp", "seq", None),
            P(both),
            P(both, None),
            P(both, None),
            P(both, None),
            P(both, None),
            P(both),
            P(both, None),
            P(both, None),
            P(both, None),
        ),
        out_specs=(
            P("dp", "seq", None),
            P("dp", "seq", None),
            P(both),
            P(both, None),
            P(both, None),
            P(both, None),
            P(both, None),
            P(both),
            P(both, None),
            P(both, None),
            P(both, None),
        ),
        check_vma=False,
    )
```

```python
import functools

import jax
import jax.numpy as jnp
from jax import lax
from jax.experimental import pallas as pl
from jax.experimental.pallas import tpu as pltpu
from jax.sharding import PartitionSpec as P

H = 32
HD = 64
PAIR = 2 * HD

rope_base = 130000.0
norm_eps = 1e-05

bf16 = jnp.bfloat16
f32 = jnp.float32
MESH = pl.DeviceIdType.MESH
ANY = pl.BlockSpec(memory_space=pl.ANY)
VMEM = pl.BlockSpec(memory_space=pltpu.VMEM)
DMA = pltpu.SemaphoreType.DMA
MIB = 1 << 20


def lasting(us):
    return pl.CostEstimate(flops=0, transcendentals=0, bytes_accessed=int(us * 3_500_000))


def plane():
    dp, s = lax.axis_index("dp"), lax.axis_index("seq")
    core, xb, yb = lax.rem(s, 2), lax.rem(lax.div(s, 2), 2), lax.div(s, 4)
    at = lambda y, x, c: y * 4 + x * 2 + c
    return dict(
        dp=dp,
        me=s,
        sib=at(yb, xb, 1 - core),
        xp=at(yb, 1 - xb, core),
        yp=at(1 - yb, xb, core),
        dg=at(1 - yb, 1 - xb, core),
        xs=at(yb, 1 - xb, 1 - core),
        ys=at(1 - yb, xb, 1 - core),
        ds=at(1 - yb, 1 - xb, 1 - core),
    )


def greet(p, names):
    barrier = pltpu.get_barrier_semaphore()
    for name in names:
        pl.semaphore_signal(barrier, inc=1, device_id=(p["dp"], p[name]), device_id_type=MESH)
    pl.semaphore_wait(barrier, len(names))


def remote(p, src, dst, send, recv, i, to):
    return pltpu.make_async_remote_copy(
        src_ref=src,
        dst_ref=dst,
        send_sem=send.at[i],
        recv_sem=recv.at[i],
        device_id=(p["dp"], p[to]),
        device_id_type=MESH,
    )


GATHER_SEMS = 25


def gather_start(p, src, out, send, recv, base):
    quarter = src.shape[0] // 4
    part = lambda ref, k: ref.at[pl.ds(k * quarter, quarter)]
    mine = out.at[p["me"]]
    sent = {}
    for j in range(4):
        kx, ky = j, (j + 2) % 4
        sent["x", kx] = remote(p, part(src, kx), part(mine, kx), send, recv, base + kx, "xp")
        sent["y", ky] = remote(p, part(src, ky), part(mine, ky), send, recv, base + 4 + ky, "yp")
        sent["x", kx].start()
        sent["y", ky].start()
    sent["s"] = remote(p, src, mine, send, recv, base + 8, "sib")
    sent["s"].start()
    return sent


def gather_finish(p, sent, src, out, send, recv, base):
    quarter = src.shape[0] // 4
    part = lambda ref, k: ref.at[pl.ds(k * quarter, quarter)]
    passed = []

    def forward(owner, k, i, to):
        ref = part(out.at[p[owner]], k)
        copy = remote(p, ref, ref, send, recv, base + i, to)
        copy.start()
        return copy

    for j in range(4):
        kx, ky = j, (j + 2) % 4
        sent["x", kx].wait_recv()
        if j < 2:
            sent["far", kx] = forward("xp", kx, 9 + kx, "yp")
        passed.append(forward("xp", kx, 13 + kx, "sib"))
        sent["y", ky].wait_recv()
        if j < 2:
            sent["far", ky] = forward("yp", ky, 9 + ky, "xp")
        passed.append(forward("yp", ky, 17 + ky, "sib"))
    for k in (0, 2, 1, 3):
        sent["far", k].wait_recv()
        passed.append(forward("dg", k, 21 + k, "sib"))
    sent["s"].wait_recv()
    for copy in passed:
        copy.wait_recv()
    for copy in list(sent.values()) + passed:
        copy.wait_send()


def gather_kernel(count, *refs):
    sources, outs = refs[:count], refs[count : 2 * count]
    send, recv, local = refs[2 * count :]
    p = plane()
    greet(p, ("sib", "xp", "yp"))
    sent, kept = [], []
    for i in range(count):
        sent.append(gather_start(p, sources[i], outs[i], send, recv, i * GATHER_SEMS))
        kept.append(pltpu.make_async_copy(sources[i], outs[i].at[p["me"]], local.at[i]))
        kept[i].start()
    for i in range(count):
        gather_finish(p, sent[i], sources[i], outs[i], send, recv, i * GATHER_SEMS)
    for copy in kept:
        copy.wait()


def gather_plane(arrays, shards, collective_id):
    if shards != 8:
        return [lax.all_gather(a, "seq") for a in arrays]
    count = len(arrays)
    return pl.pallas_call(
        functools.partial(gather_kernel, count),
        out_shape=[jax.ShapeDtypeStruct((8,) + a.shape, a.dtype) for a in arrays],
        in_specs=[ANY] * count,
        out_specs=[ANY] * count,
        scratch_shapes=[DMA((GATHER_SEMS * count,)), DMA((GATHER_SEMS * count,)), DMA((count,))],
        compiler_params=pltpu.CompilerParams(collective_id=collective_id, has_side_effects=True),
        cost_estimate=lasting(40 * count),
    )(*arrays)


def exchange_kernel(count, *refs):
    sources, outs = refs[:count], refs[count : 2 * count]
    send, recv, local = refs[2 * count :]
    p = plane()
    names = ("dg", "ds", "xp", "yp", "xs", "ys", "sib")
    greet(p, names)
    copies = []
    for i in range(count):
        for j, name in enumerate(names):
            copies.append(
                remote(
                    p, sources[i].at[p[name]], outs[i].at[p["me"]], send, recv, i * 7 + j, name
                )
            )
            copies[-1].start()
        copies.append(
            pltpu.make_async_copy(sources[i].at[p["me"]], outs[i].at[p["me"]], local.at[i])
        )
        copies[-1].start()
    for copy in copies:
        copy.wait()


def exchange_plane(arrays, shards, collective_id):
    if shards != 8:
        return [lax.all_to_all(a, "seq", split_axis=0, concat_axis=0) for a in arrays]
    count = len(arrays)
    return pl.pallas_call(
        functools.partial(exchange_kernel, count),
        out_shape=[jax.ShapeDtypeStruct(a.shape, a.dtype) for a in arrays],
        in_specs=[ANY] * count,
        out_specs=[ANY] * count,
        scratch_shapes=[DMA((7 * count,)), DMA((7 * count,)), DMA((count,))],
        compiler_params=pltpu.CompilerParams(collective_id=collective_id, has_side_effects=True),
        cost_estimate=lasting(35),
    )(*arrays)


BLOCK = 16


def over_rows(rows, step):
    @pl.loop(0, rows // BLOCK)
    def _(i):
        step(pl.ds(pl.multiple_of(i * BLOCK, BLOCK), BLOCK))


def scatter_scratch(rows, width):
    return [
        pltpu.VMEM((4, rows, width), bf16),
        pltpu.VMEM((4, rows, width), bf16),
        pltpu.VMEM((2, rows // 2, width), bf16),
        pltpu.VMEM((2, rows, width), bf16),
        DMA((12,)),
        DMA((12,)),
        DMA((4,)),
    ]


class FromMemory:
    def __init__(self, p, terms, kept, paired, send, recv, local):
        self.loads, self.pairs = {}, {}
        for i, own, other in ORDER:
            self.loads[i] = pltpu.make_async_copy(terms.at[p[own]], kept.at[i], local.at[i])
            self.loads[i].start()
            self.pairs[i] = remote(p, terms.at[p[other]], paired.at[i], send, recv, i, "sib")
            self.pairs[i].start()

    def ready(self, i):
        self.loads[i].wait()
        self.pairs[i].wait_recv()

    def finish(self):
        for copy in self.pairs.values():
            copy.wait_send()


ORDER = ((3, "dg", "ds"), (1, "xp", "xs"), (2, "yp", "ys"), (0, "me", "sib"))


def scatter_plane(p, source, rows, kept, paired, far, final, send, recv, meanwhile=None):
    half = rows // 2
    low, high = pl.ds(0, half), pl.ds(half, half)
    sends = []

    def add_pair(i):
        source.ready(i)

        def step(at):
            kept[i, at, :] = (kept[i, at, :].astype(f32) + paired[i, at, :].astype(f32)).astype(
                bf16
            )

        over_rows(rows, step)

    def put(src, dst, i, to):
        copy = remote(p, src, dst, send, recv, i, to)
        copy.start()
        sends.append(copy)
        return copy

    add_pair(3)
    far_x = put(kept.at[3, low], far.at[0], 4, "xp")
    far_y = put(kept.at[3, high], far.at[1], 5, "yp")
    add_pair(1)
    near = [put(kept.at[1, low], final.at[0, low], 6, "xp")]
    add_pair(2)
    near.append(put(kept.at[2, high], final.at[1, high], 7, "yp"))
    far_x.wait_recv()

    def step_x(at):
        kept[2, at, :] = (kept[2, at, :].astype(f32) + far[0, at, :].astype(f32)).astype(bf16)

    over_rows(half, step_x)
    near.append(put(kept.at[2, low], final.at[1, low], 8, "yp"))
    far_y.wait_recv()

    def step_y(at):
        up = pl.ds(pl.multiple_of(at.start + half, BLOCK), BLOCK)
        kept[1, up, :] = (kept[1, up, :].astype(f32) + far[1, at, :].astype(f32)).astype(bf16)

    over_rows(half, step_y)
    near.append(put(kept.at[1, high], final.at[0, high], 9, "xp"))
    source.ready(0)
    if meanwhile is not None:
        meanwhile()
    for copy in near:
        copy.wait_recv()
    return sends


def total(kept, paired, final, at):
    return (kept[0, at, :].astype(f32) + paired[0, at, :].astype(f32)) + (
        final[0, at, :].astype(f32) + final[1, at, :].astype(f32)
    )


def forward_kernel(
    terms, tokens, gain, hidden, normed, kept, paired, far, final, send, recv, local, mine, gsend, grecv
):
    p = plane()
    greet(p, ("sib", "xp", "yp"))
    source = FromMemory(p, terms, kept, paired, send, recv, local)
    sends = scatter_plane(p, source, tokens.shape[0], kept, paired, far, final, send, recv)

    def step(at):
        h = tokens[at, :].astype(f32) + total(kept, paired, final, at)
        hidden[at, :] = h
        scale = lax.rsqrt(jnp.mean(h * h, axis=-1, keepdims=True) + norm_eps)
        mine[at, :] = (h * scale * gain[...]).astype(bf16)

    over_rows(tokens.shape[0], step)
    sent = gather_start(p, mine, normed, gsend, grecv, 0)
    own = pltpu.make_async_copy(mine, normed.at[p["me"]], local.at[0])
    own.start()
    gather_finish(p, sent, mine, normed, gsend, grecv, 0)
    own.wait()
    source.finish()
    for copy in sends:
        copy.wait_send()


def reduce_plane(terms):
    rows = terms.shape[1]
    return lax.psum_scatter(terms, "seq", scatter_dimension=0, tiled=False).astype(f32).reshape(
        rows, terms.shape[2]
    )


def rms_scale(values):
    return lax.rsqrt(jnp.mean(values * values, axis=-1, keepdims=True) + norm_eps)


def forward_plane(terms, tokens, gain, collective_id):
    shards, rows, width = terms.shape
    if shards != 8:
        hidden = tokens.astype(f32) + reduce_plane(terms)
        normed = (hidden * rms_scale(hidden) * gain).astype(bf16)
        return hidden, lax.all_gather(normed, "seq")
    return pl.pallas_call(
        forward_kernel,
        out_shape=[
            jax.ShapeDtypeStruct((rows, width), f32),
            jax.ShapeDtypeStruct((8, rows, width), bf16),
        ],
        in_specs=[ANY, VMEM, VMEM],
        out_specs=[VMEM, ANY],
        scratch_shapes=scatter_scratch(rows, width)
        + [pltpu.VMEM((rows, width), bf16), DMA((GATHER_SEMS,)), DMA((GATHER_SEMS,))],
        compiler_params=pltpu.CompilerParams(
            collective_id=collective_id, has_side_effects=True, vmem_limit_bytes=40 * MIB
        ),
        cost_estimate=lasting(80),
    )(terms, tokens, gain)


def norm_back(values, scale, gain, grad):
    weighted = grad * gain
    inner = jnp.mean(weighted * values, axis=-1, keepdims=True)
    return (
        scale * weighted - values * (scale * scale * scale) * inner,
        jnp.sum(grad * values * scale, axis=0, keepdims=True),
    )


def swap_halves(v, first):
    width = v.shape[-1]
    return jnp.where(first, pltpu.roll(v, width - HD // 2, 1), pltpu.roll(v, HD // 2, 1))


def dot_t(a, b):
    return lax.dot_general(a, b, (((1,), (1,)), ((), ())), preferred_element_type=f32)


def dot(a, b):
    return jnp.dot(a, b, preferred_element_type=f32)


def allowed_pairs(start, keys, queries, offset):
    key = lax.broadcasted_iota(jnp.int32, (keys, queries), 0)
    query = lax.broadcasted_iota(jnp.int32, (keys, queries), 1) + offset
    return (key >= start) & (key <= query)


def attend_kernel(pre, cos, sin, starts, rotated, attended, stats):
    shards, _, shard_len, _ = pre.shape
    length = shards * shard_len
    block = min(256, length)
    per = block // shard_len
    pre_all = pre[...].reshape(length, 3 * PAIR)
    lane = lax.broadcasted_iota(jnp.int32, (length, PAIR), 1)
    first = lax.rem(lane, HD) < HD // 2
    cos_all, sin_all = cos[...].reshape(length, PAIR), sin[...].reshape(length, PAIR)

    def rotate(v):
        return v * cos_all + swap_halves(v, first) * sin_all

    query = rotate(pre_all[:, :PAIR]).astype(bf16)
    key = rotate(pre_all[:, PAIR : 2 * PAIR]).astype(bf16)
    value = pre_all[:, 2 * PAIR :]
    value_t = value.T.astype(bf16)
    rotated[:, 0, :, :PAIR] = query.reshape(shards, shard_len, PAIR)
    rotated[:, 0, :, PAIR : 2 * PAIR] = key.reshape(shards, shard_len, PAIR)
    rotated[:, 0, :, 2 * PAIR :] = value.astype(bf16).reshape(shards, shard_len, PAIR)
    left = lax.broadcasted_iota(jnp.int32, (block, PAIR), 1) < HD
    top = lax.broadcasted_iota(jnp.int32, (PAIR, block), 0) < HD
    scaled = query * jnp.asarray(0.125, bf16)
    for i in range(length // block):
        keys = (i + 1) * block
        start = starts[0, :, i * block : (i + 1) * block]
        mask = allowed_pairs(start, keys, block, i * block)
        here = scaled[i * block : (i + 1) * block]
        results = []
        for h in range(2):
            own = jnp.where(left if h == 0 else ~left, here, jnp.zeros_like(here))
            scores = jnp.where(mask, dot_t(key[:keys], own), -1e30)
            peak = jnp.max(scores, axis=0, keepdims=True)
            shifted = jnp.exp(scores - peak)
            summed = jnp.sum(shifted, axis=0, keepdims=True)
            probs = (shifted * (1.0 / summed)).astype(bf16)
            results.append(dot(value_t[:, :keys], probs))
            stats[0, 0, h : h + 1, i * block : (i + 1) * block] = peak + jnp.log(summed)
        merged = jnp.where(top, results[0], results[1]).T.astype(bf16)
        attended[i * per : (i + 1) * per, 0, :, :] = merged.reshape(per, shard_len, PAIR)


def attend(pre, cos, sin, starts):
    shards, rows, shard_len, width = pre.shape
    pairs = width // (3 * PAIR)
    length = shards * shard_len
    wide = pl.BlockSpec((shards, 1, shard_len, 3 * PAIR), lambda r, p: (0, r, 0, p))
    narrow = pl.BlockSpec((shards, 1, shard_len, PAIR), lambda r, p: (0, r, 0, p))
    table = pl.BlockSpec((shards, 1, shard_len, PAIR), lambda r, p: (0, r, 0, 0))
    return pl.pallas_call(
        attend_kernel,
        grid=(rows, pairs),
        out_shape=[
            jax.ShapeDtypeStruct(pre.shape, bf16),
            jax.ShapeDtypeStruct((shards, rows, shard_len, pairs * PAIR), bf16),
            jax.ShapeDtypeStruct((rows, pairs, 2, length), f32),
        ],
        in_specs=[wide, table, table, pl.BlockSpec((1, 1, length), lambda r, p: (r, 0, 0))],
        out_specs=[wide, narrow, pl.BlockSpec((1, 1, 2, length), lambda r, p: (r, p, 0, 0))],
        compiler_params=pltpu.CompilerParams(vmem_limit_bytes=48 * MIB),
        cost_estimate=pl.CostEstimate(
            flops=rows * pairs * 2 * length * length * 256 * 2,
            bytes_accessed=pre.size * 8,
            transcendentals=rows * pairs * length * length,
        ),
    )(pre, cos, sin, starts)


def attend_back_kernel(rotated, grad, cos, sin, starts, stats, result, key_acc, value_acc):
    shards, _, shard_len, _ = rotated.shape
    length = shards * shard_len
    block = min(256, length)
    per = block // shard_len
    all_in = rotated[...].reshape(length, 3 * PAIR)
    query, key, value = all_in[:, :PAIR], all_in[:, PAIR : 2 * PAIR], all_in[:, 2 * PAIR :]
    grad_all = grad[...].reshape(length, PAIR)
    key_t = key.astype(f32).T.astype(bf16)
    left = lax.broadcasted_iota(jnp.int32, (block, PAIR), 1) < HD
    top = lax.broadcasted_iota(jnp.int32, (PAIR, block), 0) < HD
    first = lax.rem(lax.broadcasted_iota(jnp.int32, (length, PAIR), 1), HD) < HD // 2
    key_acc[...] = jnp.zeros_like(key_acc)
    value_acc[...] = jnp.zeros_like(value_acc)

    for i in range(length // block):
        keys = (i + 1) * block
        at = slice(i * block, (i + 1) * block)
        start = starts[0, :, at]
        mask = allowed_pairs(start, keys, block, i * block)
        results = []
        for h in range(2):
            side = left if h == 0 else ~left
            own = jnp.where(side, query[at], jnp.zeros_like(query[at]))
            own_grad = jnp.where(side, grad_all[at], jnp.zeros_like(grad_all[at]))
            scores = dot_t(key[:keys], own * jnp.asarray(0.125, bf16))
            probs = jnp.exp(jnp.where(mask, scores - stats[0, 0, h : h + 1, at], -1e30))
            grad_probs = dot_t(value[:keys], own_grad)
            inner = jnp.sum(probs * grad_probs, axis=0, keepdims=True)
            grad_scores = (probs * (grad_probs - inner) * 0.125).astype(bf16)
            key_acc[:keys, :] += dot(grad_scores, own)
            value_acc[:keys, :] += dot(probs.astype(bf16), own_grad)
            results.append(dot(key_t[:, :keys], grad_scores))
        merged = jnp.where(top, results[0], results[1]).T
        cos_here = cos[i * per : (i + 1) * per].reshape(block, PAIR)
        sin_here = sin[i * per : (i + 1) * per].reshape(block, PAIR)
        turned = merged * cos_here - swap_halves(merged, first[:block]) * sin_here
        result[i * per : (i + 1) * per, 0, :, :PAIR] = turned.astype(bf16).reshape(
            per, shard_len, PAIR
        )
    cos_all, sin_all = cos[...].reshape(length, PAIR), sin[...].reshape(length, PAIR)
    key_grad = key_acc[...]
    turned = key_grad * cos_all - swap_halves(key_grad, first) * sin_all
    result[:, 0, :, PAIR : 2 * PAIR] = turned.astype(bf16).reshape(shards, shard_len, PAIR)
    result[:, 0, :, 2 * PAIR :] = value_acc[...].astype(bf16).reshape(shards, shard_len, PAIR)


def attend_back(rotated, grad, cos, sin, starts, stats):
    shards, rows, shard_len, width = rotated.shape
    pairs = width // (3 * PAIR)
    length = shards * shard_len
    wide = pl.BlockSpec((shards, 1, shard_len, 3 * PAIR), lambda r, p: (0, r, 0, p))
    narrow = pl.BlockSpec((shards, 1, shard_len, PAIR), lambda r, p: (0, r, 0, p))
    table = pl.BlockSpec((shards, 1, shard_len, PAIR), lambda r, p: (0, r, 0, 0))
    return pl.pallas_call(
        attend_back_kernel,
        grid=(rows, pairs),
        out_shape=jax.ShapeDtypeStruct(rotated.shape, bf16),
        in_specs=[
            wide,
            narrow,
            table,
            table,
            pl.BlockSpec((1, 1, length), lambda r, p: (r, 0, 0)),
            pl.BlockSpec((1, 1, 2, length), lambda r, p: (r, p, 0, 0)),
        ],
        out_specs=wide,
        scratch_shapes=[pltpu.VMEM((length, PAIR), f32), pltpu.VMEM((length, PAIR), f32)],
        compiler_params=pltpu.CompilerParams(vmem_limit_bytes=48 * MIB),
        cost_estimate=pl.CostEstimate(
            flops=rows * pairs * 5 * length * length * 256 * 2,
            bytes_accessed=rotated.size * 6,
            transcendentals=rows * pairs * length * length,
        ),
    )(rotated, grad, cos, sin, starts, stats)


def rope_tables(doc_ids, shards):
    rows, length = doc_ids.shape
    places = lax.broadcasted_iota(jnp.int32, doc_ids.shape, 1)
    earlier = jnp.concatenate([doc_ids[:, :1], doc_ids[:, :-1]], axis=1)
    starts = lax.cummax(jnp.where(doc_ids != earlier, places, 0), axis=1)
    positions = (places - starts).astype(f32)
    frequency = rope_base ** (-(jnp.arange(HD // 2, dtype=f32) * 2.0 / HD))
    angles = positions[..., None] * frequency
    cos, sin = jnp.cos(angles), jnp.sin(angles)
    lay = lambda v: jnp.moveaxis(
        jnp.concatenate(v, axis=-1).reshape(rows, shards, length // shards, PAIR), 0, 1
    )
    return lay([cos] * 4), lay([-sin, sin, -sin, sin]), starts


class LineSum:
    def __init__(self, p, view, land, send, recv, base):
        self.p, self.view, self.land = p, view, land
        self.send, self.recv, self.base = send, recv, base
        self.z = p["dp"]
        self.inward = 1 - 2 * lax.div(self.z, 2)
        self.end = (self.z == 0) | (self.z == 3)

    def copy(self, src, slot, i, to):
        return pltpu.make_async_remote_copy(
            src_ref=src,
            dst_ref=self.land.at[slot],
            send_sem=self.send.at[self.base + i],
            recv_sem=self.recv.at[self.base + slot],
            device_id=(to, self.p["me"]),
            device_id_type=MESH,
        )

    def arrived(self, slot):
        self.copy(self.land.at[slot], slot, 0, self.z).wait_recv()

    def first(self):
        self.first_far()
        self.first_rest()

    def first_far(self):
        z, inward = self.z, self.inward

        @pl.when(self.end)
        def _():
            near, far = z + inward, z + 3 * inward
            self.copy(self.view(far), near, 0, near).start()

    def first_rest(self):
        z, inward = self.z, self.inward

        @pl.when(self.end)
        def _():
            near, mid = z + inward, z + 2 * inward
            self.copy(self.view(mid), z, 1, mid).start()
            self.copy(self.view(near), z, 2, near).start()

        @pl.when(jnp.logical_not(self.end))
        def _():
            inner, outer = z + inward, z - inward
            self.copy(self.view(inner), z, 0, inner).start()
            self.copy(self.view(outer), z, 1, outer).start()

    def second(self, acc, extra, local, i):
        @pl.when(jnp.logical_not(self.end))
        def _():
            far = self.z + 2 * self.inward
            own = pltpu.make_async_copy(self.view(far), acc, local.at[i])
            own.start()
            self.arrived(self.z)
            other = pltpu.make_async_copy(self.land.at[self.z], extra, local.at[i + 1])
            other.start()
            own.wait()
            other.wait()

            def step(at):
                acc[at, :] = (acc[at, :].astype(f32) + extra[at, :].astype(f32)).astype(bf16)

            over_rows(acc.shape[0], step)
            self.copy(acc, self.z, 2, far).start()

    def total(self, parts, local, i):
        z, inward = self.z, self.inward
        self.arrived(z + inward)
        self.arrived(z + 2 * inward)
        loads = [
            pltpu.make_async_copy(src, parts.at[k], local.at[i + k])
            for k, src in enumerate(
                (self.view(z), self.land.at[z + inward], self.land.at[z + 2 * inward])
            )
        ]
        for load in loads:
            load.start()
        for load in loads:
            load.wait()
        rows = parts.shape[1]
        three = lambda at: (parts[0, at, :].astype(f32) + parts[1, at, :].astype(f32)) + parts[
            2, at, :
        ].astype(f32)

        @pl.when(self.end)
        def _():
            def step(at):
                parts[0, at, :] = three(at).astype(bf16)

            over_rows(rows, step)

        @pl.when(jnp.logical_not(self.end))
        def _():
            self.arrived(z - inward)
            load = pltpu.make_async_copy(self.land.at[z - inward], parts.at[3], local.at[i + 3])
            load.start()
            load.wait()

            def step(at):
                parts[0, at, :] = (three(at) + parts[3, at, :].astype(f32)).astype(bf16)

            over_rows(rows, step)

    def finish(self):
        for i in range(3):
            self.copy(self.land.at[0], 0, i, self.z).wait_send()


CHUNKS = 4
EARLY = 3


class Local:
    def __init__(self, sems):
        self.sems, self.used = sems, 0

    def take(self, count=1):
        self.used += count
        return self.used - count


def feed_kernel(
    normed,
    cot,
    units,
    down,
    own_cot,
    hidden,
    gain,
    grad_hidden,
    gain_term,
    branch,
    out_terms,
    unit_sums,
    down_sums,
    unit_terms,
    down_terms,
    kept_units,
    kept_acts,
    unit_land,
    down_land,
    x,
    c,
    w,
    d,
    unit_stage,
    act_stage,
    unit_t,
    act_t,
    unit_grad,
    down_grad,
    unit_acc,
    down_acc,
    unit_parts,
    down_parts,
    turned,
    kept,
    paired,
    far,
    final,
    send,
    recv,
    gsend,
    grecv,
    zsend,
    zrecv,
    local,
):
    p = plane()
    barrier = pltpu.get_barrier_semaphore()
    others = [(p["dp"], p[name]) for name in ("sib", "xp", "yp")]
    for k in range(1, 4):
        others.append((lax.rem(p["dp"] + k, 4), p["me"]))
    for where in others:
        pl.semaphore_signal(barrier, inc=1, device_id=where, device_id_type=MESH)
    sems = Local(local)
    x_sem, c_sem, w_sem, d_sem = sems.take(8), sems.take(8), sems.take(2), sems.take(8)
    us_sem, as_sem, ug_sem, dg_sem = (sems.take() for _ in range(4))
    ub_sem, ab_sem, out_sem, last_w, last_d = (
        sems.take(2),
        sems.take(2),
        sems.take(2),
        sems.take(),
        sems.take(16),
    )
    z_sem, own_sem, turn_sem = sems.take(8), sems.take(), sems.take(2)
    shards, rows, width = normed.shape
    chunk = w.shape[3]
    part = chunk // 2
    piece = down.shape[2]

    def move(src, dst, i):
        return pltpu.make_async_copy(src, dst, local.at[i])

    def w_load(j):
        return move(units.at[:, :, pl.ds(j * chunk, chunk)], w.at[j % 2], w_sem + j % 2)

    def d_load(j):
        return [
            move(down.at[k, j], d.at[j % 2, pl.ds(k * piece, piece)], d_sem + 4 * (j % 2) + k)
            for k in range(4)
        ]

    def start_chunk(j):
        w_load(j).start()
        for load in d_load(j):
            load.start()

    start_chunk(0)
    for s in range(shards):
        move(normed.at[s], x.at[s], x_sem + s).start()
        move(cot.at[s], c.at[s], c_sem + s).start()
    pl.semaphore_wait(barrier, len(others))

    line = {}
    for j in range(EARLY):
        line[j] = (
            LineSum(
                p,
                lambda owner, j=j: unit_terms.at[
                    j, :, pl.ds(pl.multiple_of(owner * chunk, chunk), chunk)
                ],
                unit_land.at[j],
                zsend,
                zrecv,
                8 * j,
            ),
            LineSum(
                p,
                lambda owner, j=j: down_terms.at[
                    j, pl.ds(pl.multiple_of(owner * piece, piece), piece)
                ],
                down_land.at[j],
                zsend,
                zrecv,
                8 * j + 4,
            ),
        )

    def pass_on(j):
        line[j][0].second(unit_acc.at[j], unit_parts.at[0], local, z_sem)
        line[j][1].second(down_acc.at[j], down_parts.at[0], local, z_sem + 2)

    for j in range(CHUNKS):
        slot = j % 2
        w_load(j).wait()
        for load in d_load(j):
            load.wait()
        if j + 1 < CHUNKS:
            start_chunk(j + 1)
        if j > 0:
            move(unit_stage, kept_units.at[:, :, pl.ds(0, chunk)], us_sem).wait()
            move(act_stage, kept_acts.at[:, :, pl.ds(0, part)], as_sem).wait()

        @pl.loop(0, shards)
        def _(s):
            if j == 0:
                move(normed.at[s], x.at[s], x_sem + s).wait()
                move(cot.at[s], c.at[s], c_sem + s).wait()
            pre = dot(x[s], w[slot].reshape(shards * rows, chunk))
            grad_act = dot_t(c[s], d[slot])
            gate, up = pre[:, :part], pre[:, part:]
            sigmoid = 1.0 / (1.0 + jnp.exp(-gate))
            silu = gate * sigmoid
            act = (silu * up).astype(bf16).astype(f32)
            grad_gate = (grad_act * up * sigmoid * (1.0 + gate * (1.0 - sigmoid))).astype(bf16)
            grad_up = (grad_act * silu).astype(bf16)
            at = pl.ds(pl.multiple_of(s * rows, rows), rows)
            act_stage[s] = act.astype(bf16)
            unit_stage[s, :, :part] = grad_gate
            unit_stage[s, :, part:] = grad_up
            act_t[:, at] = act.T.astype(bf16)
            unit_t[:part, at] = grad_gate.astype(f32).T.astype(bf16)
            unit_t[part:, at] = grad_up.astype(f32).T.astype(bf16)

        move(unit_stage, kept_units.at[:, :, pl.ds(j * chunk, chunk)], us_sem).start()
        move(act_stage, kept_acts.at[:, :, pl.ds(j * part, part)], as_sem).start()

        @pl.loop(0, width // 256)
        def _(n):
            at = pl.ds(pl.multiple_of(n * 256, 256), 256)
            unit_grad[:, at] = dot(unit_t[...], x[:, :, at].reshape(shards * rows, 256)).astype(
                bf16
            )
            down_grad[:, at] = dot(act_t[...], c[:, :, at].reshape(shards * rows, 256)).astype(
                bf16
            )

        keep_unit = move(unit_grad, unit_terms.at[j], ug_sem)
        keep_down = move(down_grad, down_terms.at[j], dg_sem)
        keep_unit.start()
        keep_down.start()
        keep_unit.wait()
        keep_down.wait()
        if j < EARLY:
            for sums in line[j]:
                sums.first()
        if j >= 2:
            pass_on(j - 2)
    move(unit_stage, kept_units.at[:, :, pl.ds(0, chunk)], us_sem).wait()
    move(act_stage, kept_acts.at[:, :, pl.ds(0, part)], as_sem).wait()

    load_w = move(units, x, last_w)
    load_w.start()
    load_d = [
        move(down.at[k, j], c.at[j, pl.ds(k * piece, piece)], last_d + 4 * j + k)
        for j in range(CHUNKS)
        for k in range(4)
    ]
    for load in load_d:
        load.start()

    class Computed:
        names = [name for i, own, other in ORDER for name in (other, own)]

        def __init__(self):
            self.pairs, self.done = {}, 0
            self.load(0).start()

        def load(self, k):
            return move(
                kept_units.at[p[self.names[k]]],
                unit_t.at[pl.ds(k % 2 * rows, rows)],
                ub_sem + k % 2,
            )

        def compute(self, out):
            k = self.done
            self.load(k).wait()
            if k + 1 < len(self.names):
                self.load(k + 1).start()
            if k == 0:
                load_w.wait()

            @pl.loop(0, shards)
            def _(n):
                at = pl.ds(pl.multiple_of(n * rows, rows), rows)
                out[:, at] = dot_t(unit_t[k % 2 * rows : (k % 2 + 1) * rows], x[n]).astype(bf16)

            self.done += 1

        def ready(self, i):
            k = self.done // 2
            stage = unit_grad.at[pl.ds(k % 2 * rows, rows)]
            if k >= 2:
                self.pairs[ORDER[k - 2][0]].wait_send()
            self.compute(stage)
            self.pairs[i] = remote(p, stage, paired.at[i], send, recv, i, "sib")
            self.pairs[i].start()
            self.compute(kept.at[i])
            self.pairs[i].wait_recv()

        def finish(self):
            for i, _, _ in ORDER[2:]:
                self.pairs[i].wait_send()

    def act_load(s):
        slot = lax.rem(s, 2)
        half = pl.multiple_of(slot * (width // 2), width // 2)
        return move(kept_acts.at[s], act_t.at[:, pl.ds(half, width // 2)], ab_sem + slot)

    def out_store(s):
        slot = lax.rem(s, 2)
        at = pl.ds(pl.multiple_of(slot * rows, rows), rows)
        return move(unit_grad.at[at], out_terms.at[s], out_sem + slot)

    def forward_terms():
        source.finish()
        for load in load_d:
            load.wait()
        act_load(0).start()

        @pl.loop(0, shards)
        def _(s):
            act_load(s).wait()

            @pl.when(s + 1 < shards)
            def _():
                act_load(s + 1).start()

            @pl.when(s >= 2)
            def _():
                out_store(s - 2).wait()

            slot = lax.rem(s, 2)
            to = pl.ds(pl.multiple_of(slot * rows, rows), rows)

            @pl.loop(0, width // 256)
            def _(n):
                at = pl.ds(pl.multiple_of(n * 256, 256), 256)
                summed = jnp.zeros((rows, 256), f32)
                for j in range(CHUNKS):
                    base = pl.multiple_of(slot * (width // 2) + j * part, part)
                    summed = summed + dot(act_t[:, pl.ds(base, part)], c[j, :, at])
                unit_grad[to, at] = summed.astype(bf16)

            out_store(s).start()

        out_store(shards - 2).wait()
        out_store(shards - 1).wait()
        pass_on(2)

    source = Computed()
    sends = scatter_plane(
        p, source, rows, kept, paired, far, final, send, recv, meanwhile=forward_terms
    )
    gain_term[...] = jnp.zeros_like(gain_term)

    def step(at):
        g = total(kept, paired, final, at)
        h = hidden[at, :]
        scale = lax.rsqrt(jnp.mean(h * h, axis=-1, keepdims=True) + norm_eps)
        weighted = g * gain[...]
        inner = jnp.mean(weighted * h, axis=-1, keepdims=True)
        out = own_cot[at, :].astype(f32) + scale * weighted - h * (scale * scale * scale * inner)
        grad_hidden[at, :] = out
        down_grad[at, :] = out.astype(bf16)
        gain_term[...] += jnp.sum(g * h * scale, axis=0, keepdims=True)

    over_rows(rows, step)
    sent = gather_start(p, down_grad, branch, gsend, grecv, 0)
    own = move(down_grad, branch.at[p["me"]], own_sem)
    own.start()

    def sum_up(j):
        line[j][0].total(unit_parts, local, z_sem)

        @pl.loop(0, chunk // 128)
        def _(n):
            at = pl.ds(pl.multiple_of(n * 128, 128), 128)
            turned[:, at] = unit_parts[0, at, :].astype(f32).T.astype(bf16)

        line[j][1].total(down_parts, local, z_sem + 4)
        out = [move(turned, unit_sums.at[j], turn_sem), move(down_parts.at[0], down_sums.at[j], turn_sem + 1)]
        for copy in out:
            copy.start()
        for copy in out:
            copy.wait()

    sum_up(0)
    gather_finish(p, sent, down_grad, branch, gsend, grecv, 0)
    own.wait()
    sum_up(1)
    sum_up(2)
    for j in range(EARLY):
        for sums in line[j]:
            sums.finish()
    for copy in sends:
        copy.wait_send()


def feed_plane(normed, cot, units, down, own_cot, hidden, gain, collective_id):
    shards, rows, width = normed.shape
    wide = units.shape[1]
    chunk = wide // CHUNKS
    part = chunk // 2
    piece = down.shape[0] // 16
    sds = jax.ShapeDtypeStruct
    return pl.pallas_call(
        feed_kernel,
        out_shape=[
            sds((rows, width), f32),
            sds((1, width), f32),
            sds((shards, rows, width), bf16),
            sds((shards, rows, width), bf16),
            sds((EARLY, chunk, chunk), bf16),
            sds((EARLY, piece, width), bf16),
            sds((CHUNKS, chunk, width), bf16),
            sds((CHUNKS, part, width), bf16),
            sds((shards, rows, wide), bf16),
            sds((shards, rows, wide // 2), bf16),
            sds((EARLY, 4, chunk, chunk), bf16),
            sds((EARLY, 4, piece, width), bf16),
        ],
        in_specs=[ANY] * 4 + [VMEM] * 3,
        out_specs=[VMEM, VMEM] + [ANY] * 10,
        scratch_shapes=[
            pltpu.VMEM((shards, rows, width), bf16),
            pltpu.VMEM((shards, rows, width), bf16),
            pltpu.VMEM((2, shards, rows, chunk), bf16),
            pltpu.VMEM((2, part, width), bf16),
            pltpu.VMEM((shards, rows, chunk), bf16),
            pltpu.VMEM((shards, rows, part), bf16),
            pltpu.VMEM((chunk, shards * rows), bf16),
            pltpu.VMEM((part, shards * rows), bf16),
            pltpu.VMEM((chunk, width), bf16),
            pltpu.VMEM((part, width), bf16),
            pltpu.VMEM((EARLY, chunk, chunk), bf16),
            pltpu.VMEM((EARLY, piece, width), bf16),
            pltpu.VMEM((4, chunk, chunk), bf16),
            pltpu.VMEM((4, piece, width), bf16),
            pltpu.VMEM((chunk, chunk), bf16),
        ]
        + scatter_scratch(rows, width)[:6]
        + [
            DMA((GATHER_SEMS,)),
            DMA((GATHER_SEMS,)),
            DMA((8 * EARLY,)),
            DMA((8 * EARLY,)),
            DMA((72,)),
        ],
        compiler_params=pltpu.CompilerParams(
            collective_id=collective_id, has_side_effects=True, vmem_limit_bytes=62 * MIB
        ),
        cost_estimate=lasting(160),
    )(
        normed,
        cot,
        units.reshape(shards, rows, wide),
        down.reshape(4, CHUNKS, piece, width),
        own_cot,
        hidden,
        gain,
    )


def tail_kernel(
    devices,
    terms,
    out_terms,
    unit_terms,
    down_terms,
    head_terms,
    wo_terms,
    unit_sums,
    tokens,
    hidden,
    grad_hidden,
    gain,
    gain_two_term,
    grad_tokens,
    out_tokens,
    gain_sums,
    down_sum,
    wo_sum,
    units_out,
    heads_out,
    unit_sum,
    head_sum,
    unit_land,
    down_land,
    head_land,
    wo_land,
    gain_one_term,
    gain_mine,
    gain_land,
    unit_acc,
    down_acc,
    head_acc,
    wo_acc,
    unit_parts,
    down_parts,
    head_parts,
    turned,
    zsend,
    zrecv,
    esend,
    erecv,
    gsend,
    grecv,
    local,
    *scratch,
):
    p = plane()
    names = ("dg", "ds", "xp", "yp", "xs", "ys", "sib")
    mine = p["dp"] * 8 + p["me"]
    barrier = pltpu.get_barrier_semaphore()

    def other(k):
        to = lax.rem(mine + k, devices)
        return dict(device_id=(lax.div(to, 8), lax.rem(to, 8)), device_id_type=MESH), to

    @pl.loop(1, devices)
    def _(k):
        pl.semaphore_signal(barrier, inc=1, **other(k)[0])

    pl.semaphore_wait(barrier, devices - 1)
    chunk = unit_terms.shape[1]
    piece = down_terms.shape[1] // 4
    rows = tokens.shape[0]
    held = units_out.shape[2]
    line = [
        LineSum(p, lambda owner: head_terms.at[owner], head_land, zsend, zrecv, 0),
        LineSum(
            p,
            lambda owner: unit_terms.at[
                EARLY, :, pl.ds(pl.multiple_of(owner * chunk, chunk), chunk)
            ],
            unit_land,
            zsend,
            zrecv,
            4,
        ),
        LineSum(
            p,
            lambda owner: down_terms.at[EARLY, pl.ds(pl.multiple_of(owner * piece, piece), piece)],
            down_land,
            zsend,
            zrecv,
            8,
        ),
        LineSum(p, lambda owner: wo_terms.at[owner], wo_land, zsend, zrecv, 12),
    ]
    for sums in line:
        sums.first_far()
    for sums in line:
        sums.first_rest()
    kept, paired, far, final, send, recv, loads = scratch[:7]
    source = FromMemory(p, terms, kept, paired, send, recv, loads)
    copies = []

    def exchange(i, block, out):
        for j, name in enumerate(names):
            copies.append(remote(p, block(p[name]), out, esend, erecv, i * 7 + j, name))
            copies[-1].start()
        copies.append(pltpu.make_async_copy(block(p["me"]), out, local.at[i]))
        copies[-1].start()

    sends = scatter_plane(p, source, rows, kept, paired, far, final, send, recv)
    gain_one_term[...] = jnp.zeros_like(gain_one_term)

    def step(at):
        g = total(kept, paired, final, at)
        t = tokens[at, :].astype(f32)
        scale = lax.rsqrt(jnp.mean(t * t, axis=-1, keepdims=True) + norm_eps)
        weighted = g * gain[...]
        inner = jnp.mean(weighted * t, axis=-1, keepdims=True)
        grad_tokens[at, :] = (
            grad_hidden[at, :] + scale * weighted - t * (scale * scale * scale * inner)
        ).astype(bf16)
        gain_one_term[...] += jnp.sum(g * t * scale, axis=0, keepdims=True)

    over_rows(rows, step)
    line[0].second(head_acc, head_parts.at[0], local, 8)
    line[1].second(unit_acc, unit_parts.at[0], local, 8)
    line[2].second(down_acc, down_parts.at[0], local, 8)
    line[3].second(wo_acc, down_parts.at[1], local, 8)
    gain_mine[...] = jnp.zeros_like(gain_mine)
    for k in range(devices):
        at = slice(k * held, (k + 1) * held)
        gain_mine[k, 0:1, :held] = gain_one_term[:, at]
        gain_mine[k, 1:2, :held] = gain_two_term[:, at]

    def gain_copy(k):
        where, to = other(k)
        return pltpu.make_async_remote_copy(
            src_ref=gain_mine.at[to],
            dst_ref=gain_land.at[k],
            send_sem=gsend.at[k],
            recv_sem=grecv.at[k],
            **where,
        )

    @pl.loop(1, devices)
    def _(k):
        gain_copy(k).start()

    def rows_of(ref):
        return lambda s: ref.at[pl.ds(pl.multiple_of(s * held, held), held)]

    for j in range(EARLY):
        exchange(j, rows_of(unit_sums.at[j]), units_out.at[j, p["me"]])
    kept, paired, far, final, send, recv, loads = scratch[7:]
    source_out = FromMemory(p, out_terms, kept, paired, send, recv, loads)
    sends += scatter_plane(p, source_out, rows, kept, paired, far, final, send, recv)

    def step_out(at):
        out_tokens[at, :] = (hidden[at, :] + total(kept, paired, final, at)).astype(bf16)

    over_rows(rows, step_out)
    gain_land[0] = gain_mine[mine]

    @pl.loop(1, devices)
    def _(k):
        gain_copy(k).wait()

    gain_sums[...] = jnp.sum(gain_land[...], axis=0)

    def store(src, dst, i):
        copy = pltpu.make_async_copy(src, dst, local.at[i])
        copy.start()
        copy.wait()

    line[0].total(head_parts, local, 8)
    store(head_parts.at[0], head_sum, 8)
    exchange(EARLY + 1, rows_of(head_sum), heads_out.at[p["me"]])
    line[1].total(unit_parts, local, 8)

    @pl.loop(0, chunk // 128)
    def _(n):
        at = pl.ds(pl.multiple_of(n * 128, 128), 128)
        turned[:, at] = unit_parts[0, at, :].astype(f32).T.astype(bf16)

    store(turned, unit_sum, 8)
    exchange(EARLY, rows_of(unit_sum), units_out.at[EARLY, p["me"]])
    line[2].total(down_parts, local, 8)
    store(down_parts.at[0], down_sum, 8)
    line[3].total(down_parts, local, 8)
    store(down_parts.at[0], wo_sum, 8)
    for copy in copies:
        copy.wait()
    for sums in line:
        sums.finish()
    source.finish()
    source_out.finish()
    for copy in sends:
        copy.wait_send()


def tail_plane(
    groups,
    shards,
    terms,
    out_terms,
    unit_terms,
    down_terms,
    head_terms,
    wo_terms,
    unit_sums,
    tokens,
    hidden,
    grad_hidden,
    gain,
    gain_two_term,
    collective_id,
):
    rows, width = tokens.shape
    devices = groups * shards
    chunk, piece = unit_terms.shape[1], down_terms.shape[1] // 4
    held = width // devices
    span, heads_wide = head_terms.shape[1:]
    wo_rows = wo_terms.shape[1]
    sds = jax.ShapeDtypeStruct
    unit, down_, head, wo_ = (
        (chunk, chunk),
        (piece, width),
        (span, heads_wide),
        (wo_rows, width),
    )
    return pl.pallas_call(
        functools.partial(tail_kernel, devices),
        out_shape=[
            sds((rows, width), bf16),
            sds((rows, width), bf16),
            sds((8, 128), f32),
            sds(down_, bf16),
            sds(wo_, bf16),
            sds((CHUNKS, shards, held, chunk), bf16),
            sds((shards, held, heads_wide), bf16),
            sds(unit, bf16),
            sds(head, bf16),
            sds((4,) + unit, bf16),
            sds((4,) + down_, bf16),
            sds((4,) + head, bf16),
            sds((4,) + wo_, bf16),
        ],
        in_specs=[ANY] * 7 + [VMEM] * 5,
        out_specs=[VMEM] * 3 + [ANY] * 10,
        scratch_shapes=[
            pltpu.VMEM((1, width), f32),
            pltpu.VMEM((devices, 8, 128), f32),
            pltpu.VMEM((devices, 8, 128), f32),
            pltpu.VMEM(unit, bf16),
            pltpu.VMEM(down_, bf16),
            pltpu.VMEM(head, bf16),
            pltpu.VMEM(wo_, bf16),
            pltpu.VMEM((4,) + unit, bf16),
            pltpu.VMEM((4,) + down_, bf16),
            pltpu.VMEM((4,) + head, bf16),
            pltpu.VMEM(unit, bf16),
            DMA((16,)),
            DMA((16,)),
            DMA((35,)),
            DMA((35,)),
            DMA((devices,)),
            DMA((devices,)),
            DMA((12,)),
        ]
        + scatter_scratch(rows, width) * 2,
        compiler_params=pltpu.CompilerParams(
            collective_id=collective_id, has_side_effects=True, vmem_limit_bytes=60 * MIB
        ),
        cost_estimate=lasting(120),
    )(
        terms,
        out_terms,
        unit_terms,
        down_terms,
        head_terms,
        wo_terms,
        unit_sums,
        tokens,
        hidden,
        grad_hidden,
        gain,
        gain_two_term,
    )


def layer(
    groups,
    shards,
    tokens,
    doc_ids,
    cotangent,
    norm1_gain,
    w_query,
    w_key,
    w_value,
    w_out,
    norm2_gain,
    w_gate,
    w_up,
    w_down,
):
    rows, shard_len, width = tokens.shape
    count = rows * shard_len
    held = w_query.shape[0]
    hidden_held = w_down.shape[0]
    hidden_here = groups * hidden_held
    whole_heads = held % HD == 0
    outer, inner = (groups, held) if whole_heads else (1, width // shards)
    pairs = width // shards // PAIR
    flat = lambda v: v.reshape(shards * count, v.shape[-1])
    split = lambda v: v.reshape(shards, count, v.shape[-1])

    gains = lax.all_gather(
        jnp.stack([norm1_gain, norm2_gain]), ("dp", "seq"), axis=1, tiled=True
    ).astype(f32)
    gain_one, gain_two = gains[:1], gains[1:]

    def by_head(w):
        blocks = w.reshape(held, outer, shards, inner)
        return jnp.moveaxis(blocks, 2, 0).reshape(shards, held, pairs, PAIR)

    chunks = CHUNKS if shards == 8 else 1
    piece = hidden_held // chunks

    def by_unit(gate, up):
        blocks = jnp.stack([gate, up]).reshape(2, held, groups, shards, chunks, piece)
        return jnp.transpose(blocks, (3, 1, 4, 0, 2, 5)).reshape(shards, held, 2 * hidden_here)

    heads = jnp.stack([by_head(w) for w in (w_query, w_key, w_value)], axis=3)
    heads = heads.reshape(shards, held, 3 * pairs * PAIR)
    heads, units = exchange_plane([heads, by_unit(w_gate, w_up)], shards, 1)
    heads = heads.reshape(shards * held, heads.shape[-1])
    units = units.reshape(shards * held, units.shape[-1])
    qkv_weight = lax.all_gather(heads, "dp", axis=0, tiled=True)
    if whole_heads:
        out_weight = lax.all_gather(w_out, "dp", axis=0, tiled=True)
    else:
        whole = lax.all_gather(w_out, ("dp", "seq"), axis=0, tiled=True)
        out_weight = lax.dynamic_slice_in_dim(whole, lax.axis_index("seq") * inner, inner, 0)
    unit_weight = lax.all_gather(units, "dp", axis=0, tiled=True)
    down_weight = lax.all_gather(w_down, "dp", axis=0, tiled=True)

    own_tokens = tokens.reshape(count, width)
    own_cotangent = cotangent.reshape(count, width)
    inputs = own_tokens.astype(f32)
    own_normed = (inputs * rms_scale(inputs) * gain_one).astype(bf16)
    normed_split, cot_split = gather_plane([own_normed, own_cotangent], shards, 2)
    normed_one = flat(normed_split)

    cos, sin, starts = rope_tables(doc_ids, shards)
    starts = starts[:, None, :]
    by_row = lambda v: v.reshape(shards, rows, shard_len, v.shape[-1])
    pre = by_row(dot(normed_one, qkv_weight))
    rotated, attended, stats = attend(pre, cos, sin, starts)
    attended = flat(attended)
    hidden, normed_two = forward_plane(
        split(dot(attended, out_weight).astype(bf16)), own_tokens, gain_two, 3
    )

    if shards == 8:
        (
            grad_hidden,
            gain_two_term,
            branch,
            out_terms,
            unit_sums,
            _,
            unit_terms,
            down_terms,
            *_,
        ) = fed = feed_plane(
            normed_two, cot_split, unit_weight, down_weight, own_cotangent, hidden, gain_two, 4
        )
        down_sums = fed[5]
    else:
        cot = flat(cot_split)
        normed_two = flat(normed_two)
        gate_weight, up_weight = unit_weight[:, :hidden_here], unit_weight[:, hidden_here:]
        gate_pre, up_pre = dot(normed_two, gate_weight), dot(normed_two, up_weight)
        sigmoid = jax.nn.sigmoid(gate_pre)
        silu = gate_pre * sigmoid
        activated = (silu * up_pre).astype(bf16)
        out_terms = split(dot(activated, down_weight).astype(bf16))
        grad_act = dot_t(cot, down_weight)
        grad_gate_pre = grad_act * up_pre * sigmoid * (1.0 + gate_pre * (1.0 - sigmoid))
        grad_up_pre = grad_act * silu
        grad_units = jnp.concatenate([grad_gate_pre, grad_up_pre], axis=-1).astype(bf16)
        middle_terms = split(dot_t(grad_units, unit_weight).astype(bf16))
        unit_sums = lax.psum_scatter(
            dot(normed_two.T, grad_units).astype(bf16), "dp", scatter_dimension=0, tiled=True
        )
        down_sums = lax.psum_scatter(
            dot(activated.T, cot).astype(bf16), "dp", scatter_dimension=0, tiled=True
        )
        back, gain_two_term = norm_back(
            hidden, rms_scale(hidden), gain_two, reduce_plane(middle_terms)
        )
        grad_hidden = own_cotangent.astype(f32) + back
        branch = lax.all_gather(grad_hidden.astype(bf16), "seq")

    branch = flat(branch)
    out_w_terms = dot(attended.T, branch).astype(bf16)
    grad_attended = by_row(dot_t(branch, out_weight).astype(bf16))
    grad_pre = flat(attend_back(rotated, grad_attended, cos, sin, starts, stats))
    last_terms = split(dot_t(grad_pre, qkv_weight).astype(bf16))
    head_terms = dot(normed_one.T, grad_pre).astype(bf16)

    if shards == 8:
        (
            grad_tokens,
            out_tokens,
            gain_sums,
            down_last,
            grad_out,
            units_back,
            heads_back,
            *_,
        ) = tail_plane(
            groups,
            shards,
            last_terms,
            out_terms,
            unit_terms,
            down_terms,
            head_terms.reshape(groups, -1, head_terms.shape[-1]),
            out_w_terms.reshape(groups, -1, width),
            unit_sums,
            own_tokens,
            hidden,
            grad_hidden,
            gain_one,
            gain_two_term,
            5,
        )
        grad_norms = gain_sums[:2, :held]
        down_sums = jnp.concatenate([down_sums, down_last[None]]).reshape(hidden_held, width)
    else:
        if whole_heads:
            grad_out = lax.psum_scatter(out_w_terms, "dp", scatter_dimension=0, tiled=True)
        else:
            placed = lax.dynamic_update_slice_in_dim(
                jnp.zeros((width, width), bf16), out_w_terms, lax.axis_index("seq") * inner, 0
            )
            grad_out = lax.psum_scatter(placed, ("dp", "seq"), scatter_dimension=0, tiled=True)
        back, gain_one_term = norm_back(
            inputs, rms_scale(inputs), gain_one, reduce_plane(last_terms)
        )
        grad_tokens = (grad_hidden + back).astype(bf16)
        out_tokens = (hidden + reduce_plane(out_terms)).astype(bf16)
        head_sums = lax.psum_scatter(head_terms, "dp", scatter_dimension=0, tiled=True)
        heads_back, units_back = exchange_plane(
            [head_sums.reshape(shards, held, -1), unit_sums.reshape(shards, held, -1)], shards, 6
        )
        grad_norms = lax.psum_scatter(
            jnp.concatenate([gain_one_term, gain_two_term]),
            ("dp", "seq"),
            scatter_dimension=1,
            tiled=True,
        )

    heads_back = heads_back.reshape(shards, held, pairs, 3, PAIR)
    units_back = units_back.reshape(chunks, shards, held, 2, groups, piece)

    def head_grad(i):
        blocks = heads_back[:, :, :, i, :].reshape(shards, held, outer, inner)
        return jnp.moveaxis(blocks, 0, 2).reshape(held, width).astype(f32)

    def unit_grad(i):
        return (
            jnp.transpose(units_back[:, :, :, i], (2, 3, 1, 0, 4)).reshape(held, -1).astype(f32)
        )

    return (
        out_tokens.reshape(tokens.shape),
        grad_tokens.reshape(tokens.shape),
        grad_norms[0],
        head_grad(0),
        head_grad(1),
        head_grad(2),
        grad_out.astype(f32),
        grad_norms[1],
        unit_grad(0),
        unit_grad(1),
        down_sums.astype(f32),
    )


def solution(mesh):
    both = ("dp", "seq")
    return jax.shard_map(
        functools.partial(layer, mesh.shape["dp"], mesh.shape["seq"]),
        mesh=mesh,
        in_specs=(
            P("dp", "seq", None),
            P("dp", None),
            P("dp", "seq", None),
            P(both),
            P(both, None),
            P(both, None),
            P(both, None),
            P(both, None),
            P(both),
            P(both, None),
            P(both, None),
            P(both, None),
        ),
        out_specs=(
            P("dp", "seq", None),
            P("dp", "seq", None),
            P(both),
            P(both, None),
            P(both, None),
            P(both, None),
            P(both, None),
            P(both),
            P(both, None),
            P(both, None),
            P(both, None),
        ),
        check_vma=False,
    )
```

```python
import functools

import jax
import jax.numpy as jnp
from jax import lax
from jax.experimental import pallas as pl
from jax.experimental.pallas import tpu as pltpu
from jax.sharding import PartitionSpec as P

H = 32
HD = 64
PAIR = 2 * HD

rope_base = 130000.0
norm_eps = 1e-05

bf16 = jnp.bfloat16
f32 = jnp.float32
MESH = pl.DeviceIdType.MESH
ANY = pl.BlockSpec(memory_space=pl.ANY)
VMEM = pl.BlockSpec(memory_space=pltpu.VMEM)
DMA = pltpu.SemaphoreType.DMA
MIB = 1 << 20


def lasting(us):
    return pl.CostEstimate(flops=0, transcendentals=0, bytes_accessed=int(us * 3_500_000))


def plane():
    dp, s = lax.axis_index("dp"), lax.axis_index("seq")
    core, xb, yb = lax.rem(s, 2), lax.rem(lax.div(s, 2), 2), lax.div(s, 4)
    at = lambda y, x, c: y * 4 + x * 2 + c
    return dict(
        dp=dp,
        me=s,
        sib=at(yb, xb, 1 - core),
        xp=at(yb, 1 - xb, core),
        yp=at(1 - yb, xb, core),
        dg=at(1 - yb, 1 - xb, core),
        xs=at(yb, 1 - xb, 1 - core),
        ys=at(1 - yb, xb, 1 - core),
        ds=at(1 - yb, 1 - xb, 1 - core),
    )


def greet(p, names):
    barrier = pltpu.get_barrier_semaphore()
    for name in names:
        pl.semaphore_signal(barrier, inc=1, device_id=(p["dp"], p[name]), device_id_type=MESH)
    pl.semaphore_wait(barrier, len(names))


def remote(p, src, dst, send, recv, i, to):
    return pltpu.make_async_remote_copy(
        src_ref=src,
        dst_ref=dst,
        send_sem=send.at[i],
        recv_sem=recv.at[i],
        device_id=(p["dp"], p[to]),
        device_id_type=MESH,
    )


GATHER_SEMS = 25


def gather_start(p, src, out, send, recv, base):
    quarter = src.shape[0] // 4
    part = lambda ref, k: ref.at[pl.ds(k * quarter, quarter)]
    mine = out.at[p["me"]]
    sent = {}
    for j in range(4):
        kx, ky = j, (j + 2) % 4
        sent["x", kx] = remote(p, part(src, kx), part(mine, kx), send, recv, base + kx, "xp")
        sent["y", ky] = remote(p, part(src, ky), part(mine, ky), send, recv, base + 4 + ky, "yp")
        sent["x", kx].start()
        sent["y", ky].start()
    sent["s"] = remote(p, src, mine, send, recv, base + 8, "sib")
    sent["s"].start()
    return sent


def gather_pass(p, ref, send, recv, i, to):
    copy = remote(p, ref, ref, send, recv, i, to)
    copy.start()
    return copy


def gather_forward(p, sent, out, send, recv, base):
    quarter = out.shape[1] // 4
    part = lambda owner, k: out.at[p[owner], pl.ds(k * quarter, quarter)]
    passed = []
    for j in range(4):
        kx, ky = j, (j + 2) % 4
        sent["x", kx].wait_recv()
        if j < 2:
            sent["far", kx] = gather_pass(p, part("xp", kx), send, recv, base + 9 + kx, "yp")
        passed.append(gather_pass(p, part("xp", kx), send, recv, base + 13 + kx, "sib"))
        sent["y", ky].wait_recv()
        if j < 2:
            sent["far", ky] = gather_pass(p, part("yp", ky), send, recv, base + 9 + ky, "xp")
        passed.append(gather_pass(p, part("yp", ky), send, recv, base + 17 + ky, "sib"))

    def last():
        for k in (0, 2, 1, 3):
            sent["far", k].wait_recv()
            passed.append(gather_pass(p, part("dg", k), send, recv, base + 21 + k, "sib"))

    return passed, last


def gather_wait(sent, late):
    passed, last = late
    last()
    sent["s"].wait_recv()
    for copy in passed:
        copy.wait_recv()
    for copy in list(sent.values()) + passed:
        copy.wait_send()


def gather_finish(p, sent, out, send, recv, base):
    gather_wait(sent, gather_forward(p, sent, out, send, recv, base))


def gather_kernel(count, *refs):
    sources, outs = refs[:count], refs[count : 2 * count]
    send, recv, local = refs[2 * count :]
    p = plane()
    greet(p, ("sib", "xp", "yp"))
    sent, kept = [], []
    for i in range(count):
        sent.append(gather_start(p, sources[i], outs[i], send, recv, i * GATHER_SEMS))
        kept.append(pltpu.make_async_copy(sources[i], outs[i].at[p["me"]], local.at[i]))
        kept[i].start()
    for i in range(count):
        gather_finish(p, sent[i], outs[i], send, recv, i * GATHER_SEMS)
    for copy in kept:
        copy.wait()


def gather_plane(arrays, shards, collective_id):
    if shards != 8:
        return [lax.all_gather(a, "seq") for a in arrays]
    count = len(arrays)
    return pl.pallas_call(
        functools.partial(gather_kernel, count),
        out_shape=[jax.ShapeDtypeStruct((8,) + a.shape, a.dtype) for a in arrays],
        in_specs=[ANY] * count,
        out_specs=[ANY] * count,
        scratch_shapes=[DMA((GATHER_SEMS * count,)), DMA((GATHER_SEMS * count,)), DMA((count,))],
        compiler_params=pltpu.CompilerParams(collective_id=collective_id, has_side_effects=True),
        cost_estimate=lasting(40 * count),
    )(*arrays)


def exchange_kernel(count, *refs):
    sources, outs = refs[:count], refs[count : 2 * count]
    send, recv, local = refs[2 * count :]
    p = plane()
    names = ("dg", "ds", "xp", "yp", "xs", "ys", "sib")
    greet(p, names)
    copies = []
    for i in range(count):
        for j, name in enumerate(names):
            copies.append(
                remote(
                    p, sources[i].at[p[name]], outs[i].at[p["me"]], send, recv, i * 7 + j, name
                )
            )
            copies[-1].start()
        copies.append(
            pltpu.make_async_copy(sources[i].at[p["me"]], outs[i].at[p["me"]], local.at[i])
        )
        copies[-1].start()
    for copy in copies:
        copy.wait()


def exchange_plane(arrays, shards, collective_id):
    if shards != 8:
        return [lax.all_to_all(a, "seq", split_axis=0, concat_axis=0) for a in arrays]
    count = len(arrays)
    return pl.pallas_call(
        functools.partial(exchange_kernel, count),
        out_shape=[jax.ShapeDtypeStruct(a.shape, a.dtype) for a in arrays],
        in_specs=[ANY] * count,
        out_specs=[ANY] * count,
        scratch_shapes=[DMA((7 * count,)), DMA((7 * count,)), DMA((count,))],
        compiler_params=pltpu.CompilerParams(collective_id=collective_id, has_side_effects=True),
        cost_estimate=lasting(35),
    )(*arrays)


BLOCK = 16


def over_rows(rows, step):
    @pl.loop(0, rows // BLOCK)
    def _(i):
        step(pl.ds(pl.multiple_of(i * BLOCK, BLOCK), BLOCK))


def scatter_scratch(rows, width):
    return [
        pltpu.VMEM((4, rows, width), bf16),
        pltpu.VMEM((4, rows, width), bf16),
        pltpu.VMEM((2, rows // 2, width), bf16),
        pltpu.VMEM((2, rows, width), bf16),
        DMA((12,)),
        DMA((12,)),
        DMA((4,)),
    ]


class FromMemory:
    def __init__(self, p, terms, kept, paired, send, recv, local):
        self.loads, self.pairs = {}, {}
        for i, own, other in ORDER:
            self.loads[i] = pltpu.make_async_copy(terms.at[p[own]], kept.at[i], local.at[i])
            self.loads[i].start()
            self.pairs[i] = remote(p, terms.at[p[other]], paired.at[i], send, recv, i, "sib")
            self.pairs[i].start()

    def ready(self, i):
        self.loads[i].wait()
        self.pairs[i].wait_recv()

    def finish(self):
        for copy in self.pairs.values():
            copy.wait_send()


ORDER = ((3, "dg", "ds"), (1, "xp", "xs"), (2, "yp", "ys"), (0, "me", "sib"))


def scatter_plane(p, source, rows, kept, paired, far, final, send, recv, meanwhile=None):
    half = rows // 2
    low, high = pl.ds(0, half), pl.ds(half, half)
    sends = []

    def add_pair(i):
        source.ready(i)

        def step(at):
            kept[i, at, :] = (kept[i, at, :].astype(f32) + paired[i, at, :].astype(f32)).astype(
                bf16
            )

        over_rows(rows, step)

    def put(src, dst, i, to):
        copy = remote(p, src, dst, send, recv, i, to)
        copy.start()
        sends.append(copy)
        return copy

    add_pair(3)
    far_x = put(kept.at[3, low], far.at[0], 4, "xp")
    far_y = put(kept.at[3, high], far.at[1], 5, "yp")
    add_pair(1)
    near = [put(kept.at[1, low], final.at[0, low], 6, "xp")]
    add_pair(2)
    near.append(put(kept.at[2, high], final.at[1, high], 7, "yp"))
    far_x.wait_recv()

    def step_x(at):
        kept[2, at, :] = (kept[2, at, :].astype(f32) + far[0, at, :].astype(f32)).astype(bf16)

    over_rows(half, step_x)
    near.append(put(kept.at[2, low], final.at[1, low], 8, "yp"))
    far_y.wait_recv()

    def step_y(at):
        up = pl.ds(pl.multiple_of(at.start + half, BLOCK), BLOCK)
        kept[1, up, :] = (kept[1, up, :].astype(f32) + far[1, at, :].astype(f32)).astype(bf16)

    over_rows(half, step_y)
    near.append(put(kept.at[1, high], final.at[0, high], 9, "xp"))
    source.ready(0)
    if meanwhile is not None:
        meanwhile()
    for copy in near:
        copy.wait_recv()
    return sends


def total(kept, paired, final, at):
    return (kept[0, at, :].astype(f32) + paired[0, at, :].astype(f32)) + (
        final[0, at, :].astype(f32) + final[1, at, :].astype(f32)
    )


def reduce_plane(terms):
    rows = terms.shape[1]
    return lax.psum_scatter(terms, "seq", scatter_dimension=0, tiled=False).astype(f32).reshape(
        rows, terms.shape[2]
    )


def rms_scale(values):
    return lax.rsqrt(jnp.mean(values * values, axis=-1, keepdims=True) + norm_eps)


def norm_back(values, scale, gain, grad):
    weighted = grad * gain
    inner = jnp.mean(weighted * values, axis=-1, keepdims=True)
    return (
        scale * weighted - values * (scale * scale * scale) * inner,
        jnp.sum(grad * values * scale, axis=0, keepdims=True),
    )


def swap_halves(v, first):
    width = v.shape[-1]
    return jnp.where(first, pltpu.roll(v, width - HD // 2, 1), pltpu.roll(v, HD // 2, 1))


def dot_t(a, b):
    return lax.dot_general(a, b, (((1,), (1,)), ((), ())), preferred_element_type=f32)


def dot(a, b):
    return jnp.dot(a, b, preferred_element_type=f32)


def allowed_pairs(start, keys, queries, offset):
    key = lax.broadcasted_iota(jnp.int32, (keys, queries), 0)
    query = lax.broadcasted_iota(jnp.int32, (keys, queries), 1) + offset
    return (key >= start) & (key <= query)


def attend_pair(pre, cos, sin, starts, rotated, attended, stats, r, pair):
    shards, _, shard_len, _ = pre.shape
    length = shards * shard_len
    block = min(256, length)
    per = block // shard_len
    lanes = lambda i: pl.ds(pl.multiple_of((pair * 3 + i) * PAIR, PAIR), PAIR)
    first = lax.rem(lax.broadcasted_iota(jnp.int32, (length, PAIR), 1), HD) < HD // 2
    cos_all, sin_all = cos[:, r].reshape(length, PAIR), sin[:, r].reshape(length, PAIR)

    def rotate(i):
        v = pre[:, r, :, lanes(i)].reshape(length, PAIR)
        return (v * cos_all + swap_halves(v, first) * sin_all).astype(bf16)

    query, key = rotate(0), rotate(1)
    value = pre[:, r, :, lanes(2)].reshape(length, PAIR)
    value_t = value.T.astype(bf16)
    for i, v in enumerate((query, key, value.astype(bf16))):
        rotated[:, r, :, lanes(i)] = v.reshape(shards, shard_len, PAIR)
    left = lax.broadcasted_iota(jnp.int32, (block, PAIR), 1) < HD
    top = lax.broadcasted_iota(jnp.int32, (PAIR, block), 0) < HD
    scaled = query * jnp.asarray(0.125, bf16)
    here_lanes = pl.ds(pl.multiple_of(pair * PAIR, PAIR), PAIR)
    for i in range(length // block):
        keys = (i + 1) * block
        at = slice(i * block, (i + 1) * block)
        mask = allowed_pairs(starts[:, at], keys, block, i * block)
        here = scaled[at]
        results = []
        for h in range(2):
            own = jnp.where(left if h == 0 else ~left, here, jnp.zeros_like(here))
            scores = jnp.where(mask, dot_t(key[:keys], own), -1e30)
            peak = jnp.max(scores, axis=0, keepdims=True)
            shifted = jnp.exp(scores - peak)
            summed = jnp.sum(shifted, axis=0, keepdims=True)
            probs = (shifted * (1.0 / summed)).astype(bf16)
            results.append(dot(value_t[:, :keys], probs))
            stats[r, pair, h : h + 1, at] = peak + jnp.log(summed)
        merged = jnp.where(top, results[0], results[1]).T.astype(bf16)
        attended[i * per : (i + 1) * per, r, :, here_lanes] = merged.reshape(
            per, shard_len, PAIR
        )


def attend_kernel(pre, cos, sin, starts, rotated, attended, stats):
    attend_pair(pre, cos, sin, starts[0], rotated, attended, stats, 0, 0)


def attend(pre, cos, sin, starts):
    shards, rows, shard_len, width = pre.shape
    pairs = width // (3 * PAIR)
    length = shards * shard_len
    wide = pl.BlockSpec((shards, 1, shard_len, 3 * PAIR), lambda r, p: (0, r, 0, p))
    narrow = pl.BlockSpec((shards, 1, shard_len, PAIR), lambda r, p: (0, r, 0, p))
    table = pl.BlockSpec((shards, 1, shard_len, PAIR), lambda r, p: (0, r, 0, 0))
    return pl.pallas_call(
        attend_kernel,
        grid=(rows, pairs),
        out_shape=[
            jax.ShapeDtypeStruct(pre.shape, bf16),
            jax.ShapeDtypeStruct((shards, rows, shard_len, pairs * PAIR), bf16),
            jax.ShapeDtypeStruct((rows, pairs, 2, length), f32),
        ],
        in_specs=[wide, table, table, pl.BlockSpec((1, 1, length), lambda r, p: (r, 0, 0))],
        out_specs=[wide, narrow, pl.BlockSpec((1, 1, 2, length), lambda r, p: (r, p, 0, 0))],
        compiler_params=pltpu.CompilerParams(vmem_limit_bytes=48 * MIB),
        cost_estimate=pl.CostEstimate(
            flops=rows * pairs * 2 * length * length * 256 * 2,
            bytes_accessed=pre.size * 8,
            transcendentals=rows * pairs * length * length,
        ),
    )(pre, cos, sin, starts)


def attend_back_kernel(rotated, grad, cos, sin, starts, stats, result, key_acc, value_acc):
    shards, _, shard_len, _ = rotated.shape
    length = shards * shard_len
    block = min(256, length)
    per = block // shard_len
    all_in = rotated[...].reshape(length, 3 * PAIR)
    query, key, value = all_in[:, :PAIR], all_in[:, PAIR : 2 * PAIR], all_in[:, 2 * PAIR :]
    grad_all = grad[...].reshape(length, PAIR)
    key_t = key.astype(f32).T.astype(bf16)
    left = lax.broadcasted_iota(jnp.int32, (block, PAIR), 1) < HD
    top = lax.broadcasted_iota(jnp.int32, (PAIR, block), 0) < HD
    first = lax.rem(lax.broadcasted_iota(jnp.int32, (length, PAIR), 1), HD) < HD // 2
    key_acc[...] = jnp.zeros_like(key_acc)
    value_acc[...] = jnp.zeros_like(value_acc)

    for i in range(length // block):
        keys = (i + 1) * block
        at = slice(i * block, (i + 1) * block)
        start = starts[0, :, at]
        mask = allowed_pairs(start, keys, block, i * block)
        results = []
        for h in range(2):
            side = left if h == 0 else ~left
            own = jnp.where(side, query[at], jnp.zeros_like(query[at]))
            own_grad = jnp.where(side, grad_all[at], jnp.zeros_like(grad_all[at]))
            scores = dot_t(key[:keys], own * jnp.asarray(0.125, bf16))
            probs = jnp.exp(jnp.where(mask, scores - stats[0, 0, h : h + 1, at], -1e30))
            grad_probs = dot_t(value[:keys], own_grad)
            inner = jnp.sum(probs * grad_probs, axis=0, keepdims=True)
            grad_scores = (probs * (grad_probs - inner) * 0.125).astype(bf16)
            key_acc[:keys, :] += dot(grad_scores, own)
            value_acc[:keys, :] += dot(probs.astype(bf16), own_grad)
            results.append(dot(key_t[:, :keys], grad_scores))
        merged = jnp.where(top, results[0], results[1]).T
        cos_here = cos[i * per : (i + 1) * per].reshape(block, PAIR)
        sin_here = sin[i * per : (i + 1) * per].reshape(block, PAIR)
        turned = merged * cos_here - swap_halves(merged, first[:block]) * sin_here
        result[i * per : (i + 1) * per, 0, :, :PAIR] = turned.astype(bf16).reshape(
            per, shard_len, PAIR
        )
    cos_all, sin_all = cos[...].reshape(length, PAIR), sin[...].reshape(length, PAIR)
    key_grad = key_acc[...]
    turned = key_grad * cos_all - swap_halves(key_grad, first) * sin_all
    result[:, 0, :, PAIR : 2 * PAIR] = turned.astype(bf16).reshape(shards, shard_len, PAIR)
    result[:, 0, :, 2 * PAIR :] = value_acc[...].astype(bf16).reshape(shards, shard_len, PAIR)


def attend_back(rotated, grad, cos, sin, starts, stats):
    shards, rows, shard_len, width = rotated.shape
    pairs = width // (3 * PAIR)
    length = shards * shard_len
    wide = pl.BlockSpec((shards, 1, shard_len, 3 * PAIR), lambda r, p: (0, r, 0, p))
    narrow = pl.BlockSpec((shards, 1, shard_len, PAIR), lambda r, p: (0, r, 0, p))
    table = pl.BlockSpec((shards, 1, shard_len, PAIR), lambda r, p: (0, r, 0, 0))
    return pl.pallas_call(
        attend_back_kernel,
        grid=(rows, pairs),
        out_shape=jax.ShapeDtypeStruct(rotated.shape, bf16),
        in_specs=[
            wide,
            narrow,
            table,
            table,
            pl.BlockSpec((1, 1, length), lambda r, p: (r, 0, 0)),
            pl.BlockSpec((1, 1, 2, length), lambda r, p: (r, p, 0, 0)),
        ],
        out_specs=wide,
        scratch_shapes=[pltpu.VMEM((length, PAIR), f32), pltpu.VMEM((length, PAIR), f32)],
        compiler_params=pltpu.CompilerParams(vmem_limit_bytes=48 * MIB),
        cost_estimate=pl.CostEstimate(
            flops=rows * pairs * 5 * length * length * 256 * 2,
            bytes_accessed=rotated.size * 6,
            transcendentals=rows * pairs * length * length,
        ),
    )(rotated, grad, cos, sin, starts, stats)


def rope_tables(doc_ids, shards):
    rows, length = doc_ids.shape
    places = lax.broadcasted_iota(jnp.int32, doc_ids.shape, 1)
    earlier = jnp.concatenate([doc_ids[:, :1], doc_ids[:, :-1]], axis=1)
    starts = lax.cummax(jnp.where(doc_ids != earlier, places, 0), axis=1)
    positions = (places - starts).astype(f32)
    frequency = rope_base ** (-(jnp.arange(HD // 2, dtype=f32) * 2.0 / HD))
    angles = positions[..., None] * frequency
    cos, sin = jnp.cos(angles), jnp.sin(angles)
    lay = lambda v: jnp.moveaxis(
        jnp.concatenate(v, axis=-1).reshape(rows, shards, length // shards, PAIR), 0, 1
    )
    return lay([cos] * 4), lay([-sin, sin, -sin, sin]), starts


class LineSum:
    def __init__(self, p, view, land, send, recv, base):
        self.p, self.view, self.land = p, view, land
        self.send, self.recv, self.base = send, recv, base
        self.z = p["dp"]
        self.inward = 1 - 2 * lax.div(self.z, 2)
        self.end = (self.z == 0) | (self.z == 3)

    def copy(self, src, slot, i, to):
        return pltpu.make_async_remote_copy(
            src_ref=src,
            dst_ref=self.land.at[slot],
            send_sem=self.send.at[self.base + i],
            recv_sem=self.recv.at[self.base + slot],
            device_id=(to, self.p["me"]),
            device_id_type=MESH,
        )

    def arrived(self, slot):
        self.copy(self.land.at[slot], slot, 0, self.z).wait_recv()

    def first(self):
        self.first_far()
        self.first_rest()

    def first_far(self):
        z, inward = self.z, self.inward

        @pl.when(self.end)
        def _():
            near, far = z + inward, z + 3 * inward
            self.copy(self.view(far), near, 0, near).start()

    def first_rest(self):
        z, inward = self.z, self.inward

        @pl.when(self.end)
        def _():
            near, mid = z + inward, z + 2 * inward
            self.copy(self.view(mid), z, 1, mid).start()
            self.copy(self.view(near), z, 2, near).start()

        @pl.when(jnp.logical_not(self.end))
        def _():
            inner, outer = z + inward, z - inward
            self.copy(self.view(inner), z, 0, inner).start()
            self.copy(self.view(outer), z, 1, outer).start()

    def second(self, acc, extra, local, i):
        @pl.when(jnp.logical_not(self.end))
        def _():
            far = self.z + 2 * self.inward
            own = pltpu.make_async_copy(self.view(far), acc, local.at[i])
            own.start()
            self.arrived(self.z)
            other = pltpu.make_async_copy(self.land.at[self.z], extra, local.at[i + 1])
            other.start()
            own.wait()
            other.wait()

            def step(at):
                acc[at, :] = (acc[at, :].astype(f32) + extra[at, :].astype(f32)).astype(bf16)

            over_rows(acc.shape[0], step)
            self.copy(acc, self.z, 2, far).start()

    def total(self, parts, local, i):
        z, inward = self.z, self.inward
        self.arrived(z + inward)
        self.arrived(z + 2 * inward)
        loads = [
            pltpu.make_async_copy(src, parts.at[k], local.at[i + k])
            for k, src in enumerate(
                (self.view(z), self.land.at[z + inward], self.land.at[z + 2 * inward])
            )
        ]
        for load in loads:
            load.start()
        for load in loads:
            load.wait()
        rows = parts.shape[1]
        three = lambda at: (parts[0, at, :].astype(f32) + parts[1, at, :].astype(f32)) + parts[
            2, at, :
        ].astype(f32)

        @pl.when(self.end)
        def _():
            def step(at):
                parts[0, at, :] = three(at).astype(bf16)

            over_rows(rows, step)

        @pl.when(jnp.logical_not(self.end))
        def _():
            self.arrived(z - inward)
            load = pltpu.make_async_copy(self.land.at[z - inward], parts.at[3], local.at[i + 3])
            load.start()
            load.wait()

            def step(at):
                parts[0, at, :] = (three(at) + parts[3, at, :].astype(f32)).astype(bf16)

            over_rows(rows, step)

    def finish(self):
        for i in range(3):
            self.copy(self.land.at[0], 0, i, self.z).wait_send()


def feed_kernel(
    normed,
    cot,
    units,
    down,
    w_down,
    own_cot,
    hidden,
    gain,
    grad_hidden,
    gain_term,
    branch,
    out_terms,
    unit_sums,
    down_sums,
    unit_terms,
    down_terms,
    kept_units,
    kept_acts,
    unit_land,
    down_land,
    late_units,
    late_down,
    x,
    c,
    w,
    d,
    unit_stage,
    act_stage,
    unit_t,
    act_t,
    unit_grad,
    down_grad,
    unit_acc,
    down_acc,
    unit_parts,
    down_parts,
    turned,
    kept,
    paired,
    far,
    final,
    send,
    recv,
    gsend,
    grecv,
    zsend,
    zrecv,
    lsend,
    lrecv,
    local,
):
    p = plane()
    barrier = pltpu.get_barrier_semaphore()
    others = [(p["dp"], p[name]) for name in ("sib", "xp", "yp")]
    for k in range(1, 4):
        others.append((lax.rem(p["dp"] + k, 4), p["me"]))
    for where in others:
        pl.semaphore_signal(barrier, inc=1, device_id=where, device_id_type=MESH)
    sems = Local(local)
    x_sem, c_sem, w_sem, d_sem = sems.take(8), sems.take(8), sems.take(2), sems.take(2)
    us_sem, as_sem, ug_sem, dg_sem = (sems.take() for _ in range(4))
    ub_sem, ab_sem, out_sem, last_w, last_d = (
        sems.take(2),
        sems.take(2),
        sems.take(2),
        sems.take(32),
        sems.take(16),
    )
    z_sem, own_sem, turn_sem = sems.take(8), sems.take(), sems.take(2)
    shards, rows, width = normed.shape
    chunk = w.shape[3]
    part = chunk // 2
    piece = down.shape[2]
    all_units = lambda j: units.at[j] if j < EARLY else late_units
    all_down = lambda j: down.at[j] if j < EARLY else late_down
    late = (
        LineGather(
            p, units.at[EARLY, p["dp"]], late_units, lsend, lrecv, 0, local.at[sems.take()]
        ),
        LineGather(
            p,
            w_down.at[pl.ds(EARLY * piece, piece)],
            late_down,
            lsend,
            lrecv,
            1,
            local.at[sems.take()],
        ),
    )

    def move(src, dst, i):
        return pltpu.make_async_copy(src, dst, local.at[i])

    def chunk_loads(j):
        return (
            move(all_units(j), w.at[j % 2], w_sem + j % 2),
            move(all_down(j), d.at[j % 2], d_sem + j % 2),
        )

    def start_chunk(j):
        for load in chunk_loads(j):
            load.start()

    start_chunk(0)
    for s in range(shards):
        move(normed.at[s], x.at[s], x_sem + s).start()
        move(cot.at[s], c.at[s], c_sem + s).start()
    pl.semaphore_wait(barrier, len(others))
    for gather in late:
        gather.start()

    line = {}
    for j in range(EARLY):
        line[j] = (
            LineSum(
                p,
                lambda owner, j=j: unit_terms.at[
                    j, :, pl.ds(pl.multiple_of(owner * chunk, chunk), chunk)
                ],
                unit_land.at[j],
                zsend,
                zrecv,
                8 * j,
            ),
            LineSum(
                p,
                lambda owner, j=j: down_terms.at[
                    j, pl.ds(pl.multiple_of(owner * piece, piece), piece)
                ],
                down_land.at[j],
                zsend,
                zrecv,
                8 * j + 4,
            ),
        )

    def pass_on(j):
        line[j][0].second(unit_acc.at[j], unit_parts.at[0], local, z_sem)
        line[j][1].second(down_acc.at[j], down_parts.at[0], local, z_sem + 2)

    for j in range(CHUNKS):
        slot = j % 2
        if j == EARLY:
            for gather in late:
                gather.finish()
            start_chunk(j)
        for load in chunk_loads(j):
            load.wait()
        if j + 1 < EARLY:
            start_chunk(j + 1)
        if j > 0:
            move(unit_stage, kept_units.at[:, :, pl.ds(0, chunk)], us_sem).wait()
            move(act_stage, kept_acts.at[:, :, pl.ds(0, part)], as_sem).wait()

        @pl.loop(0, shards)
        def _(s):
            if j == 0:
                move(normed.at[s], x.at[s], x_sem + s).wait()
                move(cot.at[s], c.at[s], c_sem + s).wait()
            pre = dot(x[s], w[slot].reshape(shards * rows, chunk))
            grad_act = dot_t(c[s], d[slot].reshape(part, width))
            gate, up = pre[:, :part], pre[:, part:]
            sigmoid = 1.0 / (1.0 + jnp.exp(-gate))
            silu = gate * sigmoid
            act = (silu * up).astype(bf16).astype(f32)
            grad_gate = (grad_act * up * sigmoid * (1.0 + gate * (1.0 - sigmoid))).astype(bf16)
            grad_up = (grad_act * silu).astype(bf16)
            at = pl.ds(pl.multiple_of(s * rows, rows), rows)
            act_stage[s] = act.astype(bf16)
            unit_stage[s, :, :part] = grad_gate
            unit_stage[s, :, part:] = grad_up
            act_t[:, at] = act.T.astype(bf16)
            unit_t[:part, at] = grad_gate.astype(f32).T.astype(bf16)
            unit_t[part:, at] = grad_up.astype(f32).T.astype(bf16)

        move(unit_stage, kept_units.at[:, :, pl.ds(j * chunk, chunk)], us_sem).start()
        move(act_stage, kept_acts.at[:, :, pl.ds(j * part, part)], as_sem).start()

        @pl.loop(0, width // 256)
        def _(n):
            at = pl.ds(pl.multiple_of(n * 256, 256), 256)
            unit_grad[:, at] = dot(unit_t[...], x[:, :, at].reshape(shards * rows, 256)).astype(
                bf16
            )
            down_grad[:, at] = dot(act_t[...], c[:, :, at].reshape(shards * rows, 256)).astype(
                bf16
            )

        keep_unit = move(unit_grad, unit_terms.at[j], ug_sem)
        keep_down = move(down_grad, down_terms.at[j], dg_sem)
        keep_unit.start()
        keep_down.start()
        keep_unit.wait()
        keep_down.wait()
        for gather in late:
            if j == 0:
                gather.second()
            if j == 1:
                gather.third()
        if j < EARLY:
            for sums in line[j]:
                sums.first()
        if j >= 2:
            pass_on(j - 2)
    move(unit_stage, kept_units.at[:, :, pl.ds(0, chunk)], us_sem).wait()
    move(act_stage, kept_acts.at[:, :, pl.ds(0, part)], as_sem).wait()

    load_w = [
        move(
            all_units(j).at[k // 2, pl.ds(k % 2 * rows, rows)],
            x.at[k, :, pl.ds(j * chunk, chunk)],
            last_w + 8 * j + k,
        )
        for j in range(CHUNKS)
        for k in range(shards)
    ]
    load_d = [
        move(all_down(j).at[k], c.at[j, pl.ds(k * piece, piece)], last_d + 4 * j + k)
        for j in range(CHUNKS)
        for k in range(4)
    ]
    for load in load_w + load_d:
        load.start()

    order = [name for _, own, far_name in ORDER for name in (far_name, own)]

    def load_kept(k):
        return move(
            kept_units.at[p[order[k]]], unit_t.at[pl.ds(k % 2 * rows, rows)], ub_sem + k % 2
        )

    load_kept(0).start()

    def produce(name, out):
        k = order.index(name)
        load_kept(k).wait()
        if k + 1 < len(order):
            load_kept(k + 1).start()
        if k == 0:
            for load in load_w:
                load.wait()

        @pl.loop(0, shards)
        def _(n):
            at = pl.ds(pl.multiple_of(n * rows, rows), rows)
            out[:, at] = dot_t(unit_t[k % 2 * rows : (k % 2 + 1) * rows], x[n]).astype(bf16)

    def act_load(s):
        slot = lax.rem(s, 2)
        half = pl.multiple_of(slot * (width // 2), width // 2)
        return move(kept_acts.at[s], act_t.at[:, pl.ds(half, width // 2)], ab_sem + slot)

    def out_store(s):
        slot = lax.rem(s, 2)
        at = pl.ds(pl.multiple_of(slot * rows, rows), rows)
        return move(unit_grad.at[at], out_terms.at[s], out_sem + slot)

    def forward_terms():
        source.finish()
        for load in load_d:
            load.wait()
        act_load(0).start()

        @pl.loop(0, shards)
        def _(s):
            act_load(s).wait()

            @pl.when(s + 1 < shards)
            def _():
                act_load(s + 1).start()

            @pl.when(s >= 2)
            def _():
                out_store(s - 2).wait()

            slot = lax.rem(s, 2)
            to = pl.ds(pl.multiple_of(slot * rows, rows), rows)

            @pl.loop(0, width // 256)
            def _(n):
                at = pl.ds(pl.multiple_of(n * 256, 256), 256)
                summed = jnp.zeros((rows, 256), f32)
                for j in range(CHUNKS):
                    base = pl.multiple_of(slot * (width // 2) + j * part, part)
                    summed = summed + dot(act_t[:, pl.ds(base, part)], c[j, :, at])
                unit_grad[to, at] = summed.astype(bf16)

            out_store(s).start()

        out_store(shards - 2).wait()
        out_store(shards - 1).wait()
        pass_on(2)

    source = Produced(p, produce, unit_grad, kept, paired, send, recv)
    sends = scatter_plane(
        p, source, rows, kept, paired, far, final, send, recv, meanwhile=forward_terms
    )
    gain_term[...] = jnp.zeros_like(gain_term)

    def step(at):
        g = total(kept, paired, final, at)
        h = hidden[at, :]
        scale = lax.rsqrt(jnp.mean(h * h, axis=-1, keepdims=True) + norm_eps)
        weighted = g * gain[...]
        inner = jnp.mean(weighted * h, axis=-1, keepdims=True)
        out = own_cot[at, :].astype(f32) + scale * weighted - h * (scale * scale * scale * inner)
        grad_hidden[at, :] = out
        down_grad[at, :] = out.astype(bf16)
        gain_term[...] += jnp.sum(g * h * scale, axis=0, keepdims=True)

    over_rows(rows, step)
    sent = gather_start(p, down_grad, branch, gsend, grecv, 0)
    own = move(down_grad, branch.at[p["me"]], own_sem)
    own.start()

    def sum_up(j):
        line[j][0].total(unit_parts, local, z_sem)

        @pl.loop(0, chunk // 128)
        def _(n):
            at = pl.ds(pl.multiple_of(n * 128, 128), 128)
            turned[:, at] = unit_parts[0, at, :].astype(f32).T.astype(bf16)

        line[j][1].total(down_parts, local, z_sem + 4)
        out = [move(turned, unit_sums.at[j], turn_sem), move(down_parts.at[0], down_sums.at[j], turn_sem + 1)]
        for copy in out:
            copy.start()
        for copy in out:
            copy.wait()

    sum_up(0)
    gather_finish(p, sent, branch, gsend, grecv, 0)
    own.wait()
    sum_up(1)
    sum_up(2)
    for j in range(EARLY):
        for sums in line[j]:
            sums.finish()
    for copy in sends:
        copy.wait_send()


def feed_plane(normed, cot, units, down, w_down, own_cot, hidden, gain, collective_id):
    shards, rows, width = normed.shape
    chunk = units.shape[3]
    wide = chunk * CHUNKS
    part = chunk // 2
    piece = down.shape[2]
    sds = jax.ShapeDtypeStruct
    return pl.pallas_call(
        feed_kernel,
        out_shape=[
            sds((rows, width), f32),
            sds((1, width), f32),
            sds((shards, rows, width), bf16),
            sds((shards, rows, width), bf16),
            sds((EARLY, chunk, chunk), bf16),
            sds((EARLY, piece, width), bf16),
            sds((CHUNKS, chunk, width), bf16),
            sds((CHUNKS, part, width), bf16),
            sds((shards, rows, wide), bf16),
            sds((shards, rows, wide // 2), bf16),
            sds((EARLY, 4, chunk, chunk), bf16),
            sds((EARLY, 4, piece, width), bf16),
            sds((4, width // 4, chunk), bf16),
            sds((4, piece, width), bf16),
        ],
        in_specs=[ANY] * 5 + [VMEM] * 3,
        out_specs=[VMEM, VMEM] + [ANY] * 12,
        scratch_shapes=[
            pltpu.VMEM((shards, rows, width), bf16),
            pltpu.VMEM((shards, rows, width), bf16),
            pltpu.VMEM((2, 4, width // 4, chunk), bf16),
            pltpu.VMEM((2, 4, piece, width), bf16),
            pltpu.VMEM((shards, rows, chunk), bf16),
            pltpu.VMEM((shards, rows, part), bf16),
            pltpu.VMEM((chunk, shards * rows), bf16),
            pltpu.VMEM((part, shards * rows), bf16),
            pltpu.VMEM((chunk, width), bf16),
            pltpu.VMEM((part, width), bf16),
            pltpu.VMEM((EARLY, chunk, chunk), bf16),
            pltpu.VMEM((EARLY, piece, width), bf16),
            pltpu.VMEM((4, chunk, chunk), bf16),
            pltpu.VMEM((4, piece, width), bf16),
            pltpu.VMEM((chunk, chunk), bf16),
        ]
        + scatter_scratch(rows, width)[:6]
        + [
            DMA((GATHER_SEMS,)),
            DMA((GATHER_SEMS,)),
            DMA((8 * EARLY,)),
            DMA((8 * EARLY,)),
            DMA((2 * LINE_SEMS,)),
            DMA((2 * LINE_SEMS,)),
            DMA((100,)),
        ],
        compiler_params=pltpu.CompilerParams(
            collective_id=collective_id, has_side_effects=True, vmem_limit_bytes=62 * MIB
        ),
        cost_estimate=lasting(160),
    )(
        normed,
        cot,
        units,
        down,
        w_down,
        own_cot,
        hidden,
        gain,
    )


def tail_kernel(
    devices,
    terms,
    out_terms,
    unit_terms,
    down_terms,
    head_terms,
    wo_terms,
    unit_sums,
    tokens,
    hidden,
    grad_hidden,
    gain,
    gain_two_term,
    grad_tokens,
    out_tokens,
    gain_sums,
    down_sum,
    wo_sum,
    units_out,
    heads_out,
    unit_sum,
    head_sum,
    unit_land,
    down_land,
    head_land,
    wo_land,
    gain_one_term,
    gain_mine,
    gain_land,
    unit_acc,
    down_acc,
    head_acc,
    wo_acc,
    unit_parts,
    down_parts,
    head_parts,
    turned,
    zsend,
    zrecv,
    esend,
    erecv,
    gsend,
    grecv,
    local,
    *scratch,
):
    p = plane()
    names = ("dg", "ds", "xp", "yp", "xs", "ys", "sib")
    mine = p["dp"] * 8 + p["me"]
    barrier = pltpu.get_barrier_semaphore()

    def other(k):
        to = lax.rem(mine + k, devices)
        return dict(device_id=(lax.div(to, 8), lax.rem(to, 8)), device_id_type=MESH), to

    @pl.loop(1, devices)
    def _(k):
        pl.semaphore_signal(barrier, inc=1, **other(k)[0])

    pl.semaphore_wait(barrier, devices - 1)
    chunk = unit_terms.shape[1]
    piece = down_terms.shape[1] // 4
    rows = tokens.shape[0]
    held = units_out.shape[2]
    line = [
        LineSum(p, lambda owner: head_terms.at[owner], head_land, zsend, zrecv, 0),
        LineSum(
            p,
            lambda owner: unit_terms.at[
                EARLY, :, pl.ds(pl.multiple_of(owner * chunk, chunk), chunk)
            ],
            unit_land,
            zsend,
            zrecv,
            4,
        ),
        LineSum(
            p,
            lambda owner: down_terms.at[EARLY, pl.ds(pl.multiple_of(owner * piece, piece), piece)],
            down_land,
            zsend,
            zrecv,
            8,
        ),
        LineSum(p, lambda owner: wo_terms.at[owner], wo_land, zsend, zrecv, 12),
    ]
    for sums in line:
        sums.first_far()
    for sums in line:
        sums.first_rest()
    kept, paired, far, final, send, recv, loads = scratch[:7]
    source = FromMemory(p, terms, kept, paired, send, recv, loads)
    copies = []

    def exchange(i, block, out):
        for j, name in enumerate(names):
            copies.append(remote(p, block(p[name]), out, esend, erecv, i * 7 + j, name))
            copies[-1].start()
        copies.append(pltpu.make_async_copy(block(p["me"]), out, local.at[i]))
        copies[-1].start()

    sends = scatter_plane(p, source, rows, kept, paired, far, final, send, recv)
    gain_one_term[...] = jnp.zeros_like(gain_one_term)

    def step(at):
        g = total(kept, paired, final, at)
        t = tokens[at, :].astype(f32)
        scale = lax.rsqrt(jnp.mean(t * t, axis=-1, keepdims=True) + norm_eps)
        weighted = g * gain[...]
        inner = jnp.mean(weighted * t, axis=-1, keepdims=True)
        grad_tokens[at, :] = (
            grad_hidden[at, :] + scale * weighted - t * (scale * scale * scale * inner)
        ).astype(bf16)
        gain_one_term[...] += jnp.sum(g * t * scale, axis=0, keepdims=True)

    over_rows(rows, step)
    line[0].second(head_acc, head_parts.at[0], local, 8)
    line[1].second(unit_acc, unit_parts.at[0], local, 8)
    line[2].second(down_acc, down_parts.at[0], local, 8)
    line[3].second(wo_acc, down_parts.at[1], local, 8)
    gain_mine[...] = jnp.zeros_like(gain_mine)
    for k in range(devices):
        at = slice(k * held, (k + 1) * held)
        gain_mine[k, 0:1, :held] = gain_one_term[:, at]
        gain_mine[k, 1:2, :held] = gain_two_term[:, at]

    def gain_copy(k):
        where, to = other(k)
        return pltpu.make_async_remote_copy(
            src_ref=gain_mine.at[to],
            dst_ref=gain_land.at[k],
            send_sem=gsend.at[k],
            recv_sem=grecv.at[k],
            **where,
        )

    @pl.loop(1, devices)
    def _(k):
        gain_copy(k).start()

    def rows_of(ref):
        return lambda s: ref.at[pl.ds(pl.multiple_of(s * held, held), held)]

    for j in range(EARLY):
        exchange(j, rows_of(unit_sums.at[j]), units_out.at[j, p["me"]])
    kept, paired, far, final, send, recv, loads = scratch[7:]
    source_out = FromMemory(p, out_terms, kept, paired, send, recv, loads)
    sends += scatter_plane(p, source_out, rows, kept, paired, far, final, send, recv)

    def step_out(at):
        out_tokens[at, :] = (hidden[at, :] + total(kept, paired, final, at)).astype(bf16)

    over_rows(rows, step_out)
    gain_land[0] = gain_mine[mine]

    @pl.loop(1, devices)
    def _(k):
        gain_copy(k).wait()

    gain_sums[...] = jnp.sum(gain_land[...], axis=0)

    def store(src, dst, i):
        copy = pltpu.make_async_copy(src, dst, local.at[i])
        copy.start()
        copy.wait()

    line[0].total(head_parts, local, 8)
    store(head_parts.at[0], head_sum, 8)
    exchange(EARLY + 1, rows_of(head_sum), heads_out.at[p["me"]])
    line[1].total(unit_parts, local, 8)

    @pl.loop(0, chunk // 128)
    def _(n):
        at = pl.ds(pl.multiple_of(n * 128, 128), 128)
        turned[:, at] = unit_parts[0, at, :].astype(f32).T.astype(bf16)

    store(turned, unit_sum, 8)
    exchange(EARLY, rows_of(unit_sum), units_out.at[EARLY, p["me"]])
    line[2].total(down_parts, local, 8)
    store(down_parts.at[0], down_sum, 8)
    line[3].total(down_parts, local, 8)
    store(down_parts.at[0], wo_sum, 8)
    for copy in copies:
        copy.wait()
    for sums in line:
        sums.finish()
    source.finish()
    source_out.finish()
    for copy in sends:
        copy.wait_send()


def tail_plane(
    groups,
    shards,
    terms,
    out_terms,
    unit_terms,
    down_terms,
    head_terms,
    wo_terms,
    unit_sums,
    tokens,
    hidden,
    grad_hidden,
    gain,
    gain_two_term,
    collective_id,
):
    rows, width = tokens.shape
    devices = groups * shards
    chunk, piece = unit_terms.shape[1], down_terms.shape[1] // 4
    held = width // devices
    span, heads_wide = head_terms.shape[1:]
    wo_rows = wo_terms.shape[1]
    sds = jax.ShapeDtypeStruct
    unit, down_, head, wo_ = (
        (chunk, chunk),
        (piece, width),
        (span, heads_wide),
        (wo_rows, width),
    )
    return pl.pallas_call(
        functools.partial(tail_kernel, devices),
        out_shape=[
            sds((rows, width), bf16),
            sds((rows, width), bf16),
            sds((8, 128), f32),
            sds(down_, bf16),
            sds(wo_, bf16),
            sds((CHUNKS, shards, held, chunk), bf16),
            sds((shards, held, heads_wide), bf16),
            sds(unit, bf16),
            sds(head, bf16),
            sds((4,) + unit, bf16),
            sds((4,) + down_, bf16),
            sds((4,) + head, bf16),
            sds((4,) + wo_, bf16),
        ],
        in_specs=[ANY] * 7 + [VMEM] * 5,
        out_specs=[VMEM] * 3 + [ANY] * 10,
        scratch_shapes=[
            pltpu.VMEM((1, width), f32),
            pltpu.VMEM((devices, 8, 128), f32),
            pltpu.VMEM((devices, 8, 128), f32),
            pltpu.VMEM(unit, bf16),
            pltpu.VMEM(down_, bf16),
            pltpu.VMEM(head, bf16),
            pltpu.VMEM(wo_, bf16),
            pltpu.VMEM((4,) + unit, bf16),
            pltpu.VMEM((4,) + down_, bf16),
            pltpu.VMEM((4,) + head, bf16),
            pltpu.VMEM(unit, bf16),
            DMA((16,)),
            DMA((16,)),
            DMA((35,)),
            DMA((35,)),
            DMA((devices,)),
            DMA((devices,)),
            DMA((12,)),
        ]
        + scatter_scratch(rows, width) * 2,
        compiler_params=pltpu.CompilerParams(
            collective_id=collective_id, has_side_effects=True, vmem_limit_bytes=60 * MIB
        ),
        cost_estimate=lasting(120),
    )(
        terms,
        out_terms,
        unit_terms,
        down_terms,
        head_terms,
        wo_terms,
        unit_sums,
        tokens,
        hidden,
        grad_hidden,
        gain,
        gain_two_term,
    )


LINE_SEMS = 5


class LineGather:
    def __init__(self, p, src, out, send, recv, base, own=None):
        self.p, self.src, self.out = p, src, out
        self.send, self.recv, self.base = send, recv, base * LINE_SEMS
        self.z = p["dp"]
        self.inward = 1 - 2 * lax.div(self.z, 2)
        self.end = (self.z == 0) | (self.z == 3)
        self.own = None if own is None else pltpu.make_async_copy(src, out.at[self.z], own)

    def copy(self, src, owner, i, to):
        return pltpu.make_async_remote_copy(
            src_ref=src,
            dst_ref=self.out.at[owner],
            send_sem=self.send.at[self.base + i],
            recv_sem=self.recv.at[self.base + owner],
            device_id=(to, self.p["me"]),
            device_id_type=MESH,
        )

    def arrived(self, owner):
        self.copy(self.src, owner, 0, self.z).wait_recv()

    def start(self):
        z, inward = self.z, self.inward
        if self.own is not None:
            self.own.start()
        self.copy(self.src, z, 0, z + inward).start()

        @pl.when(jnp.logical_not(self.end))
        def _():
            self.copy(self.src, z, 1, z - inward).start()

    def second(self):
        z, inward = self.z, self.inward

        @pl.when(jnp.logical_not(self.end))
        def _():
            outer, inner = z - inward, z + inward
            self.arrived(inner)
            self.copy(self.out.at[inner], inner, 2, outer).start()
            self.arrived(outer)
            self.copy(self.out.at[outer], outer, 3, inner).start()

    def third(self):
        z, inward = self.z, self.inward

        @pl.when(jnp.logical_not(self.end))
        def _():
            far = z + 2 * inward
            self.arrived(far)
            self.copy(self.out.at[far], far, 4, z - inward).start()

    def finish(self):
        z, inward = self.z, self.inward

        @pl.when(self.end)
        def _():
            for k in range(1, 4):
                self.arrived(z + k * inward)

        if self.own is not None:
            self.own.wait()
        self.copy(self.src, 0, 0, z).wait_send()

        @pl.when(jnp.logical_not(self.end))
        def _():
            for i in range(1, 5):
                self.copy(self.src, 0, i, z).wait_send()


CHUNKS = 4
EARLY = 3
OTHERS = ("dg", "ds", "xp", "yp", "xs", "ys", "sib")


def meet_all(p, devices):
    mine = p["dp"] * 8 + p["me"]
    barrier = pltpu.get_barrier_semaphore()

    def other(k):
        to = lax.rem(mine + k, devices)
        return dict(device_id=(lax.div(to, 8), lax.rem(to, 8)), device_id_type=MESH), to

    @pl.loop(1, devices)
    def _(k):
        pl.semaphore_signal(barrier, inc=1, **other(k)[0])

    return other, lambda: pl.semaphore_wait(barrier, devices - 1)


class Local:
    def __init__(self, sems):
        self.sems, self.used = sems, 0

    def take(self, count=1):
        self.used += count
        return self.used - count


class Produced:
    def __init__(self, p, produce, stage, kept, paired, send, recv):
        self.p, self.produce, self.stage = p, produce, stage
        self.kept, self.paired, self.send, self.recv = kept, paired, send, recv
        self.pairs = {}

    def ready(self, i):
        k = len(self.pairs)
        _, own, other = ORDER[k]
        rows = self.kept.shape[1]
        stage = self.stage.at[pl.ds(k % 2 * rows, rows)]
        if k >= 2:
            self.pairs[ORDER[k - 2][0]].wait_send()
        self.produce(other, stage)
        self.pairs[i] = remote(self.p, stage, self.paired.at[i], self.send, self.recv, i, "sib")
        self.pairs[i].start()
        self.produce(own, self.kept.at[i])
        self.pairs[i].wait_recv()

    def finish(self):
        for i, _, _ in ORDER[2:]:
            self.pairs[i].wait_send()


def front_kernel(
    groups,
    own_cot,
    w_out,
    w_down,
    tokens,
    gains,
    w_query,
    w_key,
    w_value,
    w_gate,
    w_up,
    cos,
    sin,
    starts,
    hidden,
    gain_one,
    gain_two,
    rotated,
    attended,
    stats,
    normed_one,
    cot,
    normed_two,
    qkv,
    out_weight,
    units,
    down,
    gains_land,
    head_blocks,
    unit_blocks,
    x,
    w,
    wo,
    pre,
    mine,
    stage,
    kept,
    paired,
    far,
    final,
    send,
    recv,
    asend,
    arecv,
    csend,
    crecv,
    nsend,
    nrecv,
    gsend,
    grecv,
    esend,
    erecv,
    zsend,
    zrecv,
    local,
):
    p = plane()
    devices = groups * 8
    other, met = meet_all(p, devices)
    shards, rows, width = x.shape
    held = w_query.shape[0]
    pairs = width // 8 // PAIR
    piece = down.shape[2]
    me, z = p["me"], p["dp"]
    mine_index = z * 8 + me
    sems = Local(local)

    def move(src, dst, i):
        return pltpu.make_async_copy(src, dst, local.at[i])

    for s in range(shards):
        for pair in range(pairs):
            for i, weight in enumerate((w_query, w_key, w_value)):
                head = lambda k: ((2 * pair + k) * 8 + s) * HD
                base = (pair * 3 + i) * PAIR
                head_blocks[s, :, base : base + PAIR] = jnp.concatenate(
                    [weight[:, head(k) : head(k) + HD] for k in range(2)], axis=1
                )
    met()

    def gain_copy(k, sender):
        return pltpu.make_async_remote_copy(
            src_ref=gains,
            dst_ref=gains_land.at[sender],
            send_sem=gsend.at[k],
            recv_sem=grecv.at[sender],
            **other(k)[0],
        )

    @pl.loop(1, devices)
    def _(k):
        gain_copy(k, mine_index).start()

    gains_land[mine_index] = gains[...]
    held_at = pl.ds(pl.multiple_of(me * held, held), held)

    def exchange(block, out, i):
        copies = [
            remote(p, block(p[name]), out, esend, erecv, i * 7 + j, name)
            for j, name in enumerate(OTHERS)
        ]
        copies.append(move(block(me), out, sems.take()))
        for copy in copies:
            copy.start()
        return copies

    head_copies = exchange(lambda s: head_blocks.at[s], qkv.at[z, held_at], 0)
    wo_line = LineGather(p, w_out, out_weight, zsend, zrecv, 0, local.at[sems.take()])
    wo_line.start()

    for s in range(shards):
        for i, weight in enumerate((w_gate, w_up)):
            for j in range(CHUNKS):
                for pair in range(groups // 2):
                    unit = lambda k: ((2 * pair + k) * 8 + s) * CHUNKS * piece + j * piece
                    base = i * groups * piece + pair * 2 * piece
                    unit_blocks[s, j, :, base : base + 2 * piece] = jnp.concatenate(
                        [weight[:, unit(k) : unit(k) + piece] for k in range(2)], axis=1
                    )

    unit_copies = exchange(lambda s: unit_blocks.at[s], units.at[:, z, held_at], 1)

    @pl.loop(1, devices)
    def _(k):
        gain_copy(k, lax.rem(mine_index + devices - k, devices)).wait()

    for out, base in ((gain_one, 0), (gain_two, held)):
        for k in range(0, devices, 2):
            out[:, k * held : (k + 2) * held] = jnp.concatenate(
                [gains_land[k + i, 0:1, base : base + held] for i in range(2)], axis=1
            )

    def norm_tokens(at):
        t = tokens[at, :].astype(f32)
        scale = lax.rsqrt(jnp.mean(t * t, axis=-1, keepdims=True) + norm_eps)
        mine[at, :] = (t * scale * gain_one[...]).astype(bf16)

    over_rows(rows, norm_tokens)
    n1_sent = gather_start(p, mine, x, asend, arecv, 0)
    n1_own = move(mine, x.at[me], sems.take())
    n1_own.start()
    for copy in head_copies:
        copy.wait()
    qkv_line = LineGather(p, qkv.at[z], qkv, zsend, zrecv, 1)
    qkv_line.start()
    n1_late = gather_forward(p, n1_sent, x, asend, arecv, 0)
    wo_line.second()
    qkv_line.second()
    for copy in unit_copies:
        copy.wait()
    chunk_lines = [
        (
            LineGather(p, units.at[j, z], units.at[j], zsend, zrecv, 2 + 2 * j),
            LineGather(
                p,
                w_down.at[pl.ds(j * piece, piece)],
                down.at[j],
                zsend,
                zrecv,
                3 + 2 * j,
                local.at[sems.take()],
            ),
        )
        for j in range(EARLY)
    ]

    def serve(j, what):
        for line in chunk_lines[j]:
            getattr(line, what)()

    gather_wait(n1_sent, n1_late)
    n1_own.wait()
    cot_sent = gather_start(p, own_cot, cot, csend, crecv, 0)
    cot_own = move(own_cot, cot.at[me], sems.take())
    cot_own.start()
    wo_line.third()
    qkv_line.third()
    serve(0, "start")
    keep_normed = move(x, normed_one, sems.take())
    keep_normed.start()
    qkv_line.finish()
    load_w = move(qkv, w, sems.take())
    load_w.start()
    load_w.wait()

    @pl.loop(0, shards)
    def _(s):
        pre[s] = dot(x[s], w[...].reshape(width, w.shape[2])).reshape(pre.shape[1:])

    def attention(r):
        @pl.loop(0, pairs)
        def _(pair):
            attend_pair(
                pre,
                cos,
                sin,
                starts[r],
                rotated,
                attended,
                stats,
                r,
                pair,
            )

    attention(0)
    serve(0, "second")
    serve(1, "start")
    cot_late = gather_forward(p, cot_sent, cot, csend, crecv, 0)
    attention(1)
    serve(0, "third")
    wo_line.finish()
    load_wo = move(out_weight, wo, sems.take())
    load_wo.start()
    load_wo.wait()
    gather_wait(cot_sent, cot_late)
    cot_own.wait()

    def produce(name, out):
        s = p[name]
        terms = attended[s].reshape(rows, attended.shape[3])

        @pl.loop(0, width // 512)
        def _(n):
            at = pl.ds(pl.multiple_of(n * 512, 512), 512)
            out[:, at] = dot(terms, wo[:, :, at].reshape(terms.shape[1], 512)).astype(bf16)

    def meanwhile():
        serve(1, "second")
        serve(2, "start")

    source = Produced(p, produce, stage, kept, paired, send, recv)
    sends = scatter_plane(p, source, rows, kept, paired, far, final, send, recv, meanwhile)
    keep_normed.wait()

    def step(at):
        h = tokens[at, :].astype(f32) + total(kept, paired, final, at)
        hidden[at, :] = h
        scale = lax.rsqrt(jnp.mean(h * h, axis=-1, keepdims=True) + norm_eps)
        mine[at, :] = (h * scale * gain_two[...]).astype(bf16)

    over_rows(rows, step)
    n2_sent = gather_start(p, mine, normed_two, nsend, nrecv, 0)
    n2_own = move(mine, normed_two.at[me], sems.take())
    n2_own.start()
    serve(1, "third")
    serve(2, "second")
    n2_late = gather_forward(p, n2_sent, normed_two, nsend, nrecv, 0)
    serve(2, "third")
    gather_wait(n2_sent, n2_late)
    n2_own.wait()
    for j in range(EARLY):
        serve(j, "finish")
    source.finish()
    for copy in sends:
        copy.wait_send()


def front_plane(
    groups, tokens, cotangent, gains, w_query, w_key, w_value, w_out, w_gate, w_up, w_down, tables, collective_id
):
    cos, sin, starts = tables
    shards, batch, shard_len, _ = cos.shape
    rows, width = tokens.shape
    held, devices = w_query.shape[0], groups * shards
    mine = width // shards
    wide = 3 * mine
    pairs = mine // PAIR
    chunk = 2 * groups * w_down.shape[0] // CHUNKS
    piece = w_down.shape[0] // CHUNKS
    length = shards * shard_len
    sds = jax.ShapeDtypeStruct
    full = (shards, rows, width)
    scratch = [
        pltpu.VMEM((devices, 8, 2 * held), f32),
        pltpu.VMEM((shards, held, wide), bf16),
        pltpu.VMEM((shards, CHUNKS, held, chunk), bf16),
        pltpu.VMEM(full, bf16),
        pltpu.VMEM((groups, shards * held, wide), bf16),
        pltpu.VMEM((groups, held, width), bf16),
        pltpu.VMEM((shards, batch, shard_len, wide), f32),
        pltpu.VMEM((rows, width), bf16),
        pltpu.VMEM((2 * rows, width), bf16),
        *scatter_scratch(rows, width)[:6],
        *[DMA((GATHER_SEMS,))] * 6,
        *[DMA((devices,))] * 2,
        *[DMA((14,))] * 2,
        *[DMA((LINE_SEMS * (2 + 2 * EARLY),))] * 2,
        DMA((24,)),
    ]
    return pl.pallas_call(
        functools.partial(front_kernel, groups),
        out_shape=[
            sds((rows, width), f32),
            sds((1, width), f32),
            sds((1, width), f32),
            sds((shards, batch, shard_len, wide), bf16),
            sds((shards, batch, shard_len, mine), bf16),
            sds((batch, pairs, 2, length), f32),
            sds(full, bf16),
            sds(full, bf16),
            sds(full, bf16),
            sds((groups, shards * held, wide), bf16),
            sds((groups, held, width), bf16),
            sds((CHUNKS, groups, shards * held, chunk), bf16),
            sds((EARLY, groups, piece, width), bf16),
        ],
        in_specs=[ANY] * 3 + [VMEM] * 10,
        out_specs=[VMEM] * 6 + [ANY] * 7,
        scratch_shapes=scratch,
        compiler_params=pltpu.CompilerParams(
            collective_id=collective_id, has_side_effects=True, vmem_limit_bytes=62 * MIB
        ),
        cost_estimate=lasting(200),
    )(
        cotangent,
        w_out,
        w_down,
        tokens,
        jnp.broadcast_to(gains.reshape(1, -1).astype(f32), (8, 2 * held)),
        w_query,
        w_key,
        w_value,
        w_gate,
        w_up,
        cos,
        sin,
        starts,
    )


def layer(
    groups,
    shards,
    tokens,
    doc_ids,
    cotangent,
    norm1_gain,
    w_query,
    w_key,
    w_value,
    w_out,
    norm2_gain,
    w_gate,
    w_up,
    w_down,
):
    rows, shard_len, width = tokens.shape
    count = rows * shard_len
    held = w_query.shape[0]
    hidden_held = w_down.shape[0]
    hidden_here = groups * hidden_held
    whole_heads = held % HD == 0
    outer, inner = (groups, held) if whole_heads else (1, width // shards)
    pairs = width // shards // PAIR
    both = ("dp", "seq")
    fast = groups == 4 and shards == 8
    flat = lambda v: v.reshape(shards * count, v.shape[-1])
    split = lambda v: v.reshape(shards, count, v.shape[-1])

    chunks = CHUNKS if fast else 1
    piece = hidden_held // chunks
    gains = jnp.stack([norm1_gain, norm2_gain])
    own_tokens = tokens.reshape(count, width)
    own_cotangent = cotangent.reshape(count, width)
    inputs = own_tokens.astype(f32)
    cos, sin, starts = rope_tables(doc_ids, shards)
    starts = starts[:, None, :]
    by_row = lambda v: v.reshape(shards, rows, shard_len, v.shape[-1])

    if fast:
        (
            hidden,
            gain_one,
            gain_two,
            rotated,
            attended,
            stats,
            normed_one,
            cot,
            normed_two,
            qkv_weight,
            out_weight,
            unit_weight,
            down_weight,
        ) = front_plane(
            groups,
            own_tokens,
            own_cotangent,
            gains,
            w_query,
            w_key,
            w_value,
            w_out,
            w_gate,
            w_up,
            w_down,
            (cos, sin, starts),
            1,
        )
        qkv_weight = qkv_weight.reshape(width, -1)
        out_weight = out_weight.reshape(-1, width)
        attended, normed_one = flat(attended), flat(normed_one)
        (
            grad_hidden,
            gain_two_term,
            branch,
            out_terms,
            unit_sums,
            down_sums,
            unit_terms,
            down_terms,
            *_,
        ) = feed_plane(
            normed_two,
            cot,
            unit_weight,
            down_weight,
            w_down,
            own_cotangent,
            hidden,
            gain_two,
            2,
        )
    else:
        gains = lax.all_gather(gains, both, axis=1, tiled=True).astype(f32)
        gain_one, gain_two = gains[:1], gains[1:]

        def by_head(w):
            blocks = w.reshape(held, outer, shards, inner)
            return jnp.moveaxis(blocks, 2, 0).reshape(shards, held, pairs, PAIR)

        blocks = jnp.stack([w_gate, w_up]).reshape(2, held, groups, shards, hidden_held)
        units = jnp.transpose(blocks, (3, 1, 0, 2, 4)).reshape(shards, held, 2 * hidden_here)
        heads = jnp.stack([by_head(w) for w in (w_query, w_key, w_value)], axis=3)
        heads, units = exchange_plane([heads.reshape(shards, held, -1), units], shards, 1)
        spread = lambda w: lax.all_gather(w, "dp", axis=0, tiled=True)
        qkv_weight = spread(heads.reshape(shards * held, -1))
        unit_weight = spread(units.reshape(shards * held, -1))
        down_weight = spread(w_down)
        if whole_heads:
            out_weight = spread(w_out)
        else:
            whole = lax.all_gather(w_out, both, axis=0, tiled=True)
            out_weight = lax.dynamic_slice_in_dim(whole, lax.axis_index("seq") * inner, inner, 0)
        own_normed = (inputs * rms_scale(inputs) * gain_one).astype(bf16)
        normed_one, cot = [flat(v) for v in gather_plane([own_normed, own_cotangent], shards, 2)]
        pre = by_row(dot(normed_one, qkv_weight))
        rotated, attended, stats = attend(pre, cos, sin, starts)
        attended = flat(attended)
        hidden = inputs + reduce_plane(split(dot(attended, out_weight).astype(bf16)))
        normed_two = (hidden * rms_scale(hidden) * gain_two).astype(bf16)
        normed_two = flat(lax.all_gather(normed_two, "seq"))
        gate_weight, up_weight = unit_weight[:, :hidden_here], unit_weight[:, hidden_here:]
        gate_pre, up_pre = dot(normed_two, gate_weight), dot(normed_two, up_weight)
        sigmoid = jax.nn.sigmoid(gate_pre)
        silu = gate_pre * sigmoid
        activated = (silu * up_pre).astype(bf16)
        out_terms = split(dot(activated, down_weight).astype(bf16))
        grad_act = dot_t(cot, down_weight)
        grad_gate_pre = grad_act * up_pre * sigmoid * (1.0 + gate_pre * (1.0 - sigmoid))
        grad_up_pre = grad_act * silu
        grad_units = jnp.concatenate([grad_gate_pre, grad_up_pre], axis=-1).astype(bf16)
        middle_terms = split(dot_t(grad_units, unit_weight).astype(bf16))
        unit_sums = lax.psum_scatter(
            dot(normed_two.T, grad_units).astype(bf16), "dp", scatter_dimension=0, tiled=True
        )
        down_sums = lax.psum_scatter(
            dot(activated.T, cot).astype(bf16), "dp", scatter_dimension=0, tiled=True
        )
        back, gain_two_term = norm_back(
            hidden, rms_scale(hidden), gain_two, reduce_plane(middle_terms)
        )
        grad_hidden = own_cotangent.astype(f32) + back
        branch = lax.all_gather(grad_hidden.astype(bf16), "seq")

    branch = flat(branch)
    out_w_terms = dot(attended.T, branch).astype(bf16)
    grad_attended = by_row(dot_t(branch, out_weight).astype(bf16))
    grad_pre = flat(attend_back(rotated, grad_attended, cos, sin, starts, stats))
    last_terms = split(dot_t(grad_pre, qkv_weight).astype(bf16))
    head_terms = dot(normed_one.T, grad_pre).astype(bf16)

    if fast:
        (
            grad_tokens,
            out_tokens,
            gain_sums,
            down_last,
            grad_out,
            units_back,
            heads_back,
            *_,
        ) = tail_plane(
            groups,
            shards,
            last_terms,
            out_terms,
            unit_terms,
            down_terms,
            head_terms.reshape(groups, -1, head_terms.shape[-1]),
            out_w_terms.reshape(groups, -1, width),
            unit_sums,
            own_tokens,
            hidden,
            grad_hidden,
            gain_one,
            gain_two_term,
            3,
        )
        grad_norms = gain_sums[:2, :held]
        down_sums = jnp.concatenate([down_sums, down_last[None]]).reshape(hidden_held, width)
    else:
        if whole_heads:
            grad_out = lax.psum_scatter(out_w_terms, "dp", scatter_dimension=0, tiled=True)
        else:
            placed = lax.dynamic_update_slice_in_dim(
                jnp.zeros((width, width), bf16), out_w_terms, lax.axis_index("seq") * inner, 0
            )
            grad_out = lax.psum_scatter(placed, ("dp", "seq"), scatter_dimension=0, tiled=True)
        back, gain_one_term = norm_back(
            inputs, rms_scale(inputs), gain_one, reduce_plane(last_terms)
        )
        grad_tokens = (grad_hidden + back).astype(bf16)
        out_tokens = (hidden + reduce_plane(out_terms)).astype(bf16)
        head_sums = lax.psum_scatter(head_terms, "dp", scatter_dimension=0, tiled=True)
        heads_back, units_back = exchange_plane(
            [head_sums.reshape(shards, held, -1), unit_sums.reshape(shards, held, -1)], shards, 6
        )
        grad_norms = lax.psum_scatter(
            jnp.concatenate([gain_one_term, gain_two_term]),
            ("dp", "seq"),
            scatter_dimension=1,
            tiled=True,
        )

    heads_back = heads_back.reshape(shards, held, pairs, 3, PAIR)
    units_back = units_back.reshape(chunks, shards, held, 2, groups, piece)

    def head_grad(i):
        blocks = heads_back[:, :, :, i, :].reshape(shards, held, outer, inner)
        return jnp.moveaxis(blocks, 0, 2).reshape(held, width).astype(f32)

    def unit_grad(i):
        return (
            jnp.transpose(units_back[:, :, :, i], (2, 3, 1, 0, 4)).reshape(held, -1).astype(f32)
        )

    return (
        out_tokens.reshape(tokens.shape),
        grad_tokens.reshape(tokens.shape),
        grad_norms[0],
        head_grad(0),
        head_grad(1),
        head_grad(2),
        grad_out.astype(f32),
        grad_norms[1],
        unit_grad(0),
        unit_grad(1),
        down_sums.astype(f32),
    )


def solution(mesh):
    both = ("dp", "seq")
    return jax.shard_map(
        functools.partial(layer, mesh.shape["dp"], mesh.shape["seq"]),
        mesh=mesh,
        in_specs=(
            P("dp", "seq", None),
            P("dp", None),
            P("dp", "seq", None),
            P(both),
            P(both, None),
            P(both, None),
            P(both, None),
            P(both, None),
            P(both),
            P(both, None),
            P(both, None),
            P(both, None),
        ),
        out_specs=(
            P("dp", "seq", None),
            P("dp", "seq", None),
            P(both),
            P(both, None),
            P(both, None),
            P(both, None),
            P(both, None),
            P(both),
            P(both, None),
            P(both, None),
            P(both, None),
        ),
        check_vma=False,
    )
```

```python
import functools

import jax
import jax.numpy as jnp
from jax import lax
from jax.experimental import pallas as pl
from jax.experimental.pallas import tpu as pltpu
from jax.sharding import PartitionSpec as P

H = 32
HD = 64
PAIR = 2 * HD

rope_base = 130000.0
norm_eps = 1e-05

bf16 = jnp.bfloat16
f32 = jnp.float32
MESH = pl.DeviceIdType.MESH
ANY = pl.BlockSpec(memory_space=pl.ANY)
VMEM = pl.BlockSpec(memory_space=pltpu.VMEM)
DMA = pltpu.SemaphoreType.DMA
MIB = 1 << 20


def lasting(us):
    return pl.CostEstimate(flops=0, transcendentals=0, bytes_accessed=int(us * 3_500_000))


def plane():
    dp, s = lax.axis_index("dp"), lax.axis_index("seq")
    core, xb, yb = lax.rem(s, 2), lax.rem(lax.div(s, 2), 2), lax.div(s, 4)
    at = lambda y, x, c: y * 4 + x * 2 + c
    return dict(
        dp=dp,
        me=s,
        sib=at(yb, xb, 1 - core),
        xp=at(yb, 1 - xb, core),
        yp=at(1 - yb, xb, core),
        dg=at(1 - yb, 1 - xb, core),
        xs=at(yb, 1 - xb, 1 - core),
        ys=at(1 - yb, xb, 1 - core),
        ds=at(1 - yb, 1 - xb, 1 - core),
    )


def greet(p, names):
    barrier = pltpu.get_barrier_semaphore()
    for name in names:
        pl.semaphore_signal(barrier, inc=1, device_id=(p["dp"], p[name]), device_id_type=MESH)
    pl.semaphore_wait(barrier, len(names))


def remote(p, src, dst, send, recv, i, to):
    return pltpu.make_async_remote_copy(
        src_ref=src,
        dst_ref=dst,
        send_sem=send.at[i],
        recv_sem=recv.at[i],
        device_id=(p["dp"], p[to]),
        device_id_type=MESH,
    )


GATHER_SEMS = 25


def gather_start(p, src, out, send, recv, base):
    quarter = src.shape[0] // 4
    part = lambda ref, k: ref.at[pl.ds(k * quarter, quarter)]
    mine = out.at[p["me"]]
    sent = {}
    for j in range(4):
        kx, ky = j, (j + 2) % 4
        sent["x", kx] = remote(p, part(src, kx), part(mine, kx), send, recv, base + kx, "xp")
        sent["y", ky] = remote(p, part(src, ky), part(mine, ky), send, recv, base + 4 + ky, "yp")
        sent["x", kx].start()
        sent["y", ky].start()
    sent["s"] = remote(p, src, mine, send, recv, base + 8, "sib")
    sent["s"].start()
    return sent


def gather_pass(p, ref, send, recv, i, to):
    copy = remote(p, ref, ref, send, recv, i, to)
    copy.start()
    return copy


def gather_forward(p, sent, out, send, recv, base, halfway=None):
    quarter = out.shape[1] // 4
    part = lambda owner, k: out.at[p[owner], pl.ds(k * quarter, quarter)]
    passed = []
    for j in range(4):
        kx, ky = j, (j + 2) % 4
        sent["x", kx].wait_recv()
        if j < 2:
            sent["far", kx] = gather_pass(p, part("xp", kx), send, recv, base + 9 + kx, "yp")
        passed.append(gather_pass(p, part("xp", kx), send, recv, base + 13 + kx, "sib"))
        sent["y", ky].wait_recv()
        if j < 2:
            sent["far", ky] = gather_pass(p, part("yp", ky), send, recv, base + 9 + ky, "xp")
        passed.append(gather_pass(p, part("yp", ky), send, recv, base + 17 + ky, "sib"))
        if j == 1 and halfway is not None:
            halfway()

    def last():
        for k in (0, 2, 1, 3):
            sent["far", k].wait_recv()
            passed.append(gather_pass(p, part("dg", k), send, recv, base + 21 + k, "sib"))

    return passed, last


def gather_wait(sent, late):
    passed, last = late
    last()
    sent["s"].wait_recv()
    for copy in passed:
        copy.wait_recv()
    for copy in list(sent.values()) + passed:
        copy.wait_send()


def gather_finish(p, sent, out, send, recv, base):
    gather_wait(sent, gather_forward(p, sent, out, send, recv, base))


def gather_kernel(count, *refs):
    sources, outs = refs[:count], refs[count : 2 * count]
    send, recv, local = refs[2 * count :]
    p = plane()
    greet(p, ("sib", "xp", "yp"))
    sent, kept = [], []
    for i in range(count):
        sent.append(gather_start(p, sources[i], outs[i], send, recv, i * GATHER_SEMS))
        kept.append(pltpu.make_async_copy(sources[i], outs[i].at[p["me"]], local.at[i]))
        kept[i].start()
    for i in range(count):
        gather_finish(p, sent[i], outs[i], send, recv, i * GATHER_SEMS)
    for copy in kept:
        copy.wait()


def gather_plane(arrays, shards, collective_id):
    if shards != 8:
        return [lax.all_gather(a, "seq") for a in arrays]
    count = len(arrays)
    return pl.pallas_call(
        functools.partial(gather_kernel, count),
        out_shape=[jax.ShapeDtypeStruct((8,) + a.shape, a.dtype) for a in arrays],
        in_specs=[ANY] * count,
        out_specs=[ANY] * count,
        scratch_shapes=[DMA((GATHER_SEMS * count,)), DMA((GATHER_SEMS * count,)), DMA((count,))],
        compiler_params=pltpu.CompilerParams(collective_id=collective_id, has_side_effects=True),
        cost_estimate=lasting(40 * count),
    )(*arrays)


def exchange_kernel(count, *refs):
    sources, outs = refs[:count], refs[count : 2 * count]
    send, recv, local = refs[2 * count :]
    p = plane()
    names = ("dg", "ds", "xp", "yp", "xs", "ys", "sib")
    greet(p, names)
    copies = []
    for i in range(count):
        for j, name in enumerate(names):
            copies.append(
                remote(
                    p, sources[i].at[p[name]], outs[i].at[p["me"]], send, recv, i * 7 + j, name
                )
            )
            copies[-1].start()
        copies.append(
            pltpu.make_async_copy(sources[i].at[p["me"]], outs[i].at[p["me"]], local.at[i])
        )
        copies[-1].start()
    for copy in copies:
        copy.wait()


def exchange_plane(arrays, shards, collective_id):
    if shards != 8:
        return [lax.all_to_all(a, "seq", split_axis=0, concat_axis=0) for a in arrays]
    count = len(arrays)
    return pl.pallas_call(
        functools.partial(exchange_kernel, count),
        out_shape=[jax.ShapeDtypeStruct(a.shape, a.dtype) for a in arrays],
        in_specs=[ANY] * count,
        out_specs=[ANY] * count,
        scratch_shapes=[DMA((7 * count,)), DMA((7 * count,)), DMA((count,))],
        compiler_params=pltpu.CompilerParams(collective_id=collective_id, has_side_effects=True),
        cost_estimate=lasting(35),
    )(*arrays)


BLOCK = 16


def over_rows(rows, step):
    @pl.loop(0, rows // BLOCK)
    def _(i):
        step(pl.ds(pl.multiple_of(i * BLOCK, BLOCK), BLOCK))


def scatter_scratch(rows, width):
    return [
        pltpu.VMEM((4, rows, width), bf16),
        pltpu.VMEM((4, rows, width), bf16),
        pltpu.VMEM((2, rows // 2, width), bf16),
        pltpu.VMEM((2, rows, width), bf16),
        DMA((12,)),
        DMA((12,)),
        DMA((4,)),
    ]


class FromMemory:
    def __init__(self, p, terms, kept, paired, send, recv, local):
        self.loads, self.pairs = {}, {}
        for i, own, other in ORDER:
            self.loads[i] = pltpu.make_async_copy(terms.at[p[own]], kept.at[i], local.at[i])
            self.loads[i].start()
            self.pairs[i] = remote(p, terms.at[p[other]], paired.at[i], send, recv, i, "sib")
            self.pairs[i].start()

    def ready(self, i):
        self.loads[i].wait()
        self.pairs[i].wait_recv()

    def finish(self):
        for copy in self.pairs.values():
            copy.wait_send()


ORDER = ((3, "dg", "ds"), (1, "xp", "xs"), (2, "yp", "ys"), (0, "me", "sib"))


class PlaneSum:
    def __init__(self, p, source, rows, kept, paired, far, final, send, recv):
        self.p, self.source, self.rows = p, source, rows
        self.kept, self.paired, self.far, self.final = kept, paired, far, final
        self.send, self.recv = send, recv
        self.half = rows // 2
        self.low, self.high = pl.ds(0, self.half), pl.ds(self.half, self.half)
        self.sends, self.near = [], []

    def add_pair(self, i):
        kept, paired = self.kept, self.paired
        self.source.ready(i)

        def step(at):
            kept[i, at, :] = (kept[i, at, :].astype(f32) + paired[i, at, :].astype(f32)).astype(
                bf16
            )

        over_rows(self.rows, step)

    def put(self, src, dst, i, to):
        copy = remote(self.p, src, dst, self.send, self.recv, i, to)
        copy.start()
        self.sends.append(copy)
        return copy

    def first(self):
        kept, far, final, low, high = self.kept, self.far, self.final, self.low, self.high
        self.add_pair(3)
        self.far_x = self.put(kept.at[3, low], far.at[0], 4, "xp")
        self.far_y = self.put(kept.at[3, high], far.at[1], 5, "yp")
        self.add_pair(1)
        self.near.append(self.put(kept.at[1, low], final.at[0, low], 6, "xp"))
        self.add_pair(2)
        self.near.append(self.put(kept.at[2, high], final.at[1, high], 7, "yp"))

    def second(self):
        kept, far, final, low, high = self.kept, self.far, self.final, self.low, self.high
        half = self.half
        self.far_x.wait_recv()

        def step_x(at):
            kept[2, at, :] = (kept[2, at, :].astype(f32) + far[0, at, :].astype(f32)).astype(bf16)

        over_rows(half, step_x)
        self.near.append(self.put(kept.at[2, low], final.at[1, low], 8, "yp"))
        self.far_y.wait_recv()

        def step_y(at):
            up = pl.ds(pl.multiple_of(at.start + half, BLOCK), BLOCK)
            kept[1, up, :] = (kept[1, up, :].astype(f32) + far[1, at, :].astype(f32)).astype(bf16)

        over_rows(half, step_y)
        self.near.append(self.put(kept.at[1, high], final.at[0, high], 9, "xp"))
        self.source.ready(0)

    def third(self):
        for copy in self.near:
            copy.wait_recv()

    def finish(self):
        self.source.finish()
        for copy in self.sends:
            copy.wait_send()


def scatter_plane(p, source, rows, kept, paired, far, final, send, recv, meanwhile=None):
    sums = PlaneSum(p, source, rows, kept, paired, far, final, send, recv)
    sums.first()
    sums.second()
    if meanwhile is not None:
        meanwhile()
    sums.third()
    return sums


def total(kept, paired, final, at):
    return (kept[0, at, :].astype(f32) + paired[0, at, :].astype(f32)) + (
        final[0, at, :].astype(f32) + final[1, at, :].astype(f32)
    )


def reduce_plane(terms):
    rows = terms.shape[1]
    return lax.psum_scatter(terms, "seq", scatter_dimension=0, tiled=False).astype(f32).reshape(
        rows, terms.shape[2]
    )


def rms_scale(values):
    return lax.rsqrt(jnp.mean(values * values, axis=-1, keepdims=True) + norm_eps)


def norm_back(values, scale, gain, grad):
    weighted = grad * gain
    inner = jnp.mean(weighted * values, axis=-1, keepdims=True)
    return (
        scale * weighted - values * (scale * scale * scale) * inner,
        jnp.sum(grad * values * scale, axis=0, keepdims=True),
    )


def swap_halves(v, first):
    width = v.shape[-1]
    return jnp.where(first, pltpu.roll(v, width - HD // 2, 1), pltpu.roll(v, HD // 2, 1))


def dot_t(a, b):
    return lax.dot_general(a, b, (((1,), (1,)), ((), ())), preferred_element_type=f32)


def dot(a, b):
    return jnp.dot(a, b, preferred_element_type=f32)


def dot_l(a, b):
    return lax.dot_general(a, b, (((0,), (0,)), ((), ())), preferred_element_type=f32)


def allowed_pairs(start, keys, queries, offset):
    key = lax.broadcasted_iota(jnp.int32, (keys, queries), 0)
    query = lax.broadcasted_iota(jnp.int32, (keys, queries), 1) + offset
    return (key >= start) & (key <= query)


def attend_pair(pre, cos, sin, starts, rotated, attended, stats, r, pair):
    shards, _, shard_len, _ = pre.shape
    length = shards * shard_len
    block = min(256, length)
    per = block // shard_len
    lanes = lambda i: pl.ds(pl.multiple_of((pair * 3 + i) * PAIR, PAIR), PAIR)
    first = lax.rem(lax.broadcasted_iota(jnp.int32, (length, PAIR), 1), HD) < HD // 2
    cos_all, sin_all = cos[:, r].reshape(length, PAIR), sin[:, r].reshape(length, PAIR)

    def rotate(i):
        v = pre[:, r, :, lanes(i)].reshape(length, PAIR)
        return (v * cos_all + swap_halves(v, first) * sin_all).astype(bf16)

    query, key = rotate(0), rotate(1)
    value = pre[:, r, :, lanes(2)].reshape(length, PAIR)
    value_t = value.T.astype(bf16)
    for i, v in enumerate((query, key, value.astype(bf16))):
        rotated[:, r, :, lanes(i)] = v.reshape(shards, shard_len, PAIR)
    left = lax.broadcasted_iota(jnp.int32, (block, PAIR), 1) < HD
    top = lax.broadcasted_iota(jnp.int32, (PAIR, block), 0) < HD
    scaled = query * jnp.asarray(0.125, bf16)
    here_lanes = pl.ds(pl.multiple_of(pair * PAIR, PAIR), PAIR)
    for i in range(length // block):
        keys = (i + 1) * block
        at = slice(i * block, (i + 1) * block)
        mask = allowed_pairs(starts[:, at], keys, block, i * block)
        here = scaled[at]
        results = []
        for h in range(2):
            own = jnp.where(left if h == 0 else ~left, here, jnp.zeros_like(here))
            scores = jnp.where(mask, dot_t(key[:keys], own), -1e30)
            peak = jnp.max(scores, axis=0, keepdims=True)
            shifted = jnp.exp(scores - peak)
            summed = jnp.sum(shifted, axis=0, keepdims=True)
            probs = (shifted * (1.0 / summed)).astype(bf16)
            results.append(dot(value_t[:, :keys], probs))
            stats[r, pair, h : h + 1, at] = peak + jnp.log(summed)
        merged = jnp.where(top, results[0], results[1]).T.astype(bf16)
        attended[i * per : (i + 1) * per, r, :, here_lanes] = merged.reshape(
            per, shard_len, PAIR
        )


def attend_kernel(pre, cos, sin, starts, rotated, attended, stats):
    attend_pair(pre, cos, sin, starts[0], rotated, attended, stats, 0, 0)


def attend(pre, cos, sin, starts):
    shards, rows, shard_len, width = pre.shape
    pairs = width // (3 * PAIR)
    length = shards * shard_len
    wide = pl.BlockSpec((shards, 1, shard_len, 3 * PAIR), lambda r, p: (0, r, 0, p))
    narrow = pl.BlockSpec((shards, 1, shard_len, PAIR), lambda r, p: (0, r, 0, p))
    table = pl.BlockSpec((shards, 1, shard_len, PAIR), lambda r, p: (0, r, 0, 0))
    return pl.pallas_call(
        attend_kernel,
        grid=(rows, pairs),
        out_shape=[
            jax.ShapeDtypeStruct(pre.shape, bf16),
            jax.ShapeDtypeStruct((shards, rows, shard_len, pairs * PAIR), bf16),
            jax.ShapeDtypeStruct((rows, pairs, 2, length), f32),
        ],
        in_specs=[wide, table, table, pl.BlockSpec((1, 1, length), lambda r, p: (r, 0, 0))],
        out_specs=[wide, narrow, pl.BlockSpec((1, 1, 2, length), lambda r, p: (r, p, 0, 0))],
        compiler_params=pltpu.CompilerParams(vmem_limit_bytes=48 * MIB),
        cost_estimate=pl.CostEstimate(
            flops=rows * pairs * 2 * length * length * 256 * 2,
            bytes_accessed=pre.size * 8,
            transcendentals=rows * pairs * length * length,
        ),
    )(pre, cos, sin, starts)


def attend_back_pair(rotated, grad, cos, sin, starts, stats, result, key_acc, value_acc, r, pair):
    shards, _, shard_len, _ = rotated.shape
    length = shards * shard_len
    block = min(256, length)
    per = block // shard_len
    lanes = lambda i: pl.ds(pl.multiple_of((pair * 3 + i) * PAIR, PAIR), PAIR)
    query, key, value = (rotated[:, r, :, lanes(i)].reshape(length, PAIR) for i in range(3))
    grad_all = grad[:, r, :, pl.ds(pl.multiple_of(pair * PAIR, PAIR), PAIR)].reshape(length, PAIR)
    key_t = key.astype(f32).T.astype(bf16)
    left = lax.broadcasted_iota(jnp.int32, (block, PAIR), 1) < HD
    top = lax.broadcasted_iota(jnp.int32, (PAIR, block), 0) < HD
    first = lax.rem(lax.broadcasted_iota(jnp.int32, (length, PAIR), 1), HD) < HD // 2
    key_acc[...] = jnp.zeros_like(key_acc)
    value_acc[...] = jnp.zeros_like(value_acc)

    for i in range(length // block):
        keys = (i + 1) * block
        at = slice(i * block, (i + 1) * block)
        here = slice(i * per, (i + 1) * per)
        mask = allowed_pairs(starts[:, at], keys, block, i * block)
        results = []
        for h in range(2):
            side = left if h == 0 else ~left
            own = jnp.where(side, query[at], jnp.zeros_like(query[at]))
            own_grad = jnp.where(side, grad_all[at], jnp.zeros_like(grad_all[at]))
            scores = dot_t(key[:keys], own * jnp.asarray(0.125, bf16))
            probs = jnp.exp(jnp.where(mask, scores - stats[r, pair, h : h + 1, at], -1e30))
            grad_probs = dot_t(value[:keys], own_grad)
            inner = jnp.sum(probs * grad_probs, axis=0, keepdims=True)
            grad_scores = (probs * (grad_probs - inner) * 0.125).astype(bf16)
            key_acc[:keys, :] += dot(grad_scores, own)
            value_acc[:keys, :] += dot(probs.astype(bf16), own_grad)
            results.append(dot(key_t[:, :keys], grad_scores))
        merged = jnp.where(top, results[0], results[1]).T
        cos_here, sin_here = cos[here, r].reshape(block, PAIR), sin[here, r].reshape(block, PAIR)
        turned = merged * cos_here - swap_halves(merged, first[:block]) * sin_here
        result[here, r, :, lanes(0)] = turned.astype(bf16).reshape(per, shard_len, PAIR)
    cos_all, sin_all = cos[:, r].reshape(length, PAIR), sin[:, r].reshape(length, PAIR)
    key_grad = key_acc[...]
    turned = key_grad * cos_all - swap_halves(key_grad, first) * sin_all
    result[:, r, :, lanes(1)] = turned.astype(bf16).reshape(shards, shard_len, PAIR)
    result[:, r, :, lanes(2)] = value_acc[...].astype(bf16).reshape(shards, shard_len, PAIR)


def attend_back_kernel(rotated, grad, cos, sin, starts, stats, result, key_acc, value_acc):
    attend_back_pair(
        rotated, grad, cos, sin, starts[0], stats, result, key_acc, value_acc, 0, 0
    )


def attend_back(rotated, grad, cos, sin, starts, stats):
    shards, rows, shard_len, width = rotated.shape
    pairs = width // (3 * PAIR)
    length = shards * shard_len
    wide = pl.BlockSpec((shards, 1, shard_len, 3 * PAIR), lambda r, p: (0, r, 0, p))
    narrow = pl.BlockSpec((shards, 1, shard_len, PAIR), lambda r, p: (0, r, 0, p))
    table = pl.BlockSpec((shards, 1, shard_len, PAIR), lambda r, p: (0, r, 0, 0))
    return pl.pallas_call(
        attend_back_kernel,
        grid=(rows, pairs),
        out_shape=jax.ShapeDtypeStruct(rotated.shape, bf16),
        in_specs=[
            wide,
            narrow,
            table,
            table,
            pl.BlockSpec((1, 1, length), lambda r, p: (r, 0, 0)),
            pl.BlockSpec((1, 1, 2, length), lambda r, p: (r, p, 0, 0)),
        ],
        out_specs=wide,
        scratch_shapes=[pltpu.VMEM((length, PAIR), f32), pltpu.VMEM((length, PAIR), f32)],
        compiler_params=pltpu.CompilerParams(vmem_limit_bytes=48 * MIB),
        cost_estimate=pl.CostEstimate(
            flops=rows * pairs * 5 * length * length * 256 * 2,
            bytes_accessed=rotated.size * 6,
            transcendentals=rows * pairs * length * length,
        ),
    )(rotated, grad, cos, sin, starts, stats)


def rope_tables(doc_ids, shards):
    rows, length = doc_ids.shape
    places = lax.broadcasted_iota(jnp.int32, doc_ids.shape, 1)
    earlier = jnp.concatenate([doc_ids[:, :1], doc_ids[:, :-1]], axis=1)
    starts = lax.cummax(jnp.where(doc_ids != earlier, places, 0), axis=1)
    positions = (places - starts).astype(f32)
    frequency = rope_base ** (-(jnp.arange(HD // 2, dtype=f32) * 2.0 / HD))
    angles = positions[..., None] * frequency
    cos, sin = jnp.cos(angles), jnp.sin(angles)
    lay = lambda v: jnp.moveaxis(
        jnp.concatenate(v, axis=-1).reshape(rows, shards, length // shards, PAIR), 0, 1
    )
    return lay([cos] * 4), lay([-sin, sin, -sin, sin]), starts


class LineSum:
    def __init__(self, p, view, land, send, recv, base):
        self.p, self.view, self.land = p, view, land
        self.send, self.recv, self.base = send, recv, base
        self.z = p["dp"]
        self.inward = 1 - 2 * lax.div(self.z, 2)
        self.end = (self.z == 0) | (self.z == 3)

    def copy(self, src, slot, i, to):
        return pltpu.make_async_remote_copy(
            src_ref=src,
            dst_ref=self.land.at[slot],
            send_sem=self.send.at[self.base + i],
            recv_sem=self.recv.at[self.base + slot],
            device_id=(to, self.p["me"]),
            device_id_type=MESH,
        )

    def arrived(self, slot):
        self.copy(self.land.at[slot], slot, 0, self.z).wait_recv()

    def first(self):
        self.first_far()
        self.first_rest()

    def first_far(self):
        z, inward = self.z, self.inward

        @pl.when(self.end)
        def _():
            near, far = z + inward, z + 3 * inward
            self.copy(self.view(far), near, 0, near).start()

    def first_rest(self):
        z, inward = self.z, self.inward

        @pl.when(self.end)
        def _():
            near, mid = z + inward, z + 2 * inward
            self.copy(self.view(mid), z, 1, mid).start()
            self.copy(self.view(near), z, 2, near).start()

        @pl.when(jnp.logical_not(self.end))
        def _():
            inner, outer = z + inward, z - inward
            self.copy(self.view(inner), z, 0, inner).start()
            self.copy(self.view(outer), z, 1, outer).start()

    def second(self, acc, extra, local, i):
        @pl.when(jnp.logical_not(self.end))
        def _():
            far = self.z + 2 * self.inward
            own = pltpu.make_async_copy(self.view(far), acc, local.at[i])
            own.start()
            self.arrived(self.z)
            other = pltpu.make_async_copy(self.land.at[self.z], extra, local.at[i + 1])
            other.start()
            own.wait()
            other.wait()

            def step(at):
                acc[at, :] = (acc[at, :].astype(f32) + extra[at, :].astype(f32)).astype(bf16)

            over_rows(acc.shape[0], step)
            self.copy(acc, self.z, 2, far).start()

    def total(self, parts, local, i):
        z, inward = self.z, self.inward
        self.arrived(z + inward)
        self.arrived(z + 2 * inward)
        loads = [
            pltpu.make_async_copy(src, parts.at[k], local.at[i + k])
            for k, src in enumerate(
                (self.view(z), self.land.at[z + inward], self.land.at[z + 2 * inward])
            )
        ]
        for load in loads:
            load.start()
        for load in loads:
            load.wait()
        rows = parts.shape[1]
        three = lambda at: (parts[0, at, :].astype(f32) + parts[1, at, :].astype(f32)) + parts[
            2, at, :
        ].astype(f32)

        @pl.when(self.end)
        def _():
            def step(at):
                parts[0, at, :] = three(at).astype(bf16)

            over_rows(rows, step)

        @pl.when(jnp.logical_not(self.end))
        def _():
            self.arrived(z - inward)
            load = pltpu.make_async_copy(self.land.at[z - inward], parts.at[3], local.at[i + 3])
            load.start()
            load.wait()

            def step(at):
                parts[0, at, :] = (three(at) + parts[3, at, :].astype(f32)).astype(bf16)

            over_rows(rows, step)

    def finish(self):
        for i in range(3):
            self.copy(self.land.at[0], 0, i, self.z).wait_send()


def feed_kernel(
    normed,
    cot,
    units,
    down,
    w_down,
    own_cot,
    hidden,
    gain,
    grad_hidden,
    gain_term,
    branch,
    out_terms,
    unit_sums,
    down_sums,
    unit_terms,
    down_terms,
    kept_units,
    kept_acts,
    unit_land,
    down_land,
    late_units,
    late_down,
    x,
    c,
    w,
    d,
    unit_stage,
    act_stage,
    unit_kept,
    act_kept,
    unit_grad,
    down_grad,
    unit_acc,
    down_acc,
    unit_parts,
    down_parts,
    stage,
    kept,
    paired,
    far,
    final,
    send,
    recv,
    gsend,
    grecv,
    zsend,
    zrecv,
    lsend,
    lrecv,
    local,
):
    p = plane()
    barrier = pltpu.get_barrier_semaphore()
    others = [(p["dp"], p[name]) for name in ("sib", "xp", "yp")]
    for k in range(1, 4):
        others.append((lax.rem(p["dp"] + k, 4), p["me"]))
    for where in others:
        pl.semaphore_signal(barrier, inc=1, device_id=where, device_id_type=MESH)
    sems = Local(local)
    x_sem, c_sem, w_sem, d_sem = sems.take(8), sems.take(8), sems.take(2), sems.take(2)
    us_sem, as_sem, ug_sem, dg_sem = (sems.take() for _ in range(4))
    ub_sem, ab_sem, out_sem, last_w, last_d = (
        sems.take(2),
        sems.take(2),
        sems.take(2),
        sems.take(32),
        sems.take(16),
    )
    z_sem, own_sem, turn_sem = sems.take(8), sems.take(), sems.take(2)
    shards, rows, width = normed.shape
    chunk = w.shape[3]
    part = chunk // 2
    piece = down.shape[2]
    all_units = lambda j: units.at[j] if j < EARLY else late_units
    all_down = lambda j: down.at[j] if j < EARLY else late_down
    late = (
        LineGather(
            p, units.at[EARLY, p["dp"]], late_units, lsend, lrecv, 0, local.at[sems.take()]
        ),
        LineGather(
            p,
            w_down.at[pl.ds(EARLY * piece, piece)],
            late_down,
            lsend,
            lrecv,
            1,
            local.at[sems.take()],
        ),
    )

    def move(src, dst, i):
        return pltpu.make_async_copy(src, dst, local.at[i])

    def shard_rows(s, count=1):
        return pl.ds(pl.multiple_of(s * rows, rows), count * rows)

    def chunk_loads(j):
        return (
            move(all_units(j), w.at[j % 2], w_sem + j % 2),
            move(all_down(j), d.at[j % 2], d_sem + j % 2),
        )

    def start_chunk(j):
        for load in chunk_loads(j):
            load.start()

    start_chunk(0)
    for s in range(shards):
        move(normed.at[s], x.at[shard_rows(s)], x_sem + s).start()
        move(cot.at[s], c.at[shard_rows(s)], c_sem + s).start()
    pl.semaphore_wait(barrier, len(others))
    for gather in late:
        gather.start()

    line = {}
    for j in range(EARLY):
        line[j] = (
            LineSum(
                p,
                lambda owner, j=j: unit_terms.at[
                    j, pl.ds(pl.multiple_of(owner * chunk, chunk), chunk)
                ],
                unit_land.at[j],
                zsend,
                zrecv,
                8 * j,
            ),
            LineSum(
                p,
                lambda owner, j=j: down_terms.at[
                    j, pl.ds(pl.multiple_of(owner * piece, piece), piece)
                ],
                down_land.at[j],
                zsend,
                zrecv,
                8 * j + 4,
            ),
        )

    def pass_on(j):
        line[j][0].second(unit_acc.at[j], unit_parts.at[0], local, z_sem)
        line[j][1].second(down_acc.at[j], down_parts.at[0], local, z_sem + 2)

    def work(j):
        slot = j % 2
        if j == EARLY:
            for gather in late:
                gather.finish()
            start_chunk(j)
        for load in chunk_loads(j):
            load.wait()
        if j + 1 < EARLY:
            start_chunk(j + 1)
        if j > 0:
            keep(j - 1, "wait")

        @pl.loop(0, shards, step=2)
        def _(s):
            both = shard_rows(s, 2)
            if j == 0:
                for k in range(2):
                    move(normed.at[s + k], x.at[shard_rows(s + k)], x_sem + s + k).wait()
                    move(cot.at[s + k], c.at[shard_rows(s + k)], c_sem + s + k).wait()
            pre = dot(x[both], w[slot].reshape(width, chunk))
            grad_act = dot_t(c[both], d[slot].reshape(part, width))
            gate, up = pre[:, :part], pre[:, part:]
            sigmoid = 1.0 / (1.0 + jnp.exp(-gate))
            silu = gate * sigmoid
            act_stage[both] = (silu * up).astype(bf16)
            unit_stage[both, :part] = (
                grad_act * up * sigmoid * (1.0 + gate * (1.0 - sigmoid))
            ).astype(bf16)
            unit_stage[both, part:] = (grad_act * silu).astype(bf16)

        keep(j, "start")

    def keep(j, what):
        getattr(move(unit_stage, kept_units.at[:, pl.ds(j * chunk, chunk)], us_sem), what)()
        getattr(move(act_stage, kept_acts.at[:, pl.ds(j * part, part)], as_sem), what)()

    def weigh(j, units_now, acts_now):
        @pl.loop(0, width // 512)
        def _(n):
            at = pl.ds(pl.multiple_of(n * 512, 512), 512)
            unit_grad[at] = dot_l(x[:, at], units_now[...]).astype(bf16)
            down_grad[:, at] = dot_l(acts_now[...], c[:, at]).astype(bf16)

        store = [
            move(unit_grad, unit_terms.at[j], ug_sem),
            move(down_grad, down_terms.at[j], dg_sem),
        ]
        for copy in store:
            copy.start()
        for copy in store:
            copy.wait()
        if j < EARLY:
            for sums in line[j]:
                sums.first()

    for j in range(CHUNKS):
        work(j)
        weigh(j, unit_stage, act_stage)
        for gather in late:
            if j == 0:
                gather.second()
            if j == 1:
                gather.third()
        if j >= 2:
            pass_on(j - 2)
    keep(CHUNKS - 1, "wait")

    load_w = [
        move(
            all_units(j).at[k // 2, pl.ds(k % 2 * rows, rows)],
            x.at[shard_rows(k), pl.ds(j * chunk, chunk)],
            last_w + 8 * j + k,
        )
        for j in range(CHUNKS)
        for k in range(shards)
    ]
    load_d = [
        move(all_down(j).at[k], c.at[pl.ds(j * part + k * piece, piece)], last_d + 4 * j + k)
        for j in range(CHUNKS)
        for k in range(4)
    ]
    for load in load_w + load_d:
        load.start()

    order = [name for _, own, far_name in ORDER for name in (far_name, own)]

    def load_kept(k):
        return move(
            kept_units.at[shard_rows(p[order[k]])],
            unit_kept.at[pl.ds(k % 2 * rows, rows)],
            ub_sem + k % 2,
        )

    load_kept(0).start()

    def produce(name, out):
        k = order.index(name)
        load_kept(k).wait()
        if k + 1 < len(order):
            load_kept(k + 1).start()
        if k == 0:
            for load in load_w:
                load.wait()

        @pl.loop(0, width // 1024)
        def _(n):
            at = pl.ds(pl.multiple_of(n * 1024, 1024), 1024)
            out[:, at] = dot_t(unit_kept[k % 2 * rows : (k % 2 + 1) * rows], x[at]).astype(bf16)

    def act_load(s):
        slot = lax.rem(s, 2)
        return move(kept_acts.at[shard_rows(s)], act_kept.at[slot], ab_sem + slot)

    def out_store(s):
        slot = lax.rem(s, 2)
        return move(unit_grad_rows(slot), out_terms.at[s], out_sem + slot)

    def unit_grad_rows(slot):
        return stage.at[shard_rows(slot)]

    def forward_terms():
        source.finish()
        source.pairs.clear()
        for load in load_d:
            load.wait()
        act_load(0).start()

        @pl.loop(0, shards)
        def _(s):
            act_load(s).wait()

            @pl.when(s + 1 < shards)
            def _():
                act_load(s + 1).start()

            @pl.when(s >= 2)
            def _():
                out_store(s - 2).wait()

            slot = lax.rem(s, 2)
            acts = act_kept[slot]

            @pl.loop(0, width // 1024)
            def _(n):
                at = pl.ds(pl.multiple_of(n * 1024, 1024), 1024)
                stage[shard_rows(slot), at] = dot(acts, c[: acts.shape[1], at]).astype(bf16)

            out_store(s).start()

        out_store(shards - 2).wait()
        out_store(shards - 1).wait()
        pass_on(2)

    source = Produced(p, produce, stage, kept, paired, send, recv)
    sends = scatter_plane(
        p, source, rows, kept, paired, far, final, send, recv, meanwhile=forward_terms
    )
    gain_term[...] = jnp.zeros_like(gain_term)

    def step(at):
        g = total(kept, paired, final, at)
        h = hidden[at, :]
        scale = lax.rsqrt(jnp.mean(h * h, axis=-1, keepdims=True) + norm_eps)
        weighted = g * gain[...]
        inner = jnp.mean(weighted * h, axis=-1, keepdims=True)
        out = own_cot[at, :].astype(f32) + scale * weighted - h * (scale * scale * scale * inner)
        grad_hidden[at, :] = out
        down_grad[at, :] = out.astype(bf16)
        gain_term[...] += jnp.sum(g * h * scale, axis=0, keepdims=True)

    over_rows(rows, step)
    sent = gather_start(p, down_grad, branch, gsend, grecv, 0)
    own = move(down_grad, branch.at[p["me"]], own_sem)
    own.start()

    def sum_up(j):
        line[j][0].total(unit_parts, local, z_sem)
        line[j][1].total(down_parts, local, z_sem + 4)
        out = [move(unit_parts.at[0], unit_sums.at[j], turn_sem), move(down_parts.at[0], down_sums.at[j], turn_sem + 1)]
        for copy in out:
            copy.start()
        for copy in out:
            copy.wait()

    sum_up(0)
    gather_finish(p, sent, branch, gsend, grecv, 0)
    own.wait()
    sum_up(1)
    sum_up(2)
    for j in range(EARLY):
        for sums in line[j]:
            sums.finish()
    sends.finish()


def feed_plane(normed, cot, units, down, w_down, own_cot, hidden, gain, collective_id):
    shards, rows, width = normed.shape
    chunk = units.shape[3]
    wide = chunk * CHUNKS
    part = chunk // 2
    piece = down.shape[2]
    sds = jax.ShapeDtypeStruct
    return pl.pallas_call(
        feed_kernel,
        out_shape=[
            sds((rows, width), f32),
            sds((1, width), f32),
            sds((shards, rows, width), bf16),
            sds((shards, rows, width), bf16),
            sds((EARLY, chunk, chunk), bf16),
            sds((EARLY, piece, width), bf16),
            sds((CHUNKS, width, chunk), bf16),
            sds((CHUNKS, part, width), bf16),
            sds((shards * rows, wide), bf16),
            sds((shards * rows, wide // 2), bf16),
            sds((EARLY, 4, chunk, chunk), bf16),
            sds((EARLY, 4, piece, width), bf16),
            sds((4, width // 4, chunk), bf16),
            sds((4, piece, width), bf16),
        ],
        in_specs=[ANY] * 5 + [VMEM] * 3,
        out_specs=[VMEM, VMEM] + [ANY] * 12,
        scratch_shapes=[
            pltpu.VMEM((shards * rows, width), bf16),
            pltpu.VMEM((shards * rows, width), bf16),
            pltpu.VMEM((2, 4, width // 4, chunk), bf16),
            pltpu.VMEM((2, 4, piece, width), bf16),
            pltpu.VMEM((shards * rows, chunk), bf16),
            pltpu.VMEM((shards * rows, part), bf16),
            pltpu.VMEM((2 * rows, wide), bf16),
            pltpu.VMEM((2, rows, wide // 2), bf16),
            pltpu.VMEM((width, chunk), bf16),
            pltpu.VMEM((part, width), bf16),
            pltpu.VMEM((EARLY, chunk, chunk), bf16),
            pltpu.VMEM((EARLY, piece, width), bf16),
            pltpu.VMEM((4, chunk, chunk), bf16),
            pltpu.VMEM((4, piece, width), bf16),
            pltpu.VMEM((2 * rows, width), bf16),
        ]
        + scatter_scratch(rows, width)[:6]
        + [
            DMA((GATHER_SEMS,)),
            DMA((GATHER_SEMS,)),
            DMA((8 * EARLY,)),
            DMA((8 * EARLY,)),
            DMA((2 * LINE_SEMS,)),
            DMA((2 * LINE_SEMS,)),
            DMA((100,)),
        ],
        compiler_params=pltpu.CompilerParams(
            collective_id=collective_id, has_side_effects=True, vmem_limit_bytes=62 * MIB
        ),
        cost_estimate=lasting(160),
    )(
        normed,
        cot,
        units,
        down,
        w_down,
        own_cot,
        hidden,
        gain,
    )


def tail_kernel(
    devices,
    branch,
    normed_one,
    rotated_in,
    out_terms,
    unit_terms,
    down_terms,
    unit_sums,
    down_sums,
    hidden,
    grad_hidden,
    qkv,
    out_weight,
    attended,
    stats,
    cos,
    sin,
    starts,
    tokens,
    gain,
    gain_two_term,
    grad_tokens,
    out_tokens,
    gain_sums,
    grad_query,
    grad_key,
    grad_value,
    grad_out,
    grad_gate,
    grad_up,
    grad_down,
    head_terms,
    wo_terms,
    unit_sum,
    head_sum,
    unit_land,
    down_land,
    head_land,
    wo_land,
    x,
    rotated,
    grads,
    key_acc,
    value_acc,
    head_grad,
    wo_grad,
    residual,
    units,
    heads,
    wide_out,
    row_out,
    gain_one_term,
    gain_mine,
    gain_land,
    unit_acc,
    down_acc,
    head_acc,
    wo_acc,
    parts,
    row_parts,
    stage,
    zsend,
    zrecv,
    esend,
    erecv,
    gsend,
    grecv,
    ready,
    local,
    kept,
    paired,
    far,
    final,
    send,
    recv,
    loads,
):
    p = plane()
    other, met = meet_all(p, devices)
    mine = p["dp"] * 8 + p["me"]
    sems = Local(local)
    rows, width = tokens.shape
    shards, batch, shard_len, wide = rotated.shape
    pairs = wide // (3 * PAIR)
    chunk = unit_terms.shape[2]
    piece = down_terms.shape[1] // 4
    span = unit_land.shape[1]
    held = units.shape[2]
    late = unit_terms.shape[0] - 1
    z_sem = sems.take(4)

    def move(src, dst, i=None):
        return pltpu.make_async_copy(src, dst, local.at[sems.take() if i is None else i])

    def shard_rows(s):
        return pl.ds(pl.multiple_of(s * rows, rows), rows)

    x_loads = [move(branch.at[s], x.at[pl.ds(s * rows, rows)]) for s in range(shards)]
    load_rotated = move(rotated_in, rotated)
    load_hidden = move(hidden, residual)
    for load in x_loads + [load_rotated, load_hidden]:
        load.start()

    def of_owner(ref, count):
        return lambda owner: ref.at[pl.ds(pl.multiple_of(owner * count, count), count)]

    unit_line = LineSum(p, of_owner(unit_terms.at[late], span), unit_land, zsend, zrecv, 0)
    down_line = LineSum(p, of_owner(down_terms.at[late], piece), down_land, zsend, zrecv, 4)
    head_line = LineSum(p, of_owner(head_terms, span), head_land, zsend, zrecv, 8)
    wo_line = LineSum(p, of_owner(wo_terms, held), wo_land, zsend, zrecv, 12)
    met()
    unit_line.first()
    down_line.first()
    out_source = FromMemory(p, out_terms, kept, paired, send, recv, loads)
    out_sum = PlaneSum(p, out_source, rows, kept, paired, far, final, send, recv)
    exchanged = {}

    def exchange(i, block, out):
        copies = [
            remote(p, block(p[name]), out, esend, erecv, i * 7 + j, name)
            for j, name in enumerate(OTHERS)
        ]
        copies.append(move(block(p["me"]), out))
        for copy in copies:
            copy.start()
        exchanged[i] = copies

    def exchange_units(j, source):
        exchange(j, of_owner(source, held), units.at[j, p["me"]])

    for load in x_loads:
        load.wait()

    @pl.loop(0, shards, step=2)
    def _(s):
        at = pl.ds(pl.multiple_of(s * rows, rows), 2 * rows)
        grad = dot_t(x[at], out_weight[...].reshape(-1, width)).astype(bf16)
        grads[pl.ds(s, 2)] = grad.reshape((2,) + grads.shape[1:])

    out_sum.first()

    @pl.loop(0, width // 512)
    def _(n):
        at = pl.ds(pl.multiple_of(n * 512, 512), 512)
        acts = attended[...].reshape(shards * rows, -1)
        wo_grad[:, at] = dot_l(acts, x[:, at]).astype(bf16)

    store_wo = move(wo_grad, wo_terms)
    store_wo.start()
    n1_loads = [move(normed_one.at[s], x.at[pl.ds(s * rows, rows)]) for s in range(shards)]
    for load in n1_loads:
        load.start()
    store_wo.wait()
    wo_line.first()
    load_rotated.wait()

    def attention(r):
        @pl.loop(0, pairs)
        def _(pair):
            attend_back_pair(
                rotated,
                grads,
                cos,
                sin,
                starts[r],
                stats,
                rotated,
                key_acc,
                value_acc,
                r,
                pair,
            )

    attention(0)
    out_sum.second()
    unit_line.second(unit_acc, parts.at[0, :, pl.ds(0, chunk)], local, z_sem)
    down_line.second(down_acc, row_parts.at[0], local, z_sem)
    for j in range(late):
        exchange_units(j, unit_sums.at[j])
    attention(1)
    for load in n1_loads:
        load.wait()
    out_sum.third()
    load_hidden.wait()

    def step_out(at):
        out_tokens[at, :] = (residual[at, :] + total(kept, paired, final, at)).astype(bf16)

    over_rows(rows, step_out)
    out_sum.finish()
    for name in ("sib", "xp", "yp"):
        pl.semaphore_signal(ready, inc=1, device_id=(p["dp"], p[name]), device_id_type=MESH)
    load_grad = move(grad_hidden, residual)
    load_grad.start()

    @pl.loop(0, width // 512)
    def _(n):
        at = pl.ds(pl.multiple_of(n * 512, 512), 512)
        head_grad[at] = dot_l(x[:, at], rotated[...].reshape(shards * rows, wide)).astype(bf16)

    store_head = move(head_grad, head_terms)
    store_head.start()
    store_head.wait()
    head_line.first()
    pl.semaphore_wait(ready, 3)

    def produce(name, out):
        s = p[name]
        grad = rotated[s].reshape(rows, wide)

        @pl.loop(0, 4)
        def _(n):
            at = pl.ds(pl.multiple_of(n * span, span), span)
            out[:, at] = dot_t(grad, qkv[n]).astype(bf16)

    source = Produced(p, produce, stage, kept, paired, send, recv)
    sums = PlaneSum(p, source, rows, kept, paired, far, final, send, recv)
    sums.first()
    wo_line.second(wo_acc, row_parts.at[1], local, z_sem)
    sums.second()
    head_line.second(head_acc, parts.at[1], local, z_sem)

    def emit_rows(source, at, out):
        row_out[...] = source.astype(f32)
        copy = move(row_out, out.at[at], z_sem)
        copy.start()
        copy.wait()

    for j in range(late):
        copy = move(down_sums.at[j], row_parts.at[0], z_sem)
        copy.start()
        copy.wait()
        emit_rows(row_parts[0], pl.ds(j * piece, piece), grad_down)
    unit_line.total(parts.at[:, :, pl.ds(0, chunk)], local, z_sem)
    copy = move(parts.at[0, :, pl.ds(0, chunk)], unit_sum, z_sem)
    copy.start()
    copy.wait()
    exchange_units(late, unit_sum)
    down_line.total(row_parts, local, z_sem)
    emit_rows(row_parts[0], pl.ds(late * piece, piece), grad_down)
    wo_line.total(row_parts, local, z_sem)
    grad_out[...] = row_parts[0].astype(f32)
    load_grad.wait()
    sums.third()
    gain_one_term[...] = jnp.zeros_like(gain_one_term)

    def step(at):
        g = total(kept, paired, final, at)
        t = tokens[at, :].astype(f32)
        scale = lax.rsqrt(jnp.mean(t * t, axis=-1, keepdims=True) + norm_eps)
        weighted = g * gain[...]
        inner = jnp.mean(weighted * t, axis=-1, keepdims=True)
        grad_tokens[at, :] = (
            residual[at, :] + scale * weighted - t * (scale * scale * scale * inner)
        ).astype(bf16)
        gain_one_term[...] += jnp.sum(g * t * scale, axis=0, keepdims=True)

    over_rows(rows, step)
    gain_mine[...] = jnp.zeros_like(gain_mine)
    for k in range(devices):
        at = slice(k * held, (k + 1) * held)
        gain_mine[k, 0:1, :held] = gain_one_term[:, at]
        gain_mine[k, 1:2, :held] = gain_two_term[:, at]

    def gain_copy(k):
        where, to = other(k)
        return pltpu.make_async_remote_copy(
            src_ref=gain_mine.at[to],
            dst_ref=gain_land.at[k],
            send_sem=gsend.at[k],
            recv_sem=grecv.at[k],
            **where,
        )

    @pl.loop(1, devices)
    def _(k):
        gain_copy(k).start()

    head_line.total(parts, local, z_sem)
    copy = move(parts.at[0], head_sum, z_sem)
    copy.start()
    copy.wait()
    exchange(late + 1, of_owner(head_sum, held), heads.at[p["me"]])
    for j in range(late + 1):
        for copy in exchanged[j]:
            copy.wait()
    stores = []
    for i, out in enumerate((grad_gate, grad_up)):
        for k in range(4):
            if len(stores) >= 2:
                stores[-2].wait()
            for s in range(shards):
                for a in range(2):
                    base = (i * 4 + k) * piece
                    tile = jnp.concatenate(
                        [units[2 * a + b, s, :, base : base + piece] for b in range(2)], axis=1
                    )
                    at = (s * 2 + a) * 2 * piece
                    wide_out[k % 2, :, at : at + 2 * piece] = tile.astype(f32)
            wide = wide_out.shape[2]
            stores.append(move(wide_out.at[k % 2], out.at[:, pl.ds(k * wide, wide)]))
            stores[-1].start()
    gain_land[0] = gain_mine[mine]

    @pl.loop(1, devices)
    def _(k):
        gain_copy(k).wait()

    gain_sums[...] = jnp.sum(gain_land[...], axis=0)
    for copy in exchanged[late + 1]:
        copy.wait()
    for i, out in enumerate((grad_query, grad_key, grad_value)):
        for k in range(4):
            for s in range(0, shards, 2):
                base = (k // 2 * 3 + i) * PAIR + k % 2 * HD
                tile = jnp.concatenate(
                    [heads[s + b, :, base : base + HD] for b in range(2)], axis=1
                )
                at = (k * shards + s) * HD
                out[:, at : at + 2 * HD] = tile.astype(f32)
    for copy in stores[-2:]:
        copy.wait()
    for line in (unit_line, down_line, head_line, wo_line):
        line.finish()
    sums.finish()


def tail_plane(
    groups,
    branch,
    normed_one,
    rotated,
    out_terms,
    unit_terms,
    down_terms,
    unit_sums,
    down_sums,
    hidden,
    grad_hidden,
    qkv,
    out_weight,
    attended,
    stats,
    cos,
    sin,
    starts,
    tokens,
    gain,
    gain_two_term,
    collective_id,
):
    rows, width = tokens.shape
    shards, batch, shard_len, wide = rotated.shape
    devices = groups * shards
    held = width // devices
    span = width // groups
    chunk = unit_terms.shape[2]
    piece = down_terms.shape[1] // groups
    units_wide = CHUNKS * chunk // 2 // groups * devices
    length = shards * shard_len
    sds = jax.ShapeDtypeStruct
    unit, down, head, wo = (span, chunk), (piece, width), (span, wide), (held, width)
    return pl.pallas_call(
        functools.partial(tail_kernel, devices),
        out_shape=[
            sds((rows, width), bf16),
            sds((rows, width), bf16),
            sds((8, 128), f32),
            *[sds((held, width), f32)] * 4,
            *[sds((held, units_wide), f32)] * 2,
            sds((CHUNKS * piece, width), f32),
            sds((width, wide), bf16),
            sds((groups * held, width), bf16),
            sds(unit, bf16),
            sds(head, bf16),
            sds((4,) + unit, bf16),
            sds((4,) + down, bf16),
            sds((4,) + head, bf16),
            sds((4,) + wo, bf16),
        ],
        in_specs=[ANY] * 10 + [VMEM] * 9 + [VMEM],
        out_specs=[VMEM] * 7 + [ANY] * 11,
        scratch_shapes=[
            pltpu.VMEM((shards * rows, width), bf16),
            pltpu.VMEM(rotated.shape, bf16),
            pltpu.VMEM(attended.shape, bf16),
            pltpu.VMEM((length, PAIR), f32),
            pltpu.VMEM((length, PAIR), f32),
            pltpu.VMEM((width, wide), bf16),
            pltpu.VMEM((groups * held, width), bf16),
            pltpu.VMEM((rows, width), f32),
            pltpu.VMEM((CHUNKS, shards, held, chunk), bf16),
            pltpu.VMEM((shards, held, wide), bf16),
            pltpu.VMEM((2, held, units_wide // groups), f32),
            pltpu.VMEM(down, f32),
            pltpu.VMEM((1, width), f32),
            pltpu.VMEM((devices, 8, 128), f32),
            pltpu.VMEM((devices, 8, 128), f32),
            pltpu.VMEM(unit, bf16),
            pltpu.VMEM(down, bf16),
            pltpu.VMEM(head, bf16),
            pltpu.VMEM(wo, bf16),
            pltpu.VMEM((4,) + head, bf16),
            pltpu.VMEM((4,) + down, bf16),
            pltpu.VMEM((2 * rows, width), bf16),
            DMA((16,)),
            DMA((16,)),
            DMA((35,)),
            DMA((35,)),
            DMA((devices,)),
            DMA((devices,)),
            pltpu.SemaphoreType.REGULAR,
            DMA((48,)),
        ]
        + scatter_scratch(rows, width),
        compiler_params=pltpu.CompilerParams(
            collective_id=collective_id, has_side_effects=True, vmem_limit_bytes=62 * MIB
        ),
        cost_estimate=lasting(130),
    )(
        branch,
        normed_one,
        rotated,
        out_terms,
        unit_terms,
        down_terms,
        unit_sums,
        down_sums,
        hidden,
        grad_hidden,
        qkv,
        out_weight,
        attended,
        stats,
        cos,
        sin,
        starts,
        tokens,
        gain,
        gain_two_term,
    )


LINE_SEMS = 5


class LineGather:
    def __init__(self, p, src, out, send, recv, base, own=None):
        self.p, self.src, self.out = p, src, out
        self.send, self.recv, self.base = send, recv, base * LINE_SEMS
        self.z = p["dp"]
        self.inward = 1 - 2 * lax.div(self.z, 2)
        self.end = (self.z == 0) | (self.z == 3)
        self.own = None if own is None else pltpu.make_async_copy(src, out.at[self.z], own)

    def copy(self, src, owner, i, to):
        return pltpu.make_async_remote_copy(
            src_ref=src,
            dst_ref=self.out.at[owner],
            send_sem=self.send.at[self.base + i],
            recv_sem=self.recv.at[self.base + owner],
            device_id=(to, self.p["me"]),
            device_id_type=MESH,
        )

    def arrived(self, owner):
        self.copy(self.src, owner, 0, self.z).wait_recv()

    def start(self):
        z, inward = self.z, self.inward
        if self.own is not None:
            self.own.start()
        self.copy(self.src, z, 0, z + inward).start()

        @pl.when(jnp.logical_not(self.end))
        def _():
            self.copy(self.src, z, 1, z - inward).start()

    def second(self):
        z, inward = self.z, self.inward

        @pl.when(jnp.logical_not(self.end))
        def _():
            outer, inner = z - inward, z + inward
            self.arrived(inner)
            self.copy(self.out.at[inner], inner, 2, outer).start()
            self.arrived(outer)
            self.copy(self.out.at[outer], outer, 3, inner).start()

    def third(self):
        z, inward = self.z, self.inward

        @pl.when(jnp.logical_not(self.end))
        def _():
            far = z + 2 * inward
            self.arrived(far)
            self.copy(self.out.at[far], far, 4, z - inward).start()

    def finish(self):
        z, inward = self.z, self.inward

        @pl.when(self.end)
        def _():
            for k in range(1, 4):
                self.arrived(z + k * inward)

        if self.own is not None:
            self.own.wait()
        self.copy(self.src, 0, 0, z).wait_send()

        @pl.when(jnp.logical_not(self.end))
        def _():
            for i in range(1, 5):
                self.copy(self.src, 0, i, z).wait_send()


CHUNKS = 4
EARLY = 3
OTHERS = ("dg", "ds", "xp", "yp", "xs", "ys", "sib")


def meet_all(p, devices):
    mine = p["dp"] * 8 + p["me"]
    barrier = pltpu.get_barrier_semaphore()

    def other(k):
        to = lax.rem(mine + k, devices)
        return dict(device_id=(lax.div(to, 8), lax.rem(to, 8)), device_id_type=MESH), to

    @pl.loop(1, devices)
    def _(k):
        pl.semaphore_signal(barrier, inc=1, **other(k)[0])

    return other, lambda: pl.semaphore_wait(barrier, devices - 1)


class Local:
    def __init__(self, sems):
        self.sems, self.used = sems, 0

    def take(self, count=1):
        self.used += count
        return self.used - count


class Produced:
    def __init__(self, p, produce, stage, kept, paired, send, recv):
        self.p, self.produce, self.stage = p, produce, stage
        self.kept, self.paired, self.send, self.recv = kept, paired, send, recv
        self.pairs = {}

    def ready(self, i):
        k = len(self.pairs)
        _, own, other = ORDER[k]
        rows = self.kept.shape[1]
        stage = self.stage.at[pl.ds(k % 2 * rows, rows)]
        if k >= 2:
            self.pairs[ORDER[k - 2][0]].wait_send()
        self.produce(other, stage)
        self.pairs[i] = remote(self.p, stage, self.paired.at[i], self.send, self.recv, i, "sib")
        self.pairs[i].start()
        self.produce(own, self.kept.at[i])
        self.pairs[i].wait_recv()

    def finish(self):
        for i, _, _ in ORDER[2:]:
            if i in self.pairs:
                self.pairs[i].wait_send()


def front_kernel(
    groups,
    own_cot,
    w_out,
    w_down,
    tokens,
    gains,
    w_query,
    w_key,
    w_value,
    w_gate,
    w_up,
    cos,
    sin,
    starts,
    hidden,
    gain_one,
    gain_two,
    rotated,
    attended,
    stats,
    normed_one,
    cot,
    normed_two,
    qkv,
    out_weight,
    units,
    down,
    gains_land,
    head_blocks,
    unit_blocks,
    x,
    w,
    wo,
    pre,
    mine,
    stage,
    kept,
    paired,
    far,
    final,
    send,
    recv,
    asend,
    arecv,
    csend,
    crecv,
    nsend,
    nrecv,
    gsend,
    grecv,
    esend,
    erecv,
    zsend,
    zrecv,
    local,
):
    p = plane()
    devices = groups * 8
    other, met = meet_all(p, devices)
    shards, rows, width = x.shape
    held = w_query.shape[0]
    pairs = width // 8 // PAIR
    piece = down.shape[2]
    me, z = p["me"], p["dp"]
    mine_index = z * 8 + me
    sems = Local(local)

    def move(src, dst, i):
        return pltpu.make_async_copy(src, dst, local.at[i])

    for s in range(shards):
        for pair in range(pairs):
            for i, weight in enumerate((w_query, w_key, w_value)):
                head = lambda k: ((2 * pair + k) * 8 + s) * HD
                base = (pair * 3 + i) * PAIR
                head_blocks[s, :, base : base + PAIR] = jnp.concatenate(
                    [weight[:, head(k) : head(k) + HD] for k in range(2)], axis=1
                )
    met()

    def gain_copy(k, sender):
        return pltpu.make_async_remote_copy(
            src_ref=gains,
            dst_ref=gains_land.at[sender],
            send_sem=gsend.at[k],
            recv_sem=grecv.at[sender],
            **other(k)[0],
        )

    @pl.loop(1, devices)
    def _(k):
        gain_copy(k, mine_index).start()

    gains_land[mine_index] = gains[...]
    held_at = pl.ds(pl.multiple_of(me * held, held), held)

    def exchange(block, out, i):
        copies = [
            remote(p, block(p[name]), out, esend, erecv, i * 7 + j, name)
            for j, name in enumerate(OTHERS)
        ]
        copies.append(move(block(me), out, sems.take()))
        for copy in copies:
            copy.start()
        return copies

    head_copies = exchange(lambda s: head_blocks.at[s], qkv.at[z, held_at], 0)
    wo_line = LineGather(p, w_out, out_weight, zsend, zrecv, 0, local.at[sems.take()])
    wo_line.start()

    for s in range(shards):
        for i, weight in enumerate((w_gate, w_up)):
            for j in range(CHUNKS):
                for pair in range(groups // 2):
                    unit = lambda k: ((2 * pair + k) * 8 + s) * CHUNKS * piece + j * piece
                    base = i * groups * piece + pair * 2 * piece
                    unit_blocks[s, j, :, base : base + 2 * piece] = jnp.concatenate(
                        [weight[:, unit(k) : unit(k) + piece] for k in range(2)], axis=1
                    )

    @pl.loop(1, devices)
    def _(k):
        gain_copy(k, lax.rem(mine_index + devices - k, devices)).wait()

    for out, base in ((gain_one, 0), (gain_two, held)):
        for k in range(0, devices, 2):
            out[:, k * held : (k + 2) * held] = jnp.concatenate(
                [gains_land[k + i, 0:1, base : base + held] for i in range(2)], axis=1
            )

    def norm_tokens(at):
        t = tokens[at, :].astype(f32)
        scale = lax.rsqrt(jnp.mean(t * t, axis=-1, keepdims=True) + norm_eps)
        mine[at, :] = (t * scale * gain_one[...]).astype(bf16)

    over_rows(rows, norm_tokens)
    for copy in head_copies:
        copy.wait()
    qkv_line = LineGather(p, qkv.at[z], qkv, zsend, zrecv, 1)
    qkv_line.start()
    n1_sent = gather_start(p, mine, x, asend, arecv, 0)
    n1_own = move(mine, x.at[me], sems.take())
    n1_own.start()
    n1_late = gather_forward(p, n1_sent, x, asend, arecv, 0, wo_line.second)
    qkv_line.second()
    unit_copies = exchange(lambda s: unit_blocks.at[s], units.at[:, z, held_at], 1)
    chunk_lines = [
        (
            LineGather(p, units.at[j, z], units.at[j], zsend, zrecv, 2 + 2 * j),
            LineGather(
                p,
                w_down.at[pl.ds(j * piece, piece)],
                down.at[j],
                zsend,
                zrecv,
                3 + 2 * j,
                local.at[sems.take()],
            ),
        )
        for j in range(EARLY)
    ]

    def serve(j, what):
        for line in chunk_lines[j]:
            getattr(line, what)()

    gather_wait(n1_sent, n1_late)
    n1_own.wait()
    qkv_line.third()
    wo_line.third()
    for copy in unit_copies:
        copy.wait()
    cot_sent = gather_start(p, own_cot, cot, csend, crecv, 0)
    cot_own = move(own_cot, cot.at[me], sems.take())
    cot_own.start()
    serve(0, "start")
    keep_normed = move(x, normed_one, sems.take())
    keep_normed.start()
    qkv_line.finish()
    load_w = move(qkv, w, sems.take())
    load_w.start()
    load_w.wait()

    @pl.loop(0, shards)
    def _(s):
        pre[s] = dot(x[s], w[...].reshape(width, w.shape[2])).reshape(pre.shape[1:])

    def attention(r):
        @pl.loop(0, pairs)
        def _(pair):
            attend_pair(
                pre,
                cos,
                sin,
                starts[r],
                rotated,
                attended,
                stats,
                r,
                pair,
            )

    attention(0)
    serve(0, "second")
    serve(1, "start")
    cot_late = gather_forward(p, cot_sent, cot, csend, crecv, 0)
    attention(1)
    serve(0, "third")
    wo_line.finish()
    load_wo = move(out_weight, wo, sems.take())
    load_wo.start()
    load_wo.wait()
    gather_wait(cot_sent, cot_late)
    cot_own.wait()

    def produce(name, out):
        s = p[name]
        terms = attended[s].reshape(rows, attended.shape[3])

        @pl.loop(0, width // 512)
        def _(n):
            at = pl.ds(pl.multiple_of(n * 512, 512), 512)
            out[:, at] = dot(terms, wo[:, :, at].reshape(terms.shape[1], 512)).astype(bf16)

    def meanwhile():
        serve(1, "second")
        serve(2, "start")

    source = Produced(p, produce, stage, kept, paired, send, recv)
    sends = scatter_plane(p, source, rows, kept, paired, far, final, send, recv, meanwhile)
    keep_normed.wait()

    def step(at):
        h = tokens[at, :].astype(f32) + total(kept, paired, final, at)
        hidden[at, :] = h
        scale = lax.rsqrt(jnp.mean(h * h, axis=-1, keepdims=True) + norm_eps)
        mine[at, :] = (h * scale * gain_two[...]).astype(bf16)

    over_rows(rows, step)
    n2_sent = gather_start(p, mine, normed_two, nsend, nrecv, 0)
    n2_own = move(mine, normed_two.at[me], sems.take())
    n2_own.start()
    serve(1, "third")
    serve(2, "second")
    n2_late = gather_forward(p, n2_sent, normed_two, nsend, nrecv, 0)
    serve(2, "third")
    gather_wait(n2_sent, n2_late)
    n2_own.wait()
    for j in range(EARLY):
        serve(j, "finish")
    sends.finish()


def front_plane(
    groups, tokens, cotangent, gains, w_query, w_key, w_value, w_out, w_gate, w_up, w_down, tables, collective_id
):
    cos, sin, starts = tables
    shards, batch, shard_len, _ = cos.shape
    rows, width = tokens.shape
    held, devices = w_query.shape[0], groups * shards
    mine = width // shards
    wide = 3 * mine
    pairs = mine // PAIR
    chunk = 2 * groups * w_down.shape[0] // CHUNKS
    piece = w_down.shape[0] // CHUNKS
    length = shards * shard_len
    sds = jax.ShapeDtypeStruct
    full = (shards, rows, width)
    scratch = [
        pltpu.VMEM((devices, 8, 2 * held), f32),
        pltpu.VMEM((shards, held, wide), bf16),
        pltpu.VMEM((shards, CHUNKS, held, chunk), bf16),
        pltpu.VMEM(full, bf16),
        pltpu.VMEM((groups, shards * held, wide), bf16),
        pltpu.VMEM((groups, held, width), bf16),
        pltpu.VMEM((shards, batch, shard_len, wide), f32),
        pltpu.VMEM((rows, width), bf16),
        pltpu.VMEM((2 * rows, width), bf16),
        *scatter_scratch(rows, width)[:6],
        *[DMA((GATHER_SEMS,))] * 6,
        *[DMA((devices,))] * 2,
        *[DMA((14,))] * 2,
        *[DMA((LINE_SEMS * (2 + 2 * EARLY),))] * 2,
        DMA((24,)),
    ]
    return pl.pallas_call(
        functools.partial(front_kernel, groups),
        out_shape=[
            sds((rows, width), f32),
            sds((1, width), f32),
            sds((1, width), f32),
            sds((shards, batch, shard_len, wide), bf16),
            sds((shards, batch, shard_len, mine), bf16),
            sds((batch, pairs, 2, length), f32),
            sds(full, bf16),
            sds(full, bf16),
            sds(full, bf16),
            sds((groups, shards * held, wide), bf16),
            sds((groups, held, width), bf16),
            sds((CHUNKS, groups, shards * held, chunk), bf16),
            sds((EARLY, groups, piece, width), bf16),
        ],
        in_specs=[ANY] * 3 + [VMEM] * 10,
        out_specs=[VMEM] * 6 + [ANY] * 7,
        scratch_shapes=scratch,
        compiler_params=pltpu.CompilerParams(
            collective_id=collective_id, has_side_effects=True, vmem_limit_bytes=62 * MIB
        ),
        cost_estimate=lasting(200),
    )(
        cotangent,
        w_out,
        w_down,
        tokens,
        jnp.broadcast_to(gains.reshape(1, -1).astype(f32), (8, 2 * held)),
        w_query,
        w_key,
        w_value,
        w_gate,
        w_up,
        cos,
        sin,
        starts,
    )


def layer(
    groups,
    shards,
    tokens,
    doc_ids,
    cotangent,
    norm1_gain,
    w_query,
    w_key,
    w_value,
    w_out,
    norm2_gain,
    w_gate,
    w_up,
    w_down,
):
    rows, shard_len, width = tokens.shape
    count = rows * shard_len
    held = w_query.shape[0]
    hidden_held = w_down.shape[0]
    hidden_here = groups * hidden_held
    whole_heads = held % HD == 0
    outer, inner = (groups, held) if whole_heads else (1, width // shards)
    pairs = width // shards // PAIR
    both = ("dp", "seq")
    fast = groups == 4 and shards == 8
    flat = lambda v: v.reshape(shards * count, v.shape[-1])
    split = lambda v: v.reshape(shards, count, v.shape[-1])

    gains = jnp.stack([norm1_gain, norm2_gain])
    own_tokens = tokens.reshape(count, width)
    own_cotangent = cotangent.reshape(count, width)
    inputs = own_tokens.astype(f32)
    cos, sin, starts = rope_tables(doc_ids, shards)
    starts = starts[:, None, :]
    by_row = lambda v: v.reshape(shards, rows, shard_len, v.shape[-1])

    if fast:
        (
            hidden,
            gain_one,
            gain_two,
            rotated,
            attended,
            stats,
            normed_one,
            cot,
            normed_two,
            qkv_weight,
            out_weight,
            unit_weight,
            down_weight,
        ) = front_plane(
            groups,
            own_tokens,
            own_cotangent,
            gains,
            w_query,
            w_key,
            w_value,
            w_out,
            w_gate,
            w_up,
            w_down,
            (cos, sin, starts),
            1,
        )
        (
            grad_hidden,
            gain_two_term,
            branch,
            out_terms,
            unit_sums,
            down_sums,
            unit_terms,
            down_terms,
            *_,
        ) = feed_plane(
            normed_two,
            cot,
            unit_weight,
            down_weight,
            w_down,
            own_cotangent,
            hidden,
            gain_two,
            2,
        )
    else:
        gains = lax.all_gather(gains, both, axis=1, tiled=True).astype(f32)
        gain_one, gain_two = gains[:1], gains[1:]

        def by_head(w):
            blocks = w.reshape(held, outer, shards, inner)
            return jnp.moveaxis(blocks, 2, 0).reshape(shards, held, pairs, PAIR)

        blocks = jnp.stack([w_gate, w_up]).reshape(2, held, groups, shards, hidden_held)
        units = jnp.transpose(blocks, (3, 1, 0, 2, 4)).reshape(shards, held, 2 * hidden_here)
        heads = jnp.stack([by_head(w) for w in (w_query, w_key, w_value)], axis=3)
        heads, units = exchange_plane([heads.reshape(shards, held, -1), units], shards, 1)
        spread = lambda w: lax.all_gather(w, "dp", axis=0, tiled=True)
        qkv_weight = spread(heads.reshape(shards * held, -1))
        unit_weight = spread(units.reshape(shards * held, -1))
        down_weight = spread(w_down)
        if whole_heads:
            out_weight = spread(w_out)
        else:
            whole = lax.all_gather(w_out, both, axis=0, tiled=True)
            out_weight = lax.dynamic_slice_in_dim(whole, lax.axis_index("seq") * inner, inner, 0)
        own_normed = (inputs * rms_scale(inputs) * gain_one).astype(bf16)
        normed_one, cot = [flat(v) for v in gather_plane([own_normed, own_cotangent], shards, 2)]
        pre = by_row(dot(normed_one, qkv_weight))
        rotated, attended, stats = attend(pre, cos, sin, starts)
        attended = flat(attended)
        hidden = inputs + reduce_plane(split(dot(attended, out_weight).astype(bf16)))
        normed_two = (hidden * rms_scale(hidden) * gain_two).astype(bf16)
        normed_two = flat(lax.all_gather(normed_two, "seq"))
        gate_weight, up_weight = unit_weight[:, :hidden_here], unit_weight[:, hidden_here:]
        gate_pre, up_pre = dot(normed_two, gate_weight), dot(normed_two, up_weight)
        sigmoid = jax.nn.sigmoid(gate_pre)
        silu = gate_pre * sigmoid
        activated = (silu * up_pre).astype(bf16)
        out_terms = split(dot(activated, down_weight).astype(bf16))
        grad_act = dot_t(cot, down_weight)
        grad_gate_pre = grad_act * up_pre * sigmoid * (1.0 + gate_pre * (1.0 - sigmoid))
        grad_up_pre = grad_act * silu
        grad_units = jnp.concatenate([grad_gate_pre, grad_up_pre], axis=-1).astype(bf16)
        middle_terms = split(dot_t(grad_units, unit_weight).astype(bf16))
        unit_sums = lax.psum_scatter(
            dot(normed_two.T, grad_units).astype(bf16), "dp", scatter_dimension=0, tiled=True
        )
        down_sums = lax.psum_scatter(
            dot(activated.T, cot).astype(bf16), "dp", scatter_dimension=0, tiled=True
        )
        back, gain_two_term = norm_back(
            hidden, rms_scale(hidden), gain_two, reduce_plane(middle_terms)
        )
        grad_hidden = own_cotangent.astype(f32) + back
        branch = lax.all_gather(grad_hidden.astype(bf16), "seq")

    if fast:
        (
            grad_tokens,
            out_tokens,
            grad_norms,
            grad_query,
            grad_key,
            grad_value,
            grad_out,
            grad_gate,
            grad_up,
            grad_down,
            *_,
        ) = tail_plane(
            groups,
            branch,
            normed_one,
            rotated,
            out_terms,
            unit_terms,
            down_terms,
            unit_sums,
            down_sums,
            hidden,
            grad_hidden,
            qkv_weight,
            out_weight,
            attended,
            stats,
            cos,
            sin,
            starts,
            own_tokens,
            gain_one,
            gain_two_term,
            3,
        )
        return (
            out_tokens.reshape(tokens.shape),
            grad_tokens.reshape(tokens.shape),
            grad_norms[0, :held],
            grad_query,
            grad_key,
            grad_value,
            grad_out,
            grad_norms[1, :held],
            grad_gate,
            grad_up,
            grad_down,
        )

    branch = flat(branch)
    out_w_terms = dot(attended.T, branch).astype(bf16)
    grad_attended = by_row(dot_t(branch, out_weight).astype(bf16))
    grad_pre = flat(attend_back(rotated, grad_attended, cos, sin, starts, stats))
    last_terms = split(dot_t(grad_pre, qkv_weight).astype(bf16))
    head_terms = dot(normed_one.T, grad_pre).astype(bf16)

    if whole_heads:
        grad_out = lax.psum_scatter(out_w_terms, "dp", scatter_dimension=0, tiled=True)
    else:
        placed = lax.dynamic_update_slice_in_dim(
            jnp.zeros((width, width), bf16), out_w_terms, lax.axis_index("seq") * inner, 0
        )
        grad_out = lax.psum_scatter(placed, both, scatter_dimension=0, tiled=True)
    back, gain_one_term = norm_back(inputs, rms_scale(inputs), gain_one, reduce_plane(last_terms))
    grad_tokens = (grad_hidden + back).astype(bf16)
    out_tokens = (hidden + reduce_plane(out_terms)).astype(bf16)
    head_sums = lax.psum_scatter(head_terms, "dp", scatter_dimension=0, tiled=True)
    heads_back, units_back = exchange_plane(
        [head_sums.reshape(shards, held, -1), unit_sums.reshape(shards, held, -1)], shards, 6
    )
    grad_norms = lax.psum_scatter(
        jnp.concatenate([gain_one_term, gain_two_term]), both, scatter_dimension=1, tiled=True
    )
    heads_back = heads_back.reshape(shards, held, pairs, 3, PAIR)
    units_back = units_back.reshape(shards, held, 2, groups, hidden_held)

    def head_grad(i):
        blocks = heads_back[:, :, :, i, :].reshape(shards, held, outer, inner)
        return jnp.moveaxis(blocks, 0, 2).reshape(held, width).astype(f32)

    def unit_grad(i):
        return jnp.transpose(units_back[:, :, i], (1, 2, 0, 3)).reshape(held, -1).astype(f32)

    return (
        out_tokens.reshape(tokens.shape),
        grad_tokens.reshape(tokens.shape),
        grad_norms[0],
        head_grad(0),
        head_grad(1),
        head_grad(2),
        grad_out.astype(f32),
        grad_norms[1],
        unit_grad(0),
        unit_grad(1),
        down_sums.astype(f32),
    )


def solution(mesh):
    both = ("dp", "seq")
    return jax.shard_map(
        functools.partial(layer, mesh.shape["dp"], mesh.shape["seq"]),
        mesh=mesh,
        in_specs=(
            P("dp", "seq", None),
            P("dp", None),
            P("dp", "seq", None),
            P(both),
            P(both, None),
            P(both, None),
            P(both, None),
            P(both, None),
            P(both),
            P(both, None),
            P(both, None),
            P(both, None),
        ),
        out_specs=(
            P("dp", "seq", None),
            P("dp", "seq", None),
            P(both),
            P(both, None),
            P(both, None),
            P(both, None),
            P(both, None),
            P(both),
            P(both, None),
            P(both, None),
            P(both, None),
        ),
        check_vma=False,
    )
```

```python
import functools
import types

import jax
import jax.numpy as jnp
from jax import lax
from jax.experimental import pallas as pl
from jax.experimental.pallas import tpu as pltpu
from jax.sharding import PartitionSpec as P

H = 32
HD = 64
PAIR = 2 * HD

rope_base = 130000.0
norm_eps = 1e-05

bf16 = jnp.bfloat16
f32 = jnp.float32
MESH = pl.DeviceIdType.MESH
ANY = pl.BlockSpec(memory_space=pl.ANY)
VMEM = pl.BlockSpec(memory_space=pltpu.VMEM)
DMA = pltpu.SemaphoreType.DMA
MIB = 1 << 20


def lasting(us):
    return pl.CostEstimate(flops=0, transcendentals=0, bytes_accessed=int(us * 3_500_000))


def plane():
    dp, s = lax.axis_index("dp"), lax.axis_index("seq")
    core, xb, yb = lax.rem(s, 2), lax.rem(lax.div(s, 2), 2), lax.div(s, 4)
    at = lambda y, x, c: y * 4 + x * 2 + c
    return dict(
        dp=dp,
        me=s,
        sib=at(yb, xb, 1 - core),
        xp=at(yb, 1 - xb, core),
        yp=at(1 - yb, xb, core),
        dg=at(1 - yb, 1 - xb, core),
        xs=at(yb, 1 - xb, 1 - core),
        ys=at(1 - yb, xb, 1 - core),
        ds=at(1 - yb, 1 - xb, 1 - core),
    )


def greet(p, names):
    barrier = pltpu.get_barrier_semaphore()
    for name in names:
        pl.semaphore_signal(barrier, inc=1, device_id=(p["dp"], p[name]), device_id_type=MESH)
    pl.semaphore_wait(barrier, len(names))


def remote(p, src, dst, send, recv, i, to):
    return pltpu.make_async_remote_copy(
        src_ref=src,
        dst_ref=dst,
        send_sem=send.at[i],
        recv_sem=recv.at[i],
        device_id=(p["dp"], p[to]),
        device_id_type=MESH,
    )


GATHER_SEMS = 25


def shard_of(out, owner):
    if len(out.shape) == 3:
        return out.at[owner]
    rows = out.shape[0] // 8
    return out.at[pl.ds(pl.multiple_of(owner * rows, rows), rows)]


def gather_copies(p, src, out, send, recv, base):
    quarter = src.shape[0] // 4
    part = lambda ref, k: ref.at[pl.ds(k * quarter, quarter)]
    mine = shard_of(out, p["me"])
    sent = {}
    for j in range(4):
        kx, ky = j, (j + 2) % 4
        sent["x", kx] = remote(p, part(src, kx), part(mine, kx), send, recv, base + kx, "xp")
        sent["y", ky] = remote(p, part(src, ky), part(mine, ky), send, recv, base + 4 + ky, "yp")
    sent["s"] = remote(p, src, mine, send, recv, base + 8, "sib")
    return sent


def gather_start(*args):
    sent = gather_copies(*args)
    for copy in sent.values():
        copy.start()
    return sent


def quarter_of(ref, k):
    rows = ref.shape[0] // 4
    return ref.at[pl.ds(k * rows, rows)]


def gather_pass(p, ref, send, recv, i, to):
    copy = remote(p, ref, ref, send, recv, i, to)
    copy.start()
    return copy


def gather_forward(p, sent, out, send, recv, base, halfway=None):
    part = lambda owner, k: quarter_of(shard_of(out, p[owner]), k)
    passed = []
    for j in range(4):
        kx, ky = j, (j + 2) % 4
        sent["x", kx].wait_recv()
        if j < 2:
            sent["far", kx] = gather_pass(p, part("xp", kx), send, recv, base + 9 + kx, "yp")
        passed.append(gather_pass(p, part("xp", kx), send, recv, base + 13 + kx, "sib"))
        sent["y", ky].wait_recv()
        if j < 2:
            sent["far", ky] = gather_pass(p, part("yp", ky), send, recv, base + 9 + ky, "xp")
        passed.append(gather_pass(p, part("yp", ky), send, recv, base + 17 + ky, "sib"))
        if j == 1 and halfway is not None:
            halfway()

    def last():
        for k in (0, 2, 1, 3):
            sent["far", k].wait_recv()
            passed.append(gather_pass(p, part("dg", k), send, recv, base + 21 + k, "sib"))

    return passed, last


def gather_wait(sent, late, halfway=None):
    passed, last = late
    last()
    if halfway is not None:
        halfway()
    sent["s"].wait_recv()
    for copy in passed:
        copy.wait_recv()
    for copy in list(sent.values()) + passed:
        copy.wait_send()


def gather_finish(p, sent, out, send, recv, base):
    gather_wait(sent, gather_forward(p, sent, out, send, recv, base))


def gather_kernel(count, *refs):
    sources, outs = refs[:count], refs[count : 2 * count]
    send, recv, local = refs[2 * count :]
    p = plane()
    greet(p, ("sib", "xp", "yp"))
    sent, kept = [], []
    for i in range(count):
        sent.append(gather_start(p, sources[i], outs[i], send, recv, i * GATHER_SEMS))
        kept.append(pltpu.make_async_copy(sources[i], outs[i].at[p["me"]], local.at[i]))
        kept[i].start()
    for i in range(count):
        gather_finish(p, sent[i], outs[i], send, recv, i * GATHER_SEMS)
    for copy in kept:
        copy.wait()


def gather_plane(arrays, shards, collective_id):
    if shards != 8:
        return [lax.all_gather(a, "seq") for a in arrays]
    count = len(arrays)
    return pl.pallas_call(
        functools.partial(gather_kernel, count),
        out_shape=[jax.ShapeDtypeStruct((8,) + a.shape, a.dtype) for a in arrays],
        in_specs=[ANY] * count,
        out_specs=[ANY] * count,
        scratch_shapes=[DMA((GATHER_SEMS * count,)), DMA((GATHER_SEMS * count,)), DMA((count,))],
        compiler_params=pltpu.CompilerParams(collective_id=collective_id, has_side_effects=True),
        cost_estimate=lasting(40 * count),
    )(*arrays)


def exchange_kernel(count, *refs):
    sources, outs = refs[:count], refs[count : 2 * count]
    send, recv, local = refs[2 * count :]
    p = plane()
    names = ("dg", "ds", "xp", "yp", "xs", "ys", "sib")
    greet(p, names)
    copies = []
    for i in range(count):
        for j, name in enumerate(names):
            copies.append(
                remote(
                    p, sources[i].at[p[name]], outs[i].at[p["me"]], send, recv, i * 7 + j, name
                )
            )
            copies[-1].start()
        copies.append(
            pltpu.make_async_copy(sources[i].at[p["me"]], outs[i].at[p["me"]], local.at[i])
        )
        copies[-1].start()
    for copy in copies:
        copy.wait()


def exchange_plane(arrays, shards, collective_id):
    if shards != 8:
        return [lax.all_to_all(a, "seq", split_axis=0, concat_axis=0) for a in arrays]
    count = len(arrays)
    return pl.pallas_call(
        functools.partial(exchange_kernel, count),
        out_shape=[jax.ShapeDtypeStruct(a.shape, a.dtype) for a in arrays],
        in_specs=[ANY] * count,
        out_specs=[ANY] * count,
        scratch_shapes=[DMA((7 * count,)), DMA((7 * count,)), DMA((count,))],
        compiler_params=pltpu.CompilerParams(collective_id=collective_id, has_side_effects=True),
        cost_estimate=lasting(35),
    )(*arrays)


BLOCK = 16


def over_rows(rows, step):
    @pl.loop(0, rows // BLOCK)
    def _(i):
        step(pl.ds(pl.multiple_of(i * BLOCK, BLOCK), BLOCK))


def scatter_scratch(rows, width):
    return [
        pltpu.VMEM((4, rows, width), bf16),
        pltpu.VMEM((4, rows, width), bf16),
        pltpu.VMEM((2, rows // 2, width), bf16),
        pltpu.VMEM((2, rows, width), bf16),
        DMA((12,)),
        DMA((12,)),
        DMA((4,)),
    ]


class FromMemory:
    def __init__(self, p, terms, kept, paired, send, recv, local):
        self.loads, self.pairs = {}, {}
        for i, own, other in ORDER:
            self.loads[i] = pltpu.make_async_copy(terms.at[p[own]], kept.at[i], local.at[i])
            self.loads[i].start()
            self.pairs[i] = remote(p, terms.at[p[other]], paired.at[i], send, recv, i, "sib")
            self.pairs[i].start()

    def ready(self, i):
        self.loads[i].wait()
        self.pairs[i].wait_recv()

    def finish(self):
        for copy in self.pairs.values():
            copy.wait_send()


ORDER = ((3, "dg", "ds"), (1, "xp", "xs"), (2, "yp", "ys"), (0, "me", "sib"))


class PlaneSum:
    def __init__(self, p, source, rows, kept, paired, far, final, send, recv):
        self.p, self.source, self.rows = p, source, rows
        self.kept, self.paired, self.far, self.final = kept, paired, far, final
        self.send, self.recv = send, recv
        self.half = rows // 2
        self.low, self.high = pl.ds(0, self.half), pl.ds(self.half, self.half)
        self.sends, self.near = [], []

    def add_pair(self, i):
        kept, paired = self.kept, self.paired
        self.source.ready(i)

        def step(at):
            kept[i, at, :] = (kept[i, at, :].astype(f32) + paired[i, at, :].astype(f32)).astype(
                bf16
            )

        over_rows(self.rows, step)

    def put(self, src, dst, i, to):
        copy = remote(self.p, src, dst, self.send, self.recv, i, to)
        copy.start()
        self.sends.append(copy)
        return copy

    def first(self):
        kept, far, final, low, high = self.kept, self.far, self.final, self.low, self.high
        self.add_pair(3)
        self.far_x = self.put(kept.at[3, low], far.at[0], 4, "xp")
        self.far_y = self.put(kept.at[3, high], far.at[1], 5, "yp")
        self.add_pair(1)
        self.near.append(self.put(kept.at[1, low], final.at[0, low], 6, "xp"))
        self.add_pair(2)
        self.near.append(self.put(kept.at[2, high], final.at[1, high], 7, "yp"))

    def second(self):
        kept, far, final, low, high = self.kept, self.far, self.final, self.low, self.high
        half = self.half
        self.far_x.wait_recv()

        def step_x(at):
            kept[2, at, :] = (kept[2, at, :].astype(f32) + far[0, at, :].astype(f32)).astype(bf16)

        over_rows(half, step_x)
        self.near.append(self.put(kept.at[2, low], final.at[1, low], 8, "yp"))
        self.far_y.wait_recv()

        def step_y(at):
            up = pl.ds(pl.multiple_of(at.start + half, BLOCK), BLOCK)
            kept[1, up, :] = (kept[1, up, :].astype(f32) + far[1, at, :].astype(f32)).astype(bf16)

        over_rows(half, step_y)
        self.near.append(self.put(kept.at[1, high], final.at[0, high], 9, "xp"))
        self.source.ready(0)

    def third(self):
        for copy in self.near:
            copy.wait_recv()

    def finish(self):
        self.source.finish()
        for copy in self.sends:
            copy.wait_send()


def scatter_plane(p, source, rows, kept, paired, far, final, send, recv, between, meanwhile):
    sums = PlaneSum(p, source, rows, kept, paired, far, final, send, recv)
    sums.first()
    between()
    sums.second()
    meanwhile()
    sums.third()
    return sums


def total(kept, paired, final, at):
    return (kept[0, at, :].astype(f32) + paired[0, at, :].astype(f32)) + (
        final[0, at, :].astype(f32) + final[1, at, :].astype(f32)
    )


def reduce_plane(terms):
    rows = terms.shape[1]
    return lax.psum_scatter(terms, "seq", scatter_dimension=0, tiled=False).astype(f32).reshape(
        rows, terms.shape[2]
    )


def rms_scale(values):
    return lax.rsqrt(jnp.mean(values * values, axis=-1, keepdims=True) + norm_eps)


def norm_back(values, scale, gain, grad):
    weighted = grad * gain
    inner = jnp.mean(weighted * values, axis=-1, keepdims=True)
    return (
        scale * weighted - values * (scale * scale * scale) * inner,
        jnp.sum(grad * values * scale, axis=0, keepdims=True),
    )


def swap_halves(v, first):
    width = v.shape[-1]
    return jnp.where(first, pltpu.roll(v, width - HD // 2, 1), pltpu.roll(v, HD // 2, 1))


def dot_t(a, b):
    return lax.dot_general(a, b, (((1,), (1,)), ((), ())), preferred_element_type=f32)


def dot(a, b):
    return jnp.dot(a, b, preferred_element_type=f32)


def dot_l(a, b):
    return lax.dot_general(a, b, (((0,), (0,)), ((), ())), preferred_element_type=f32)


def allowed_pairs(start, keys, queries, offset):
    key = lax.broadcasted_iota(jnp.int32, (keys, queries), 0)
    query = lax.broadcasted_iota(jnp.int32, (keys, queries), 1) + offset
    return (key >= start) & (key <= query)


def attend_pair(pre, cos, sin, starts, rotated, attended, stats, r, pair):
    shards, _, shard_len, _ = pre.shape
    length = shards * shard_len
    block = min(256, length)
    per = block // shard_len
    lanes = lambda i: pl.ds(pl.multiple_of((pair * 3 + i) * PAIR, PAIR), PAIR)
    first = lax.rem(lax.broadcasted_iota(jnp.int32, (length, PAIR), 1), HD) < HD // 2
    cos_all, sin_all = cos[:, r].reshape(length, PAIR), sin[:, r].reshape(length, PAIR)

    def rotate(i):
        v = pre[:, r, :, lanes(i)].reshape(length, PAIR)
        return (v * cos_all + swap_halves(v, first) * sin_all).astype(bf16)

    query, key = rotate(0), rotate(1)
    value = pre[:, r, :, lanes(2)].reshape(length, PAIR)
    value_t = value.T.astype(bf16)
    for i, v in enumerate((query, key, value.astype(bf16))):
        rotated[:, r, :, lanes(i)] = v.reshape(shards, shard_len, PAIR)
    left = lax.broadcasted_iota(jnp.int32, (block, PAIR), 1) < HD
    top = lax.broadcasted_iota(jnp.int32, (PAIR, block), 0) < HD
    scaled = query * jnp.asarray(0.125, bf16)
    here_lanes = pl.ds(pl.multiple_of(pair * PAIR, PAIR), PAIR)
    for i in range(length // block):
        keys = (i + 1) * block
        at = slice(i * block, (i + 1) * block)
        mask = allowed_pairs(starts[:, at], keys, block, i * block)
        here = scaled[at]
        results = []
        for h in range(2):
            own = jnp.where(left if h == 0 else ~left, here, jnp.zeros_like(here))
            scores = jnp.where(mask, dot_t(key[:keys], own), -1e30)
            peak = jnp.max(scores, axis=0, keepdims=True)
            shifted = jnp.exp(scores - peak)
            summed = jnp.sum(shifted, axis=0, keepdims=True)
            probs = (shifted * (1.0 / summed)).astype(bf16)
            results.append(dot(value_t[:, :keys], probs))
            stats[r, pair, h : h + 1, at] = peak + jnp.log(summed)
        merged = jnp.where(top, results[0], results[1]).T.astype(bf16)
        attended[i * per : (i + 1) * per, r, :, here_lanes] = merged.reshape(
            per, shard_len, PAIR
        )


def attend_kernel(pre, cos, sin, starts, rotated, attended, stats):
    attend_pair(pre, cos, sin, starts[0], rotated, attended, stats, 0, 0)


def attend(pre, cos, sin, starts):
    shards, rows, shard_len, width = pre.shape
    pairs = width // (3 * PAIR)
    length = shards * shard_len
    wide = pl.BlockSpec((shards, 1, shard_len, 3 * PAIR), lambda r, p: (0, r, 0, p))
    narrow = pl.BlockSpec((shards, 1, shard_len, PAIR), lambda r, p: (0, r, 0, p))
    table = pl.BlockSpec((shards, 1, shard_len, PAIR), lambda r, p: (0, r, 0, 0))
    return pl.pallas_call(
        attend_kernel,
        grid=(rows, pairs),
        out_shape=[
            jax.ShapeDtypeStruct(pre.shape, bf16),
            jax.ShapeDtypeStruct((shards, rows, shard_len, pairs * PAIR), bf16),
            jax.ShapeDtypeStruct((rows, pairs, 2, length), f32),
        ],
        in_specs=[wide, table, table, pl.BlockSpec((1, 1, length), lambda r, p: (r, 0, 0))],
        out_specs=[wide, narrow, pl.BlockSpec((1, 1, 2, length), lambda r, p: (r, p, 0, 0))],
        compiler_params=pltpu.CompilerParams(vmem_limit_bytes=48 * MIB),
        cost_estimate=pl.CostEstimate(
            flops=rows * pairs * 2 * length * length * 256 * 2,
            bytes_accessed=pre.size * 8,
            transcendentals=rows * pairs * length * length,
        ),
    )(pre, cos, sin, starts)


def attend_back_pair(rotated, grad, cos, sin, starts, stats, result, key_acc, value_acc, r, pair):
    shards, _, shard_len, _ = rotated.shape
    length = shards * shard_len
    block = min(256, length)
    per = block // shard_len
    lanes = lambda i: pl.ds(pl.multiple_of((pair * 3 + i) * PAIR, PAIR), PAIR)
    query, key, value = (rotated[:, r, :, lanes(i)].reshape(length, PAIR) for i in range(3))
    grad_all = grad[:, r, :, pl.ds(pl.multiple_of(pair * PAIR, PAIR), PAIR)].reshape(length, PAIR)
    key_t = key.astype(f32).T.astype(bf16)
    left = lax.broadcasted_iota(jnp.int32, (block, PAIR), 1) < HD
    top = lax.broadcasted_iota(jnp.int32, (PAIR, block), 0) < HD
    first = lax.rem(lax.broadcasted_iota(jnp.int32, (length, PAIR), 1), HD) < HD // 2
    key_acc[...] = jnp.zeros_like(key_acc)
    value_acc[...] = jnp.zeros_like(value_acc)

    for i in range(length // block):
        keys = (i + 1) * block
        at = slice(i * block, (i + 1) * block)
        here = slice(i * per, (i + 1) * per)
        mask = allowed_pairs(starts[:, at], keys, block, i * block)
        results = []
        for h in range(2):
            side = left if h == 0 else ~left
            own = jnp.where(side, query[at], jnp.zeros_like(query[at]))
            own_grad = jnp.where(side, grad_all[at], jnp.zeros_like(grad_all[at]))
            scores = dot_t(key[:keys], own * jnp.asarray(0.125, bf16))
            probs = jnp.exp(jnp.where(mask, scores - stats[r, pair, h : h + 1, at], -1e30))
            grad_probs = dot_t(value[:keys], own_grad)
            inner = jnp.sum(probs * grad_probs, axis=0, keepdims=True)
            grad_scores = (probs * (grad_probs - inner) * 0.125).astype(bf16)
            key_acc[:keys, :] += dot(grad_scores, own)
            value_acc[:keys, :] += dot(probs.astype(bf16), own_grad)
            results.append(dot(key_t[:, :keys], grad_scores))
        merged = jnp.where(top, results[0], results[1]).T
        cos_here, sin_here = cos[here, r].reshape(block, PAIR), sin[here, r].reshape(block, PAIR)
        turned = merged * cos_here - swap_halves(merged, first[:block]) * sin_here
        result[here, r, :, lanes(0)] = turned.astype(bf16).reshape(per, shard_len, PAIR)
    cos_all, sin_all = cos[:, r].reshape(length, PAIR), sin[:, r].reshape(length, PAIR)
    key_grad = key_acc[...]
    turned = key_grad * cos_all - swap_halves(key_grad, first) * sin_all
    result[:, r, :, lanes(1)] = turned.astype(bf16).reshape(shards, shard_len, PAIR)
    result[:, r, :, lanes(2)] = value_acc[...].astype(bf16).reshape(shards, shard_len, PAIR)


def attend_back_kernel(rotated, grad, cos, sin, starts, stats, result, key_acc, value_acc):
    attend_back_pair(
        rotated, grad, cos, sin, starts[0], stats, result, key_acc, value_acc, 0, 0
    )


def attend_back(rotated, grad, cos, sin, starts, stats):
    shards, rows, shard_len, width = rotated.shape
    pairs = width // (3 * PAIR)
    length = shards * shard_len
    wide = pl.BlockSpec((shards, 1, shard_len, 3 * PAIR), lambda r, p: (0, r, 0, p))
    narrow = pl.BlockSpec((shards, 1, shard_len, PAIR), lambda r, p: (0, r, 0, p))
    table = pl.BlockSpec((shards, 1, shard_len, PAIR), lambda r, p: (0, r, 0, 0))
    return pl.pallas_call(
        attend_back_kernel,
        grid=(rows, pairs),
        out_shape=jax.ShapeDtypeStruct(rotated.shape, bf16),
        in_specs=[
            wide,
            narrow,
            table,
            table,
            pl.BlockSpec((1, 1, length), lambda r, p: (r, 0, 0)),
            pl.BlockSpec((1, 1, 2, length), lambda r, p: (r, p, 0, 0)),
        ],
        out_specs=wide,
        scratch_shapes=[pltpu.VMEM((length, PAIR), f32), pltpu.VMEM((length, PAIR), f32)],
        compiler_params=pltpu.CompilerParams(vmem_limit_bytes=48 * MIB),
        cost_estimate=pl.CostEstimate(
            flops=rows * pairs * 5 * length * length * 256 * 2,
            bytes_accessed=rotated.size * 6,
            transcendentals=rows * pairs * length * length,
        ),
    )(rotated, grad, cos, sin, starts, stats)


def document_starts(doc_ids):
    places = lax.broadcasted_iota(jnp.int32, doc_ids.shape, 1)
    earlier = jnp.concatenate([doc_ids[:, :1], doc_ids[:, :-1]], axis=1)
    return lax.cummax(jnp.where(doc_ids != earlier, places, 0), axis=1)


def rope_frequency():
    return rope_base ** (-(jnp.arange(HD // 2, dtype=f32) * 2.0 / HD))


def rope_tables(starts, shards):
    rows, length = starts.shape
    positions = (lax.broadcasted_iota(jnp.int32, starts.shape, 1) - starts).astype(f32)
    angles = positions[..., None] * rope_frequency()
    cos, sin = jnp.cos(angles), jnp.sin(angles)
    lay = lambda v: jnp.moveaxis(
        jnp.concatenate(v, axis=-1).reshape(rows, shards, length // shards, PAIR), 0, 1
    )
    return lay([cos] * 4), lay([-sin, sin, -sin, sin])


class LineSum:
    def __init__(self, p, view, land, send, recv, base):
        self.p, self.view, self.land = p, view, land
        self.send, self.recv, self.base = send, recv, base
        self.z = p["dp"]
        self.inward = 1 - 2 * lax.div(self.z, 2)
        self.end = (self.z == 0) | (self.z == 3)

    def copy(self, src, slot, i, to):
        return pltpu.make_async_remote_copy(
            src_ref=src,
            dst_ref=self.land.at[slot],
            send_sem=self.send.at[self.base + i],
            recv_sem=self.recv.at[self.base + slot],
            device_id=(to, self.p["me"]),
            device_id_type=MESH,
        )

    def arrived(self, slot):
        self.copy(self.land.at[slot], slot, 0, self.z).wait_recv()

    def first(self):
        z, inward = self.z, self.inward

        @pl.when(self.end)
        def _():
            near, mid, far = z + inward, z + 2 * inward, z + 3 * inward
            self.copy(self.view(far), near, 0, near).start()
            self.copy(self.view(mid), far, 1, near).start()
            self.copy(self.view(near), z, 2, near).start()

    def second(self, acc, extra, local, i):
        z, inward = self.z, self.inward

        @pl.when(jnp.logical_not(self.end))
        def _():
            outer, inner, far = z - inward, z + inward, z + 2 * inward
            own = [
                pltpu.make_async_copy(self.view(to), acc.at[k], local.at[i + k])
                for k, to in enumerate((far, inner))
            ]
            other = [
                pltpu.make_async_copy(self.land.at[slot], extra.at[k], local.at[i + 2 + k])
                for k, slot in enumerate((z, far))
            ]
            for copy in own:
                copy.start()
            for k, slot in enumerate((z, far)):
                self.arrived(slot)
                other[k].start()
            for k, to in enumerate((far, inner)):
                own[k].wait()
                other[k].wait()

                def step(at):
                    acc[k, at, :] = (acc[k, at, :].astype(f32) + extra[k, at, :].astype(f32)).astype(
                        bf16
                    )

                over_rows(acc.shape[1], step)
                self.copy(acc.at[k], z, k, to).start()
            self.copy(self.view(outer), z, 2, outer).start()

    def total(self, parts, local, i):
        z, inward = self.z, self.inward
        one = jnp.where(self.end, z + 2 * inward, z - inward)
        two = z + inward
        loads = [pltpu.make_async_copy(self.view(z), parts.at[0], local.at[i])]
        loads[0].start()
        for k, slot in ((1, one), (2, two)):
            self.arrived(slot)
            loads.append(pltpu.make_async_copy(self.land.at[slot], parts.at[k], local.at[i + k]))
            loads[k].start()
        for load in loads:
            load.wait()

        def step(at):
            parts[0, at, :] = (
                (parts[0, at, :].astype(f32) + parts[1, at, :].astype(f32))
                + parts[2, at, :].astype(f32)
            ).astype(bf16)

        over_rows(parts.shape[1], step)

    def finish(self):
        for i in range(3):
            self.copy(self.land.at[0], 0, i, self.z).wait_send()


LINE_SEMS = 5


class LineGather:
    def __init__(self, p, src, out, send, recv, base, own=None):
        self.p, self.src, self.out = p, src, out
        self.send, self.recv, self.base = send, recv, base * LINE_SEMS
        self.z = p["dp"]
        self.inward = 1 - 2 * lax.div(self.z, 2)
        self.end = (self.z == 0) | (self.z == 3)
        self.own = None if own is None else pltpu.make_async_copy(src, out.at[self.z], own)

    def copy(self, src, owner, i, to):
        return pltpu.make_async_remote_copy(
            src_ref=src,
            dst_ref=self.out.at[owner],
            send_sem=self.send.at[self.base + i],
            recv_sem=self.recv.at[self.base + owner],
            device_id=(to, self.p["me"]),
            device_id_type=MESH,
        )

    def arrived(self, owner):
        self.copy(self.src, owner, 0, self.z).wait_recv()

    def start(self):
        z, inward = self.z, self.inward
        if self.own is not None:
            self.own.start()
        self.copy(self.src, z, 0, z + inward).start()

        @pl.when(jnp.logical_not(self.end))
        def _():
            self.copy(self.src, z, 1, z - inward).start()

    def second(self):
        z, inward = self.z, self.inward

        @pl.when(jnp.logical_not(self.end))
        def _():
            outer, inner = z - inward, z + inward
            self.arrived(inner)
            self.copy(self.out.at[inner], inner, 2, outer).start()
            self.arrived(outer)
            self.copy(self.out.at[outer], outer, 3, inner).start()

    def third(self):
        z, inward = self.z, self.inward

        @pl.when(jnp.logical_not(self.end))
        def _():
            far = z + 2 * inward
            self.arrived(far)
            self.copy(self.out.at[far], far, 4, z - inward).start()

    def finish(self):
        z, inward = self.z, self.inward

        @pl.when(self.end)
        def _():
            for k in range(1, 4):
                self.arrived(z + k * inward)

        if self.own is not None:
            self.own.wait()
        self.copy(self.src, 0, 0, z).wait_send()

        @pl.when(jnp.logical_not(self.end))
        def _():
            for i in range(1, 5):
                self.copy(self.src, 0, i, z).wait_send()


CHUNKS = 4
OTHERS = ("dg", "ds", "xp", "yp", "xs", "ys", "sib")


def meet_all(p, devices):
    mine = p["dp"] * 8 + p["me"]
    barrier = pltpu.get_barrier_semaphore()

    def other(k):
        to = lax.rem(mine + k, devices)
        return dict(device_id=(lax.div(to, 8), lax.rem(to, 8)), device_id_type=MESH), to

    @pl.loop(1, devices)
    def _(k):
        pl.semaphore_signal(barrier, inc=1, **other(k)[0])

    return other, lambda: pl.semaphore_wait(barrier, devices - 1)


class Local:
    def __init__(self, sems):
        self.sems, self.used, self.free = sems, 0, []

    def take(self, count=1):
        if count == 1 and self.free:
            return self.free.pop(0)
        self.used += count
        assert self.used <= self.sems.shape[0], self.used
        return self.used - count


class Produced:
    def __init__(self, p, produce, stage, kept, paired, send, recv):
        self.p, self.produce, self.stage = p, produce, stage
        self.kept, self.paired, self.send, self.recv = kept, paired, send, recv
        self.pairs = {}

    def ready(self, i):
        k = len(self.pairs)
        _, own, other = ORDER[k]
        rows = self.kept.shape[1]
        stage = self.stage.at[pl.ds(k % 2 * rows, rows)]
        if k >= 2:
            self.pairs[ORDER[k - 2][0]].wait_send()
        self.produce(other, stage)
        self.pairs[i] = remote(self.p, stage, self.paired.at[i], self.send, self.recv, i, "sib")
        self.pairs[i].start()
        self.produce(own, self.kept.at[i])
        self.pairs[i].wait_recv()

    def finish(self):
        for i, _, _ in ORDER[2:]:
            if i in self.pairs:
                self.pairs[i].wait_send()


MAIN_INPUTS = (
    "w_query",
    "w_key",
    "w_value",
    "w_gate",
    "w_up",
    "w_out",
    "w_down",
    "tokens",
    "own_cot",
    "gains",
    "starts",
    "frequency",
)
RESULTS = (
    "gain_sums",
    "grad_tokens",
    "out_tokens",
    "grad_query",
    "grad_key",
    "grad_value",
    "grad_out",
    "grad_gate",
    "grad_up",
    "grad_down",
)
HELD_IN_HBM = (
    "cos",
    "sin",
    "rotated",
    "attended",
    "normed_one",
    "cot",
    "branch",
    "qkv",
    "out_weight",
    "units",
    "down",
    "out_terms",
    "unit_sums",
    "unit_terms",
    "down_terms",
    "kept_units",
    "kept_acts",
    "head_terms",
    "wo_terms",
    "head_sums",
    "unit_land",
    "down_land",
    "head_land",
    "wo_land",
    "units_out",
    "heads_out",
)
SCATTER_NAMES = ("kept", "paired", "far", "final", "send", "recv")
GATHER_NAMES = tuple(k + way for k in "ac" for way in ("send", "recv"))
MAIN_OUTPUTS = RESULTS + HELD_IN_HBM
MAIN_SCRATCH = (
    "hidden",
    "grad_hidden",
    "gain_one",
    "gain_two",
    "gain_term",
    "stats",
    "gains_land",
    "gain_mine",
    "gain_sum_land",
    "x",
    "unit_acc",
    "down_acc",
    "mine",
    "stage",
    "kept",
    "paired",
    "far",
    "final",
    "send",
    "recv",
    "asend",
    "arecv",
    "csend",
    "crecv",
    "gsend",
    "grecv",
    "esend",
    "erecv",
    "zsend",
    "zrecv",
    "ssend",
    "srecv",
    "ready",
    "local",
)


def main_kernel(groups, *refs):
    r = types.SimpleNamespace(**dict(zip(MAIN_INPUTS + MAIN_OUTPUTS + MAIN_SCRATCH, refs)))
    p = plane()
    devices = groups * 8
    other, met = meet_all(p, devices)
    shards = 8
    rows, width = r.tokens.shape
    held = r.w_query.shape[0]
    batch, shard_len, wide = r.rotated.shape[1:]
    pairs = width // 8 // PAIR
    piece, chunk = r.down.shape[2], r.units.shape[3]
    part = chunk // 2
    me, z = p["me"], p["dp"]
    mine_index = z * 8 + me
    held_at = pl.ds(pl.multiple_of(me * held, held), held)
    sems = Local(r.local)
    x = r.x

    lent = {}

    def move(src, dst, i=None):
        place = sems.take() if i is None else i
        copy = pltpu.make_async_copy(src, dst, r.local.at[place])
        if i is None:
            lent[id(copy)] = (copy, place)
        return copy

    def start(*copies):
        for copy in copies:
            copy.start()
        return copies

    def wait(copies):
        for copy in copies:
            copy.wait()
        for copy in copies:
            if id(copy) in lent:
                sems.free.append(lent.pop(id(copy))[1])

    def shard_rows(s, count=1):
        return pl.ds(pl.multiple_of(s * rows, rows), count * rows)

    def line(src, out, i, own):
        sem = r.local.at[sems.take()] if own else None
        return LineGather(p, src, out, r.zsend, r.zrecv, i, sem)

    wo_line = line(r.w_out, r.out_weight, 0, True)
    qkv_line = line(r.qkv.at[z], r.qkv, 1, False)
    chunk_lines = [
        (
            line(r.units.at[j, z], r.units.at[j], 2 + 2 * j, False),
            line(r.w_down.at[pl.ds(j * piece, piece)], r.down.at[j], 3 + 2 * j, True),
        )
        for j in range(CHUNKS)
    ]

    def serve(j, what, *only):
        for k in only or (0, 1):
            getattr(chunk_lines[j][k], what)()

    def gain_copy(k, sender):
        return pltpu.make_async_remote_copy(
            src_ref=r.gains,
            dst_ref=r.gains_land.at[sender],
            send_sem=r.gsend.at[k],
            recv_sem=r.grecv.at[sender],
            **other(k)[0],
        )

    def exchange(block, out, i):
        copies = [
            remote(p, block(p[name]), out, r.esend, r.erecv, i * 7 + j, name)
            for j, name in enumerate(OTHERS)
        ]
        return start(*copies, move(block(me), out))

    def of_owner(ref, count):
        return lambda owner: ref.at[pl.ds(pl.multiple_of(owner * count, count), count)]

    def scatter(produce, between, meanwhile):
        source = Produced(p, produce, r.stage, r.kept, r.paired, r.send, r.recv)
        return scatter_plane(
            p, source, rows, r.kept, r.paired, r.far, r.final, r.send, r.recv, between, meanwhile
        )

    def before(
        w_query, w_key, w_value, w_gate, w_up, cos, sin, head_blocks, unit_blocks, w, wo, pre, rotated, attended
    ):
        head_loads = start(move(r.w_query, w_query), move(r.w_key, w_key), move(r.w_value, w_value))
        unit_loads = start(move(r.w_gate, w_gate), move(r.w_up, w_up))
        wait(head_loads)
        for s in range(shards):
            for pair in range(pairs):
                for i, weight in enumerate((w_query, w_key, w_value)):
                    head = lambda k: ((2 * pair + k) * 8 + s) * HD
                    base = (pair * 3 + i) * PAIR
                    head_blocks[s, :, base : base + PAIR] = jnp.concatenate(
                        [weight[:, head(k) : head(k) + HD] for k in range(2)], axis=1
                    )
        met()

        @pl.loop(1, devices)
        def _(k):
            gain_copy(k, mine_index).start()

        r.gains_land[mine_index] = r.gains[...]
        head_copies = exchange(lambda s: head_blocks.at[s], r.qkv.at[z, held_at], 0)
        wait(unit_loads)
        for s in range(shards):
            for i, weight in enumerate((w_gate, w_up)):
                for j in range(CHUNKS):
                    for pair in range(groups // 2):
                        unit = lambda k: ((2 * pair + k) * 8 + s) * CHUNKS * piece + j * piece
                        base = i * groups * piece + pair * 2 * piece
                        unit_blocks[s, j, :, base : base + 2 * piece] = jnp.concatenate(
                            [weight[:, unit(k) : unit(k) + piece] for k in range(2)], axis=1
                        )

        @pl.loop(1, devices)
        def _(k):
            gain_copy(k, lax.rem(mine_index + devices - k, devices)).wait()

        for out, base in ((r.gain_one, 0), (r.gain_two, held)):
            for k in range(0, devices, 2):
                out[:, k * held : (k + 2) * held] = jnp.concatenate(
                    [r.gains_land[k + i, 0:1, base : base + held] for i in range(2)], axis=1
                )

        def norm_tokens(at):
            t = r.tokens[at, :].astype(f32)
            scale = lax.rsqrt(jnp.mean(t * t, axis=-1, keepdims=True) + norm_eps)
            r.mine[at, :] = (t * scale * r.gain_one[...]).astype(bf16)

        over_rows(rows, norm_tokens)
        wait(head_copies)
        qkv_line.start()
        n1_sent = gather_start(p, r.mine, x, r.asend, r.arecv, 0)
        n1_own = start(move(r.mine, x.at[shard_rows(me)]))
        n1_late = gather_forward(p, n1_sent, x, r.asend, r.arecv, 0, qkv_line.second)
        qkv_line.third()
        serve(0, "start", 1)
        wo_line.start()
        unit_exchange = lambda j: exchange(
            lambda s: unit_blocks.at[s, j], r.units.at[j, z, held_at], 1 + j
        )
        unit_copies = [unit_exchange(0)]

        def halfway():
            for j in range(1, CHUNKS):
                unit_copies.append(unit_exchange(j))

        gather_wait(n1_sent, n1_late, halfway)
        wait(n1_own)
        wait(unit_copies[0])
        serve(0, "start", 0)
        keep_normed = start(
            *[move(x.at[shard_rows(s)], r.normed_one.at[s]) for s in range(shards)]
        )
        for row in range(batch):
            length = shards * shard_len
            since = jnp.broadcast_to(r.starts[row].astype(f32), (PAIR, length)).T
            place = lax.broadcasted_iota(jnp.int32, (length, PAIR), 0).astype(f32)
            angles = (place - since) * r.frequency[...]
            lane = lax.broadcasted_iota(jnp.int32, (length, PAIR), 1)
            sign = jnp.where(lax.rem(lane, HD) < HD // 2, -1.0, 1.0)
            cos[:, row] = jnp.cos(angles).reshape(shards, shard_len, PAIR)
            sin[:, row] = (sign * jnp.sin(angles)).reshape(shards, shard_len, PAIR)
        keep_tables = start(move(cos, r.cos), move(sin, r.sin))
        qkv_line.finish()
        load_w = start(move(r.qkv, w))
        serve(0, "second", 1)
        wo_line.second()
        wait(load_w)

        @pl.loop(0, shards, step=2)
        def _(s):
            here = dot(x[shard_rows(s, 2)], w[...].reshape(width, wide))
            pre[pl.ds(s, 2)] = here.reshape((2,) + pre.shape[1:])

        for copies in unit_copies[1:]:
            wait(copies)
        serve(0, "second", 0)
        serve(0, "third", 1)
        wo_line.third()
        serve(1, "start")
        cot_sent = gather_start(p, r.own_cot, r.cot, r.csend, r.crecv, 0)
        cot_own = start(move(r.own_cot, r.cot.at[me]))

        def attention(row):
            @pl.loop(0, pairs)
            def _(pair):
                attend_pair(
                    pre, cos, sin, r.starts[row], rotated, attended, r.stats, row, pair
                )

        attention(0)
        attention(1)
        cot_late = gather_forward(p, cot_sent, r.cot, r.csend, r.crecv, 0)
        serve(0, "third", 0)
        keep_heads = start(move(rotated, r.rotated), move(attended, r.attended))
        wo_line.finish()
        wait(keep_normed)
        wait(start(move(r.out_weight, wo)))

        def produce(name, out):
            terms = attended[p[name]].reshape(rows, attended.shape[3])

            @pl.loop(0, width // 512)
            def _(n):
                at = pl.ds(pl.multiple_of(n * 512, 512), 512)
                out[:, at] = dot(terms, wo[:, :, at].reshape(terms.shape[1], 512)).astype(bf16)

        def between():
            serve(1, "second")
            serve(2, "start")

        def meanwhile():
            gather_wait(cot_sent, cot_late)
            wait(cot_own)

        scatter(produce, between, meanwhile).finish()
        wait(keep_heads)
        wait(keep_tables)

    vm = lambda shape, dtype=bf16: pltpu.VMEM(shape, dtype)
    pl.run_scoped(
        before,
        *[vm(ref.shape) for ref in (r.w_query, r.w_key, r.w_value, r.w_gate, r.w_up)],
        *[vm(ref.shape, f32) for ref in (r.cos, r.sin)],
        vm((shards, held, wide)),
        vm((shards, CHUNKS, held, chunk)),
        vm(r.qkv.shape),
        vm(r.out_weight.shape),
        vm(r.rotated.shape, f32),
        vm(r.rotated.shape),
        vm(r.attended.shape),
    )

    def norm_hidden(at):
        h = r.tokens[at, :].astype(f32) + total(r.kept, r.paired, r.final, at)
        r.hidden[at, :] = h
        scale = lax.rsqrt(jnp.mean(h * h, axis=-1, keepdims=True) + norm_eps)
        r.mine[at, :] = (h * scale * r.gain_two[...]).astype(bf16)

    over_rows(rows, norm_hidden)
    n2_sent = gather_start(p, r.mine, x, r.asend, r.arecv, 0)
    n2_own = start(move(r.mine, x.at[shard_rows(me)]))
    serve(1, "third")
    serve(2, "second")
    serve(3, "start")

    span = r.unit_land.shape[2]
    sum_lines = [
        (
            LineSum(
                p, of_owner(r.unit_terms.at[j], span), r.unit_land.at[j], r.ssend, r.srecv, 8 * j
            ),
            LineSum(
                p,
                of_owner(r.down_terms.at[j], piece),
                r.down_land.at[j],
                r.ssend,
                r.srecv,
                8 * j + 4,
            ),
        )
        for j in range(CHUNKS)
    ]
    head_lines = [
        LineSum(
            p, of_owner(r.head_terms.at[k], span), r.head_land.at[k], r.ssend, r.srecv, 8 * CHUNKS + 4 * k
        )
        for k in range(pairs)
    ]
    wo_sum = LineSum(
        p, of_owner(r.wo_terms, held), r.wo_land, r.ssend, r.srecv, 8 * CHUNKS + 4 * pairs
    )

    chunk_sem, keep_sem, term_sem, kept_sem, act_sem, out_sem, z_sem = (
        sems.take(k) for k in (4, 2, 2, 2, 2, 2, 8)
    )

    def after(
        c,
        w,
        d,
        unit_stage,
        act_stage,
        unit_kept,
        act_kept,
        unit_grad,
        down_grad,
        unit_parts,
        down_parts,
    ):
        def chunk_loads(j):
            return (
                move(r.units.at[j], w.at[j % 2], chunk_sem + j % 2),
                move(r.down.at[j], d.at[j % 2], chunk_sem + 2 + j % 2),
            )

        def pass_on(j):
            sum_lines[j][0].second(r.unit_acc.at[j], unit_parts, r.local, z_sem)
            sum_lines[j][1].second(r.down_acc.at[j], down_parts, r.local, z_sem + 4)

        def keep(j, what):
            for copy in (
                move(unit_stage, r.kept_units.at[:, pl.ds(j * chunk, chunk)], keep_sem),
                move(act_stage, r.kept_acts.at[:, pl.ds(j * part, part)], keep_sem + 1),
            ):
                getattr(copy, what)()

        def work(j):
            slot = j % 2
            wait(chunk_loads(j))
            if j > 0:
                keep(j - 1, "wait")

            @pl.loop(0, shards, step=2)
            def _(s):
                both = shard_rows(s, 2)
                pre = dot(x[both], w[slot].reshape(width, chunk))
                grad_act = dot_t(c[both], d[slot].reshape(part, width))
                gate, up = pre[:, :part], pre[:, part:]
                sigmoid = 1.0 / (1.0 + jnp.exp(-gate))
                silu = gate * sigmoid
                act_stage[both] = (silu * up).astype(bf16)
                unit_stage[both, :part] = (
                    grad_act * up * sigmoid * (1.0 + gate * (1.0 - sigmoid))
                ).astype(bf16)
                unit_stage[both, part:] = (grad_act * silu).astype(bf16)

            keep(j, "start")

        def weigh_units(j):
            @pl.loop(0, width // 512)
            def _(n):
                at = pl.ds(pl.multiple_of(n * 512, 512), 512)
                unit_grad[at] = dot_l(x[:, at], unit_stage[...]).astype(bf16)

            wait(start(move(unit_grad, r.unit_terms.at[j], term_sem)))
            sum_lines[j][0].first()

        def weigh_down(j):
            @pl.loop(0, width // 512)
            def _(n):
                at = pl.ds(pl.multiple_of(n * 512, 512), 512)
                down_grad[:, at] = dot_l(act_stage[...], c[:, at]).astype(bf16)

            wait(start(move(down_grad, r.down_terms.at[j], term_sem + 1)))
            sum_lines[j][1].first()

        c_loads = start(*[move(r.cot.at[s], c.at[shard_rows(s)]) for s in range(shards)])
        serve(0, "finish")
        start(*chunk_loads(0))
        n2_late = gather_forward(p, n2_sent, x, r.asend, r.arecv, 0)
        gather_wait(n2_sent, n2_late)
        wait(n2_own)
        wait(c_loads)
        work(0)
        serve(2, "third")
        weigh_units(0)
        serve(3, "second")
        weigh_down(0)
        serve(1, "finish")
        start(*chunk_loads(1))
        work(1)
        weigh_down(1)
        serve(3, "third")
        weigh_units(1)
        serve(2, "finish")
        start(*chunk_loads(2))
        work(2)
        pass_on(0)
        weigh_units(2)
        weigh_down(2)
        serve(3, "finish")
        start(*chunk_loads(3))
        work(3)
        weigh_down(3)
        load_w = start(
            *[
                move(
                    r.units.at[j, k // 2, pl.ds(k % 2 * rows, rows)],
                    c.at[shard_rows(k), pl.ds(j * chunk, chunk)],
                )
                for j in range(CHUNKS)
                for k in range(shards)
            ]
        )
        keep(CHUNKS - 1, "wait")
        order = [name for _, own, partner in ORDER for name in (partner, own)]

        def load_kept(k):
            return move(
                r.kept_units.at[shard_rows(p[order[k]])],
                unit_kept.at[pl.ds(k % 2 * rows, rows)],
                kept_sem + k % 2,
            )

        load_kept(0).start()

        def produce(name, out):
            k = order.index(name)
            load_kept(k).wait()
            if k + 1 < len(order):
                load_kept(k + 1).start()
            if k == 0:
                wait(load_w)

            @pl.loop(0, width // 1024)
            def _(n):
                at = pl.ds(pl.multiple_of(n * 1024, 1024), 1024)
                out[:, at] = dot_t(unit_kept[k % 2 * rows : (k % 2 + 1) * rows], c[at]).astype(
                    bf16
                )

        def act_load(s):
            slot = lax.rem(s, 2)
            return move(r.kept_acts.at[shard_rows(s)], act_kept.at[slot], act_sem + slot)

        def out_store(s):
            slot = lax.rem(s, 2)
            return move(r.stage.at[shard_rows(slot)], r.out_terms.at[s], out_sem + slot)

        def out_of_units():
            load_d = start(
                *[
                    move(r.down.at[j, k], x.at[pl.ds(j * part + k * piece, piece)])
                    for j in range(CHUNKS)
                    for k in range(groups)
                ]
            )
            act_load(0).start()
            wait(load_d)

            @pl.loop(0, shards)
            def _(s):
                act_load(s).wait()

                @pl.when(s + 1 < shards)
                def _():
                    act_load(s + 1).start()

                @pl.when(s >= 2)
                def _():
                    out_store(s - 2).wait()

                slot = lax.rem(s, 2)
                acts = act_kept[slot]

                @pl.loop(0, width // 1024)
                def _(n):
                    at = pl.ds(pl.multiple_of(n * 1024, 1024), 1024)
                    r.stage[shard_rows(slot), at] = dot(acts, x[: acts.shape[1], at]).astype(bf16)

                out_store(s).start()

            out_store(shards - 2).wait()
            out_store(shards - 1).wait()
            pass_on(2)

        def last_weights():
            weigh_units(3)
            pass_on(1)

        sums = scatter(produce, lambda: None, last_weights)
        sums.source.finish()
        sums.source.pairs.clear()
        r.gain_term[...] = jnp.zeros_like(r.gain_term)

        def norm_back_rows(at):
            g = total(r.kept, r.paired, r.final, at)
            h = r.hidden[at, :]
            scale = lax.rsqrt(jnp.mean(h * h, axis=-1, keepdims=True) + norm_eps)
            weighted = g * r.gain_two[...]
            inner = jnp.mean(weighted * h, axis=-1, keepdims=True)
            back = scale * weighted - h * (scale * scale * scale * inner)
            out = r.own_cot[at, :].astype(f32) + back
            r.grad_hidden[at, :] = out
            r.mine[at, :] = out.astype(bf16)
            r.gain_term[...] += jnp.sum(g * h * scale, axis=0, keepdims=True)

        over_rows(rows, norm_back_rows)
        gather_start(p, r.mine, r.branch, r.asend, r.arecv, 0)
        out_of_units()
        sums.finish()

    pl.run_scoped(
        after,
        vm((shards * rows, width)),
        vm((2,) + r.units.shape[1:]),
        vm((2,) + r.down.shape[1:]),
        vm((shards * rows, chunk)),
        vm((shards * rows, part)),
        vm((2 * rows, CHUNKS * chunk)),
        vm((2, rows, CHUNKS * part)),
        vm((width, chunk)),
        vm((part, width)),
        vm((2, span, chunk)),
        vm((2, piece, width)),
    )

    b_own = start(move(r.mine, r.branch.at[me]))

    def end(
        rotated,
        attended,
        cos,
        sin,
        qkv,
        wo,
        grads,
        key_acc,
        value_acc,
        head_grad,
        wo_grad,
        units,
        heads,
        wide_out,
        row_out,
        narrow_out,
        gain_one_term,
        head_acc,
        wo_acc,
        parts,
        row_parts,
    ):
        loads = start(
            move(r.out_weight, wo),
            move(r.attended, attended),
            move(r.rotated, rotated),
            move(r.cos, cos),
            move(r.sin, sin),
            move(r.qkv, qkv),
        )
        narrow = parts.at[:, :, pl.ds(0, chunk)]

        def sum_up(j):
            sum_lines[j][0].total(narrow, r.local, z_sem)
            wait(start(move(parts.at[0, :, pl.ds(0, chunk)], r.unit_sums.at[j], z_sem)))
            copies = exchange(
                of_owner(r.unit_sums.at[j], held), r.units_out.at[j, me], 1 + j
            )
            sum_lines[j][1].total(row_parts, r.local, z_sem)
            row_out[...] = row_parts[0].astype(f32)
            wait(start(move(row_out, r.grad_down.at[pl.ds(j * piece, piece)], z_sem)))
            return copies

        def pass_on(j):
            sum_lines[j][0].second(
                r.unit_acc.at[j % 3], parts.at[1:3, :, pl.ds(0, chunk)], r.local, z_sem
            )
            sum_lines[j][1].second(r.down_acc.at[j % 3], row_parts.at[1:3], r.local, z_sem + 4)

        unit_copies = []
        b_sent = gather_copies(p, r.mine, r.branch, r.asend, r.arecv, 0)
        b_late = gather_forward(p, b_sent, r.branch, r.asend, r.arecv, 0)
        unit_copies += sum_up(0)
        gather_wait(b_sent, b_late)
        wait(b_own)
        wait(start(*[move(r.branch.at[s], x.at[shard_rows(s)]) for s in range(shards)]))
        out_sem_base = sems.take(4)
        out_source = FromMemory(
            p, r.out_terms, r.kept, r.paired, r.send, r.recv, r.local.at[pl.ds(out_sem_base, 4)]
        )
        out_sum = PlaneSum(
            p, out_source, rows, r.kept, r.paired, r.far, r.final, r.send, r.recv
        )
        wait(loads[:2])

        @pl.loop(0, shards, step=2)
        def _(s):
            grad = dot_t(x[shard_rows(s, 2)], wo[...].reshape(-1, width)).astype(bf16)
            grads[pl.ds(s, 2)] = grad.reshape((2,) + grads.shape[1:])

        out_sum.first()

        @pl.loop(0, width // 512)
        def _(n):
            at = pl.ds(pl.multiple_of(n * 512, 512), 512)
            acts = attended[...].reshape(shards * rows, -1)
            wo_grad[:, at] = dot_l(acts, x[:, at]).astype(bf16)

        wait(start(move(wo_grad, r.wo_terms)))
        wo_sum.first()
        n1_loads = start(*[move(r.normed_one.at[s], x.at[shard_rows(s)]) for s in range(shards)])
        wait(loads[2:])

        def attention(pair):
            @pl.loop(0, batch)
            def _(row):
                attend_back_pair(
                    rotated,
                    grads,
                    cos,
                    sin,
                    r.starts[row],
                    r.stats,
                    rotated,
                    key_acc,
                    value_acc,
                    row,
                    pair,
                )

        def weigh_heads(pair):
            lanes = slice(pair * 3 * PAIR, (pair + 1) * 3 * PAIR)

            @pl.loop(0, width // 512)
            def _(n):
                at = pl.ds(pl.multiple_of(n * 512, 512), 512)
                grad = rotated[:, :, :, lanes].reshape(shards * rows, 3 * PAIR)
                head_grad[at] = dot_l(x[:, at], grad).astype(bf16)

            wait(start(move(head_grad, r.head_terms.at[pair])))
            head_lines[pair].first()

        attention(0)
        wait(n1_loads)
        weigh_heads(0)
        out_sum.second()
        for one in sum_lines[0]:
            one.finish()
        pass_on(CHUNKS - 1)
        for pair in range(1, pairs):
            attention(pair)
            weigh_heads(pair)
        wo_sum.second(wo_acc, row_parts.at[1:3], r.local, z_sem)
        out_sum.third()

        def step_out(at):
            out = r.hidden[at, :] + total(r.kept, r.paired, r.final, at)
            r.mine[at, :] = out.astype(bf16)

        over_rows(rows, step_out)
        keep_tokens = [*start(move(r.mine, r.out_tokens))]
        out_sum.finish()
        for name in ("sib", "xp", "yp"):
            pl.semaphore_signal(r.ready, inc=1, device_id=(z, p[name]), device_id_type=MESH)
        pl.semaphore_wait(r.ready, 3)

        def produce(name, out):
            grad = rotated[p[name]].reshape(rows, wide)

            @pl.loop(0, groups)
            def _(n):
                at = pl.ds(pl.multiple_of(n * span, span), span)
                out[:, at] = dot_t(grad, qkv[n]).astype(bf16)

        def pass_heads(k):
            head_lines[k].second(
                head_acc.at[k], parts.at[1:3, :, pl.ds(0, 3 * PAIR)], r.local, z_sem
            )

        def meanwhile():
            unit_copies.extend(sum_up(1))
            unit_copies.extend(sum_up(2))
            unit_copies.extend(sum_up(3))

        pass_heads(0)
        sums = scatter(produce, lambda: pass_heads(1), meanwhile)
        gain_one_term[...] = jnp.zeros_like(gain_one_term)

        def norm_back_rows(at):
            g = total(r.kept, r.paired, r.final, at)
            t = r.tokens[at, :].astype(f32)
            scale = lax.rsqrt(jnp.mean(t * t, axis=-1, keepdims=True) + norm_eps)
            weighted = g * r.gain_one[...]
            inner = jnp.mean(weighted * t, axis=-1, keepdims=True)
            back = scale * weighted - t * (scale * scale * scale * inner)
            r.stage[at, :] = (r.grad_hidden[at, :] + back).astype(bf16)
            gain_one_term[...] += jnp.sum(g * t * scale, axis=0, keepdims=True)

        sums.source.finish()
        sums.source.pairs.clear()
        over_rows(rows, norm_back_rows)
        keep_tokens += start(move(r.stage.at[pl.ds(0, rows)], r.grad_tokens))
        r.gain_mine[...] = jnp.zeros_like(r.gain_mine)
        for k in range(devices):
            at = slice(k * held, (k + 1) * held)
            r.gain_mine[k, 0:1, :held] = gain_one_term[:, at]
            r.gain_mine[k, 1:2, :held] = r.gain_term[:, at]

        def gain_back(k):
            where, to = other(k)
            return pltpu.make_async_remote_copy(
                src_ref=r.gain_mine.at[to],
                dst_ref=r.gain_sum_land.at[k],
                send_sem=r.gsend.at[k],
                recv_sem=r.grecv.at[k],
                **where,
            )

        @pl.loop(1, devices)
        def _(k):
            gain_back(k).start()

        wo_sum.total(row_parts, r.local, z_sem)
        row_out[...] = row_parts[0].astype(f32)
        keep_wo = start(move(row_out, r.grad_out))

        def sum_heads(k):
            head_lines[k].total(parts.at[:, :, pl.ds(0, 3 * PAIR)], r.local, z_sem)
            wait(start(move(parts.at[0, :, pl.ds(0, 3 * PAIR)], r.head_sums.at[k], z_sem)))
            return exchange(
                of_owner(r.head_sums.at[k], held), r.heads_out.at[k, me], 1 + CHUNKS + k
            )

        head_copies = [sum_heads(0)]
        wait(unit_copies)
        wait(start(move(r.units_out, units)))
        stores = []
        for i, out in enumerate((r.grad_gate, r.grad_up)):
            if i == 1:
                head_copies += [sum_heads(k) for k in range(1, pairs)]
            for k in range(groups):
                if len(stores) >= 2:
                    stores[-2].wait()
                for s in range(shards):
                    for a in range(CHUNKS // 2):
                        base = (i * groups + k) * piece
                        tile = jnp.concatenate(
                            [units[2 * a + b, s, :, base : base + piece] for b in range(2)], axis=1
                        )
                        at = (s * 2 + a) * 2 * piece
                        wide_out[k % 2, :, at : at + 2 * piece] = tile.astype(f32)
                span_out = wide_out.shape[2]
                stores.append(move(wide_out.at[k % 2], out.at[:, pl.ds(k * span_out, span_out)]))
                stores[-1].start()
        r.gain_sum_land[0] = r.gain_mine[mine_index]

        @pl.loop(1, devices)
        def _(k):
            gain_back(k).wait()

        r.gain_sums[...] = jnp.sum(r.gain_sum_land[...], axis=0)
        for copies in head_copies:
            wait(copies)
        wait(start(move(r.heads_out, heads)))
        for i, out in enumerate((r.grad_query, r.grad_key, r.grad_value)):
            for k in range(groups):
                for s in range(0, shards, 2):
                    base = i * PAIR + k % 2 * HD
                    tile = jnp.concatenate(
                        [heads[k // 2, s + b, :, base : base + HD] for b in range(2)], axis=1
                    )
                    at = (k * shards + s) * HD
                    narrow_out[i, :, at : at + 2 * HD] = tile.astype(f32)
            stores.append(move(narrow_out.at[i], out))
            stores[-1].start()
        wait(stores[-5:])
        wait(keep_tokens)
        wait(keep_wo)
        for one in (*[one for pair in sum_lines[1:] for one in pair], wo_sum, *head_lines):
            one.finish()
        sums.finish()

    pl.run_scoped(
        end,
        vm(r.rotated.shape),
        vm(r.attended.shape),
        *[vm(ref.shape, f32) for ref in (r.cos, r.sin)],
        vm(r.qkv.shape),
        vm(r.out_weight.shape),
        vm(r.attended.shape),
        vm((shards * shard_len, PAIR), f32),
        vm((shards * shard_len, PAIR), f32),
        vm((width, 3 * PAIR)),
        vm(r.wo_terms.shape),
        vm(r.units_out.shape),
        vm(r.heads_out.shape),
        vm((2, held, width), f32),
        vm((piece, width), f32),
        vm((3, held, width), f32),
        vm((1, width), f32),
        vm((pairs, 2, span, 3 * PAIR)),
        vm((2, held, width)),
        vm((3, span, chunk)),
        vm((3, piece, width)),
    )


def main_plane(groups, shards, batch, tokens, cotangent, gains, weights, starts, collective_id):
    w_query, w_key, w_value, w_out, w_gate, w_up, w_down = weights
    shard_len = tokens.shape[0] // batch
    rows, width = tokens.shape
    held, devices = w_query.shape[0], groups * shards
    mine = width // shards
    wide = 3 * mine
    hidden_here = groups * w_down.shape[0]
    chunk = 2 * hidden_here // CHUNKS
    piece = w_down.shape[0] // CHUNKS
    span = width // groups
    pairs = mine // PAIR
    low = lambda *shape: jax.ShapeDtypeStruct(shape, bf16)
    full = lambda *shape: jax.ShapeDtypeStruct(shape, f32)
    outputs = dict(
        gain_sums=full(8, 128),
        grad_tokens=low(rows, width),
        out_tokens=low(rows, width),
        grad_query=full(held, width),
        grad_key=full(held, width),
        grad_value=full(held, width),
        grad_out=full(held, width),
        grad_gate=full(held, hidden_here * shards),
        grad_up=full(held, hidden_here * shards),
        grad_down=full(CHUNKS * piece, width),
        cos=full(shards, batch, shard_len, PAIR),
        sin=full(shards, batch, shard_len, PAIR),
        rotated=low(shards, batch, shard_len, wide),
        attended=low(shards, batch, shard_len, mine),
        normed_one=low(shards, rows, width),
        cot=low(shards, rows, width),
        branch=low(shards, rows, width),
        qkv=low(groups, span, wide),
        out_weight=low(groups, held, width),
        units=low(CHUNKS, groups, span, chunk),
        down=low(CHUNKS, groups, piece, width),
        out_terms=low(shards, rows, width),
        unit_sums=low(CHUNKS, span, chunk),
        unit_terms=low(CHUNKS, width, chunk),
        down_terms=low(CHUNKS, chunk // 2, width),
        kept_units=low(shards * rows, CHUNKS * chunk),
        kept_acts=low(shards * rows, hidden_here),
        head_terms=low(pairs, width, 3 * PAIR),
        wo_terms=low(groups * held, width),
        head_sums=low(pairs, span, 3 * PAIR),
        unit_land=low(CHUNKS, 4, span, chunk),
        down_land=low(CHUNKS, 4, piece, width),
        head_land=low(pairs, 4, span, 3 * PAIR),
        wo_land=low(4, held, width),
        units_out=low(CHUNKS, shards, held, chunk),
        heads_out=low(pairs, shards, held, 3 * PAIR),
    )
    assert tuple(outputs) == tuple(MAIN_OUTPUTS)
    scratch = dict(
        hidden=pltpu.VMEM((rows, width), f32),
        grad_hidden=pltpu.VMEM((rows, width), f32),
        gain_one=pltpu.VMEM((1, width), f32),
        gain_two=pltpu.VMEM((1, width), f32),
        gain_term=pltpu.VMEM((1, width), f32),
        stats=pltpu.VMEM((batch, pairs, 2, shards * shard_len), f32),
        gains_land=pltpu.VMEM((devices, 8, 2 * held), f32),
        gain_mine=pltpu.VMEM((devices, 8, 128), f32),
        gain_sum_land=pltpu.VMEM((devices, 8, 128), f32),
        x=pltpu.VMEM((shards * rows, width), bf16),
        unit_acc=pltpu.VMEM((CHUNKS - 1, 2, span, chunk), bf16),
        down_acc=pltpu.VMEM((CHUNKS - 1, 2, piece, width), bf16),
        mine=pltpu.VMEM((rows, width), bf16),
        stage=pltpu.VMEM((2 * rows, width), bf16),
    )
    for name, buffer in zip(SCATTER_NAMES, scatter_scratch(rows, width)):
        scratch[name] = buffer
    for name in GATHER_NAMES:
        scratch[name] = DMA((GATHER_SEMS,))
    exchanges, sums = 7 * (1 + CHUNKS + pairs), 8 * CHUNKS + 4 * pairs + 4
    for name, count in (
        ("gsend", devices),
        ("grecv", devices),
        ("esend", exchanges),
        ("erecv", exchanges),
        ("zsend", LINE_SEMS * (2 + 2 * CHUNKS)),
        ("zrecv", LINE_SEMS * (2 + 2 * CHUNKS)),
        ("ssend", sums),
        ("srecv", sums),
    ):
        scratch[name] = DMA((count,))
    scratch["ready"] = pltpu.SemaphoreType.REGULAR
    scratch["local"] = DMA((104,))
    assert tuple(scratch) == tuple(MAIN_SCRATCH)
    in_vmem = 1
    done = pl.pallas_call(
        functools.partial(main_kernel, groups),
        out_shape=list(outputs.values()),
        in_specs=[ANY] * 7 + [VMEM] * 5,
        out_specs=[VMEM] * in_vmem + [ANY] * (len(outputs) - in_vmem),
        scratch_shapes=list(scratch.values()),
        compiler_params=pltpu.CompilerParams(
            collective_id=collective_id, has_side_effects=True, vmem_limit_bytes=63 * MIB
        ),
        cost_estimate=lasting(500),
    )(
        w_query,
        w_key,
        w_value,
        w_gate,
        w_up,
        w_out,
        w_down,
        tokens,
        cotangent,
        jnp.broadcast_to(gains.reshape(1, -1).astype(f32), (8, 2 * held)),
        starts,
        jnp.tile(rope_frequency(), 2 * PAIR // HD)[None],
    )
    count = len(RESULTS) - 1
    shapes = list(outputs.values())[1 : 1 + count]
    results = pl.pallas_call(
        hand_over,
        out_shape=shapes,
        in_specs=[ANY] * count,
        out_specs=[ANY] * count,
        scratch_shapes=[*[pltpu.VMEM(s.shape, s.dtype) for s in shapes], DMA((2, count))],
        compiler_params=pltpu.CompilerParams(vmem_limit_bytes=63 * MIB),
    )(*done[1 : 1 + count])
    return types.SimpleNamespace(**dict(zip(RESULTS, [done[0], *results])))


def hand_over(*refs):
    count = (len(refs) - 1) // 3
    ways = [
        [
            pltpu.make_async_copy(refs[way * 2 * count + i], refs[(2 - way) * count + i], refs[-1].at[way, i])
            for i in range(count)
        ]
        for way in range(2)
    ]
    for copy in ways[0]:
        copy.start()
    for copy, out in zip(*ways):
        copy.wait()
        out.start()
    for copy in ways[1]:
        copy.wait()


def layer(
    groups,
    shards,
    tokens,
    doc_ids,
    cotangent,
    norm1_gain,
    w_query,
    w_key,
    w_value,
    w_out,
    norm2_gain,
    w_gate,
    w_up,
    w_down,
):
    rows, shard_len, width = tokens.shape
    count = rows * shard_len
    held = w_query.shape[0]
    hidden_held = w_down.shape[0]
    hidden_here = groups * hidden_held
    whole_heads = held % HD == 0
    outer, inner = (groups, held) if whole_heads else (1, width // shards)
    pairs = width // shards // PAIR
    both = ("dp", "seq")
    fast = groups == 4 and shards == 8
    flat = lambda v: v.reshape(shards * count, v.shape[-1])
    split = lambda v: v.reshape(shards, count, v.shape[-1])

    gains = jnp.stack([norm1_gain, norm2_gain])
    own_tokens = tokens.reshape(count, width)
    own_cotangent = cotangent.reshape(count, width)
    inputs = own_tokens.astype(f32)
    starts = document_starts(doc_ids)
    by_row = lambda v: v.reshape(shards, rows, shard_len, v.shape[-1])

    if fast:
        done = main_plane(
            groups,
            shards,
            rows,
            own_tokens,
            own_cotangent,
            gains,
            (w_query, w_key, w_value, w_out, w_gate, w_up, w_down),
            starts[:, None, :],
            1,
        )
        return (
            done.out_tokens.reshape(tokens.shape),
            done.grad_tokens.reshape(tokens.shape),
            done.gain_sums[0, :held],
            done.grad_query,
            done.grad_key,
            done.grad_value,
            done.grad_out,
            done.gain_sums[1, :held],
            done.grad_gate,
            done.grad_up,
            done.grad_down,
        )

    cos, sin = rope_tables(starts, shards)
    starts = starts[:, None, :]
    gains = lax.all_gather(gains, both, axis=1, tiled=True).astype(f32)
    gain_one, gain_two = gains[:1], gains[1:]

    def by_head(w):
        blocks = w.reshape(held, outer, shards, inner)
        return jnp.moveaxis(blocks, 2, 0).reshape(shards, held, pairs, PAIR)

    blocks = jnp.stack([w_gate, w_up]).reshape(2, held, groups, shards, hidden_held)
    units = jnp.transpose(blocks, (3, 1, 0, 2, 4)).reshape(shards, held, 2 * hidden_here)
    heads = jnp.stack([by_head(w) for w in (w_query, w_key, w_value)], axis=3)
    heads, units = exchange_plane([heads.reshape(shards, held, -1), units], shards, 1)
    spread = lambda w: lax.all_gather(w, "dp", axis=0, tiled=True)
    qkv_weight = spread(heads.reshape(shards * held, -1))
    unit_weight = spread(units.reshape(shards * held, -1))
    down_weight = spread(w_down)
    if whole_heads:
        out_weight = spread(w_out)
    else:
        whole = lax.all_gather(w_out, both, axis=0, tiled=True)
        out_weight = lax.dynamic_slice_in_dim(whole, lax.axis_index("seq") * inner, inner, 0)
    own_normed = (inputs * rms_scale(inputs) * gain_one).astype(bf16)
    normed_one, cot = [flat(v) for v in gather_plane([own_normed, own_cotangent], shards, 2)]
    pre = by_row(dot(normed_one, qkv_weight))
    rotated, attended, stats = attend(pre, cos, sin, starts)
    attended = flat(attended)
    hidden = inputs + reduce_plane(split(dot(attended, out_weight).astype(bf16)))
    normed_two = (hidden * rms_scale(hidden) * gain_two).astype(bf16)
    normed_two = flat(lax.all_gather(normed_two, "seq"))
    gate_weight, up_weight = unit_weight[:, :hidden_here], unit_weight[:, hidden_here:]
    gate_pre, up_pre = dot(normed_two, gate_weight), dot(normed_two, up_weight)
    sigmoid = jax.nn.sigmoid(gate_pre)
    silu = gate_pre * sigmoid
    activated = (silu * up_pre).astype(bf16)
    out_terms = split(dot(activated, down_weight).astype(bf16))
    grad_act = dot_t(cot, down_weight)
    grad_gate_pre = grad_act * up_pre * sigmoid * (1.0 + gate_pre * (1.0 - sigmoid))
    grad_up_pre = grad_act * silu
    grad_units = jnp.concatenate([grad_gate_pre, grad_up_pre], axis=-1).astype(bf16)
    middle_terms = split(dot_t(grad_units, unit_weight).astype(bf16))
    unit_sums = lax.psum_scatter(
        dot(normed_two.T, grad_units).astype(bf16), "dp", scatter_dimension=0, tiled=True
    )
    down_sums = lax.psum_scatter(
        dot(activated.T, cot).astype(bf16), "dp", scatter_dimension=0, tiled=True
    )
    back, gain_two_term = norm_back(
        hidden, rms_scale(hidden), gain_two, reduce_plane(middle_terms)
    )
    grad_hidden = own_cotangent.astype(f32) + back
    branch = lax.all_gather(grad_hidden.astype(bf16), "seq")

    branch = flat(branch)
    out_w_terms = dot(attended.T, branch).astype(bf16)
    grad_attended = by_row(dot_t(branch, out_weight).astype(bf16))
    grad_pre = flat(attend_back(rotated, grad_attended, cos, sin, starts, stats))
    last_terms = split(dot_t(grad_pre, qkv_weight).astype(bf16))
    head_terms = dot(normed_one.T, grad_pre).astype(bf16)

    if whole_heads:
        grad_out = lax.psum_scatter(out_w_terms, "dp", scatter_dimension=0, tiled=True)
    else:
        placed = lax.dynamic_update_slice_in_dim(
            jnp.zeros((width, width), bf16), out_w_terms, lax.axis_index("seq") * inner, 0
        )
        grad_out = lax.psum_scatter(placed, both, scatter_dimension=0, tiled=True)
    back, gain_one_term = norm_back(inputs, rms_scale(inputs), gain_one, reduce_plane(last_terms))
    grad_tokens = (grad_hidden + back).astype(bf16)
    out_tokens = (hidden + reduce_plane(out_terms)).astype(bf16)
    head_sums = lax.psum_scatter(head_terms, "dp", scatter_dimension=0, tiled=True)
    heads_back, units_back = exchange_plane(
        [head_sums.reshape(shards, held, -1), unit_sums.reshape(shards, held, -1)], shards, 6
    )
    grad_norms = lax.psum_scatter(
        jnp.concatenate([gain_one_term, gain_two_term]), both, scatter_dimension=1, tiled=True
    )
    heads_back = heads_back.reshape(shards, held, pairs, 3, PAIR)
    units_back = units_back.reshape(shards, held, 2, groups, hidden_held)

    def head_grad(i):
        blocks = heads_back[:, :, :, i, :].reshape(shards, held, outer, inner)
        return jnp.moveaxis(blocks, 0, 2).reshape(held, width).astype(f32)

    def unit_grad(i):
        return jnp.transpose(units_back[:, :, i], (1, 2, 0, 3)).reshape(held, -1).astype(f32)

    return (
        out_tokens.reshape(tokens.shape),
        grad_tokens.reshape(tokens.shape),
        grad_norms[0],
        head_grad(0),
        head_grad(1),
        head_grad(2),
        grad_out.astype(f32),
        grad_norms[1],
        unit_grad(0),
        unit_grad(1),
        down_sums.astype(f32),
    )


def solution(mesh):
    both = ("dp", "seq")
    return jax.shard_map(
        functools.partial(layer, mesh.shape["dp"], mesh.shape["seq"]),
        mesh=mesh,
        in_specs=(
            P("dp", "seq", None),
            P("dp", None),
            P("dp", "seq", None),
            P(both),
            P(both, None),
            P(both, None),
            P(both, None),
            P(both, None),
            P(both),
            P(both, None),
            P(both, None),
            P(both, None),
        ),
        out_specs=(
            P("dp", "seq", None),
            P("dp", "seq", None),
            P(both),
            P(both, None),
            P(both, None),
            P(both, None),
            P(both, None),
            P(both),
            P(both, None),
            P(both, None),
            P(both, None),
        ),
        check_vma=False,
    )
```

```python
import functools
import types

import jax
import jax.numpy as jnp
from jax import lax
from jax.experimental import pallas as pl
from jax.experimental.pallas import tpu as pltpu
from jax.sharding import PartitionSpec as P

H = 32
HD = 64
PAIR = 2 * HD

rope_base = 130000.0
norm_eps = 1e-05

bf16 = jnp.bfloat16
f32 = jnp.float32
MESH = pl.DeviceIdType.MESH
ANY = pl.BlockSpec(memory_space=pl.ANY)
VMEM = pl.BlockSpec(memory_space=pltpu.VMEM)
DMA = pltpu.SemaphoreType.DMA
MIB = 1 << 20


def lasting(us):
    return pl.CostEstimate(flops=0, transcendentals=0, bytes_accessed=int(us * 3_500_000))


def plane():
    dp, s = lax.axis_index("dp"), lax.axis_index("seq")
    core, xb, yb = lax.rem(s, 2), lax.rem(lax.div(s, 2), 2), lax.div(s, 4)
    at = lambda y, x, c: y * 4 + x * 2 + c
    return dict(
        dp=dp,
        me=s,
        sib=at(yb, xb, 1 - core),
        xp=at(yb, 1 - xb, core),
        yp=at(1 - yb, xb, core),
        dg=at(1 - yb, 1 - xb, core),
        xs=at(yb, 1 - xb, 1 - core),
        ys=at(1 - yb, xb, 1 - core),
        ds=at(1 - yb, 1 - xb, 1 - core),
    )


def greet(p, names):
    barrier = pltpu.get_barrier_semaphore()
    for name in names:
        pl.semaphore_signal(barrier, inc=1, device_id=(p["dp"], p[name]), device_id_type=MESH)
    pl.semaphore_wait(barrier, len(names))


def remote(p, src, dst, send, recv, i, to):
    return pltpu.make_async_remote_copy(
        src_ref=src,
        dst_ref=dst,
        send_sem=send.at[i],
        recv_sem=recv.at[i],
        device_id=(p["dp"], p[to]),
        device_id_type=MESH,
    )


GATHER_SEMS = 25


def shard_of(out, owner):
    if len(out.shape) == 3:
        return out.at[owner]
    rows = out.shape[0] // 8
    return out.at[pl.ds(pl.multiple_of(owner * rows, rows), rows)]


def gather_copies(p, src, out, send, recv, base):
    quarter = src.shape[0] // 4
    part = lambda ref, k: ref.at[pl.ds(k * quarter, quarter)]
    mine = shard_of(out, p["me"])
    sent = {}
    for j in range(4):
        kx, ky = j, (j + 2) % 4
        sent["x", kx] = remote(p, part(src, kx), part(mine, kx), send, recv, base + kx, "xp")
        sent["y", ky] = remote(p, part(src, ky), part(mine, ky), send, recv, base + 4 + ky, "yp")
    sent["s"] = remote(p, src, mine, send, recv, base + 8, "sib")
    return sent


def gather_start(*args):
    sent = gather_copies(*args)
    for copy in sent.values():
        copy.start()
    return sent


def quarter_of(ref, k):
    rows = ref.shape[0] // 4
    return ref.at[pl.ds(k * rows, rows)]


def gather_pass(p, ref, send, recv, i, to):
    copy = remote(p, ref, ref, send, recv, i, to)
    copy.start()
    return copy


def gather_forward(p, sent, out, send, recv, base, halfway=None):
    part = lambda owner, k: quarter_of(shard_of(out, p[owner]), k)
    passed = []
    for j in range(4):
        kx, ky = j, (j + 2) % 4
        sent["x", kx].wait_recv()
        if j < 2:
            sent["far", kx] = gather_pass(p, part("xp", kx), send, recv, base + 9 + kx, "yp")
        passed.append(gather_pass(p, part("xp", kx), send, recv, base + 13 + kx, "sib"))
        sent["y", ky].wait_recv()
        if j < 2:
            sent["far", ky] = gather_pass(p, part("yp", ky), send, recv, base + 9 + ky, "xp")
        passed.append(gather_pass(p, part("yp", ky), send, recv, base + 17 + ky, "sib"))
        if j == 1 and halfway is not None:
            halfway()

    def last():
        for k in (0, 2, 1, 3):
            sent["far", k].wait_recv()
            passed.append(gather_pass(p, part("dg", k), send, recv, base + 21 + k, "sib"))

    return passed, last


def gather_wait(sent, late, halfway=None):
    passed, last = late
    last()
    if halfway is not None:
        halfway()
    sent["s"].wait_recv()
    for copy in passed:
        copy.wait_recv()
    for copy in list(sent.values()) + passed:
        copy.wait_send()


def gather_finish(p, sent, out, send, recv, base):
    gather_wait(sent, gather_forward(p, sent, out, send, recv, base))


def gather_kernel(count, *refs):
    sources, outs = refs[:count], refs[count : 2 * count]
    send, recv, local = refs[2 * count :]
    p = plane()
    greet(p, ("sib", "xp", "yp"))
    sent, kept = [], []
    for i in range(count):
        sent.append(gather_start(p, sources[i], outs[i], send, recv, i * GATHER_SEMS))
        kept.append(pltpu.make_async_copy(sources[i], outs[i].at[p["me"]], local.at[i]))
        kept[i].start()
    for i in range(count):
        gather_finish(p, sent[i], outs[i], send, recv, i * GATHER_SEMS)
    for copy in kept:
        copy.wait()


def gather_plane(arrays, shards, collective_id):
    if shards != 8:
        return [lax.all_gather(a, "seq") for a in arrays]
    count = len(arrays)
    return pl.pallas_call(
        functools.partial(gather_kernel, count),
        out_shape=[jax.ShapeDtypeStruct((8,) + a.shape, a.dtype) for a in arrays],
        in_specs=[ANY] * count,
        out_specs=[ANY] * count,
        scratch_shapes=[DMA((GATHER_SEMS * count,)), DMA((GATHER_SEMS * count,)), DMA((count,))],
        compiler_params=pltpu.CompilerParams(collective_id=collective_id, has_side_effects=True),
        cost_estimate=lasting(40 * count),
    )(*arrays)


def exchange_kernel(count, *refs):
    sources, outs = refs[:count], refs[count : 2 * count]
    send, recv, local = refs[2 * count :]
    p = plane()
    names = ("dg", "ds", "xp", "yp", "xs", "ys", "sib")
    greet(p, names)
    copies = []
    for i in range(count):
        for j, name in enumerate(names):
            copies.append(
                remote(
                    p, sources[i].at[p[name]], outs[i].at[p["me"]], send, recv, i * 7 + j, name
                )
            )
            copies[-1].start()
        copies.append(
            pltpu.make_async_copy(sources[i].at[p["me"]], outs[i].at[p["me"]], local.at[i])
        )
        copies[-1].start()
    for copy in copies:
        copy.wait()


def exchange_plane(arrays, shards, collective_id):
    if shards != 8:
        return [lax.all_to_all(a, "seq", split_axis=0, concat_axis=0) for a in arrays]
    count = len(arrays)
    return pl.pallas_call(
        functools.partial(exchange_kernel, count),
        out_shape=[jax.ShapeDtypeStruct(a.shape, a.dtype) for a in arrays],
        in_specs=[ANY] * count,
        out_specs=[ANY] * count,
        scratch_shapes=[DMA((7 * count,)), DMA((7 * count,)), DMA((count,))],
        compiler_params=pltpu.CompilerParams(collective_id=collective_id, has_side_effects=True),
        cost_estimate=lasting(35),
    )(*arrays)


BLOCK = 16


def over_rows(rows, step):
    @pl.loop(0, rows // BLOCK)
    def _(i):
        step(pl.ds(pl.multiple_of(i * BLOCK, BLOCK), BLOCK))


def scatter_scratch(rows, width):
    return [
        pltpu.VMEM((4, rows, width), bf16),
        pltpu.VMEM((4, rows, width), bf16),
        pltpu.VMEM((2, rows // 2, width), bf16),
        pltpu.VMEM((2, rows, width), bf16),
        DMA((12,)),
        DMA((12,)),
        DMA((4,)),
    ]


class FromMemory:
    def __init__(self, p, terms, kept, paired, send, recv, local):
        self.loads, self.pairs = {}, {}
        for i, own, other in ORDER:
            self.loads[i] = pltpu.make_async_copy(terms.at[p[own]], kept.at[i], local.at[i])
            self.loads[i].start()
            self.pairs[i] = remote(p, terms.at[p[other]], paired.at[i], send, recv, i, "sib")
            self.pairs[i].start()

    def ready(self, i):
        self.loads[i].wait()
        self.pairs[i].wait_recv()

    def finish(self):
        for copy in self.pairs.values():
            copy.wait_send()


ORDER = ((3, "dg", "ds"), (1, "xp", "xs"), (2, "yp", "ys"), (0, "me", "sib"))


class PlaneSum:
    def __init__(self, p, source, rows, kept, paired, far, final, send, recv):
        self.p, self.source, self.rows = p, source, rows
        self.kept, self.paired, self.far, self.final = kept, paired, far, final
        self.send, self.recv = send, recv
        self.half = rows // 2
        self.low, self.high = pl.ds(0, self.half), pl.ds(self.half, self.half)
        self.sends, self.near = [], []

    def add_pair(self, i):
        kept, paired = self.kept, self.paired
        self.source.ready(i)

        def step(at):
            kept[i, at, :] = (kept[i, at, :].astype(f32) + paired[i, at, :].astype(f32)).astype(
                bf16
            )

        over_rows(self.rows, step)

    def put(self, src, dst, i, to):
        copy = remote(self.p, src, dst, self.send, self.recv, i, to)
        copy.start()
        self.sends.append(copy)
        return copy

    def first(self):
        kept, far, final, low, high = self.kept, self.far, self.final, self.low, self.high
        self.add_pair(3)
        self.far_x = self.put(kept.at[3, low], far.at[0], 4, "xp")
        self.far_y = self.put(kept.at[3, high], far.at[1], 5, "yp")
        self.add_pair(1)
        self.near.append(self.put(kept.at[1, low], final.at[0, low], 6, "xp"))
        self.add_pair(2)
        self.near.append(self.put(kept.at[2, high], final.at[1, high], 7, "yp"))

    def second(self):
        kept, far, final, low, high = self.kept, self.far, self.final, self.low, self.high
        half = self.half
        self.far_x.wait_recv()

        def step_x(at):
            kept[2, at, :] = (kept[2, at, :].astype(f32) + far[0, at, :].astype(f32)).astype(bf16)

        over_rows(half, step_x)
        self.near.append(self.put(kept.at[2, low], final.at[1, low], 8, "yp"))
        self.far_y.wait_recv()

        def step_y(at):
            up = pl.ds(pl.multiple_of(at.start + half, BLOCK), BLOCK)
            kept[1, up, :] = (kept[1, up, :].astype(f32) + far[1, at, :].astype(f32)).astype(bf16)

        over_rows(half, step_y)
        self.near.append(self.put(kept.at[1, high], final.at[0, high], 9, "xp"))
        self.source.ready(0)

    def third(self):
        for copy in self.near:
            copy.wait_recv()

    def finish(self):
        self.source.finish()
        for copy in self.sends:
            copy.wait_send()


def scatter_plane(p, source, rows, kept, paired, far, final, send, recv, between, meanwhile):
    sums = PlaneSum(p, source, rows, kept, paired, far, final, send, recv)
    sums.first()
    between()
    sums.second()
    meanwhile()
    sums.third()
    return sums


def total(kept, paired, final, at):
    return (kept[0, at, :].astype(f32) + paired[0, at, :].astype(f32)) + (
        final[0, at, :].astype(f32) + final[1, at, :].astype(f32)
    )


def reduce_plane(terms):
    rows = terms.shape[1]
    return lax.psum_scatter(terms, "seq", scatter_dimension=0, tiled=False).astype(f32).reshape(
        rows, terms.shape[2]
    )


def rms_scale(values):
    return lax.rsqrt(jnp.mean(values * values, axis=-1, keepdims=True) + norm_eps)


def norm_back(values, scale, gain, grad):
    weighted = grad * gain
    inner = jnp.mean(weighted * values, axis=-1, keepdims=True)
    return (
        scale * weighted - values * (scale * scale * scale) * inner,
        jnp.sum(grad * values * scale, axis=0, keepdims=True),
    )


def swap_halves(v, first):
    width = v.shape[-1]
    return jnp.where(first, pltpu.roll(v, width - HD // 2, 1), pltpu.roll(v, HD // 2, 1))


def dot_t(a, b):
    return lax.dot_general(a, b, (((1,), (1,)), ((), ())), preferred_element_type=f32)


def dot(a, b):
    return jnp.dot(a, b, preferred_element_type=f32)


def dot_l(a, b):
    return lax.dot_general(a, b, (((0,), (0,)), ((), ())), preferred_element_type=f32)


def allowed_pairs(start, keys, queries, offset):
    key = lax.broadcasted_iota(jnp.int32, (keys, queries), 0)
    query = lax.broadcasted_iota(jnp.int32, (keys, queries), 1) + offset
    return (key >= start) & (key <= query)


def attend_pair(pre, cos, sin, starts, rotated, attended, stats, r, pair):
    shards, _, shard_len, _ = pre.shape
    length = shards * shard_len
    block = min(256, length)
    per = block // shard_len
    lanes = lambda i: pl.ds(pl.multiple_of((pair * 3 + i) * PAIR, PAIR), PAIR)
    first = lax.rem(lax.broadcasted_iota(jnp.int32, (length, PAIR), 1), HD) < HD // 2
    cos_all, sin_all = cos[:, r].reshape(length, PAIR), sin[:, r].reshape(length, PAIR)

    def rotate(i):
        v = pre[:, r, :, lanes(i)].reshape(length, PAIR)
        return (v * cos_all + swap_halves(v, first) * sin_all).astype(bf16)

    query, key = rotate(0), rotate(1)
    value = pre[:, r, :, lanes(2)].reshape(length, PAIR)
    value_t = value.T.astype(bf16)
    for i, v in enumerate((query, key, value.astype(bf16))):
        rotated[:, r, :, lanes(i)] = v.reshape(shards, shard_len, PAIR)
    left = lax.broadcasted_iota(jnp.int32, (block, PAIR), 1) < HD
    top = lax.broadcasted_iota(jnp.int32, (PAIR, block), 0) < HD
    scaled = query * jnp.asarray(0.125, bf16)
    here_lanes = pl.ds(pl.multiple_of(pair * PAIR, PAIR), PAIR)
    for i in range(length // block):
        keys = (i + 1) * block
        at = slice(i * block, (i + 1) * block)
        mask = allowed_pairs(starts[:, at], keys, block, i * block)
        here = scaled[at]
        results = []
        for h in range(2):
            own = jnp.where(left if h == 0 else ~left, here, jnp.zeros_like(here))
            scores = jnp.where(mask, dot_t(key[:keys], own), -1e30)
            peak = jnp.max(scores, axis=0, keepdims=True)
            shifted = jnp.exp(scores - peak)
            summed = jnp.sum(shifted, axis=0, keepdims=True)
            probs = (shifted * (1.0 / summed)).astype(bf16)
            results.append(dot(value_t[:, :keys], probs))
            stats[r, pair, h : h + 1, at] = peak + jnp.log(summed)
        merged = jnp.where(top, results[0], results[1]).T.astype(bf16)
        attended[i * per : (i + 1) * per, r, :, here_lanes] = merged.reshape(
            per, shard_len, PAIR
        )


def attend_kernel(pre, cos, sin, starts, rotated, attended, stats):
    attend_pair(pre, cos, sin, starts[0], rotated, attended, stats, 0, 0)


def attend(pre, cos, sin, starts):
    shards, rows, shard_len, width = pre.shape
    pairs = width // (3 * PAIR)
    length = shards * shard_len
    wide = pl.BlockSpec((shards, 1, shard_len, 3 * PAIR), lambda r, p: (0, r, 0, p))
    narrow = pl.BlockSpec((shards, 1, shard_len, PAIR), lambda r, p: (0, r, 0, p))
    table = pl.BlockSpec((shards, 1, shard_len, PAIR), lambda r, p: (0, r, 0, 0))
    return pl.pallas_call(
        attend_kernel,
        grid=(rows, pairs),
        out_shape=[
            jax.ShapeDtypeStruct(pre.shape, bf16),
            jax.ShapeDtypeStruct((shards, rows, shard_len, pairs * PAIR), bf16),
            jax.ShapeDtypeStruct((rows, pairs, 2, length), f32),
        ],
        in_specs=[wide, table, table, pl.BlockSpec((1, 1, length), lambda r, p: (r, 0, 0))],
        out_specs=[wide, narrow, pl.BlockSpec((1, 1, 2, length), lambda r, p: (r, p, 0, 0))],
        compiler_params=pltpu.CompilerParams(vmem_limit_bytes=48 * MIB),
        cost_estimate=pl.CostEstimate(
            flops=rows * pairs * 2 * length * length * 256 * 2,
            bytes_accessed=pre.size * 8,
            transcendentals=rows * pairs * length * length,
        ),
    )(pre, cos, sin, starts)


def attend_back_pair(rotated, grad, cos, sin, starts, stats, result, key_acc, value_acc, r, pair):
    shards, _, shard_len, _ = rotated.shape
    length = shards * shard_len
    block = min(256, length)
    per = block // shard_len
    lanes = lambda i: pl.ds(pl.multiple_of((pair * 3 + i) * PAIR, PAIR), PAIR)
    query, key, value = (rotated[:, r, :, lanes(i)].reshape(length, PAIR) for i in range(3))
    grad_all = grad[:, r, :, pl.ds(pl.multiple_of(pair * PAIR, PAIR), PAIR)].reshape(length, PAIR)
    key_t = key.astype(f32).T.astype(bf16)
    left = lax.broadcasted_iota(jnp.int32, (block, PAIR), 1) < HD
    top = lax.broadcasted_iota(jnp.int32, (PAIR, block), 0) < HD
    first = lax.rem(lax.broadcasted_iota(jnp.int32, (length, PAIR), 1), HD) < HD // 2
    key_acc[...] = jnp.zeros_like(key_acc)
    value_acc[...] = jnp.zeros_like(value_acc)

    for i in range(length // block):
        keys = (i + 1) * block
        at = slice(i * block, (i + 1) * block)
        here = slice(i * per, (i + 1) * per)
        mask = allowed_pairs(starts[:, at], keys, block, i * block)
        results = []
        for h in range(2):
            side = left if h == 0 else ~left
            own = jnp.where(side, query[at], jnp.zeros_like(query[at]))
            own_grad = jnp.where(side, grad_all[at], jnp.zeros_like(grad_all[at]))
            scores = dot_t(key[:keys], own * jnp.asarray(0.125, bf16))
            probs = jnp.exp(jnp.where(mask, scores - stats[r, pair, h : h + 1, at], -1e30))
            grad_probs = dot_t(value[:keys], own_grad)
            inner = jnp.sum(probs * grad_probs, axis=0, keepdims=True)
            grad_scores = (probs * (grad_probs - inner) * 0.125).astype(bf16)
            key_acc[:keys, :] += dot(grad_scores, own)
            value_acc[:keys, :] += dot(probs.astype(bf16), own_grad)
            results.append(dot(key_t[:, :keys], grad_scores))
        merged = jnp.where(top, results[0], results[1]).T
        cos_here, sin_here = cos[here, r].reshape(block, PAIR), sin[here, r].reshape(block, PAIR)
        turned = merged * cos_here - swap_halves(merged, first[:block]) * sin_here
        result[here, r, :, lanes(0)] = turned.astype(bf16).reshape(per, shard_len, PAIR)
    cos_all, sin_all = cos[:, r].reshape(length, PAIR), sin[:, r].reshape(length, PAIR)
    key_grad = key_acc[...]
    turned = key_grad * cos_all - swap_halves(key_grad, first) * sin_all
    result[:, r, :, lanes(1)] = turned.astype(bf16).reshape(shards, shard_len, PAIR)
    result[:, r, :, lanes(2)] = value_acc[...].astype(bf16).reshape(shards, shard_len, PAIR)


def attend_back_kernel(rotated, grad, cos, sin, starts, stats, result, key_acc, value_acc):
    attend_back_pair(
        rotated, grad, cos, sin, starts[0], stats, result, key_acc, value_acc, 0, 0
    )


def attend_back(rotated, grad, cos, sin, starts, stats):
    shards, rows, shard_len, width = rotated.shape
    pairs = width // (3 * PAIR)
    length = shards * shard_len
    wide = pl.BlockSpec((shards, 1, shard_len, 3 * PAIR), lambda r, p: (0, r, 0, p))
    narrow = pl.BlockSpec((shards, 1, shard_len, PAIR), lambda r, p: (0, r, 0, p))
    table = pl.BlockSpec((shards, 1, shard_len, PAIR), lambda r, p: (0, r, 0, 0))
    return pl.pallas_call(
        attend_back_kernel,
        grid=(rows, pairs),
        out_shape=jax.ShapeDtypeStruct(rotated.shape, bf16),
        in_specs=[
            wide,
            narrow,
            table,
            table,
            pl.BlockSpec((1, 1, length), lambda r, p: (r, 0, 0)),
            pl.BlockSpec((1, 1, 2, length), lambda r, p: (r, p, 0, 0)),
        ],
        out_specs=wide,
        scratch_shapes=[pltpu.VMEM((length, PAIR), f32), pltpu.VMEM((length, PAIR), f32)],
        compiler_params=pltpu.CompilerParams(vmem_limit_bytes=48 * MIB),
        cost_estimate=pl.CostEstimate(
            flops=rows * pairs * 5 * length * length * 256 * 2,
            bytes_accessed=rotated.size * 6,
            transcendentals=rows * pairs * length * length,
        ),
    )(rotated, grad, cos, sin, starts, stats)


def document_starts(doc_ids):
    places = lax.broadcasted_iota(jnp.int32, doc_ids.shape, 1)
    earlier = jnp.concatenate([doc_ids[:, :1], doc_ids[:, :-1]], axis=1)
    return lax.cummax(jnp.where(doc_ids != earlier, places, 0), axis=1)


def rope_frequency():
    return rope_base ** (-(jnp.arange(HD // 2, dtype=f32) * 2.0 / HD))


def rope_tables(starts, shards):
    rows, length = starts.shape
    positions = (lax.broadcasted_iota(jnp.int32, starts.shape, 1) - starts).astype(f32)
    angles = positions[..., None] * rope_frequency()
    cos, sin = jnp.cos(angles), jnp.sin(angles)
    lay = lambda v: jnp.moveaxis(
        jnp.concatenate(v, axis=-1).reshape(rows, shards, length // shards, PAIR), 0, 1
    )
    return lay([cos] * 4), lay([-sin, sin, -sin, sin])


class LineSum:
    def __init__(self, p, view, land, send, recv, base):
        self.p, self.view, self.land = p, view, land
        self.send, self.recv, self.base = send, recv, base
        self.z = p["dp"]
        self.inward = 1 - 2 * lax.div(self.z, 2)
        self.end = (self.z == 0) | (self.z == 3)

    def copy(self, src, slot, i, to):
        return pltpu.make_async_remote_copy(
            src_ref=src,
            dst_ref=self.land.at[slot],
            send_sem=self.send.at[self.base + i],
            recv_sem=self.recv.at[self.base + slot],
            device_id=(to, self.p["me"]),
            device_id_type=MESH,
        )

    def arrived(self, slot):
        self.copy(self.land.at[slot], slot, 0, self.z).wait_recv()

    def first(self):
        z, inward = self.z, self.inward

        @pl.when(self.end)
        def _():
            near, mid, far = z + inward, z + 2 * inward, z + 3 * inward
            self.copy(self.view(far), near, 0, near).start()
            self.copy(self.view(mid), far, 1, near).start()
            self.copy(self.view(near), z, 2, near).start()

    def second(self, acc, extra, local, i):
        z, inward = self.z, self.inward

        @pl.when(jnp.logical_not(self.end))
        def _():
            outer, inner, far = z - inward, z + inward, z + 2 * inward
            own = [
                pltpu.make_async_copy(self.view(to), acc.at[k], local.at[i + k])
                for k, to in enumerate((far, inner))
            ]
            other = [
                pltpu.make_async_copy(self.land.at[slot], extra.at[k], local.at[i + 2 + k])
                for k, slot in enumerate((z, far))
            ]
            for copy in own:
                copy.start()
            for k, slot in enumerate((z, far)):
                self.arrived(slot)
                other[k].start()
            for k, to in enumerate((far, inner)):
                own[k].wait()
                other[k].wait()

                def step(at):
                    acc[k, at, :] = (acc[k, at, :].astype(f32) + extra[k, at, :].astype(f32)).astype(
                        bf16
                    )

                over_rows(acc.shape[1], step)
                self.copy(acc.at[k], z, k, to).start()
            self.copy(self.view(outer), z, 2, outer).start()

    def total(self, parts, local, i):
        z, inward = self.z, self.inward
        one = jnp.where(self.end, z + 2 * inward, z - inward)
        two = z + inward
        loads = [pltpu.make_async_copy(self.view(z), parts.at[0], local.at[i])]
        loads[0].start()
        for k, slot in ((1, one), (2, two)):
            self.arrived(slot)
            loads.append(pltpu.make_async_copy(self.land.at[slot], parts.at[k], local.at[i + k]))
            loads[k].start()
        for load in loads:
            load.wait()

        def step(at):
            parts[0, at, :] = (
                (parts[0, at, :].astype(f32) + parts[1, at, :].astype(f32))
                + parts[2, at, :].astype(f32)
            ).astype(bf16)

        over_rows(parts.shape[1], step)

    def finish(self):
        for i in range(3):
            self.copy(self.land.at[0], 0, i, self.z).wait_send()


LINE_SEMS = 5


class LineGather:
    def __init__(self, p, src, out, send, recv, base, own=None):
        self.p, self.src, self.out = p, src, out
        self.send, self.recv, self.base = send, recv, base * LINE_SEMS
        self.z = p["dp"]
        self.inward = 1 - 2 * lax.div(self.z, 2)
        self.end = (self.z == 0) | (self.z == 3)
        self.own = None if own is None else pltpu.make_async_copy(src, out.at[self.z], own)

    def copy(self, src, owner, i, to):
        return pltpu.make_async_remote_copy(
            src_ref=src,
            dst_ref=self.out.at[owner],
            send_sem=self.send.at[self.base + i],
            recv_sem=self.recv.at[self.base + owner],
            device_id=(to, self.p["me"]),
            device_id_type=MESH,
        )

    def arrived(self, owner):
        self.copy(self.src, owner, 0, self.z).wait_recv()

    def start(self):
        z, inward = self.z, self.inward
        if self.own is not None:
            self.own.start()
        self.copy(self.src, z, 0, z + inward).start()

        @pl.when(jnp.logical_not(self.end))
        def _():
            self.copy(self.src, z, 1, z - inward).start()

    def second(self):
        z, inward = self.z, self.inward

        @pl.when(jnp.logical_not(self.end))
        def _():
            outer, inner = z - inward, z + inward
            self.arrived(inner)
            self.copy(self.out.at[inner], inner, 2, outer).start()
            self.arrived(outer)
            self.copy(self.out.at[outer], outer, 3, inner).start()

    def third(self):
        z, inward = self.z, self.inward

        @pl.when(jnp.logical_not(self.end))
        def _():
            far = z + 2 * inward
            self.arrived(far)
            self.copy(self.out.at[far], far, 4, z - inward).start()

    def finish(self):
        z, inward = self.z, self.inward

        @pl.when(self.end)
        def _():
            for k in range(1, 4):
                self.arrived(z + k * inward)

        if self.own is not None:
            self.own.wait()
        self.copy(self.src, 0, 0, z).wait_send()

        @pl.when(jnp.logical_not(self.end))
        def _():
            for i in range(1, 5):
                self.copy(self.src, 0, i, z).wait_send()


CHUNKS = 4
OTHERS = ("dg", "ds", "xp", "yp", "xs", "ys", "sib")


def meet_all(p, devices):
    mine = p["dp"] * 8 + p["me"]
    barrier = pltpu.get_barrier_semaphore()

    def other(k):
        to = lax.rem(mine + k, devices)
        return dict(device_id=(lax.div(to, 8), lax.rem(to, 8)), device_id_type=MESH), to

    @pl.loop(1, devices)
    def _(k):
        pl.semaphore_signal(barrier, inc=1, **other(k)[0])

    return other, lambda: pl.semaphore_wait(barrier, devices - 1)


class Local:
    def __init__(self, sems):
        self.sems, self.used, self.free = sems, 0, []

    def take(self, count=1):
        if count == 1 and self.free:
            return self.free.pop(0)
        self.used += count
        assert self.used <= self.sems.shape[0], self.used
        return self.used - count


class Produced:
    def __init__(self, p, produce, stage, kept, paired, send, recv):
        self.p, self.produce, self.stage = p, produce, stage
        self.kept, self.paired, self.send, self.recv = kept, paired, send, recv
        self.pairs = {}

    def ready(self, i):
        k = len(self.pairs)
        _, own, other = ORDER[k]
        rows = self.kept.shape[1]
        stage = self.stage.at[pl.ds(k % 2 * rows, rows)]
        if k >= 2:
            self.pairs[ORDER[k - 2][0]].wait_send()
        self.produce(other, stage)
        self.pairs[i] = remote(self.p, stage, self.paired.at[i], self.send, self.recv, i, "sib")
        self.pairs[i].start()
        self.produce(own, self.kept.at[i])
        self.pairs[i].wait_recv()

    def finish(self):
        for i, _, _ in ORDER[2:]:
            if i in self.pairs:
                self.pairs[i].wait_send()


MAIN_INPUTS = (
    "w_query",
    "w_key",
    "w_value",
    "w_gate",
    "w_up",
    "w_out",
    "w_down",
    "tokens",
    "own_cot",
    "gains",
    "starts",
    "frequency",
)
RESULTS = (
    "gain_sums",
    "grad_tokens",
    "out_tokens",
    "grad_query",
    "grad_key",
    "grad_value",
    "grad_out",
    "grad_gate",
    "grad_up",
    "grad_down",
)
HELD_IN_HBM = (
    "cos",
    "sin",
    "rotated",
    "attended",
    "normed_one",
    "cot",
    "branch",
    "qkv",
    "out_weight",
    "units",
    "down",
    "out_terms",
    "unit_sums",
    "unit_terms",
    "down_terms",
    "kept_units",
    "kept_acts",
    "head_terms",
    "wo_terms",
    "head_sums",
    "unit_land",
    "down_land",
    "head_land",
    "wo_land",
    "units_out",
    "heads_out",
)
SCATTER_NAMES = ("kept", "paired", "far", "final", "send", "recv")
GATHER_NAMES = tuple(k + way for k in "ac" for way in ("send", "recv"))
MAIN_OUTPUTS = RESULTS + HELD_IN_HBM
MAIN_SCRATCH = (
    "hidden",
    "grad_hidden",
    "gain_one",
    "gain_two",
    "gain_term",
    "stats",
    "gains_land",
    "gain_mine",
    "gain_sum_land",
    "x",
    "unit_acc",
    "down_acc",
    "mine",
    "stage",
    "kept",
    "paired",
    "far",
    "final",
    "send",
    "recv",
    "asend",
    "arecv",
    "csend",
    "crecv",
    "gsend",
    "grecv",
    "esend",
    "erecv",
    "zsend",
    "zrecv",
    "ssend",
    "srecv",
    "ready",
    "local",
)


def main_kernel(groups, *refs):
    r = types.SimpleNamespace(**dict(zip(MAIN_INPUTS + MAIN_OUTPUTS + MAIN_SCRATCH, refs)))
    p = plane()
    devices = groups * 8
    other, met = meet_all(p, devices)
    shards = 8
    rows, width = r.tokens.shape
    held = r.w_query.shape[0]
    batch, shard_len, wide = r.rotated.shape[1:]
    pairs = width // 8 // PAIR
    piece, chunk = r.down.shape[2], r.units.shape[3]
    part = chunk // 2
    me, z = p["me"], p["dp"]
    mine_index = z * 8 + me
    held_at = pl.ds(pl.multiple_of(me * held, held), held)
    sems = Local(r.local)
    x = r.x

    lent = {}

    def move(src, dst, i=None):
        place = sems.take() if i is None else i
        copy = pltpu.make_async_copy(src, dst, r.local.at[place])
        if i is None:
            lent[id(copy)] = (copy, place)
        return copy

    def start(*copies):
        for copy in copies:
            copy.start()
        return copies

    def wait(copies):
        for copy in copies:
            copy.wait()
        for copy in copies:
            if id(copy) in lent:
                sems.free.append(lent.pop(id(copy))[1])

    def shard_rows(s, count=1):
        return pl.ds(pl.multiple_of(s * rows, rows), count * rows)

    def line(src, out, i, own):
        sem = r.local.at[sems.take()] if own else None
        return LineGather(p, src, out, r.zsend, r.zrecv, i, sem)

    wo_line = line(r.w_out, r.out_weight, 0, True)
    qkv_line = line(r.qkv.at[z], r.qkv, 1, False)
    chunk_lines = [
        (
            line(r.units.at[j, z], r.units.at[j], 2 + 2 * j, False),
            line(r.w_down.at[pl.ds(j * piece, piece)], r.down.at[j], 3 + 2 * j, True),
        )
        for j in range(CHUNKS)
    ]

    def serve(j, what, *only):
        for k in only or (0, 1):
            getattr(chunk_lines[j][k], what)()

    def gain_copy(k, sender):
        return pltpu.make_async_remote_copy(
            src_ref=r.gains,
            dst_ref=r.gains_land.at[sender],
            send_sem=r.gsend.at[k],
            recv_sem=r.grecv.at[sender],
            **other(k)[0],
        )

    def exchange(block, out, i):
        copies = [
            remote(p, block(p[name]), out, r.esend, r.erecv, i * 7 + j, name)
            for j, name in enumerate(OTHERS)
        ]
        return start(*copies, move(block(me), out))

    def of_owner(ref, count):
        return lambda owner: ref.at[pl.ds(pl.multiple_of(owner * count, count), count)]

    def scatter(produce, between, meanwhile):
        source = Produced(p, produce, r.stage, r.kept, r.paired, r.send, r.recv)
        return scatter_plane(
            p, source, rows, r.kept, r.paired, r.far, r.final, r.send, r.recv, between, meanwhile
        )

    def before(
        w_query, w_key, w_value, w_gate, w_up, cos, sin, head_blocks, unit_blocks, w, wo, pre, rotated, attended
    ):
        head_loads = start(move(r.w_query, w_query), move(r.w_key, w_key), move(r.w_value, w_value))
        unit_loads = start(move(r.w_gate, w_gate), move(r.w_up, w_up))
        wait(head_loads)
        for s in range(shards):
            for pair in range(pairs):
                for i, weight in enumerate((w_query, w_key, w_value)):
                    head = lambda k: ((2 * pair + k) * 8 + s) * HD
                    base = (pair * 3 + i) * PAIR
                    head_blocks[s, :, base : base + PAIR] = jnp.concatenate(
                        [weight[:, head(k) : head(k) + HD] for k in range(2)], axis=1
                    )
        met()

        @pl.loop(1, devices)
        def _(k):
            gain_copy(k, mine_index).start()

        r.gains_land[mine_index] = r.gains[...]
        head_copies = exchange(lambda s: head_blocks.at[s], r.qkv.at[z, held_at], 0)
        wait(unit_loads)
        for s in range(shards):
            for i, weight in enumerate((w_gate, w_up)):
                for j in range(CHUNKS):
                    for pair in range(groups // 2):
                        unit = lambda k: ((2 * pair + k) * 8 + s) * CHUNKS * piece + j * piece
                        base = i * groups * piece + pair * 2 * piece
                        unit_blocks[s, j, :, base : base + 2 * piece] = jnp.concatenate(
                            [weight[:, unit(k) : unit(k) + piece] for k in range(2)], axis=1
                        )

        @pl.loop(1, devices)
        def _(k):
            gain_copy(k, lax.rem(mine_index + devices - k, devices)).wait()

        for out, base in ((r.gain_one, 0), (r.gain_two, held)):
            for k in range(0, devices, 2):
                out[:, k * held : (k + 2) * held] = jnp.concatenate(
                    [r.gains_land[k + i, 0:1, base : base + held] for i in range(2)], axis=1
                )

        def norm_tokens(at):
            t = r.tokens[at, :].astype(f32)
            scale = lax.rsqrt(jnp.mean(t * t, axis=-1, keepdims=True) + norm_eps)
            r.mine[at, :] = (t * scale * r.gain_one[...]).astype(bf16)

        over_rows(rows, norm_tokens)
        wait(head_copies)
        qkv_line.start()
        n1_sent = gather_start(p, r.mine, x, r.asend, r.arecv, 0)
        n1_own = start(move(r.mine, x.at[shard_rows(me)]))
        n1_late = gather_forward(p, n1_sent, x, r.asend, r.arecv, 0, qkv_line.second)
        qkv_line.third()
        wo_line.start()
        unit_exchange = lambda j: exchange(
            lambda s: unit_blocks.at[s, j], r.units.at[j, z, held_at], 1 + j
        )
        unit_copies = [unit_exchange(0)]

        def halfway():
            for j in range(1, CHUNKS):
                unit_copies.append(unit_exchange(j))

        gather_wait(n1_sent, n1_late, halfway)
        wait(n1_own)
        wait(unit_copies[0])
        serve(0, "start")
        keep_normed = start(
            *[move(x.at[shard_rows(s)], r.normed_one.at[s]) for s in range(shards)]
        )
        for row in range(batch):
            length = shards * shard_len
            since = jnp.broadcast_to(r.starts[row].astype(f32), (PAIR, length)).T
            place = lax.broadcasted_iota(jnp.int32, (length, PAIR), 0).astype(f32)
            angles = (place - since) * r.frequency[...]
            lane = lax.broadcasted_iota(jnp.int32, (length, PAIR), 1)
            sign = jnp.where(lax.rem(lane, HD) < HD // 2, -1.0, 1.0)
            cos[:, row] = jnp.cos(angles).reshape(shards, shard_len, PAIR)
            sin[:, row] = (sign * jnp.sin(angles)).reshape(shards, shard_len, PAIR)
        keep_tables = start(move(cos, r.cos), move(sin, r.sin))
        wo_line.second()
        qkv_line.finish()
        wait(start(move(r.qkv, w)))

        @pl.loop(0, shards, step=2)
        def _(s):
            here = dot(x[shard_rows(s, 2)], w[...].reshape(width, wide))
            pre[pl.ds(s, 2)] = here.reshape((2,) + pre.shape[1:])

        for copies in unit_copies[1:]:
            wait(copies)
        wo_line.third()
        cot_sent = gather_start(p, r.own_cot, r.cot, r.csend, r.crecv, 0)
        cot_own = start(move(r.own_cot, r.cot.at[me]))

        def attention(row):
            @pl.loop(0, pairs)
            def _(pair):
                attend_pair(
                    pre, cos, sin, r.starts[row], rotated, attended, r.stats, row, pair
                )

        attention(0)
        serve(0, "second")
        serve(1, "start")
        attention(1)
        cot_late = gather_forward(p, cot_sent, r.cot, r.csend, r.crecv, 0)
        keep_heads = start(move(rotated, r.rotated), move(attended, r.attended))
        wo_line.finish()
        wait(keep_normed)
        wait(start(move(r.out_weight, wo)))

        def produce(name, out):
            terms = attended[p[name]].reshape(rows, attended.shape[3])

            @pl.loop(0, width // 512)
            def _(n):
                at = pl.ds(pl.multiple_of(n * 512, 512), 512)
                out[:, at] = dot(terms, wo[:, :, at].reshape(terms.shape[1], 512)).astype(bf16)

        def between():
            serve(0, "third")
            serve(1, "second")
            serve(2, "start")

        def meanwhile():
            gather_wait(cot_sent, cot_late)
            wait(cot_own)

        scatter(produce, between, meanwhile).finish()
        wait(keep_heads)
        wait(keep_tables)

    vm = lambda shape, dtype=bf16: pltpu.VMEM(shape, dtype)
    pl.run_scoped(
        before,
        *[vm(ref.shape) for ref in (r.w_query, r.w_key, r.w_value, r.w_gate, r.w_up)],
        *[vm(ref.shape, f32) for ref in (r.cos, r.sin)],
        vm((shards, held, wide)),
        vm((shards, CHUNKS, held, chunk)),
        vm(r.qkv.shape),
        vm(r.out_weight.shape),
        vm(r.rotated.shape, f32),
        vm(r.rotated.shape),
        vm(r.attended.shape),
    )

    def norm_hidden(at):
        h = r.tokens[at, :].astype(f32) + total(r.kept, r.paired, r.final, at)
        r.hidden[at, :] = h
        scale = lax.rsqrt(jnp.mean(h * h, axis=-1, keepdims=True) + norm_eps)
        r.mine[at, :] = (h * scale * r.gain_two[...]).astype(bf16)

    over_rows(rows, norm_hidden)
    n2_sent = gather_start(p, r.mine, x, r.asend, r.arecv, 0)
    n2_own = start(move(r.mine, x.at[shard_rows(me)]))

    span = r.unit_land.shape[2]
    sum_lines = [
        (
            LineSum(
                p, of_owner(r.unit_terms.at[j], span), r.unit_land.at[j], r.ssend, r.srecv, 8 * j
            ),
            LineSum(
                p,
                of_owner(r.down_terms.at[j], piece),
                r.down_land.at[j],
                r.ssend,
                r.srecv,
                8 * j + 4,
            ),
        )
        for j in range(CHUNKS)
    ]
    head_lines = [
        LineSum(
            p, of_owner(r.head_terms.at[k], span), r.head_land.at[k], r.ssend, r.srecv, 8 * CHUNKS + 4 * k
        )
        for k in range(pairs)
    ]
    wo_sum = LineSum(
        p, of_owner(r.wo_terms, held), r.wo_land, r.ssend, r.srecv, 8 * CHUNKS + 4 * pairs
    )

    chunk_sem, keep_sem, term_sem, kept_sem, act_sem, out_sem, z_sem = (
        sems.take(k) for k in (4, 2, 2, 2, 2, 2, 8)
    )

    def after(
        c,
        w,
        d,
        unit_stage,
        act_stage,
        unit_kept,
        act_kept,
        unit_grad,
        down_grad,
        unit_parts,
        down_parts,
    ):
        def chunk_loads(j):
            return (
                move(r.units.at[j], w.at[j % 2], chunk_sem + j % 2),
                move(r.down.at[j], d.at[j % 2], chunk_sem + 2 + j % 2),
            )

        def pass_on(j):
            sum_lines[j][0].second(r.unit_acc.at[j], unit_parts, r.local, z_sem)
            sum_lines[j][1].second(r.down_acc.at[j], down_parts, r.local, z_sem + 4)

        def keep(j, what):
            for copy in (
                move(unit_stage, r.kept_units.at[:, pl.ds(j * chunk, chunk)], keep_sem),
                move(act_stage, r.kept_acts.at[:, pl.ds(j * part, part)], keep_sem + 1),
            ):
                getattr(copy, what)()

        def work(j):
            slot = j % 2
            wait(chunk_loads(j))
            if j > 0:
                keep(j - 1, "wait")

            @pl.loop(0, shards, step=2)
            def _(s):
                both = shard_rows(s, 2)
                pre = dot(x[both], w[slot].reshape(width, chunk))
                grad_act = dot_t(c[both], d[slot].reshape(part, width))
                gate, up = pre[:, :part], pre[:, part:]
                sigmoid = 1.0 / (1.0 + jnp.exp(-gate))
                silu = gate * sigmoid
                act_stage[both] = (silu * up).astype(bf16)
                unit_stage[both, :part] = (
                    grad_act * up * sigmoid * (1.0 + gate * (1.0 - sigmoid))
                ).astype(bf16)
                unit_stage[both, part:] = (grad_act * silu).astype(bf16)

            keep(j, "start")

        def weigh_units(j):
            @pl.loop(0, width // 512)
            def _(n):
                at = pl.ds(pl.multiple_of(n * 512, 512), 512)
                unit_grad[at] = dot_l(x[:, at], unit_stage[...]).astype(bf16)

            wait(start(move(unit_grad, r.unit_terms.at[j], term_sem)))
            sum_lines[j][0].first()

        def weigh_down(j):
            @pl.loop(0, width // 512)
            def _(n):
                at = pl.ds(pl.multiple_of(n * 512, 512), 512)
                down_grad[:, at] = dot_l(act_stage[...], c[:, at]).astype(bf16)

            wait(start(move(down_grad, r.down_terms.at[j], term_sem + 1)))
            sum_lines[j][1].first()

        c_loads = start(*[move(r.cot.at[s], c.at[shard_rows(s)]) for s in range(shards)])
        serve(0, "finish")
        start(*chunk_loads(0))
        n2_late = gather_forward(p, n2_sent, x, r.asend, r.arecv, 0)
        serve(1, "third")

        def next_chunks():
            serve(2, "second")
            serve(3, "start")

        gather_wait(n2_sent, n2_late, next_chunks)
        wait(n2_own)
        wait(c_loads)
        work(0)
        weigh_units(0)
        weigh_down(0)
        serve(1, "finish")
        start(*chunk_loads(1))
        work(1)
        serve(2, "third")
        weigh_down(1)
        serve(3, "second")
        weigh_units(1)
        serve(2, "finish")
        start(*chunk_loads(2))
        work(2)
        serve(3, "third")
        weigh_units(2)
        weigh_down(2)
        serve(3, "finish")
        start(*chunk_loads(3))
        work(3)
        weigh_down(3)
        load_w = start(
            *[
                move(
                    r.units.at[j, k // 2, pl.ds(k % 2 * rows, rows)],
                    c.at[shard_rows(k), pl.ds(j * chunk, chunk)],
                )
                for j in range(CHUNKS)
                for k in range(shards)
            ]
        )
        keep(CHUNKS - 1, "wait")
        order = [name for _, own, partner in ORDER for name in (partner, own)]

        def load_kept(k):
            return move(
                r.kept_units.at[shard_rows(p[order[k]])],
                unit_kept.at[pl.ds(k % 2 * rows, rows)],
                kept_sem + k % 2,
            )

        load_kept(0).start()

        def produce(name, out):
            k = order.index(name)
            load_kept(k).wait()
            if k + 1 < len(order):
                load_kept(k + 1).start()
            if k == 0:
                wait(load_w)

            @pl.loop(0, width // 1024)
            def _(n):
                at = pl.ds(pl.multiple_of(n * 1024, 1024), 1024)
                out[:, at] = dot_t(unit_kept[k % 2 * rows : (k % 2 + 1) * rows], c[at]).astype(
                    bf16
                )

        def act_load(s):
            slot = lax.rem(s, 2)
            return move(r.kept_acts.at[shard_rows(s)], act_kept.at[slot], act_sem + slot)

        def out_store(s):
            slot = lax.rem(s, 2)
            return move(r.stage.at[shard_rows(slot)], r.out_terms.at[s], out_sem + slot)

        def out_of_units():
            load_d = start(
                *[
                    move(r.down.at[j, k], x.at[pl.ds(j * part + k * piece, piece)])
                    for j in range(CHUNKS)
                    for k in range(groups)
                ]
            )
            act_load(0).start()
            wait(load_d)

            @pl.loop(0, shards)
            def _(s):
                act_load(s).wait()

                @pl.when(s + 1 < shards)
                def _():
                    act_load(s + 1).start()

                @pl.when(s >= 2)
                def _():
                    out_store(s - 2).wait()

                slot = lax.rem(s, 2)
                acts = act_kept[slot]

                @pl.loop(0, width // 1024)
                def _(n):
                    at = pl.ds(pl.multiple_of(n * 1024, 1024), 1024)
                    r.stage[shard_rows(slot), at] = dot(acts, x[: acts.shape[1], at]).astype(bf16)

                out_store(s).start()

            out_store(shards - 2).wait()
            out_store(shards - 1).wait()
            pass_on(2)

        def last_weights():
            weigh_units(3)
            pass_on(1)

        sums = scatter(produce, lambda: pass_on(0), last_weights)
        sums.source.finish()
        sums.source.pairs.clear()
        r.gain_term[...] = jnp.zeros_like(r.gain_term)

        def norm_back_rows(at):
            g = total(r.kept, r.paired, r.final, at)
            h = r.hidden[at, :]
            scale = lax.rsqrt(jnp.mean(h * h, axis=-1, keepdims=True) + norm_eps)
            weighted = g * r.gain_two[...]
            inner = jnp.mean(weighted * h, axis=-1, keepdims=True)
            back = scale * weighted - h * (scale * scale * scale * inner)
            out = r.own_cot[at, :].astype(f32) + back
            r.grad_hidden[at, :] = out
            r.mine[at, :] = out.astype(bf16)
            r.gain_term[...] += jnp.sum(g * h * scale, axis=0, keepdims=True)

        over_rows(rows, norm_back_rows)
        gather_start(p, r.mine, r.branch, r.asend, r.arecv, 0)
        out_of_units()
        sums.finish()

    pl.run_scoped(
        after,
        vm((shards * rows, width)),
        vm((2,) + r.units.shape[1:]),
        vm((2,) + r.down.shape[1:]),
        vm((shards * rows, chunk)),
        vm((shards * rows, part)),
        vm((2 * rows, CHUNKS * chunk)),
        vm((2, rows, CHUNKS * part)),
        vm((width, chunk)),
        vm((part, width)),
        vm((2, span, chunk)),
        vm((2, piece, width)),
    )

    b_own = start(move(r.mine, r.branch.at[me]))

    def end(
        rotated,
        attended,
        cos,
        sin,
        qkv,
        wo,
        grads,
        key_acc,
        value_acc,
        head_grad,
        wo_grad,
        units,
        heads,
        wide_out,
        row_out,
        narrow_out,
        gain_one_term,
        head_acc,
        wo_acc,
        parts,
        row_parts,
    ):
        loads = start(
            move(r.out_weight, wo),
            move(r.attended, attended),
            move(r.rotated, rotated),
            move(r.cos, cos),
            move(r.sin, sin),
            move(r.qkv, qkv),
        )
        narrow = parts.at[:, :, pl.ds(0, chunk)]

        def sum_up(j):
            sum_lines[j][0].total(narrow, r.local, z_sem)
            wait(start(move(parts.at[0, :, pl.ds(0, chunk)], r.unit_sums.at[j], z_sem)))
            copies = exchange(
                of_owner(r.unit_sums.at[j], held), r.units_out.at[j, me], 1 + j
            )
            sum_lines[j][1].total(row_parts, r.local, z_sem)
            row_out[...] = row_parts[0].astype(f32)
            wait(start(move(row_out, r.grad_down.at[pl.ds(j * piece, piece)], z_sem)))
            return copies

        def pass_on(j):
            sum_lines[j][0].second(
                r.unit_acc.at[j % 3], parts.at[1:3, :, pl.ds(0, chunk)], r.local, z_sem
            )
            sum_lines[j][1].second(r.down_acc.at[j % 3], row_parts.at[1:3], r.local, z_sem + 4)

        unit_copies = []
        b_sent = gather_copies(p, r.mine, r.branch, r.asend, r.arecv, 0)
        b_late = gather_forward(p, b_sent, r.branch, r.asend, r.arecv, 0)
        unit_copies += sum_up(0)
        gather_wait(b_sent, b_late)
        wait(b_own)
        wait(start(*[move(r.branch.at[s], x.at[shard_rows(s)]) for s in range(shards)]))
        out_sem_base = sems.take(4)
        out_source = FromMemory(
            p, r.out_terms, r.kept, r.paired, r.send, r.recv, r.local.at[pl.ds(out_sem_base, 4)]
        )
        out_sum = PlaneSum(
            p, out_source, rows, r.kept, r.paired, r.far, r.final, r.send, r.recv
        )
        wait(loads[:2])

        @pl.loop(0, shards, step=2)
        def _(s):
            grad = dot_t(x[shard_rows(s, 2)], wo[...].reshape(-1, width)).astype(bf16)
            grads[pl.ds(s, 2)] = grad.reshape((2,) + grads.shape[1:])

        out_sum.first()

        @pl.loop(0, width // 512)
        def _(n):
            at = pl.ds(pl.multiple_of(n * 512, 512), 512)
            acts = attended[...].reshape(shards * rows, -1)
            wo_grad[:, at] = dot_l(acts, x[:, at]).astype(bf16)

        wait(start(move(wo_grad, r.wo_terms)))
        wo_sum.first()
        n1_loads = start(*[move(r.normed_one.at[s], x.at[shard_rows(s)]) for s in range(shards)])
        wait(loads[2:])

        def attention(pair):
            @pl.loop(0, batch)
            def _(row):
                attend_back_pair(
                    rotated,
                    grads,
                    cos,
                    sin,
                    r.starts[row],
                    r.stats,
                    rotated,
                    key_acc,
                    value_acc,
                    row,
                    pair,
                )

        def weigh_heads(pair):
            lanes = slice(pair * 3 * PAIR, (pair + 1) * 3 * PAIR)

            @pl.loop(0, width // 512)
            def _(n):
                at = pl.ds(pl.multiple_of(n * 512, 512), 512)
                grad = rotated[:, :, :, lanes].reshape(shards * rows, 3 * PAIR)
                head_grad[at] = dot_l(x[:, at], grad).astype(bf16)

            wait(start(move(head_grad, r.head_terms.at[pair])))
            head_lines[pair].first()

        attention(0)
        wait(n1_loads)
        weigh_heads(0)
        out_sum.second()
        for one in sum_lines[0]:
            one.finish()
        pass_on(CHUNKS - 1)
        for pair in range(1, pairs):
            attention(pair)
            weigh_heads(pair)
        wo_sum.second(wo_acc, row_parts.at[1:3], r.local, z_sem)
        out_sum.third()

        def step_out(at):
            out = r.hidden[at, :] + total(r.kept, r.paired, r.final, at)
            r.mine[at, :] = out.astype(bf16)

        over_rows(rows, step_out)
        keep_tokens = [*start(move(r.mine, r.out_tokens))]
        out_sum.finish()
        for name in ("sib", "xp", "yp"):
            pl.semaphore_signal(r.ready, inc=1, device_id=(z, p[name]), device_id_type=MESH)
        pl.semaphore_wait(r.ready, 3)

        def produce(name, out):
            grad = rotated[p[name]].reshape(rows, wide)

            @pl.loop(0, groups)
            def _(n):
                at = pl.ds(pl.multiple_of(n * span, span), span)
                out[:, at] = dot_t(grad, qkv[n]).astype(bf16)

        def pass_heads(k):
            head_lines[k].second(
                head_acc.at[k], parts.at[1:3, :, pl.ds(0, 3 * PAIR)], r.local, z_sem
            )

        def meanwhile():
            unit_copies.extend(sum_up(1))
            unit_copies.extend(sum_up(2))
            unit_copies.extend(sum_up(3))

        pass_heads(0)
        sums = scatter(produce, lambda: pass_heads(1), meanwhile)
        gain_one_term[...] = jnp.zeros_like(gain_one_term)

        def norm_back_rows(at):
            g = total(r.kept, r.paired, r.final, at)
            t = r.tokens[at, :].astype(f32)
            scale = lax.rsqrt(jnp.mean(t * t, axis=-1, keepdims=True) + norm_eps)
            weighted = g * r.gain_one[...]
            inner = jnp.mean(weighted * t, axis=-1, keepdims=True)
            back = scale * weighted - t * (scale * scale * scale * inner)
            r.stage[at, :] = (r.grad_hidden[at, :] + back).astype(bf16)
            gain_one_term[...] += jnp.sum(g * t * scale, axis=0, keepdims=True)

        sums.source.finish()
        sums.source.pairs.clear()
        over_rows(rows, norm_back_rows)
        keep_tokens += start(move(r.stage.at[pl.ds(0, rows)], r.grad_tokens))
        r.gain_mine[...] = jnp.zeros_like(r.gain_mine)
        for k in range(devices):
            at = slice(k * held, (k + 1) * held)
            r.gain_mine[k, 0:1, :held] = gain_one_term[:, at]
            r.gain_mine[k, 1:2, :held] = r.gain_term[:, at]

        def gain_back(k):
            where, to = other(k)
            return pltpu.make_async_remote_copy(
                src_ref=r.gain_mine.at[to],
                dst_ref=r.gain_sum_land.at[k],
                send_sem=r.gsend.at[k],
                recv_sem=r.grecv.at[k],
                **where,
            )

        @pl.loop(1, devices)
        def _(k):
            gain_back(k).start()

        wo_sum.total(row_parts, r.local, z_sem)
        row_out[...] = row_parts[0].astype(f32)
        keep_wo = start(move(row_out, r.grad_out))

        def sum_heads(k):
            head_lines[k].total(parts.at[:, :, pl.ds(0, 3 * PAIR)], r.local, z_sem)
            wait(start(move(parts.at[0, :, pl.ds(0, 3 * PAIR)], r.head_sums.at[k], z_sem)))
            return exchange(
                of_owner(r.head_sums.at[k], held), r.heads_out.at[k, me], 1 + CHUNKS + k
            )

        head_copies = [sum_heads(0)]
        wait(unit_copies)
        wait(start(move(r.units_out, units)))
        stores = []
        for i, out in enumerate((r.grad_gate, r.grad_up)):
            if i == 1:
                head_copies += [sum_heads(k) for k in range(1, pairs)]
            for k in range(groups):
                if len(stores) >= 2:
                    stores[-2].wait()
                for s in range(shards):
                    for a in range(CHUNKS // 2):
                        base = (i * groups + k) * piece
                        tile = jnp.concatenate(
                            [units[2 * a + b, s, :, base : base + piece] for b in range(2)], axis=1
                        )
                        at = (s * 2 + a) * 2 * piece
                        wide_out[k % 2, :, at : at + 2 * piece] = tile.astype(f32)
                span_out = wide_out.shape[2]
                stores.append(move(wide_out.at[k % 2], out.at[:, pl.ds(k * span_out, span_out)]))
                stores[-1].start()
        r.gain_sum_land[0] = r.gain_mine[mine_index]

        @pl.loop(1, devices)
        def _(k):
            gain_back(k).wait()

        r.gain_sums[...] = jnp.sum(r.gain_sum_land[...], axis=0)
        for copies in head_copies:
            wait(copies)
        wait(start(move(r.heads_out, heads)))
        for i, out in enumerate((r.grad_query, r.grad_key, r.grad_value)):
            for k in range(groups):
                for s in range(0, shards, 2):
                    base = i * PAIR + k % 2 * HD
                    tile = jnp.concatenate(
                        [heads[k // 2, s + b, :, base : base + HD] for b in range(2)], axis=1
                    )
                    at = (k * shards + s) * HD
                    narrow_out[i, :, at : at + 2 * HD] = tile.astype(f32)
            stores.append(move(narrow_out.at[i], out))
            stores[-1].start()
        wait(stores[-5:])
        wait(keep_tokens)
        wait(keep_wo)
        for one in (*[one for pair in sum_lines[1:] for one in pair], wo_sum, *head_lines):
            one.finish()
        sums.finish()

    pl.run_scoped(
        end,
        vm(r.rotated.shape),
        vm(r.attended.shape),
        *[vm(ref.shape, f32) for ref in (r.cos, r.sin)],
        vm(r.qkv.shape),
        vm(r.out_weight.shape),
        vm(r.attended.shape),
        vm((shards * shard_len, PAIR), f32),
        vm((shards * shard_len, PAIR), f32),
        vm((width, 3 * PAIR)),
        vm(r.wo_terms.shape),
        vm(r.units_out.shape),
        vm(r.heads_out.shape),
        vm((2, held, width), f32),
        vm((piece, width), f32),
        vm((3, held, width), f32),
        vm((1, width), f32),
        vm((pairs, 2, span, 3 * PAIR)),
        vm((2, held, width)),
        vm((3, span, chunk)),
        vm((3, piece, width)),
    )


def main_plane(groups, shards, batch, tokens, cotangent, gains, weights, starts, collective_id):
    w_query, w_key, w_value, w_out, w_gate, w_up, w_down = weights
    shard_len = tokens.shape[0] // batch
    rows, width = tokens.shape
    held, devices = w_query.shape[0], groups * shards
    mine = width // shards
    wide = 3 * mine
    hidden_here = groups * w_down.shape[0]
    chunk = 2 * hidden_here // CHUNKS
    piece = w_down.shape[0] // CHUNKS
    span = width // groups
    pairs = mine // PAIR
    low = lambda *shape: jax.ShapeDtypeStruct(shape, bf16)
    full = lambda *shape: jax.ShapeDtypeStruct(shape, f32)
    outputs = dict(
        gain_sums=full(8, 128),
        grad_tokens=low(rows, width),
        out_tokens=low(rows, width),
        grad_query=full(held, width),
        grad_key=full(held, width),
        grad_value=full(held, width),
        grad_out=full(held, width),
        grad_gate=full(held, hidden_here * shards),
        grad_up=full(held, hidden_here * shards),
        grad_down=full(CHUNKS * piece, width),
        cos=full(shards, batch, shard_len, PAIR),
        sin=full(shards, batch, shard_len, PAIR),
        rotated=low(shards, batch, shard_len, wide),
        attended=low(shards, batch, shard_len, mine),
        normed_one=low(shards, rows, width),
        cot=low(shards, rows, width),
        branch=low(shards, rows, width),
        qkv=low(groups, span, wide),
        out_weight=low(groups, held, width),
        units=low(CHUNKS, groups, span, chunk),
        down=low(CHUNKS, groups, piece, width),
        out_terms=low(shards, rows, width),
        unit_sums=low(CHUNKS, span, chunk),
        unit_terms=low(CHUNKS, width, chunk),
        down_terms=low(CHUNKS, chunk // 2, width),
        kept_units=low(shards * rows, CHUNKS * chunk),
        kept_acts=low(shards * rows, hidden_here),
        head_terms=low(pairs, width, 3 * PAIR),
        wo_terms=low(groups * held, width),
        head_sums=low(pairs, span, 3 * PAIR),
        unit_land=low(CHUNKS, 4, span, chunk),
        down_land=low(CHUNKS, 4, piece, width),
        head_land=low(pairs, 4, span, 3 * PAIR),
        wo_land=low(4, held, width),
        units_out=low(CHUNKS, shards, held, chunk),
        heads_out=low(pairs, shards, held, 3 * PAIR),
    )
    assert tuple(outputs) == tuple(MAIN_OUTPUTS)
    scratch = dict(
        hidden=pltpu.VMEM((rows, width), f32),
        grad_hidden=pltpu.VMEM((rows, width), f32),
        gain_one=pltpu.VMEM((1, width), f32),
        gain_two=pltpu.VMEM((1, width), f32),
        gain_term=pltpu.VMEM((1, width), f32),
        stats=pltpu.VMEM((batch, pairs, 2, shards * shard_len), f32),
        gains_land=pltpu.VMEM((devices, 8, 2 * held), f32),
        gain_mine=pltpu.VMEM((devices, 8, 128), f32),
        gain_sum_land=pltpu.VMEM((devices, 8, 128), f32),
        x=pltpu.VMEM((shards * rows, width), bf16),
        unit_acc=pltpu.VMEM((CHUNKS - 1, 2, span, chunk), bf16),
        down_acc=pltpu.VMEM((CHUNKS - 1, 2, piece, width), bf16),
        mine=pltpu.VMEM((rows, width), bf16),
        stage=pltpu.VMEM((2 * rows, width), bf16),
    )
    for name, buffer in zip(SCATTER_NAMES, scatter_scratch(rows, width)):
        scratch[name] = buffer
    for name in GATHER_NAMES:
        scratch[name] = DMA((GATHER_SEMS,))
    exchanges, sums = 7 * (1 + CHUNKS + pairs), 8 * CHUNKS + 4 * pairs + 4
    for name, count in (
        ("gsend", devices),
        ("grecv", devices),
        ("esend", exchanges),
        ("erecv", exchanges),
        ("zsend", LINE_SEMS * (2 + 2 * CHUNKS)),
        ("zrecv", LINE_SEMS * (2 + 2 * CHUNKS)),
        ("ssend", sums),
        ("srecv", sums),
    ):
        scratch[name] = DMA((count,))
    scratch["ready"] = pltpu.SemaphoreType.REGULAR
    scratch["local"] = DMA((104,))
    assert tuple(scratch) == tuple(MAIN_SCRATCH)
    in_vmem = 1
    done = pl.pallas_call(
        functools.partial(main_kernel, groups),
        out_shape=list(outputs.values()),
        in_specs=[ANY] * 7 + [VMEM] * 5,
        out_specs=[VMEM] * in_vmem + [ANY] * (len(outputs) - in_vmem),
        scratch_shapes=list(scratch.values()),
        compiler_params=pltpu.CompilerParams(
            collective_id=collective_id, has_side_effects=True, vmem_limit_bytes=63 * MIB
        ),
        cost_estimate=lasting(500),
    )(
        w_query,
        w_key,
        w_value,
        w_gate,
        w_up,
        w_out,
        w_down,
        tokens,
        cotangent,
        jnp.broadcast_to(gains.reshape(1, -1).astype(f32), (8, 2 * held)),
        starts,
        jnp.tile(rope_frequency(), 2 * PAIR // HD)[None],
    )
    count = len(RESULTS) - 1
    shapes = list(outputs.values())[1 : 1 + count]
    results = pl.pallas_call(
        hand_over,
        out_shape=shapes,
        in_specs=[ANY] * count,
        out_specs=[ANY] * count,
        scratch_shapes=[*[pltpu.VMEM(s.shape, s.dtype) for s in shapes], DMA((2, count))],
        compiler_params=pltpu.CompilerParams(vmem_limit_bytes=63 * MIB),
    )(*done[1 : 1 + count])
    return types.SimpleNamespace(**dict(zip(RESULTS, [done[0], *results])))


def hand_over(*refs):
    count = (len(refs) - 1) // 3
    ways = [
        [
            pltpu.make_async_copy(refs[way * 2 * count + i], refs[(2 - way) * count + i], refs[-1].at[way, i])
            for i in range(count)
        ]
        for way in range(2)
    ]
    for copy in ways[0]:
        copy.start()
    for copy, out in zip(*ways):
        copy.wait()
        out.start()
    for copy in ways[1]:
        copy.wait()


def layer(
    groups,
    shards,
    tokens,
    doc_ids,
    cotangent,
    norm1_gain,
    w_query,
    w_key,
    w_value,
    w_out,
    norm2_gain,
    w_gate,
    w_up,
    w_down,
):
    rows, shard_len, width = tokens.shape
    count = rows * shard_len
    held = w_query.shape[0]
    hidden_held = w_down.shape[0]
    hidden_here = groups * hidden_held
    whole_heads = held % HD == 0
    outer, inner = (groups, held) if whole_heads else (1, width // shards)
    pairs = width // shards // PAIR
    both = ("dp", "seq")
    fast = groups == 4 and shards == 8
    flat = lambda v: v.reshape(shards * count, v.shape[-1])
    split = lambda v: v.reshape(shards, count, v.shape[-1])

    gains = jnp.stack([norm1_gain, norm2_gain])
    own_tokens = tokens.reshape(count, width)
    own_cotangent = cotangent.reshape(count, width)
    inputs = own_tokens.astype(f32)
    starts = document_starts(doc_ids)
    by_row = lambda v: v.reshape(shards, rows, shard_len, v.shape[-1])

    if fast:
        done = main_plane(
            groups,
            shards,
            rows,
            own_tokens,
            own_cotangent,
            gains,
            (w_query, w_key, w_value, w_out, w_gate, w_up, w_down),
            starts[:, None, :],
            1,
        )
        return (
            done.out_tokens.reshape(tokens.shape),
            done.grad_tokens.reshape(tokens.shape),
            done.gain_sums[0, :held],
            done.grad_query,
            done.grad_key,
            done.grad_value,
            done.grad_out,
            done.gain_sums[1, :held],
            done.grad_gate,
            done.grad_up,
            done.grad_down,
        )

    cos, sin = rope_tables(starts, shards)
    starts = starts[:, None, :]
    gains = lax.all_gather(gains, both, axis=1, tiled=True).astype(f32)
    gain_one, gain_two = gains[:1], gains[1:]

    def by_head(w):
        blocks = w.reshape(held, outer, shards, inner)
        return jnp.moveaxis(blocks, 2, 0).reshape(shards, held, pairs, PAIR)

    blocks = jnp.stack([w_gate, w_up]).reshape(2, held, groups, shards, hidden_held)
    units = jnp.transpose(blocks, (3, 1, 0, 2, 4)).reshape(shards, held, 2 * hidden_here)
    heads = jnp.stack([by_head(w) for w in (w_query, w_key, w_value)], axis=3)
    heads, units = exchange_plane([heads.reshape(shards, held, -1), units], shards, 1)
    spread = lambda w: lax.all_gather(w, "dp", axis=0, tiled=True)
    qkv_weight = spread(heads.reshape(shards * held, -1))
    unit_weight = spread(units.reshape(shards * held, -1))
    down_weight = spread(w_down)
    if whole_heads:
        out_weight = spread(w_out)
    else:
        whole = lax.all_gather(w_out, both, axis=0, tiled=True)
        out_weight = lax.dynamic_slice_in_dim(whole, lax.axis_index("seq") * inner, inner, 0)
    own_normed = (inputs * rms_scale(inputs) * gain_one).astype(bf16)
    normed_one, cot = [flat(v) for v in gather_plane([own_normed, own_cotangent], shards, 2)]
    pre = by_row(dot(normed_one, qkv_weight))
    rotated, attended, stats = attend(pre, cos, sin, starts)
    attended = flat(attended)
    hidden = inputs + reduce_plane(split(dot(attended, out_weight).astype(bf16)))
    normed_two = (hidden * rms_scale(hidden) * gain_two).astype(bf16)
    normed_two = flat(lax.all_gather(normed_two, "seq"))
    gate_weight, up_weight = unit_weight[:, :hidden_here], unit_weight[:, hidden_here:]
    gate_pre, up_pre = dot(normed_two, gate_weight), dot(normed_two, up_weight)
    sigmoid = jax.nn.sigmoid(gate_pre)
    silu = gate_pre * sigmoid
    activated = (silu * up_pre).astype(bf16)
    out_terms = split(dot(activated, down_weight).astype(bf16))
    grad_act = dot_t(cot, down_weight)
    grad_gate_pre = grad_act * up_pre * sigmoid * (1.0 + gate_pre * (1.0 - sigmoid))
    grad_up_pre = grad_act * silu
    grad_units = jnp.concatenate([grad_gate_pre, grad_up_pre], axis=-1).astype(bf16)
    middle_terms = split(dot_t(grad_units, unit_weight).astype(bf16))
    unit_sums = lax.psum_scatter(
        dot(normed_two.T, grad_units).astype(bf16), "dp", scatter_dimension=0, tiled=True
    )
    down_sums = lax.psum_scatter(
        dot(activated.T, cot).astype(bf16), "dp", scatter_dimension=0, tiled=True
    )
    back, gain_two_term = norm_back(
        hidden, rms_scale(hidden), gain_two, reduce_plane(middle_terms)
    )
    grad_hidden = own_cotangent.astype(f32) + back
    branch = lax.all_gather(grad_hidden.astype(bf16), "seq")

    branch = flat(branch)
    out_w_terms = dot(attended.T, branch).astype(bf16)
    grad_attended = by_row(dot_t(branch, out_weight).astype(bf16))
    grad_pre = flat(attend_back(rotated, grad_attended, cos, sin, starts, stats))
    last_terms = split(dot_t(grad_pre, qkv_weight).astype(bf16))
    head_terms = dot(normed_one.T, grad_pre).astype(bf16)

    if whole_heads:
        grad_out = lax.psum_scatter(out_w_terms, "dp", scatter_dimension=0, tiled=True)
    else:
        placed = lax.dynamic_update_slice_in_dim(
            jnp.zeros((width, width), bf16), out_w_terms, lax.axis_index("seq") * inner, 0
        )
        grad_out = lax.psum_scatter(placed, both, scatter_dimension=0, tiled=True)
    back, gain_one_term = norm_back(inputs, rms_scale(inputs), gain_one, reduce_plane(last_terms))
    grad_tokens = (grad_hidden + back).astype(bf16)
    out_tokens = (hidden + reduce_plane(out_terms)).astype(bf16)
    head_sums = lax.psum_scatter(head_terms, "dp", scatter_dimension=0, tiled=True)
    heads_back, units_back = exchange_plane(
        [head_sums.reshape(shards, held, -1), unit_sums.reshape(shards, held, -1)], shards, 6
    )
    grad_norms = lax.psum_scatter(
        jnp.concatenate([gain_one_term, gain_two_term]), both, scatter_dimension=1, tiled=True
    )
    heads_back = heads_back.reshape(shards, held, pairs, 3, PAIR)
    units_back = units_back.reshape(shards, held, 2, groups, hidden_held)

    def head_grad(i):
        blocks = heads_back[:, :, :, i, :].reshape(shards, held, outer, inner)
        return jnp.moveaxis(blocks, 0, 2).reshape(held, width).astype(f32)

    def unit_grad(i):
        return jnp.transpose(units_back[:, :, i], (1, 2, 0, 3)).reshape(held, -1).astype(f32)

    return (
        out_tokens.reshape(tokens.shape),
        grad_tokens.reshape(tokens.shape),
        grad_norms[0],
        head_grad(0),
        head_grad(1),
        head_grad(2),
        grad_out.astype(f32),
        grad_norms[1],
        unit_grad(0),
        unit_grad(1),
        down_sums.astype(f32),
    )


def solution(mesh):
    both = ("dp", "seq")
    return jax.shard_map(
        functools.partial(layer, mesh.shape["dp"], mesh.shape["seq"]),
        mesh=mesh,
        in_specs=(
            P("dp", "seq", None),
            P("dp", None),
            P("dp", "seq", None),
            P(both),
            P(both, None),
            P(both, None),
            P(both, None),
            P(both, None),
            P(both),
            P(both, None),
            P(both, None),
            P(both, None),
        ),
        out_specs=(
            P("dp", "seq", None),
            P("dp", "seq", None),
            P(both),
            P(both, None),
            P(both, None),
            P(both, None),
            P(both, None),
            P(both),
            P(both, None),
            P(both, None),
            P(both, None),
        ),
        check_vma=False,
    )
```

```python
import functools
import types

import jax
import jax.numpy as jnp
from jax import lax
from jax.experimental import pallas as pl
from jax.experimental.pallas import tpu as pltpu
from jax.sharding import PartitionSpec as P

H = 32
HD = 64
PAIR = 2 * HD

rope_base = 130000.0
norm_eps = 1e-05

bf16 = jnp.bfloat16
f32 = jnp.float32
MESH = pl.DeviceIdType.MESH
ANY = pl.BlockSpec(memory_space=pl.ANY)
VMEM = pl.BlockSpec(memory_space=pltpu.VMEM)
DMA = pltpu.SemaphoreType.DMA
MIB = 1 << 20


def lasting(us):
    return pl.CostEstimate(flops=0, transcendentals=0, bytes_accessed=int(us * 3_500_000))


def plane():
    dp, s = lax.axis_index("dp"), lax.axis_index("seq")
    core, xb, yb = lax.rem(s, 2), lax.rem(lax.div(s, 2), 2), lax.div(s, 4)
    at = lambda y, x, c: y * 4 + x * 2 + c
    return dict(
        dp=dp,
        me=s,
        sib=at(yb, xb, 1 - core),
        xp=at(yb, 1 - xb, core),
        yp=at(1 - yb, xb, core),
        dg=at(1 - yb, 1 - xb, core),
        xs=at(yb, 1 - xb, 1 - core),
        ys=at(1 - yb, xb, 1 - core),
        ds=at(1 - yb, 1 - xb, 1 - core),
    )


def greet(p, names):
    barrier = pltpu.get_barrier_semaphore()
    for name in names:
        pl.semaphore_signal(barrier, inc=1, device_id=(p["dp"], p[name]), device_id_type=MESH)
    pl.semaphore_wait(barrier, len(names))


def remote(p, src, dst, send, recv, i, to):
    return pltpu.make_async_remote_copy(
        src_ref=src,
        dst_ref=dst,
        send_sem=send.at[i],
        recv_sem=recv.at[i],
        device_id=(p["dp"], p[to]),
        device_id_type=MESH,
    )


GATHER_SEMS = 25


def shard_of(out, owner):
    if len(out.shape) == 3:
        return out.at[owner]
    rows = out.shape[0] // 8
    return out.at[pl.ds(pl.multiple_of(owner * rows, rows), rows)]


def gather_copies(p, src, out, send, recv, base):
    quarter = src.shape[0] // 4
    part = lambda ref, k: ref.at[pl.ds(k * quarter, quarter)]
    mine = shard_of(out, p["me"])
    sent = {}
    for j in range(4):
        kx, ky = j, (j + 2) % 4
        sent["x", kx] = remote(p, part(src, kx), part(mine, kx), send, recv, base + kx, "xp")
        sent["y", ky] = remote(p, part(src, ky), part(mine, ky), send, recv, base + 4 + ky, "yp")
    sent["s"] = remote(p, src, mine, send, recv, base + 8, "sib")
    return sent


def gather_start(*args):
    sent = gather_copies(*args)
    for copy in sent.values():
        copy.start()
    return sent


def quarter_of(ref, k):
    rows = ref.shape[0] // 4
    return ref.at[pl.ds(k * rows, rows)]


def gather_pass(p, ref, send, recv, i, to):
    copy = remote(p, ref, ref, send, recv, i, to)
    copy.start()
    return copy


def gather_forward(p, sent, out, send, recv, base, halfway=None):
    part = lambda owner, k: quarter_of(shard_of(out, p[owner]), k)
    passed = []
    for j in range(4):
        kx, ky = j, (j + 2) % 4
        sent["x", kx].wait_recv()
        if j < 2:
            sent["far", kx] = gather_pass(p, part("xp", kx), send, recv, base + 9 + kx, "yp")
        passed.append(gather_pass(p, part("xp", kx), send, recv, base + 13 + kx, "sib"))
        sent["y", ky].wait_recv()
        if j < 2:
            sent["far", ky] = gather_pass(p, part("yp", ky), send, recv, base + 9 + ky, "xp")
        passed.append(gather_pass(p, part("yp", ky), send, recv, base + 17 + ky, "sib"))
        if j == 1 and halfway is not None:
            halfway()

    def last():
        for k in (0, 2, 1, 3):
            sent["far", k].wait_recv()
            passed.append(gather_pass(p, part("dg", k), send, recv, base + 21 + k, "sib"))

    return passed, last


def gather_wait(sent, late, halfway=None):
    passed, last = late
    last()
    if halfway is not None:
        halfway()
    sent["s"].wait_recv()
    for copy in passed:
        copy.wait_recv()
    for copy in list(sent.values()) + passed:
        copy.wait_send()


def gather_finish(p, sent, out, send, recv, base):
    gather_wait(sent, gather_forward(p, sent, out, send, recv, base))


def gather_kernel(count, *refs):
    sources, outs = refs[:count], refs[count : 2 * count]
    send, recv, local = refs[2 * count :]
    p = plane()
    greet(p, ("sib", "xp", "yp"))
    sent, kept = [], []
    for i in range(count):
        sent.append(gather_start(p, sources[i], outs[i], send, recv, i * GATHER_SEMS))
        kept.append(pltpu.make_async_copy(sources[i], outs[i].at[p["me"]], local.at[i]))
        kept[i].start()
    for i in range(count):
        gather_finish(p, sent[i], outs[i], send, recv, i * GATHER_SEMS)
    for copy in kept:
        copy.wait()


def gather_plane(arrays, shards, collective_id):
    if shards != 8:
        return [lax.all_gather(a, "seq") for a in arrays]
    count = len(arrays)
    return pl.pallas_call(
        functools.partial(gather_kernel, count),
        out_shape=[jax.ShapeDtypeStruct((8,) + a.shape, a.dtype) for a in arrays],
        in_specs=[ANY] * count,
        out_specs=[ANY] * count,
        scratch_shapes=[DMA((GATHER_SEMS * count,)), DMA((GATHER_SEMS * count,)), DMA((count,))],
        compiler_params=pltpu.CompilerParams(collective_id=collective_id, has_side_effects=True),
        cost_estimate=lasting(40 * count),
    )(*arrays)


def exchange_kernel(count, *refs):
    sources, outs = refs[:count], refs[count : 2 * count]
    send, recv, local = refs[2 * count :]
    p = plane()
    names = ("dg", "ds", "xp", "yp", "xs", "ys", "sib")
    greet(p, names)
    copies = []
    for i in range(count):
        for j, name in enumerate(names):
            copies.append(
                remote(
                    p, sources[i].at[p[name]], outs[i].at[p["me"]], send, recv, i * 7 + j, name
                )
            )
            copies[-1].start()
        copies.append(
            pltpu.make_async_copy(sources[i].at[p["me"]], outs[i].at[p["me"]], local.at[i])
        )
        copies[-1].start()
    for copy in copies:
        copy.wait()


def exchange_plane(arrays, shards, collective_id):
    if shards != 8:
        return [lax.all_to_all(a, "seq", split_axis=0, concat_axis=0) for a in arrays]
    count = len(arrays)
    return pl.pallas_call(
        functools.partial(exchange_kernel, count),
        out_shape=[jax.ShapeDtypeStruct(a.shape, a.dtype) for a in arrays],
        in_specs=[ANY] * count,
        out_specs=[ANY] * count,
        scratch_shapes=[DMA((7 * count,)), DMA((7 * count,)), DMA((count,))],
        compiler_params=pltpu.CompilerParams(collective_id=collective_id, has_side_effects=True),
        cost_estimate=lasting(35),
    )(*arrays)


BLOCK = 16


def over_rows(rows, step):
    @pl.loop(0, rows // BLOCK)
    def _(i):
        step(pl.ds(pl.multiple_of(i * BLOCK, BLOCK), BLOCK))


def scatter_scratch(rows, width):
    return [
        pltpu.VMEM((4, rows, width), bf16),
        pltpu.VMEM((4, rows, width), bf16),
        pltpu.VMEM((2, rows // 2, width), bf16),
        pltpu.VMEM((2, rows, width), bf16),
        DMA((12,)),
        DMA((12,)),
        DMA((4,)),
    ]


class FromMemory:
    def __init__(self, p, terms, kept, paired, send, recv, local):
        self.loads, self.pairs = {}, {}
        for i, own, other in ORDER:
            self.loads[i] = pltpu.make_async_copy(terms.at[p[own]], kept.at[i], local.at[i])
            self.loads[i].start()
            self.pairs[i] = remote(p, terms.at[p[other]], paired.at[i], send, recv, i, "sib")
            self.pairs[i].start()

    def ready(self, i):
        self.loads[i].wait()
        self.pairs[i].wait_recv()

    def finish(self):
        for copy in self.pairs.values():
            copy.wait_send()


ORDER = ((3, "dg", "ds"), (1, "xp", "xs"), (2, "yp", "ys"), (0, "me", "sib"))


class PlaneSum:
    def __init__(self, p, source, rows, kept, paired, far, final, send, recv):
        self.p, self.source, self.rows = p, source, rows
        self.kept, self.paired, self.far, self.final = kept, paired, far, final
        self.send, self.recv = send, recv
        self.half = rows // 2
        self.low, self.high = pl.ds(0, self.half), pl.ds(self.half, self.half)
        self.sends, self.near = [], []

    def add_pair(self, i):
        kept, paired = self.kept, self.paired
        self.source.ready(i)

        def step(at):
            kept[i, at, :] = (kept[i, at, :].astype(f32) + paired[i, at, :].astype(f32)).astype(
                bf16
            )

        over_rows(self.rows, step)

    def put(self, src, dst, i, to):
        copy = remote(self.p, src, dst, self.send, self.recv, i, to)
        copy.start()
        self.sends.append(copy)
        return copy

    def first(self):
        kept, far, final, low, high = self.kept, self.far, self.final, self.low, self.high
        self.add_pair(3)
        self.far_x = self.put(kept.at[3, low], far.at[0], 4, "xp")
        self.far_y = self.put(kept.at[3, high], far.at[1], 5, "yp")
        self.add_pair(1)
        self.near.append(self.put(kept.at[1, low], final.at[0, low], 6, "xp"))
        self.add_pair(2)
        self.near.append(self.put(kept.at[2, high], final.at[1, high], 7, "yp"))

    def second(self):
        kept, far, final, low, high = self.kept, self.far, self.final, self.low, self.high
        half = self.half
        self.far_x.wait_recv()

        def step_x(at):
            kept[2, at, :] = (kept[2, at, :].astype(f32) + far[0, at, :].astype(f32)).astype(bf16)

        over_rows(half, step_x)
        self.near.append(self.put(kept.at[2, low], final.at[1, low], 8, "yp"))
        self.far_y.wait_recv()

        def step_y(at):
            up = pl.ds(pl.multiple_of(at.start + half, BLOCK), BLOCK)
            kept[1, up, :] = (kept[1, up, :].astype(f32) + far[1, at, :].astype(f32)).astype(bf16)

        over_rows(half, step_y)
        self.near.append(self.put(kept.at[1, high], final.at[0, high], 9, "xp"))
        self.source.ready(0)

    def third(self):
        for copy in self.near:
            copy.wait_recv()

    def finish(self):
        self.source.finish()
        for copy in self.sends:
            copy.wait_send()


def scatter_plane(p, source, rows, kept, paired, far, final, send, recv, between, meanwhile):
    sums = PlaneSum(p, source, rows, kept, paired, far, final, send, recv)
    sums.first()
    between()
    sums.second()
    meanwhile()
    sums.third()
    return sums


def total(kept, paired, final, at):
    return (kept[0, at, :].astype(f32) + paired[0, at, :].astype(f32)) + (
        final[0, at, :].astype(f32) + final[1, at, :].astype(f32)
    )


def reduce_plane(terms):
    rows = terms.shape[1]
    return lax.psum_scatter(terms, "seq", scatter_dimension=0, tiled=False).astype(f32).reshape(
        rows, terms.shape[2]
    )


def rms_scale(values):
    return lax.rsqrt(jnp.mean(values * values, axis=-1, keepdims=True) + norm_eps)


def norm_back(values, scale, gain, grad):
    weighted = grad * gain
    inner = jnp.mean(weighted * values, axis=-1, keepdims=True)
    return (
        scale * weighted - values * (scale * scale * scale) * inner,
        jnp.sum(grad * values * scale, axis=0, keepdims=True),
    )


def swap_halves(v, first):
    width = v.shape[-1]
    return jnp.where(first, pltpu.roll(v, width - HD // 2, 1), pltpu.roll(v, HD // 2, 1))


def dot_t(a, b):
    return lax.dot_general(a, b, (((1,), (1,)), ((), ())), preferred_element_type=f32)


def dot(a, b):
    return jnp.dot(a, b, preferred_element_type=f32)


def dot_l(a, b):
    return lax.dot_general(a, b, (((0,), (0,)), ((), ())), preferred_element_type=f32)


def allowed_pairs(start, keys, queries, offset):
    key = lax.broadcasted_iota(jnp.int32, (keys, queries), 0)
    query = lax.broadcasted_iota(jnp.int32, (keys, queries), 1) + offset
    return (key >= start) & (key <= query)


def attend_pair(pre, cos, sin, starts, rotated, attended, stats, r, pair):
    shards, _, shard_len, _ = pre.shape
    length = shards * shard_len
    block = min(256, length)
    per = block // shard_len
    lanes = lambda i: pl.ds(pl.multiple_of((pair * 3 + i) * PAIR, PAIR), PAIR)
    first = lax.rem(lax.broadcasted_iota(jnp.int32, (length, PAIR), 1), HD) < HD // 2
    cos_all, sin_all = cos[:, r].reshape(length, PAIR), sin[:, r].reshape(length, PAIR)

    def rotate(i):
        v = pre[:, r, :, lanes(i)].reshape(length, PAIR)
        return (v * cos_all + swap_halves(v, first) * sin_all).astype(bf16)

    query, key = rotate(0), rotate(1)
    value = pre[:, r, :, lanes(2)].reshape(length, PAIR)
    value_t = value.T.astype(bf16)
    for i, v in enumerate((query, key, value.astype(bf16))):
        rotated[:, r, :, lanes(i)] = v.reshape(shards, shard_len, PAIR)
    left = lax.broadcasted_iota(jnp.int32, (block, PAIR), 1) < HD
    top = lax.broadcasted_iota(jnp.int32, (PAIR, block), 0) < HD
    scaled = query * jnp.asarray(0.125, bf16)
    here_lanes = pl.ds(pl.multiple_of(pair * PAIR, PAIR), PAIR)
    for i in range(length // block):
        keys = (i + 1) * block
        at = slice(i * block, (i + 1) * block)
        mask = allowed_pairs(starts[:, at], keys, block, i * block)
        here = scaled[at]
        results = []
        for h in range(2):
            own = jnp.where(left if h == 0 else ~left, here, jnp.zeros_like(here))
            scores = jnp.where(mask, dot_t(key[:keys], own), -1e30)
            peak = jnp.max(scores, axis=0, keepdims=True)
            shifted = jnp.exp(scores - peak)
            summed = jnp.sum(shifted, axis=0, keepdims=True)
            probs = (shifted * (1.0 / summed)).astype(bf16)
            results.append(dot(value_t[:, :keys], probs))
            stats[r, pair, h : h + 1, at] = peak + jnp.log(summed)
        merged = jnp.where(top, results[0], results[1]).T.astype(bf16)
        attended[i * per : (i + 1) * per, r, :, here_lanes] = merged.reshape(
            per, shard_len, PAIR
        )


def attend_kernel(pre, cos, sin, starts, rotated, attended, stats):
    attend_pair(pre, cos, sin, starts[0], rotated, attended, stats, 0, 0)


def attend(pre, cos, sin, starts):
    shards, rows, shard_len, width = pre.shape
    pairs = width // (3 * PAIR)
    length = shards * shard_len
    wide = pl.BlockSpec((shards, 1, shard_len, 3 * PAIR), lambda r, p: (0, r, 0, p))
    narrow = pl.BlockSpec((shards, 1, shard_len, PAIR), lambda r, p: (0, r, 0, p))
    table = pl.BlockSpec((shards, 1, shard_len, PAIR), lambda r, p: (0, r, 0, 0))
    return pl.pallas_call(
        attend_kernel,
        grid=(rows, pairs),
        out_shape=[
            jax.ShapeDtypeStruct(pre.shape, bf16),
            jax.ShapeDtypeStruct((shards, rows, shard_len, pairs * PAIR), bf16),
            jax.ShapeDtypeStruct((rows, pairs, 2, length), f32),
        ],
        in_specs=[wide, table, table, pl.BlockSpec((1, 1, length), lambda r, p: (r, 0, 0))],
        out_specs=[wide, narrow, pl.BlockSpec((1, 1, 2, length), lambda r, p: (r, p, 0, 0))],
        compiler_params=pltpu.CompilerParams(vmem_limit_bytes=48 * MIB),
        cost_estimate=pl.CostEstimate(
            flops=rows * pairs * 2 * length * length * 256 * 2,
            bytes_accessed=pre.size * 8,
            transcendentals=rows * pairs * length * length,
        ),
    )(pre, cos, sin, starts)


def attend_back_pair(rotated, grad, cos, sin, starts, stats, result, key_acc, value_acc, r, pair):
    shards, _, shard_len, _ = rotated.shape
    length = shards * shard_len
    block = min(256, length)
    per = block // shard_len
    lanes = lambda i: pl.ds(pl.multiple_of((pair * 3 + i) * PAIR, PAIR), PAIR)
    query, key, value = (rotated[:, r, :, lanes(i)].reshape(length, PAIR) for i in range(3))
    grad_all = grad[:, r, :, pl.ds(pl.multiple_of(pair * PAIR, PAIR), PAIR)].reshape(length, PAIR)
    key_t = key.astype(f32).T.astype(bf16)
    left = lax.broadcasted_iota(jnp.int32, (block, PAIR), 1) < HD
    top = lax.broadcasted_iota(jnp.int32, (PAIR, block), 0) < HD
    first = lax.rem(lax.broadcasted_iota(jnp.int32, (length, PAIR), 1), HD) < HD // 2
    key_acc[...] = jnp.zeros_like(key_acc)
    value_acc[...] = jnp.zeros_like(value_acc)

    for i in range(length // block):
        keys = (i + 1) * block
        at = slice(i * block, (i + 1) * block)
        here = slice(i * per, (i + 1) * per)
        mask = allowed_pairs(starts[:, at], keys, block, i * block)
        results = []
        for h in range(2):
            side = left if h == 0 else ~left
            own = jnp.where(side, query[at], jnp.zeros_like(query[at]))
            own_grad = jnp.where(side, grad_all[at], jnp.zeros_like(grad_all[at]))
            scores = dot_t(key[:keys], own * jnp.asarray(0.125, bf16))
            probs = jnp.exp(jnp.where(mask, scores - stats[r, pair, h : h + 1, at], -1e30))
            grad_probs = dot_t(value[:keys], own_grad)
            inner = jnp.sum(probs * grad_probs, axis=0, keepdims=True)
            grad_scores = (probs * (grad_probs - inner) * 0.125).astype(bf16)
            key_acc[:keys, :] += dot(grad_scores, own)
            value_acc[:keys, :] += dot(probs.astype(bf16), own_grad)
            results.append(dot(key_t[:, :keys], grad_scores))
        merged = jnp.where(top, results[0], results[1]).T
        cos_here, sin_here = cos[here, r].reshape(block, PAIR), sin[here, r].reshape(block, PAIR)
        turned = merged * cos_here - swap_halves(merged, first[:block]) * sin_here
        result[here, r, :, lanes(0)] = turned.astype(bf16).reshape(per, shard_len, PAIR)
    cos_all, sin_all = cos[:, r].reshape(length, PAIR), sin[:, r].reshape(length, PAIR)
    key_grad = key_acc[...]
    turned = key_grad * cos_all - swap_halves(key_grad, first) * sin_all
    result[:, r, :, lanes(1)] = turned.astype(bf16).reshape(shards, shard_len, PAIR)
    result[:, r, :, lanes(2)] = value_acc[...].astype(bf16).reshape(shards, shard_len, PAIR)


def attend_back_kernel(rotated, grad, cos, sin, starts, stats, result, key_acc, value_acc):
    attend_back_pair(
        rotated, grad, cos, sin, starts[0], stats, result, key_acc, value_acc, 0, 0
    )


def attend_back(rotated, grad, cos, sin, starts, stats):
    shards, rows, shard_len, width = rotated.shape
    pairs = width // (3 * PAIR)
    length = shards * shard_len
    wide = pl.BlockSpec((shards, 1, shard_len, 3 * PAIR), lambda r, p: (0, r, 0, p))
    narrow = pl.BlockSpec((shards, 1, shard_len, PAIR), lambda r, p: (0, r, 0, p))
    table = pl.BlockSpec((shards, 1, shard_len, PAIR), lambda r, p: (0, r, 0, 0))
    return pl.pallas_call(
        attend_back_kernel,
        grid=(rows, pairs),
        out_shape=jax.ShapeDtypeStruct(rotated.shape, bf16),
        in_specs=[
            wide,
            narrow,
            table,
            table,
            pl.BlockSpec((1, 1, length), lambda r, p: (r, 0, 0)),
            pl.BlockSpec((1, 1, 2, length), lambda r, p: (r, p, 0, 0)),
        ],
        out_specs=wide,
        scratch_shapes=[pltpu.VMEM((length, PAIR), f32), pltpu.VMEM((length, PAIR), f32)],
        compiler_params=pltpu.CompilerParams(vmem_limit_bytes=48 * MIB),
        cost_estimate=pl.CostEstimate(
            flops=rows * pairs * 5 * length * length * 256 * 2,
            bytes_accessed=rotated.size * 6,
            transcendentals=rows * pairs * length * length,
        ),
    )(rotated, grad, cos, sin, starts, stats)


def document_starts(doc_ids):
    places = lax.broadcasted_iota(jnp.int32, doc_ids.shape, 1)
    earlier = jnp.concatenate([doc_ids[:, :1], doc_ids[:, :-1]], axis=1)
    return lax.cummax(jnp.where(doc_ids != earlier, places, 0), axis=1)


def rope_frequency():
    return rope_base ** (-(jnp.arange(HD // 2, dtype=f32) * 2.0 / HD))


def rope_tables(starts, shards):
    rows, length = starts.shape
    positions = (lax.broadcasted_iota(jnp.int32, starts.shape, 1) - starts).astype(f32)
    angles = positions[..., None] * rope_frequency()
    cos, sin = jnp.cos(angles), jnp.sin(angles)
    lay = lambda v: jnp.moveaxis(
        jnp.concatenate(v, axis=-1).reshape(rows, shards, length // shards, PAIR), 0, 1
    )
    return lay([cos] * 4), lay([-sin, sin, -sin, sin])


class LineSum:
    def __init__(self, p, view, land, send, recv, base):
        self.p, self.view, self.land = p, view, land
        self.send, self.recv, self.base = send, recv, base
        self.z = p["dp"]
        self.inward = 1 - 2 * lax.div(self.z, 2)
        self.end = (self.z == 0) | (self.z == 3)

    def copy(self, src, slot, i, to):
        return pltpu.make_async_remote_copy(
            src_ref=src,
            dst_ref=self.land.at[slot],
            send_sem=self.send.at[self.base + i],
            recv_sem=self.recv.at[self.base + slot],
            device_id=(to, self.p["me"]),
            device_id_type=MESH,
        )

    def arrived(self, slot):
        self.copy(self.land.at[slot], slot, 0, self.z).wait_recv()

    def first(self):
        z, inward = self.z, self.inward

        @pl.when(self.end)
        def _():
            near, mid, far = z + inward, z + 2 * inward, z + 3 * inward
            self.copy(self.view(far), near, 0, near).start()
            self.copy(self.view(mid), far, 1, near).start()
            self.copy(self.view(near), z, 2, near).start()

    def second(self, acc, extra, local, i):
        z, inward = self.z, self.inward

        @pl.when(jnp.logical_not(self.end))
        def _():
            outer, inner, far = z - inward, z + inward, z + 2 * inward
            own = [
                pltpu.make_async_copy(self.view(to), acc.at[k], local.at[i + k])
                for k, to in enumerate((far, inner))
            ]
            other = [
                pltpu.make_async_copy(self.land.at[slot], extra.at[k], local.at[i + 2 + k])
                for k, slot in enumerate((z, far))
            ]
            for copy in own:
                copy.start()
            for k, slot in enumerate((z, far)):
                self.arrived(slot)
                other[k].start()
            for k, to in enumerate((far, inner)):
                own[k].wait()
                other[k].wait()

                def step(at):
                    acc[k, at, :] = (acc[k, at, :].astype(f32) + extra[k, at, :].astype(f32)).astype(
                        bf16
                    )

                over_rows(acc.shape[1], step)
                self.copy(acc.at[k], z, k, to).start()
            self.copy(self.view(outer), z, 2, outer).start()

    def total(self, parts, local, i):
        z, inward = self.z, self.inward
        one = jnp.where(self.end, z + 2 * inward, z - inward)
        two = z + inward
        loads = [pltpu.make_async_copy(self.view(z), parts.at[0], local.at[i])]
        loads[0].start()
        for k, slot in ((1, one), (2, two)):
            self.arrived(slot)
            loads.append(pltpu.make_async_copy(self.land.at[slot], parts.at[k], local.at[i + k]))
            loads[k].start()
        for load in loads:
            load.wait()

        def step(at):
            parts[0, at, :] = (
                (parts[0, at, :].astype(f32) + parts[1, at, :].astype(f32))
                + parts[2, at, :].astype(f32)
            ).astype(bf16)

        over_rows(parts.shape[1], step)

    def finish(self):
        for i in range(3):
            self.copy(self.land.at[0], 0, i, self.z).wait_send()


LINE_SEMS = 5


class LineGather:
    def __init__(self, p, src, out, send, recv, base, own=None):
        self.p, self.src, self.out = p, src, out
        self.send, self.recv, self.base = send, recv, base * LINE_SEMS
        self.z = p["dp"]
        self.inward = 1 - 2 * lax.div(self.z, 2)
        self.end = (self.z == 0) | (self.z == 3)
        self.own = None if own is None else pltpu.make_async_copy(src, out.at[self.z], own)

    def copy(self, src, owner, i, to):
        return pltpu.make_async_remote_copy(
            src_ref=src,
            dst_ref=self.out.at[owner],
            send_sem=self.send.at[self.base + i],
            recv_sem=self.recv.at[self.base + owner],
            device_id=(to, self.p["me"]),
            device_id_type=MESH,
        )

    def arrived(self, owner):
        self.copy(self.src, owner, 0, self.z).wait_recv()

    def start(self):
        z, inward = self.z, self.inward
        if self.own is not None:
            self.own.start()
        self.copy(self.src, z, 0, z + inward).start()

        @pl.when(jnp.logical_not(self.end))
        def _():
            self.copy(self.src, z, 1, z - inward).start()

    def second(self):
        z, inward = self.z, self.inward

        @pl.when(jnp.logical_not(self.end))
        def _():
            outer, inner = z - inward, z + inward
            self.arrived(inner)
            self.copy(self.out.at[inner], inner, 2, outer).start()
            self.arrived(outer)
            self.copy(self.out.at[outer], outer, 3, inner).start()

    def third(self):
        z, inward = self.z, self.inward

        @pl.when(jnp.logical_not(self.end))
        def _():
            far = z + 2 * inward
            self.arrived(far)
            self.copy(self.out.at[far], far, 4, z - inward).start()

    def finish(self):
        z, inward = self.z, self.inward

        @pl.when(self.end)
        def _():
            for k in range(1, 4):
                self.arrived(z + k * inward)

        if self.own is not None:
            self.own.wait()
        self.copy(self.src, 0, 0, z).wait_send()

        @pl.when(jnp.logical_not(self.end))
        def _():
            for i in range(1, 5):
                self.copy(self.src, 0, i, z).wait_send()


CHUNKS = 4
OTHERS = ("dg", "ds", "xp", "yp", "xs", "ys", "sib")


def meet_all(p, devices):
    mine = p["dp"] * 8 + p["me"]
    barrier = pltpu.get_barrier_semaphore()

    def other(k):
        to = lax.rem(mine + k, devices)
        return dict(device_id=(lax.div(to, 8), lax.rem(to, 8)), device_id_type=MESH), to

    @pl.loop(1, devices)
    def _(k):
        pl.semaphore_signal(barrier, inc=1, **other(k)[0])

    return other, lambda: pl.semaphore_wait(barrier, devices - 1)


class Local:
    def __init__(self, sems):
        self.sems, self.used, self.free = sems, 0, []

    def take(self, count=1):
        if count == 1 and self.free:
            return self.free.pop(0)
        self.used += count
        assert self.used <= self.sems.shape[0], self.used
        return self.used - count


class Produced:
    def __init__(self, p, produce, stage, kept, paired, send, recv):
        self.p, self.produce, self.stage = p, produce, stage
        self.kept, self.paired, self.send, self.recv = kept, paired, send, recv
        self.pairs = {}

    def ready(self, i):
        k = len(self.pairs)
        _, own, other = ORDER[k]
        rows = self.kept.shape[1]
        stage = self.stage.at[pl.ds(k % 2 * rows, rows)]
        if k >= 2:
            self.pairs[ORDER[k - 2][0]].wait_send()
        self.produce(other, stage)
        self.pairs[i] = remote(self.p, stage, self.paired.at[i], self.send, self.recv, i, "sib")
        self.pairs[i].start()
        self.produce(own, self.kept.at[i])
        self.pairs[i].wait_recv()

    def finish(self):
        for i, _, _ in ORDER[2:]:
            if i in self.pairs:
                self.pairs[i].wait_send()


MAIN_INPUTS = (
    "w_query",
    "w_key",
    "w_value",
    "w_gate",
    "w_up",
    "w_out",
    "w_down",
    "tokens",
    "own_cot",
    "gains",
    "starts",
    "frequency",
)
RESULTS = (
    "gain_sums",
    "grad_tokens",
    "out_tokens",
    "grad_query",
    "grad_key",
    "grad_value",
    "grad_out",
    "grad_gate",
    "grad_up",
    "grad_down",
)
HELD_IN_HBM = (
    "cos",
    "sin",
    "rotated",
    "attended",
    "normed_one",
    "cot",
    "branch",
    "qkv",
    "out_weight",
    "units",
    "down",
    "out_terms",
    "unit_sums",
    "unit_terms",
    "down_terms",
    "kept_units",
    "kept_acts",
    "head_terms",
    "wo_terms",
    "head_sums",
    "unit_land",
    "down_land",
    "head_land",
    "wo_land",
    "units_out",
    "heads_out",
)
SCATTER_NAMES = ("kept", "paired", "far", "final", "send", "recv")
GATHER_NAMES = tuple(k + way for k in "ac" for way in ("send", "recv"))
MAIN_OUTPUTS = RESULTS + HELD_IN_HBM
MAIN_SCRATCH = (
    "hidden",
    "grad_hidden",
    "gain_one",
    "gain_two",
    "gain_term",
    "stats",
    "gains_land",
    "gain_mine",
    "gain_sum_land",
    "x",
    "unit_acc",
    "down_acc",
    "mine",
    "stage",
    "kept",
    "paired",
    "far",
    "final",
    "send",
    "recv",
    "asend",
    "arecv",
    "csend",
    "crecv",
    "gsend",
    "grecv",
    "esend",
    "erecv",
    "zsend",
    "zrecv",
    "ssend",
    "srecv",
    "ready",
    "local",
)


def main_kernel(groups, *refs):
    r = types.SimpleNamespace(**dict(zip(MAIN_INPUTS + MAIN_OUTPUTS + MAIN_SCRATCH, refs)))
    p = plane()
    devices = groups * 8
    other, met = meet_all(p, devices)
    shards = 8
    rows, width = r.tokens.shape
    held = r.w_query.shape[0]
    batch, shard_len, wide = r.rotated.shape[1:]
    pairs = width // 8 // PAIR
    piece, chunk = r.down.shape[2], r.units.shape[3]
    part = chunk // 2
    me, z = p["me"], p["dp"]
    mine_index = z * 8 + me
    held_at = pl.ds(pl.multiple_of(me * held, held), held)
    sems = Local(r.local)
    x = r.x

    lent = {}

    def move(src, dst, i=None):
        place = sems.take() if i is None else i
        copy = pltpu.make_async_copy(src, dst, r.local.at[place])
        if i is None:
            lent[id(copy)] = (copy, place)
        return copy

    def start(*copies):
        for copy in copies:
            copy.start()
        return copies

    def wait(copies):
        for copy in copies:
            copy.wait()
        for copy in copies:
            if id(copy) in lent:
                sems.free.append(lent.pop(id(copy))[1])

    def shard_rows(s, count=1):
        return pl.ds(pl.multiple_of(s * rows, rows), count * rows)

    def line(src, out, i, own):
        sem = r.local.at[sems.take()] if own else None
        return LineGather(p, src, out, r.zsend, r.zrecv, i, sem)

    wo_line = line(r.w_out, r.out_weight, 0, True)
    qkv_line = line(r.qkv.at[z], r.qkv, 1, False)
    chunk_lines = [
        (
            line(r.units.at[j, z], r.units.at[j], 2 + 2 * j, False),
            line(r.w_down.at[pl.ds(j * piece, piece)], r.down.at[j], 3 + 2 * j, True),
        )
        for j in range(CHUNKS)
    ]

    def serve(j, what, *only):
        for k in only or (0, 1):
            getattr(chunk_lines[j][k], what)()

    def gain_copy(k, sender):
        return pltpu.make_async_remote_copy(
            src_ref=r.gains,
            dst_ref=r.gains_land.at[sender],
            send_sem=r.gsend.at[k],
            recv_sem=r.grecv.at[sender],
            **other(k)[0],
        )

    def exchange(block, out, i):
        copies = [
            remote(p, block(p[name]), out, r.esend, r.erecv, i * 7 + j, name)
            for j, name in enumerate(OTHERS)
        ]
        return start(*copies, move(block(me), out))

    def of_owner(ref, count):
        return lambda owner: ref.at[pl.ds(pl.multiple_of(owner * count, count), count)]

    def scatter(produce, between, meanwhile):
        source = Produced(p, produce, r.stage, r.kept, r.paired, r.send, r.recv)
        return scatter_plane(
            p, source, rows, r.kept, r.paired, r.far, r.final, r.send, r.recv, between, meanwhile
        )

    def before(
        w_query, w_key, w_value, w_gate, w_up, cos, sin, head_blocks, unit_blocks, w, wo, pre, rotated, attended
    ):
        head_loads = start(move(r.w_query, w_query), move(r.w_key, w_key), move(r.w_value, w_value))
        unit_loads = start(move(r.w_gate, w_gate), move(r.w_up, w_up))
        wait(head_loads)
        for s in range(shards):
            for pair in range(pairs):
                for i, weight in enumerate((w_query, w_key, w_value)):
                    head = lambda k: ((2 * pair + k) * 8 + s) * HD
                    base = (pair * 3 + i) * PAIR
                    head_blocks[s, :, base : base + PAIR] = jnp.concatenate(
                        [weight[:, head(k) : head(k) + HD] for k in range(2)], axis=1
                    )
        met()

        @pl.loop(1, devices)
        def _(k):
            gain_copy(k, mine_index).start()

        r.gains_land[mine_index] = r.gains[...]
        head_copies = exchange(lambda s: head_blocks.at[s], r.qkv.at[z, held_at], 0)
        wait(unit_loads)
        for s in range(shards):
            for i, weight in enumerate((w_gate, w_up)):
                for j in range(CHUNKS):
                    for pair in range(groups // 2):
                        unit = lambda k: ((2 * pair + k) * 8 + s) * CHUNKS * piece + j * piece
                        base = i * groups * piece + pair * 2 * piece
                        unit_blocks[s, j, :, base : base + 2 * piece] = jnp.concatenate(
                            [weight[:, unit(k) : unit(k) + piece] for k in range(2)], axis=1
                        )

        @pl.loop(1, devices)
        def _(k):
            gain_copy(k, lax.rem(mine_index + devices - k, devices)).wait()

        for out, base in ((r.gain_one, 0), (r.gain_two, held)):
            for k in range(0, devices, 2):
                out[:, k * held : (k + 2) * held] = jnp.concatenate(
                    [r.gains_land[k + i, 0:1, base : base + held] for i in range(2)], axis=1
                )

        def norm_tokens(at):
            t = r.tokens[at, :].astype(f32)
            scale = lax.rsqrt(jnp.mean(t * t, axis=-1, keepdims=True) + norm_eps)
            r.mine[at, :] = (t * scale * r.gain_one[...]).astype(bf16)

        over_rows(rows, norm_tokens)
        wait(head_copies)
        qkv_line.start()
        n1_sent = gather_start(p, r.mine, x, r.asend, r.arecv, 0)
        n1_own = start(move(r.mine, x.at[shard_rows(me)]))
        n1_late = gather_forward(p, n1_sent, x, r.asend, r.arecv, 0, qkv_line.second)
        qkv_line.third()
        wo_line.start()
        unit_exchange = lambda j: exchange(
            lambda s: unit_blocks.at[s, j], r.units.at[j, z, held_at], 1 + j
        )
        unit_copies = [unit_exchange(0)]

        def halfway():
            for j in range(1, CHUNKS):
                unit_copies.append(unit_exchange(j))

        gather_wait(n1_sent, n1_late, halfway)
        wait(n1_own)
        wait(unit_copies[0])
        serve(0, "start")
        keep_normed = start(
            *[move(x.at[shard_rows(s)], r.normed_one.at[s]) for s in range(shards)]
        )
        for row in range(batch):
            length = shards * shard_len
            since = jnp.broadcast_to(r.starts[row].astype(f32), (PAIR, length)).T
            place = lax.broadcasted_iota(jnp.int32, (length, PAIR), 0).astype(f32)
            angles = (place - since) * r.frequency[...]
            lane = lax.broadcasted_iota(jnp.int32, (length, PAIR), 1)
            sign = jnp.where(lax.rem(lane, HD) < HD // 2, -1.0, 1.0)
            cos[:, row] = jnp.cos(angles).reshape(shards, shard_len, PAIR)
            sin[:, row] = (sign * jnp.sin(angles)).reshape(shards, shard_len, PAIR)
        keep_tables = start(move(cos, r.cos), move(sin, r.sin))
        wo_line.second()
        qkv_line.finish()
        wait(start(move(r.qkv, w)))

        @pl.loop(0, shards, step=2)
        def _(s):
            here = dot(x[shard_rows(s, 2)], w[...].reshape(width, wide))
            pre[pl.ds(s, 2)] = here.reshape((2,) + pre.shape[1:])

        for copies in unit_copies[1:]:
            wait(copies)
        wo_line.third()
        cot_sent = gather_start(p, r.own_cot, r.cot, r.csend, r.crecv, 0)
        cot_own = start(move(r.own_cot, r.cot.at[me]))

        def attention(row):
            @pl.loop(0, pairs)
            def _(pair):
                attend_pair(
                    pre, cos, sin, r.starts[row], rotated, attended, r.stats, row, pair
                )

        attention(0)
        serve(0, "second")
        serve(1, "start")
        attention(1)
        cot_late = gather_forward(p, cot_sent, r.cot, r.csend, r.crecv, 0)
        keep_heads = start(move(rotated, r.rotated), move(attended, r.attended))
        wo_line.finish()
        wait(keep_normed)
        wait(start(move(r.out_weight, wo)))

        def produce(name, out):
            terms = attended[p[name]].reshape(rows, attended.shape[3])

            @pl.loop(0, width // 512)
            def _(n):
                at = pl.ds(pl.multiple_of(n * 512, 512), 512)
                out[:, at] = dot(terms, wo[:, :, at].reshape(terms.shape[1], 512)).astype(bf16)

        def between():
            serve(0, "third")
            serve(1, "second")
            serve(2, "start")

        def meanwhile():
            gather_wait(cot_sent, cot_late)
            wait(cot_own)

        scatter(produce, between, meanwhile).finish()
        wait(keep_heads)
        wait(keep_tables)

    vm = lambda shape, dtype=bf16: pltpu.VMEM(shape, dtype)
    pl.run_scoped(
        before,
        *[vm(ref.shape) for ref in (r.w_query, r.w_key, r.w_value, r.w_gate, r.w_up)],
        *[vm(ref.shape, f32) for ref in (r.cos, r.sin)],
        vm((shards, held, wide)),
        vm((shards, CHUNKS, held, chunk)),
        vm(r.qkv.shape),
        vm(r.out_weight.shape),
        vm(r.rotated.shape, f32),
        vm(r.rotated.shape),
        vm(r.attended.shape),
    )

    def norm_hidden(at):
        h = r.tokens[at, :].astype(f32) + total(r.kept, r.paired, r.final, at)
        r.hidden[at, :] = h
        scale = lax.rsqrt(jnp.mean(h * h, axis=-1, keepdims=True) + norm_eps)
        r.mine[at, :] = (h * scale * r.gain_two[...]).astype(bf16)

    over_rows(rows, norm_hidden)
    n2_sent = gather_start(p, r.mine, x, r.asend, r.arecv, 0)
    n2_own = start(move(r.mine, x.at[shard_rows(me)]))

    span = r.unit_land.shape[2]
    sum_lines = [
        (
            LineSum(
                p, of_owner(r.unit_terms.at[j], span), r.unit_land.at[j], r.ssend, r.srecv, 8 * j
            ),
            LineSum(
                p,
                of_owner(r.down_terms.at[j], piece),
                r.down_land.at[j],
                r.ssend,
                r.srecv,
                8 * j + 4,
            ),
        )
        for j in range(CHUNKS)
    ]
    head_lines = [
        LineSum(
            p, of_owner(r.head_terms.at[k], span), r.head_land.at[k], r.ssend, r.srecv, 8 * CHUNKS + 4 * k
        )
        for k in range(pairs)
    ]
    wo_sum = LineSum(
        p, of_owner(r.wo_terms, held), r.wo_land, r.ssend, r.srecv, 8 * CHUNKS + 4 * pairs
    )

    chunk_sem, keep_sem, term_sem, kept_sem, act_sem, out_sem, z_sem = (
        sems.take(k) for k in (4, 2, 2, 2, 2, 2, 8)
    )

    def after(
        c,
        w,
        d,
        unit_stage,
        act_stage,
        unit_kept,
        act_kept,
        unit_grad,
        down_grad,
        unit_parts,
        down_parts,
    ):
        def chunk_loads(j):
            return (
                move(r.units.at[j], w.at[j % 2], chunk_sem + j % 2),
                move(r.down.at[j], d.at[j % 2], chunk_sem + 2 + j % 2),
            )

        def pass_on(j):
            sum_lines[j][0].second(r.unit_acc.at[j], unit_parts, r.local, z_sem)
            sum_lines[j][1].second(r.down_acc.at[j], down_parts, r.local, z_sem + 4)

        def keep(j, what):
            for copy in (
                move(unit_stage, r.kept_units.at[:, pl.ds(j * chunk, chunk)], keep_sem),
                move(act_stage, r.kept_acts.at[:, pl.ds(j * part, part)], keep_sem + 1),
            ):
                getattr(copy, what)()

        def work(j):
            slot = j % 2
            wait(chunk_loads(j))
            if j > 0:
                keep(j - 1, "wait")

            @pl.loop(0, shards, step=2)
            def _(s):
                both = shard_rows(s, 2)
                pre = dot(x[both], w[slot].reshape(width, chunk))
                grad_act = dot_t(c[both], d[slot].reshape(part, width))
                gate, up = pre[:, :part], pre[:, part:]
                sigmoid = 1.0 / (1.0 + jnp.exp(-gate))
                silu = gate * sigmoid
                act_stage[both] = (silu * up).astype(bf16)
                unit_stage[both, :part] = (
                    grad_act * up * sigmoid * (1.0 + gate * (1.0 - sigmoid))
                ).astype(bf16)
                unit_stage[both, part:] = (grad_act * silu).astype(bf16)

            keep(j, "start")

        def weigh_units(j):
            @pl.loop(0, width // 512)
            def _(n):
                at = pl.ds(pl.multiple_of(n * 512, 512), 512)
                unit_grad[at] = dot_l(x[:, at], unit_stage[...]).astype(bf16)

            wait(start(move(unit_grad, r.unit_terms.at[j], term_sem)))
            sum_lines[j][0].first()

        def weigh_down(j):
            @pl.loop(0, width // 512)
            def _(n):
                at = pl.ds(pl.multiple_of(n * 512, 512), 512)
                down_grad[:, at] = dot_l(act_stage[...], c[:, at]).astype(bf16)

            wait(start(move(down_grad, r.down_terms.at[j], term_sem + 1)))
            sum_lines[j][1].first()

        c_loads = start(*[move(r.cot.at[s], c.at[shard_rows(s)]) for s in range(shards)])
        serve(0, "finish")
        start(*chunk_loads(0))
        n2_late = gather_forward(p, n2_sent, x, r.asend, r.arecv, 0)
        serve(1, "third")

        def next_chunks():
            serve(2, "second")
            serve(3, "start")

        gather_wait(n2_sent, n2_late, next_chunks)
        wait(n2_own)
        wait(c_loads)
        work(0)
        weigh_units(0)
        weigh_down(0)
        serve(1, "finish")
        start(*chunk_loads(1))
        work(1)
        serve(2, "third")
        weigh_down(1)
        serve(3, "second")
        weigh_units(1)
        serve(2, "finish")
        start(*chunk_loads(2))
        work(2)
        serve(3, "third")
        weigh_units(2)
        weigh_down(2)
        serve(3, "finish")
        start(*chunk_loads(3))
        work(3)
        weigh_down(3)
        load_w = start(
            *[
                move(
                    r.units.at[j, k // 2, pl.ds(k % 2 * rows, rows)],
                    c.at[shard_rows(k), pl.ds(j * chunk, chunk)],
                )
                for j in range(CHUNKS)
                for k in range(shards)
            ]
        )
        keep(CHUNKS - 1, "wait")
        order = [name for _, own, partner in ORDER for name in (partner, own)]

        def load_kept(k):
            return move(
                r.kept_units.at[shard_rows(p[order[k]])],
                unit_kept.at[pl.ds(k % 2 * rows, rows)],
                kept_sem + k % 2,
            )

        load_kept(0).start()

        def produce(name, out):
            k = order.index(name)
            load_kept(k).wait()
            if k + 1 < len(order):
                load_kept(k + 1).start()
            if k == 0:
                wait(load_w)

            @pl.loop(0, width // 1024)
            def _(n):
                at = pl.ds(pl.multiple_of(n * 1024, 1024), 1024)
                out[:, at] = dot_t(unit_kept[k % 2 * rows : (k % 2 + 1) * rows], c[at]).astype(
                    bf16
                )

        def act_load(s):
            slot = lax.rem(s, 2)
            return move(r.kept_acts.at[shard_rows(s)], act_kept.at[slot], act_sem + slot)

        def out_store(s):
            slot = lax.rem(s, 2)
            return move(r.stage.at[shard_rows(slot)], r.out_terms.at[s], out_sem + slot)

        def out_of_units():
            load_d = start(
                *[
                    move(r.down.at[j, k], x.at[pl.ds(j * part + k * piece, piece)])
                    for j in range(CHUNKS)
                    for k in range(groups)
                ]
            )
            act_load(0).start()
            wait(load_d)

            @pl.loop(0, shards)
            def _(s):
                act_load(s).wait()

                @pl.when(s + 1 < shards)
                def _():
                    act_load(s + 1).start()

                @pl.when(s >= 2)
                def _():
                    out_store(s - 2).wait()

                slot = lax.rem(s, 2)
                acts = act_kept[slot]

                @pl.loop(0, width // 1024)
                def _(n):
                    at = pl.ds(pl.multiple_of(n * 1024, 1024), 1024)
                    r.stage[shard_rows(slot), at] = dot(acts, x[: acts.shape[1], at]).astype(bf16)

                out_store(s).start()

            out_store(shards - 2).wait()
            out_store(shards - 1).wait()
            pass_on(2)

        def last_weights():
            weigh_units(3)
            pass_on(1)

        sums = scatter(produce, lambda: pass_on(0), last_weights)
        sums.source.finish()
        sums.source.pairs.clear()
        r.gain_term[...] = jnp.zeros_like(r.gain_term)

        def norm_back_rows(at):
            g = total(r.kept, r.paired, r.final, at)
            h = r.hidden[at, :]
            scale = lax.rsqrt(jnp.mean(h * h, axis=-1, keepdims=True) + norm_eps)
            weighted = g * r.gain_two[...]
            inner = jnp.mean(weighted * h, axis=-1, keepdims=True)
            back = scale * weighted - h * (scale * scale * scale * inner)
            out = r.own_cot[at, :].astype(f32) + back
            r.grad_hidden[at, :] = out
            r.mine[at, :] = out.astype(bf16)
            r.gain_term[...] += jnp.sum(g * h * scale, axis=0, keepdims=True)

        over_rows(rows, norm_back_rows)
        gather_start(p, r.mine, r.branch, r.asend, r.arecv, 0)
        out_of_units()
        sums.finish()

    pl.run_scoped(
        after,
        vm((shards * rows, width)),
        vm((2,) + r.units.shape[1:]),
        vm((2,) + r.down.shape[1:]),
        vm((shards * rows, chunk)),
        vm((shards * rows, part)),
        vm((2 * rows, CHUNKS * chunk)),
        vm((2, rows, CHUNKS * part)),
        vm((width, chunk)),
        vm((part, width)),
        vm((2, span, chunk)),
        vm((2, piece, width)),
    )

    b_own = start(move(r.mine, r.branch.at[me]))

    def end(
        rotated,
        attended,
        cos,
        sin,
        qkv,
        wo,
        grads,
        key_acc,
        value_acc,
        head_grad,
        wo_grad,
        units,
        heads,
        wide_out,
        row_out,
        narrow_out,
        gain_one_term,
        head_acc,
        wo_acc,
        parts,
        row_parts,
    ):
        loads = start(
            move(r.out_weight, wo),
            move(r.attended, attended),
            move(r.rotated, rotated),
            move(r.cos, cos),
            move(r.sin, sin),
            move(r.qkv, qkv),
        )
        narrow = parts.at[:, :, pl.ds(0, chunk)]

        def sum_up(j):
            sum_lines[j][0].total(narrow, r.local, z_sem)
            wait(start(move(parts.at[0, :, pl.ds(0, chunk)], r.unit_sums.at[j], z_sem)))
            copies = exchange(
                of_owner(r.unit_sums.at[j], held), r.units_out.at[j, me], 1 + j
            )
            sum_lines[j][1].total(row_parts, r.local, z_sem)
            row_out[...] = row_parts[0].astype(f32)
            wait(start(move(row_out, r.grad_down.at[pl.ds(j * piece, piece)], z_sem)))
            return copies

        def pass_on(j):
            sum_lines[j][0].second(
                r.unit_acc.at[j % 3], parts.at[1:3, :, pl.ds(0, chunk)], r.local, z_sem
            )
            sum_lines[j][1].second(r.down_acc.at[j % 3], row_parts.at[1:3], r.local, z_sem + 4)

        unit_copies = []
        b_sent = gather_copies(p, r.mine, r.branch, r.asend, r.arecv, 0)
        b_late = gather_forward(p, b_sent, r.branch, r.asend, r.arecv, 0)
        unit_copies += sum_up(0)
        gather_wait(b_sent, b_late)
        wait(b_own)
        wait(start(*[move(r.branch.at[s], x.at[shard_rows(s)]) for s in range(shards)]))
        out_sem_base = sems.take(4)
        out_source = FromMemory(
            p, r.out_terms, r.kept, r.paired, r.send, r.recv, r.local.at[pl.ds(out_sem_base, 4)]
        )
        out_sum = PlaneSum(
            p, out_source, rows, r.kept, r.paired, r.far, r.final, r.send, r.recv
        )
        wait(loads[:2])

        @pl.loop(0, shards, step=2)
        def _(s):
            grad = dot_t(x[shard_rows(s, 2)], wo[...].reshape(-1, width)).astype(bf16)
            grads[pl.ds(s, 2)] = grad.reshape((2,) + grads.shape[1:])

        out_sum.first()

        @pl.loop(0, width // 512)
        def _(n):
            at = pl.ds(pl.multiple_of(n * 512, 512), 512)
            acts = attended[...].reshape(shards * rows, -1)
            wo_grad[:, at] = dot_l(acts, x[:, at]).astype(bf16)

        keep_wo_terms = start(move(wo_grad, r.wo_terms))
        n1_loads = start(*[move(r.normed_one.at[s], x.at[shard_rows(s)]) for s in range(shards)])
        wait(loads[2:])

        def attention(pair):
            @pl.loop(0, batch)
            def _(row):
                attend_back_pair(
                    rotated,
                    grads,
                    cos,
                    sin,
                    r.starts[row],
                    r.stats,
                    rotated,
                    key_acc,
                    value_acc,
                    row,
                    pair,
                )

        def weigh_heads(pair):
            lanes = slice(pair * 3 * PAIR, (pair + 1) * 3 * PAIR)

            @pl.loop(0, width // 512)
            def _(n):
                at = pl.ds(pl.multiple_of(n * 512, 512), 512)
                grad = rotated[:, :, :, lanes].reshape(shards * rows, 3 * PAIR)
                head_grad[at] = dot_l(x[:, at], grad).astype(bf16)

            wait(start(move(head_grad, r.head_terms.at[pair])))
            head_lines[pair].first()

        attention(0)
        wait(n1_loads)
        weigh_heads(0)
        out_sum.second()
        for one in sum_lines[0]:
            one.finish()
        pass_on(CHUNKS - 1)
        for pair in range(1, pairs):
            attention(pair)
            weigh_heads(pair)
        out_sum.third()

        def step_out(at):
            out = r.hidden[at, :] + total(r.kept, r.paired, r.final, at)
            r.mine[at, :] = out.astype(bf16)

        over_rows(rows, step_out)
        keep_tokens = [*start(move(r.mine, r.out_tokens))]
        out_sum.finish()
        for name in ("sib", "xp", "yp"):
            pl.semaphore_signal(r.ready, inc=1, device_id=(z, p[name]), device_id_type=MESH)
        pl.semaphore_wait(r.ready, 3)

        def produce(name, out):
            grad = rotated[p[name]].reshape(rows, wide)

            @pl.loop(0, groups)
            def _(n):
                at = pl.ds(pl.multiple_of(n * span, span), span)
                out[:, at] = dot_t(grad, qkv[n]).astype(bf16)

        def pass_heads(k):
            head_lines[k].second(
                head_acc.at[k], parts.at[1:3, :, pl.ds(0, 3 * PAIR)], r.local, z_sem
            )

        def meanwhile():
            unit_copies.extend(sum_up(1))
            unit_copies.extend(sum_up(2))
            unit_copies.extend(sum_up(3))

        def between():
            pass_heads(1)
            wait(keep_wo_terms)
            wo_sum.first()

        pass_heads(0)
        sums = scatter(produce, between, meanwhile)
        gain_one_term[...] = jnp.zeros_like(gain_one_term)

        def norm_back_rows(at):
            g = total(r.kept, r.paired, r.final, at)
            t = r.tokens[at, :].astype(f32)
            scale = lax.rsqrt(jnp.mean(t * t, axis=-1, keepdims=True) + norm_eps)
            weighted = g * r.gain_one[...]
            inner = jnp.mean(weighted * t, axis=-1, keepdims=True)
            back = scale * weighted - t * (scale * scale * scale * inner)
            r.stage[at, :] = (r.grad_hidden[at, :] + back).astype(bf16)
            gain_one_term[...] += jnp.sum(g * t * scale, axis=0, keepdims=True)

        sums.source.finish()
        sums.source.pairs.clear()
        over_rows(rows, norm_back_rows)
        keep_tokens += start(move(r.stage.at[pl.ds(0, rows)], r.grad_tokens))
        r.gain_mine[...] = jnp.zeros_like(r.gain_mine)
        for k in range(devices):
            at = slice(k * held, (k + 1) * held)
            r.gain_mine[k, 0:1, :held] = gain_one_term[:, at]
            r.gain_mine[k, 1:2, :held] = r.gain_term[:, at]

        def gain_back(k):
            where, to = other(k)
            return pltpu.make_async_remote_copy(
                src_ref=r.gain_mine.at[to],
                dst_ref=r.gain_sum_land.at[k],
                send_sem=r.gsend.at[k],
                recv_sem=r.grecv.at[k],
                **where,
            )

        @pl.loop(1, devices)
        def _(k):
            gain_back(k).start()

        wo_sum.second(wo_acc, row_parts.at[1:3], r.local, z_sem)

        def sum_heads(k):
            head_lines[k].total(parts.at[:, :, pl.ds(0, 3 * PAIR)], r.local, z_sem)
            wait(start(move(parts.at[0, :, pl.ds(0, 3 * PAIR)], r.head_sums.at[k], z_sem)))
            return exchange(
                of_owner(r.head_sums.at[k], held), r.heads_out.at[k, me], 1 + CHUNKS + k
            )

        head_copies = [sum_heads(0)]
        wait(unit_copies)
        wait(start(move(r.units_out, units)))
        stores = []
        for i, out in enumerate((r.grad_gate, r.grad_up)):
            if i == 1:
                head_copies += [sum_heads(k) for k in range(1, pairs)]
            for k in range(groups):
                if len(stores) >= 2:
                    stores[-2].wait()
                for s in range(shards):
                    for a in range(CHUNKS // 2):
                        base = (i * groups + k) * piece
                        tile = jnp.concatenate(
                            [units[2 * a + b, s, :, base : base + piece] for b in range(2)], axis=1
                        )
                        at = (s * 2 + a) * 2 * piece
                        wide_out[k % 2, :, at : at + 2 * piece] = tile.astype(f32)
                span_out = wide_out.shape[2]
                stores.append(move(wide_out.at[k % 2], out.at[:, pl.ds(k * span_out, span_out)]))
                stores[-1].start()
        wo_sum.total(row_parts, r.local, z_sem)
        row_out[...] = row_parts[0].astype(f32)
        keep_wo = start(move(row_out, r.grad_out))
        r.gain_sum_land[0] = r.gain_mine[mine_index]

        @pl.loop(1, devices)
        def _(k):
            gain_back(k).wait()

        r.gain_sums[...] = jnp.sum(r.gain_sum_land[...], axis=0)
        for copies in head_copies:
            wait(copies)
        wait(start(move(r.heads_out, heads)))
        for i, out in enumerate((r.grad_query, r.grad_key, r.grad_value)):
            for k in range(groups):
                for s in range(0, shards, 2):
                    base = i * PAIR + k % 2 * HD
                    tile = jnp.concatenate(
                        [heads[k // 2, s + b, :, base : base + HD] for b in range(2)], axis=1
                    )
                    at = (k * shards + s) * HD
                    narrow_out[i, :, at : at + 2 * HD] = tile.astype(f32)
            stores.append(move(narrow_out.at[i], out))
            stores[-1].start()
        wait(stores[-5:])
        wait(keep_tokens)
        wait(keep_wo)
        for one in (*[one for pair in sum_lines[1:] for one in pair], wo_sum, *head_lines):
            one.finish()
        sums.finish()

    pl.run_scoped(
        end,
        vm(r.rotated.shape),
        vm(r.attended.shape),
        *[vm(ref.shape, f32) for ref in (r.cos, r.sin)],
        vm(r.qkv.shape),
        vm(r.out_weight.shape),
        vm(r.attended.shape),
        vm((shards * shard_len, PAIR), f32),
        vm((shards * shard_len, PAIR), f32),
        vm((width, 3 * PAIR)),
        vm(r.wo_terms.shape),
        vm(r.units_out.shape),
        vm(r.heads_out.shape),
        vm((2, held, width), f32),
        vm((piece, width), f32),
        vm((3, held, width), f32),
        vm((1, width), f32),
        vm((pairs, 2, span, 3 * PAIR)),
        vm((2, held, width)),
        vm((3, span, chunk)),
        vm((3, piece, width)),
    )


def main_plane(groups, shards, batch, tokens, cotangent, gains, weights, starts, collective_id):
    w_query, w_key, w_value, w_out, w_gate, w_up, w_down = weights
    shard_len = tokens.shape[0] // batch
    rows, width = tokens.shape
    held, devices = w_query.shape[0], groups * shards
    mine = width // shards
    wide = 3 * mine
    hidden_here = groups * w_down.shape[0]
    chunk = 2 * hidden_here // CHUNKS
    piece = w_down.shape[0] // CHUNKS
    span = width // groups
    pairs = mine // PAIR
    low = lambda *shape: jax.ShapeDtypeStruct(shape, bf16)
    full = lambda *shape: jax.ShapeDtypeStruct(shape, f32)
    outputs = dict(
        gain_sums=full(8, 128),
        grad_tokens=low(rows, width),
        out_tokens=low(rows, width),
        grad_query=full(held, width),
        grad_key=full(held, width),
        grad_value=full(held, width),
        grad_out=full(held, width),
        grad_gate=full(held, hidden_here * shards),
        grad_up=full(held, hidden_here * shards),
        grad_down=full(CHUNKS * piece, width),
        cos=full(shards, batch, shard_len, PAIR),
        sin=full(shards, batch, shard_len, PAIR),
        rotated=low(shards, batch, shard_len, wide),
        attended=low(shards, batch, shard_len, mine),
        normed_one=low(shards, rows, width),
        cot=low(shards, rows, width),
        branch=low(shards, rows, width),
        qkv=low(groups, span, wide),
        out_weight=low(groups, held, width),
        units=low(CHUNKS, groups, span, chunk),
        down=low(CHUNKS, groups, piece, width),
        out_terms=low(shards, rows, width),
        unit_sums=low(CHUNKS, span, chunk),
        unit_terms=low(CHUNKS, width, chunk),
        down_terms=low(CHUNKS, chunk // 2, width),
        kept_units=low(shards * rows, CHUNKS * chunk),
        kept_acts=low(shards * rows, hidden_here),
        head_terms=low(pairs, width, 3 * PAIR),
        wo_terms=low(groups * held, width),
        head_sums=low(pairs, span, 3 * PAIR),
        unit_land=low(CHUNKS, 4, span, chunk),
        down_land=low(CHUNKS, 4, piece, width),
        head_land=low(pairs, 4, span, 3 * PAIR),
        wo_land=low(4, held, width),
        units_out=low(CHUNKS, shards, held, chunk),
        heads_out=low(pairs, shards, held, 3 * PAIR),
    )
    assert tuple(outputs) == tuple(MAIN_OUTPUTS)
    scratch = dict(
        hidden=pltpu.VMEM((rows, width), f32),
        grad_hidden=pltpu.VMEM((rows, width), f32),
        gain_one=pltpu.VMEM((1, width), f32),
        gain_two=pltpu.VMEM((1, width), f32),
        gain_term=pltpu.VMEM((1, width), f32),
        stats=pltpu.VMEM((batch, pairs, 2, shards * shard_len), f32),
        gains_land=pltpu.VMEM((devices, 8, 2 * held), f32),
        gain_mine=pltpu.VMEM((devices, 8, 128), f32),
        gain_sum_land=pltpu.VMEM((devices, 8, 128), f32),
        x=pltpu.VMEM((shards * rows, width), bf16),
        unit_acc=pltpu.VMEM((CHUNKS - 1, 2, span, chunk), bf16),
        down_acc=pltpu.VMEM((CHUNKS - 1, 2, piece, width), bf16),
        mine=pltpu.VMEM((rows, width), bf16),
        stage=pltpu.VMEM((2 * rows, width), bf16),
    )
    for name, buffer in zip(SCATTER_NAMES, scatter_scratch(rows, width)):
        scratch[name] = buffer
    for name in GATHER_NAMES:
        scratch[name] = DMA((GATHER_SEMS,))
    exchanges, sums = 7 * (1 + CHUNKS + pairs), 8 * CHUNKS + 4 * pairs + 4
    for name, count in (
        ("gsend", devices),
        ("grecv", devices),
        ("esend", exchanges),
        ("erecv", exchanges),
        ("zsend", LINE_SEMS * (2 + 2 * CHUNKS)),
        ("zrecv", LINE_SEMS * (2 + 2 * CHUNKS)),
        ("ssend", sums),
        ("srecv", sums),
    ):
        scratch[name] = DMA((count,))
    scratch["ready"] = pltpu.SemaphoreType.REGULAR
    scratch["local"] = DMA((104,))
    assert tuple(scratch) == tuple(MAIN_SCRATCH)
    in_vmem = 1
    done = pl.pallas_call(
        functools.partial(main_kernel, groups),
        out_shape=list(outputs.values()),
        in_specs=[ANY] * 7 + [VMEM] * 5,
        out_specs=[VMEM] * in_vmem + [ANY] * (len(outputs) - in_vmem),
        scratch_shapes=list(scratch.values()),
        compiler_params=pltpu.CompilerParams(
            collective_id=collective_id, has_side_effects=True, vmem_limit_bytes=63 * MIB
        ),
        cost_estimate=lasting(500),
    )(
        w_query,
        w_key,
        w_value,
        w_gate,
        w_up,
        w_out,
        w_down,
        tokens,
        cotangent,
        jnp.broadcast_to(gains.reshape(1, -1).astype(f32), (8, 2 * held)),
        starts,
        jnp.tile(rope_frequency(), 2 * PAIR // HD)[None],
    )
    count = len(RESULTS) - 1
    shapes = list(outputs.values())[1 : 1 + count]
    results = pl.pallas_call(
        hand_over,
        out_shape=shapes,
        in_specs=[ANY] * count,
        out_specs=[ANY] * count,
        scratch_shapes=[*[pltpu.VMEM(s.shape, s.dtype) for s in shapes], DMA((2, count))],
        compiler_params=pltpu.CompilerParams(vmem_limit_bytes=63 * MIB),
    )(*done[1 : 1 + count])
    return types.SimpleNamespace(**dict(zip(RESULTS, [done[0], *results])))


def hand_over(*refs):
    count = (len(refs) - 1) // 3
    ways = [
        [
            pltpu.make_async_copy(refs[way * 2 * count + i], refs[(2 - way) * count + i], refs[-1].at[way, i])
            for i in range(count)
        ]
        for way in range(2)
    ]
    for copy in ways[0]:
        copy.start()
    for copy, out in zip(*ways):
        copy.wait()
        out.start()
    for copy in ways[1]:
        copy.wait()


def layer(
    groups,
    shards,
    tokens,
    doc_ids,
    cotangent,
    norm1_gain,
    w_query,
    w_key,
    w_value,
    w_out,
    norm2_gain,
    w_gate,
    w_up,
    w_down,
):
    rows, shard_len, width = tokens.shape
    count = rows * shard_len
    held = w_query.shape[0]
    hidden_held = w_down.shape[0]
    hidden_here = groups * hidden_held
    whole_heads = held % HD == 0
    outer, inner = (groups, held) if whole_heads else (1, width // shards)
    pairs = width // shards // PAIR
    both = ("dp", "seq")
    fast = groups == 4 and shards == 8
    flat = lambda v: v.reshape(shards * count, v.shape[-1])
    split = lambda v: v.reshape(shards, count, v.shape[-1])

    gains = jnp.stack([norm1_gain, norm2_gain])
    own_tokens = tokens.reshape(count, width)
    own_cotangent = cotangent.reshape(count, width)
    inputs = own_tokens.astype(f32)
    starts = document_starts(doc_ids)
    by_row = lambda v: v.reshape(shards, rows, shard_len, v.shape[-1])

    if fast:
        done = main_plane(
            groups,
            shards,
            rows,
            own_tokens,
            own_cotangent,
            gains,
            (w_query, w_key, w_value, w_out, w_gate, w_up, w_down),
            starts[:, None, :],
            1,
        )
        return (
            done.out_tokens.reshape(tokens.shape),
            done.grad_tokens.reshape(tokens.shape),
            done.gain_sums[0, :held],
            done.grad_query,
            done.grad_key,
            done.grad_value,
            done.grad_out,
            done.gain_sums[1, :held],
            done.grad_gate,
            done.grad_up,
            done.grad_down,
        )

    cos, sin = rope_tables(starts, shards)
    starts = starts[:, None, :]
    gains = lax.all_gather(gains, both, axis=1, tiled=True).astype(f32)
    gain_one, gain_two = gains[:1], gains[1:]

    def by_head(w):
        blocks = w.reshape(held, outer, shards, inner)
        return jnp.moveaxis(blocks, 2, 0).reshape(shards, held, pairs, PAIR)

    blocks = jnp.stack([w_gate, w_up]).reshape(2, held, groups, shards, hidden_held)
    units = jnp.transpose(blocks, (3, 1, 0, 2, 4)).reshape(shards, held, 2 * hidden_here)
    heads = jnp.stack([by_head(w) for w in (w_query, w_key, w_value)], axis=3)
    heads, units = exchange_plane([heads.reshape(shards, held, -1), units], shards, 1)
    spread = lambda w: lax.all_gather(w, "dp", axis=0, tiled=True)
    qkv_weight = spread(heads.reshape(shards * held, -1))
    unit_weight = spread(units.reshape(shards * held, -1))
    down_weight = spread(w_down)
    if whole_heads:
        out_weight = spread(w_out)
    else:
        whole = lax.all_gather(w_out, both, axis=0, tiled=True)
        out_weight = lax.dynamic_slice_in_dim(whole, lax.axis_index("seq") * inner, inner, 0)
    own_normed = (inputs * rms_scale(inputs) * gain_one).astype(bf16)
    normed_one, cot = [flat(v) for v in gather_plane([own_normed, own_cotangent], shards, 2)]
    pre = by_row(dot(normed_one, qkv_weight))
    rotated, attended, stats = attend(pre, cos, sin, starts)
    attended = flat(attended)
    hidden = inputs + reduce_plane(split(dot(attended, out_weight).astype(bf16)))
    normed_two = (hidden * rms_scale(hidden) * gain_two).astype(bf16)
    normed_two = flat(lax.all_gather(normed_two, "seq"))
    gate_weight, up_weight = unit_weight[:, :hidden_here], unit_weight[:, hidden_here:]
    gate_pre, up_pre = dot(normed_two, gate_weight), dot(normed_two, up_weight)
    sigmoid = jax.nn.sigmoid(gate_pre)
    silu = gate_pre * sigmoid
    activated = (silu * up_pre).astype(bf16)
    out_terms = split(dot(activated, down_weight).astype(bf16))
    grad_act = dot_t(cot, down_weight)
    grad_gate_pre = grad_act * up_pre * sigmoid * (1.0 + gate_pre * (1.0 - sigmoid))
    grad_up_pre = grad_act * silu
    grad_units = jnp.concatenate([grad_gate_pre, grad_up_pre], axis=-1).astype(bf16)
    middle_terms = split(dot_t(grad_units, unit_weight).astype(bf16))
    unit_sums = lax.psum_scatter(
        dot(normed_two.T, grad_units).astype(bf16), "dp", scatter_dimension=0, tiled=True
    )
    down_sums = lax.psum_scatter(
        dot(activated.T, cot).astype(bf16), "dp", scatter_dimension=0, tiled=True
    )
    back, gain_two_term = norm_back(
        hidden, rms_scale(hidden), gain_two, reduce_plane(middle_terms)
    )
    grad_hidden = own_cotangent.astype(f32) + back
    branch = lax.all_gather(grad_hidden.astype(bf16), "seq")

    branch = flat(branch)
    out_w_terms = dot(attended.T, branch).astype(bf16)
    grad_attended = by_row(dot_t(branch, out_weight).astype(bf16))
    grad_pre = flat(attend_back(rotated, grad_attended, cos, sin, starts, stats))
    last_terms = split(dot_t(grad_pre, qkv_weight).astype(bf16))
    head_terms = dot(normed_one.T, grad_pre).astype(bf16)

    if whole_heads:
        grad_out = lax.psum_scatter(out_w_terms, "dp", scatter_dimension=0, tiled=True)
    else:
        placed = lax.dynamic_update_slice_in_dim(
            jnp.zeros((width, width), bf16), out_w_terms, lax.axis_index("seq") * inner, 0
        )
        grad_out = lax.psum_scatter(placed, both, scatter_dimension=0, tiled=True)
    back, gain_one_term = norm_back(inputs, rms_scale(inputs), gain_one, reduce_plane(last_terms))
    grad_tokens = (grad_hidden + back).astype(bf16)
    out_tokens = (hidden + reduce_plane(out_terms)).astype(bf16)
    head_sums = lax.psum_scatter(head_terms, "dp", scatter_dimension=0, tiled=True)
    heads_back, units_back = exchange_plane(
        [head_sums.reshape(shards, held, -1), unit_sums.reshape(shards, held, -1)], shards, 6
    )
    grad_norms = lax.psum_scatter(
        jnp.concatenate([gain_one_term, gain_two_term]), both, scatter_dimension=1, tiled=True
    )
    heads_back = heads_back.reshape(shards, held, pairs, 3, PAIR)
    units_back = units_back.reshape(shards, held, 2, groups, hidden_held)

    def head_grad(i):
        blocks = heads_back[:, :, :, i, :].reshape(shards, held, outer, inner)
        return jnp.moveaxis(blocks, 0, 2).reshape(held, width).astype(f32)

    def unit_grad(i):
        return jnp.transpose(units_back[:, :, i], (1, 2, 0, 3)).reshape(held, -1).astype(f32)

    return (
        out_tokens.reshape(tokens.shape),
        grad_tokens.reshape(tokens.shape),
        grad_norms[0],
        head_grad(0),
        head_grad(1),
        head_grad(2),
        grad_out.astype(f32),
        grad_norms[1],
        unit_grad(0),
        unit_grad(1),
        down_sums.astype(f32),
    )


def solution(mesh):
    both = ("dp", "seq")
    return jax.shard_map(
        functools.partial(layer, mesh.shape["dp"], mesh.shape["seq"]),
        mesh=mesh,
        in_specs=(
            P("dp", "seq", None),
            P("dp", None),
            P("dp", "seq", None),
            P(both),
            P(both, None),
            P(both, None),
            P(both, None),
            P(both, None),
            P(both),
            P(both, None),
            P(both, None),
            P(both, None),
        ),
        out_specs=(
            P("dp", "seq", None),
            P("dp", "seq", None),
            P(both),
            P(both, None),
            P(both, None),
            P(both, None),
            P(both, None),
            P(both),
            P(both, None),
            P(both, None),
            P(both, None),
        ),
        check_vma=False,
    )
```
